32 devices in a mesh: dp: 4 (over x, core), seq: 2 (over y), tensor: 4 (over z).
Axes of the slice: x: 2, y: 2, z: 4, core: 2. Of those that a mesh axis runs over, the one named last changes fastest.
Arguments:
- tokens: bfloat16 [8, 2, 544, 2304], P('dp', 'seq'), may hold values from -6 to 6
- cotangent: bfloat16 [8, 2, 544, 2304], P('dp', 'seq'), may hold values from -6 to 6
- prompt_of: int32 [8, 2], P('dp', 'seq'), may hold values from 0 to 1
- query_weight: bfloat16 [2304, 2048], P(('dp', 'seq'), 'tensor'), may hold values from -0.125 to 0.125
- key_weight: bfloat16 [2304, 1024], P(('dp', 'seq'), 'tensor'), may hold values from -0.125 to 0.125
- value_weight: bfloat16 [2304, 1024], P(('dp', 'seq'), 'tensor'), may hold values from -0.125 to 0.125
- out_weight: bfloat16 [2048, 2304], P('tensor', ('dp', 'seq')), may hold values from -0.125 to 0.125
- gate_weight: bfloat16 [2304, 9216], P(('dp', 'seq'), 'tensor'), may hold values from -0.125 to 0.125
- up_weight: bfloat16 [2304, 9216], P(('dp', 'seq'), 'tensor'), may hold values from -0.125 to 0.125
- down_weight: bfloat16 [9216, 2304], P('tensor', ('dp', 'seq')), may hold values from -0.0625 to 0.0625
- norm_gains: bfloat16 [4, 2304], P(None, ('dp', 'seq')), may hold values from 0.099609375 to 1.8984375
Outputs:
- output: bfloat16 [8, 2, 544, 2304], P('dp', 'seq')
- input_grad: float32 [8, 2, 544, 2304], P('dp', 'seq')
- grad_query: float32 [2304, 2048], P(('dp', 'seq'), 'tensor')
- grad_key: float32 [2304, 1024], P(('dp', 'seq'), 'tensor')
- grad_value: float32 [2304, 1024], P(('dp', 'seq'), 'tensor')
- grad_out: float32 [2048, 2304], P('tensor', ('dp', 'seq'))
- grad_gate: float32 [2304, 9216], P(('dp', 'seq'), 'tensor')
- grad_up: float32 [2304, 9216], P(('dp', 'seq'), 'tensor')
- grad_down: float32 [9216, 2304], P('tensor', ('dp', 'seq'))
- grad_gains: float32 [4, 2304], P(None, ('dp', 'seq'))
The draws below stay inside these ranges and needn't reach their ends.
Inputs may be any that keep to these rules, and one draw needn't show every extreme that they name: prompt_of[g, s] names one of the 2 groups held by the same index of dp.
All inputs are finite; a program needn't handle non-finite values.
Results may differ from the reference program's by a relative error of at most 0.025.
Values may be sent and summed in bfloat16 or wider, within the bound.
A program may use at most 320 MiB of HBM per device.

```python
import jax
import jax.numpy as jnp
from jax import lax

D = 2304
FF = 9216
HEAD = 256
QH = 8
KVH = 4
CONT = 32
MICRO = 2
PROMPT = 1024
P_DEV = 512
ROWS = 544
GROUPS = 8
N_DP = 4
N_SEQ = 2


def with_ends(values, stream_key, smallest, high):
    extent = values.shape
    spot = [jax.random.randint(jax.random.fold_in(stream_key, axis), (), 0, extent[axis]) for axis in range(len(extent))]
    values = values.at[tuple(spot)].set(smallest)
    longest = extent.index(max(extent))
    spot[longest] = (spot[longest] + 1) % extent[longest]
    return values.at[tuple(spot)].set(high)


def shard_levels(rng, shape, split, smallest, high):
    def one(axis_at, blocks):
        steps = jax.random.uniform(jax.random.fold_in(jax.random.fold_in(rng, 6), axis_at), (blocks,), jnp.float32, smallest / len(split), high / len(split))
        return jnp.repeat(jnp.exp(steps), shape[axis_at] // blocks).reshape((-1,) + (1,) * (len(shape) - axis_at - 1))

    factor_of = one(*split[0])
    for cut in split[1:]:
        factor_of = factor_of * one(*cut)
    return factor_of


def noise(key, shape, scale, bound, split=(), kind=jnp.bfloat16):
    level = shard_levels(key, shape, split, -0.22, 0.18) if split else 1.0
    values = jax.random.normal(key, shape, jnp.float32) * scale * level
    return jnp.minimum(jnp.maximum(values, -bound), bound).astype(kind)


def setup_inputs(seed: int = 0) -> dict:
    splits = jax.random.split(jax.random.key(seed), 12)
    return {
        "tokens": noise(splits[0], (GROUPS, N_SEQ, ROWS, D), 1.0, 6.0, ((0, 4), (1, 2))),
        "cotangent": noise(splits[1], (GROUPS, N_SEQ, ROWS, D), 1.0, 6.0, ((0, 4), (1, 2))),
        "prompt_of": with_ends(jax.random.randint(splits[2], (GROUPS, N_SEQ), 0, MICRO), jax.random.fold_in(splits[2], 1), 0, MICRO - 1).astype(jnp.int32),
        "query_weight": noise(splits[3], (D, QH * HEAD), D ** -0.5, 0.125, ((0, 8), (1, 4))),
        "key_weight": noise(splits[4], (D, KVH * HEAD), D ** -0.5, 0.125, ((0, 8), (1, 4))),
        "value_weight": noise(splits[5], (D, KVH * HEAD), D ** -0.5, 0.125, ((0, 8), (1, 4))),
        "out_weight": noise(splits[6], (QH * HEAD, D), (QH * HEAD) ** -0.5, 0.125, ((0, 4), (1, 8))),
        "gate_weight": noise(splits[7], (D, FF), D ** -0.5, 0.125, ((0, 8), (1, 4))),
        "up_weight": noise(splits[8], (D, FF), D ** -0.5, 0.125, ((0, 8), (1, 4))),
        "down_weight": noise(splits[9], (FF, D), FF ** -0.5, 0.0625, ((0, 4), (1, 8))),
        "norm_gains": jnp.clip(1.0 + 0.18 * jax.random.normal(splits[10], (4, D), jnp.float32), 0.099609375, 1.8984375).astype(jnp.bfloat16),
    }


EPS = 1e-06
SOFTCAP = 50.0
THETA = 10000.0
HIGH = lax.Precision.HIGHEST

@jax.custom_vjp
def low(v):
    return lax.optimization_barrier(v.astype(jnp.bfloat16)).astype(jnp.float32)

@jax.custom_vjp
def low_back(v):
    return v

def low_keep(v):
    return (low(v), None)

def low_pass(kept, grad):
    return (grad,)

def back_keep(v):
    return (v, None)

def back_low(kept, grad):
    return (low(grad),)
low.defvjp(low_keep, low_pass)
low_back.defvjp(back_keep, back_low)

def normalize(values):
    return values * lax.rsqrt(lax.optimization_barrier(jnp.mean(values * values, axis=-1, keepdims=True)) + EPS)

def rotate(values, places):
    half_width = values.shape[-1] // 2
    spectrum = THETA ** (-2.0 * jnp.arange(half_width, dtype=jnp.float32) / values.shape[-1])
    angles = places.astype(jnp.float32)[..., None] * spectrum
    angles = jnp.concatenate([angles, angles], axis=-1)[..., None, :]
    turned = jnp.concatenate([-values[..., half_width:], values[..., :half_width]], axis=-1)
    return values * jnp.cos(angles) + turned * jnp.sin(angles)

def project(left, right):
    return jnp.einsum('...i,ij->...j', left, right, precision=HIGH)

def visibility(seq_pos, owners):
    local_rows = jnp.arange(ROWS)
    prompt_rows = local_rows < P_DEV
    places_local = jnp.where(prompt_rows, seq_pos * P_DEV + local_rows, PROMPT + local_rows - P_DEV)
    micro_ids = jnp.arange(MICRO)
    row_micro = jnp.repeat(micro_ids, ROWS)
    row_prompt = jnp.tile(prompt_rows, MICRO)
    row_place = jnp.tile(places_local, MICRO)
    first_slot = jnp.where(row_prompt, row_micro, jnp.repeat(owners, ROWS))
    second_slot = jnp.where(row_prompt, -1, MICRO + row_micro)
    key_slot = jnp.concatenate([jnp.repeat(micro_ids, PROMPT), MICRO + jnp.repeat(micro_ids, CONT)])
    key_place = jnp.concatenate([jnp.tile(jnp.arange(PROMPT), MICRO), PROMPT + jnp.tile(jnp.arange(CONT), MICRO)])
    matched = (key_slot[None, :] == first_slot[:, None]) | (key_slot[None, :] == second_slot[:, None])
    return matched & (key_place[None, :] <= row_place[:, None])

def attend_block(query, prompt_keys, prompt_values, cont_keys, cont_values, owners, seq_pos):
    key_rows = jnp.concatenate([prompt_keys, cont_keys], axis=0)
    value_rows = jnp.concatenate([prompt_values, cont_values], axis=0)
    raw_scores = low_back(jnp.einsum('rgjd,kgd->gjrk', query, key_rows, precision=HIGH))
    curved = jnp.tanh(raw_scores * HEAD ** (-0.5) / SOFTCAP)
    masked = jnp.where(visibility(seq_pos, owners)[None, None], SOFTCAP * curved, -1e+30)
    row_peak = lax.optimization_barrier(jnp.max(masked, axis=-1, keepdims=True))
    weights = jnp.exp(masked - row_peak)
    probs = low(weights / lax.optimization_barrier(jnp.sum(weights, axis=-1, keepdims=True)))
    return jnp.einsum('gjrk,kgd->rgjd', probs, value_rows, precision=HIGH)

def reference(tokens, cotangent, prompt_of, query_weight, key_weight, value_weight, out_weight, gate_weight, up_weight, down_weight, norm_gains):
    group_size = QH // KVH
    local_rows = jnp.arange(ROWS)
    places = jnp.where(local_rows[None, :] < P_DEV, jnp.arange(N_SEQ)[:, None] * P_DEV + local_rows[None, :], PROMPT + local_rows[None, :] - P_DEV)
    owner_grid = prompt_of.reshape(N_DP, MICRO, N_SEQ).transpose(0, 2, 1)

    def layer(inputs, w_query, w_key, w_value, w_out, w_gate, w_up, w_down, gain_rows):
        normed_in = low(normalize(inputs) * gain_rows[0])
        query_raw = low_back(project(normed_in, w_query)).reshape(GROUPS, N_SEQ, ROWS, QH, HEAD)
        query_rows = low(rotate(query_raw, places))
        key_raw = low_back(project(normed_in, w_key)).reshape(GROUPS, N_SEQ, ROWS, KVH, HEAD)
        key_rows = low(rotate(key_raw, places))
        value_rows = low(low_back(project(normed_in, w_value))).reshape(GROUPS, N_SEQ, ROWS, KVH, HEAD)
        query_blocks = query_rows.reshape(N_DP, MICRO, N_SEQ, ROWS, KVH, group_size, HEAD).transpose(0, 2, 1, 3, 4, 5, 6).reshape(N_DP, N_SEQ, MICRO * ROWS, KVH, group_size, HEAD)
        key_grid = key_rows.reshape(N_DP, MICRO, N_SEQ, ROWS, KVH, HEAD)
        value_grid = value_rows.reshape(N_DP, MICRO, N_SEQ, ROWS, KVH, HEAD)
        prompt_keys = key_grid[:, :, :, :P_DEV].reshape(N_DP, MICRO * PROMPT, KVH, HEAD)
        prompt_values = value_grid[:, :, :, :P_DEV].reshape(N_DP, MICRO * PROMPT, KVH, HEAD)
        cont_keys = key_grid[:, :, :, P_DEV:].transpose(0, 2, 1, 3, 4, 5).reshape(N_DP, N_SEQ, MICRO * CONT, KVH, HEAD)
        cont_values = value_grid[:, :, :, P_DEV:].transpose(0, 2, 1, 3, 4, 5).reshape(N_DP, N_SEQ, MICRO * CONT, KVH, HEAD)

        def batch_step(packed):
            batch_query, batch_pk, batch_pv, batch_ck, batch_cv, batch_owner = packed

            def block_step(inner):
                block_query, block_ck, block_cv, block_owner, seq_pos = inner
                return jax.checkpoint(attend_block)(block_query, batch_pk, batch_pv, block_ck, block_cv, block_owner, seq_pos)
            return lax.map(block_step, (batch_query, batch_ck, batch_cv, batch_owner, jnp.arange(N_SEQ)))
        context = lax.map(jax.checkpoint(batch_step), (query_blocks, prompt_keys, prompt_values, cont_keys, cont_values, owner_grid))
        context = context.reshape(N_DP, N_SEQ, MICRO, ROWS, QH * HEAD).transpose(0, 2, 1, 3, 4).reshape(GROUPS, N_SEQ, ROWS, QH * HEAD)
        context = low_back(low(context))
        attn = low_back(project(context, w_out))
        middle = inputs + normalize(attn) * gain_rows[1]

        def feed(middle_rows):
            ffn_in = low(normalize(middle_rows) * gain_rows[2])
            gate = low_back(project(ffn_in, w_gate))
            up_val = low_back(project(ffn_in, w_up))
            hidden = low(jax.nn.gelu(gate, approximate=True) * up_val)
            ffn = low_back(project(hidden, w_down))
            return middle_rows + normalize(ffn) * gain_rows[3]
        return lax.map(jax.checkpoint(feed), middle)
    floats = tuple((member.astype(jnp.float32) for member in (tokens, query_weight, key_weight, value_weight, out_weight, gate_weight, up_weight, down_weight, norm_gains)))
    result, pull = jax.vjp(layer, *floats)
    grads = pull(cotangent.astype(jnp.float32))
    return (result.astype(jnp.bfloat16), grads[0], grads[1], grads[2], grads[3], grads[4], grads[5], grads[6], grads[7], grads[8])
```

```python
import functools

import jax
import jax.numpy as jnp
from jax import lax
from jax.experimental import pallas as pl
from jax.experimental.pallas import tpu as pltpu
from jax.sharding import PartitionSpec as P

MESH = pl.DeviceIdType.MESH

HEAD = 256
CONT = 32


EPS = 1e-06
SOFTCAP = 50.0
THETA = 10000.0


def chain_kernel(size, width, x_ref, o_ref, low_buf, high_buf, *sems):
    low_in, low_out, low_last_in, low_last_out, high_in, high_out, high_last_in, high_last_out = sems
    place = lax.axis_index("tensor")
    dp, seq = lax.axis_index("dp"), lax.axis_index("seq")
    down = (dp, seq, jnp.maximum(place - 1, 0))
    up = (dp, seq, jnp.minimum(place + 1, size - 1))
    first, last = place == 0, place == size - 1
    chunks = x_ref.shape[1] // width
    half = x_ref.shape[0] // 2
    rows = (pl.ds(0, half), pl.ds(half, half))
    barrier = pltpu.get_barrier_semaphore()

    @pl.when(jnp.logical_not(first))
    def _():
        pl.semaphore_signal(barrier, inc=1, device_id=down, device_id_type=MESH)

    @pl.when(jnp.logical_not(last))
    def _():
        pl.semaphore_signal(barrier, inc=1, device_id=up, device_id_type=MESH)
    pl.semaphore_wait(barrier, 2 - first.astype(jnp.int32) - last.astype(jnp.int32))

    def columns(c):
        return pl.ds(pl.multiple_of(c * width, 128), width)

    def side(which):
        buf = (low_buf, high_buf)[which]
        sin, sout, lin, lout = (sems[4 * which: 4 * which + 4])
        toward = (down, up)[which]
        back = (up, down)[which]
        start = (last, first)[which]
        end = (first, last)[which]
        rank = (size - 1 - place, place)[which]
        rs = rows[which]

        def passing(c, src):
            return pltpu.make_async_remote_copy(src, buf.at[c], sout.at[c], sin.at[c], device_id=toward, device_id_type=MESH)

        def sharing(c, ):
            view = o_ref.at[rs, columns(c)]
            return pltpu.make_async_remote_copy(view, view, lout.at[c], lin.at[c], device_id=back, device_id_type=MESH)

        def reduce_step(s):
            c = s - rank
            ok = (c >= 0) & (c < chunks)

            @pl.when(ok & start)
            def _():
                passing(c, x_ref.at[rs, columns(c)]).start()

            @pl.when(ok & jnp.logical_not(start))
            def _():
                passing(c, buf.at[c]).wait_recv()
                total = buf[c].astype(jnp.float32) + x_ref[rs, columns(c)].astype(jnp.float32)

                @pl.when(end)
                def _():
                    o_ref[rs, columns(c)] = total.astype(jnp.bfloat16)
                    sharing(c).start()

                @pl.when(jnp.logical_not(end))
                def _():
                    buf[c] = total.astype(jnp.bfloat16)
                    passing(c, buf.at[c]).start()

        def share_step(s):
            c = s - (size - 1) - (size - 1 - rank)
            ok = (c >= 0) & (c < chunks)

            @pl.when(ok & jnp.logical_not(end))
            def _():
                sharing(c).wait_recv()

                @pl.when(jnp.logical_not(start))
                def _():
                    sharing(c).start()

        def finish(c):
            @pl.when(jnp.logical_not(end))
            def _():
                passing(c, buf.at[c]).wait_send()

            @pl.when(jnp.logical_not(start))
            def _():
                sharing(c).wait_send()
        return reduce_step, share_step, finish

    sides = [side(0), side(1)]

    @pl.loop(0, chunks + 2 * (size - 1))
    def _(s):
        for one in sides:
            one[0](s)
        for one in sides:
            one[1](s)

    @pl.loop(0, chunks)
    def _(c):
        for one in sides:
            one[2](c)


def chain_sum(x, cid, width=256):
    size = lax.axis_size("tensor")
    rows, cols = x.shape
    chunks = cols // width
    return pl.pallas_call(
        functools.partial(chain_kernel, size, width),
        out_shape=jax.ShapeDtypeStruct(x.shape, jnp.bfloat16),
        in_specs=[pl.BlockSpec(memory_space=pltpu.VMEM)],
        out_specs=pl.BlockSpec(memory_space=pltpu.VMEM),
        scratch_shapes=[pltpu.VMEM((chunks, rows // 2, width), jnp.bfloat16)] * 2
        + [pltpu.SemaphoreType.DMA((chunks,))] * 8,
        compiler_params=pltpu.CompilerParams(collective_id=cid, has_side_effects=True, vmem_limit_bytes=48 * 2**20),
        cost_estimate=pl.CostEstimate(flops=rows*cols, bytes_accessed=200*2**20, transcendentals=0),
    )(x)


def normalize(values):
    return values * lax.rsqrt(jnp.mean(values * values, axis=-1, keepdims=True) + EPS)


def norm_back(values, gain, upstream):
    inverse = lax.rsqrt(jnp.mean(values * values, axis=-1, keepdims=True) + EPS)
    normed = values * inverse
    scaled = upstream * gain
    backed = inverse * (scaled - normed * jnp.mean(scaled * normed, axis=-1, keepdims=True))
    return (backed, jnp.sum(upstream * normed, axis=0))


def rotate(values, places):
    half_width = values.shape[-1] // 2
    spectrum = THETA ** (-2.0 * jnp.arange(half_width, dtype=jnp.float32) / values.shape[-1])
    angles = places.astype(jnp.float32)[..., None] * spectrum
    angles = jnp.concatenate([angles, angles], axis=-1)[..., None, :]
    turned = jnp.concatenate([-values[..., half_width:], values[..., :half_width]], axis=-1)
    return values * jnp.cos(angles) + turned * jnp.sin(angles)


def visibility(micro_count, row_count, prompt_dev, prompt_all, cont_rows, seq_pos, owners):
    local_rows = jnp.arange(row_count)
    prompt_rows = local_rows < prompt_dev
    places_local = jnp.where(
        prompt_rows, seq_pos * prompt_dev + local_rows, prompt_all + local_rows - prompt_dev
    )
    micro_ids = jnp.arange(micro_count)
    row_micro = jnp.repeat(micro_ids, row_count)
    row_prompt = jnp.tile(prompt_rows, micro_count)
    row_place = jnp.tile(places_local, micro_count)
    first_slot = jnp.where(row_prompt, row_micro, jnp.repeat(owners, row_count))
    second_slot = jnp.where(row_prompt, -1, micro_count + row_micro)
    key_slot = jnp.concatenate(
        [jnp.repeat(micro_ids, prompt_all), micro_count + jnp.repeat(micro_ids, cont_rows)]
    )
    key_place = jnp.concatenate(
        [
            jnp.tile(jnp.arange(prompt_all), micro_count),
            prompt_all + jnp.tile(jnp.arange(cont_rows), micro_count),
        ]
    )
    matched = (key_slot[None, :] == first_slot[:, None]) | (
        key_slot[None, :] == second_slot[:, None]
    )
    return (matched & (key_place[None, :] <= row_place[:, None]), row_place)


def scores_for(query, key_rows, visible, score_scale):
    raw_scores = jnp.einsum("rd,kd->rk", query, key_rows, preferred_element_type=jnp.float32)
    curved = jnp.tanh(raw_scores * score_scale / SOFTCAP)
    return (curved, jnp.where(visible, SOFTCAP * curved, -1e30))


def per_device(
    tokens,
    cotangent,
    prompt_of,
    query_weight,
    key_weight,
    value_weight,
    out_weight,
    gate_weight,
    up_weight,
    down_weight,
    norm_gains,
):
    micro_count = tokens.shape[0]
    row_count = tokens.shape[2]
    model_width = tokens.shape[3]
    seq_count = lax.axis_size("seq")
    seq_pos = lax.axis_index("seq")
    prompt_dev = row_count - CONT
    prompt_all = prompt_dev * seq_count
    total_rows = micro_count * row_count
    score_scale = HEAD ** (-0.5)
    visible, places = visibility(
        micro_count, row_count, prompt_dev, prompt_all, CONT, seq_pos, prompt_of[:, 0]
    )
    axes = ("dp", "seq")
    query_width = query_weight.shape[1]
    side_weights = jnp.concatenate(
        [
            query_weight,
            key_weight,
            value_weight,
            jnp.pad(norm_gains.T, ((0, 0), (0, 128 - norm_gains.shape[0]))),
        ],
        axis=1,
    )
    full_side = lax.all_gather(side_weights, axes, axis=0, tiled=True)
    full_query = full_side[:, :query_width]
    full_key = full_side[:, query_width : query_width + HEAD]
    full_value = full_side[:, query_width + HEAD : query_width + 2 * HEAD]
    gain_rows = full_side[:, query_width + 2 * HEAD : query_width + 2 * HEAD + 4].T
    full_out = lax.all_gather(out_weight, axes, axis=1, tiled=True)
    full_gate = lax.all_gather(gate_weight, axes, axis=0, tiled=True)
    full_up = lax.all_gather(up_weight, axes, axis=0, tiled=True)
    full_down = lax.all_gather(down_weight, axes, axis=1, tiled=True)
    gain_float = gain_rows.astype(jnp.float32)
    inputs = tokens.reshape(total_rows, model_width).astype(jnp.float32)
    normed_in = (normalize(inputs) * gain_float[0]).astype(jnp.bfloat16)
    query_heads = jnp.dot(normed_in, full_query, preferred_element_type=jnp.float32).reshape(
        total_rows, -1, HEAD
    )
    key_heads = jnp.dot(normed_in, full_key, preferred_element_type=jnp.float32).reshape(
        total_rows, 1, HEAD
    )
    value_raw = jnp.dot(normed_in, full_value, preferred_element_type=jnp.float32)
    query_rows = rotate(query_heads, places).astype(jnp.bfloat16)
    key_local = rotate(key_heads, places)[:, 0].astype(jnp.bfloat16)
    value_local = value_raw.astype(jnp.bfloat16)
    key_grid = key_local.reshape(micro_count, row_count, HEAD)
    value_grid = value_local.reshape(micro_count, row_count, HEAD)
    own_pair = jnp.concatenate([key_grid[:, :prompt_dev], value_grid[:, :prompt_dev]], axis=2)
    if seq_count == 2:
        other_pair = lax.ppermute(own_pair, "seq", [(0, 1), (1, 0)])
        early = seq_pos == 0
        prompt_pair = jnp.concatenate(
            [jnp.where(early, own_pair, other_pair), jnp.where(early, other_pair, own_pair)], axis=1
        )
    else:
        prompt_pair = lax.all_gather(own_pair, "seq", axis=1, tiled=True)
    prompt_keys, prompt_values = prompt_pair[..., :HEAD], prompt_pair[..., HEAD:]
    key_rows = jnp.concatenate(
        [
            prompt_keys.reshape(micro_count * prompt_all, HEAD),
            key_grid[:, prompt_dev:].reshape(micro_count * CONT, HEAD),
        ],
        axis=0,
    )
    value_rows = jnp.concatenate(
        [
            prompt_values.reshape(micro_count * prompt_all, HEAD),
            value_grid[:, prompt_dev:].reshape(micro_count * CONT, HEAD),
        ],
        axis=0,
    )
    head_count = query_rows.shape[1]
    contexts = []
    log_sums = []
    for head_pos in range(head_count):
        curved, masked = scores_for(query_rows[:, head_pos], key_rows, visible, score_scale)
        row_peak = jnp.max(masked, axis=-1, keepdims=True)
        weights = jnp.exp(masked - row_peak)
        summed = jnp.sum(weights, axis=-1, keepdims=True)
        probs = (weights / summed).astype(jnp.bfloat16)
        contexts.append(jnp.dot(probs, value_rows, preferred_element_type=jnp.float32))
        log_sums.append(row_peak + jnp.log(summed))
    context = jnp.stack(contexts, axis=1).reshape(total_rows, -1).astype(jnp.bfloat16)
    attn = chain_sum(
        jnp.dot(context, full_out, preferred_element_type=jnp.float32).astype(jnp.bfloat16),
        0,
    ).astype(jnp.float32)
    middle = inputs + normalize(attn) * gain_float[1]
    ffn_in = (normalize(middle) * gain_float[2]).astype(jnp.bfloat16)
    gate = jnp.dot(ffn_in, full_gate, preferred_element_type=jnp.float32)
    up_val = jnp.dot(ffn_in, full_up, preferred_element_type=jnp.float32)
    hidden_act, glu_pull = jax.vjp(
        lambda gate_in, up_in: jax.nn.gelu(gate_in, approximate=True) * up_in, gate, up_val
    )
    hidden = hidden_act.astype(jnp.bfloat16)
    ffn = chain_sum(
        jnp.dot(hidden, full_down, preferred_element_type=jnp.float32).astype(jnp.bfloat16),
        1,
    ).astype(jnp.float32)
    result = middle + normalize(ffn) * gain_float[3]
    upstream = cotangent.reshape(total_rows, model_width).astype(jnp.float32)
    d_ffn, gain_fourth = norm_back(ffn, gain_float[3], upstream)
    d_ffn = d_ffn.astype(jnp.bfloat16)
    grad_down = jnp.einsum("rf,rd->fd", hidden, d_ffn, preferred_element_type=jnp.float32)
    d_hidden = jnp.einsum("rd,fd->rf", d_ffn, full_down, preferred_element_type=jnp.float32)
    d_gate, d_up = glu_pull(d_hidden)
    d_gate = d_gate.astype(jnp.bfloat16)
    d_up = d_up.astype(jnp.bfloat16)
    grad_gate = jnp.einsum("rd,rf->df", ffn_in, d_gate, preferred_element_type=jnp.float32)
    grad_up = jnp.einsum("rd,rf->df", ffn_in, d_up, preferred_element_type=jnp.float32)
    ffn_part = jnp.einsum(
        "rf,df->rd", d_gate, full_gate, preferred_element_type=jnp.float32
    ) + jnp.einsum("rf,df->rd", d_up, full_up, preferred_element_type=jnp.float32)
    d_ffn_in = chain_sum(ffn_part.astype(jnp.bfloat16), 2).astype(jnp.float32)
    d_mid_norm, gain_third = norm_back(middle, gain_float[2], d_ffn_in)
    d_middle = upstream + d_mid_norm
    d_attn, gain_second = norm_back(attn, gain_float[1], d_middle)
    d_attn = d_attn.astype(jnp.bfloat16)
    grad_out = jnp.einsum("rc,rd->cd", context, d_attn, preferred_element_type=jnp.float32)
    d_context = (
        jnp.einsum("rd,cd->rc", d_attn, full_out, preferred_element_type=jnp.float32)
        .astype(jnp.bfloat16)
        .reshape(total_rows, head_count, HEAD)
    )
    key_grad = jnp.zeros((key_rows.shape[0], HEAD), jnp.float32)
    value_grad = jnp.zeros((key_rows.shape[0], HEAD), jnp.float32)
    query_grads = []
    for head_pos in range(head_count):
        curved, masked = scores_for(query_rows[:, head_pos], key_rows, visible, score_scale)
        probs = jnp.where(visible, jnp.exp(masked - log_sums[head_pos]), 0.0)
        probs_low = probs.astype(jnp.bfloat16)
        d_probs = jnp.einsum(
            "rd,kd->rk", d_context[:, head_pos], value_rows, preferred_element_type=jnp.float32
        )
        inner_sum = jnp.sum(probs * d_probs, axis=-1, keepdims=True)
        d_scores = (probs * (d_probs - inner_sum) * score_scale * (1.0 - curved * curved)).astype(
            jnp.bfloat16
        )
        query_grads.append(jnp.dot(d_scores, key_rows, preferred_element_type=jnp.float32))
        key_grad = key_grad + jnp.einsum(
            "rk,rd->kd", d_scores, query_rows[:, head_pos], preferred_element_type=jnp.float32
        )
        value_grad = value_grad + jnp.einsum(
            "rk,rd->kd", probs_low, d_context[:, head_pos], preferred_element_type=jnp.float32
        )
    split_at = micro_count * prompt_all
    pair_grad = jnp.concatenate(
        [
            key_grad[:split_at].reshape(micro_count, prompt_all, HEAD),
            value_grad[:split_at].reshape(micro_count, prompt_all, HEAD),
        ],
        axis=2,
    )
    if seq_count == 2:
        low_part, high_part = pair_grad[:, :prompt_dev], pair_grad[:, prompt_dev:]
        early = seq_pos == 0
        sent = jnp.where(early, high_part, low_part).astype(jnp.bfloat16)
        kept = jnp.where(early, low_part, high_part)
        pair_grad = kept + lax.ppermute(sent, "seq", [(0, 1), (1, 0)]).astype(jnp.float32)
    else:
        pair_grad = lax.psum_scatter(
            pair_grad.astype(jnp.bfloat16), "seq", scatter_dimension=1, tiled=True
        ).astype(jnp.float32)
    prompt_key_grad, prompt_value_grad = pair_grad[..., :HEAD], pair_grad[..., HEAD:]
    own_keys = jnp.concatenate(
        [prompt_key_grad, key_grad[split_at:].reshape(micro_count, CONT, HEAD)], axis=1
    ).reshape(total_rows, HEAD)
    own_values = jnp.concatenate(
        [prompt_value_grad, value_grad[split_at:].reshape(micro_count, CONT, HEAD)], axis=1
    ).reshape(total_rows, HEAD)
    unused_query, unturn_query = jax.vjp(lambda turned_in: rotate(turned_in, places), query_heads)
    d_query = (
        unturn_query(jnp.stack(query_grads, axis=1))[0].reshape(total_rows, -1).astype(jnp.bfloat16)
    )
    unused_key, unturn_key = jax.vjp(lambda turned_in: rotate(turned_in, places), key_heads)
    d_key = unturn_key(own_keys[:, None, :])[0].reshape(total_rows, HEAD).astype(jnp.bfloat16)
    d_value = own_values.astype(jnp.bfloat16)
    grad_query = jnp.einsum("rd,rc->dc", normed_in, d_query, preferred_element_type=jnp.float32)
    grad_key = jnp.einsum("rd,rc->dc", normed_in, d_key, preferred_element_type=jnp.float32)
    grad_value = jnp.einsum("rd,rc->dc", normed_in, d_value, preferred_element_type=jnp.float32)
    attn_part = jnp.einsum("rc,dc->rd", d_query, full_query, preferred_element_type=jnp.float32)
    attn_part = attn_part + jnp.einsum(
        "rc,dc->rd", d_key, full_key, preferred_element_type=jnp.float32
    )
    attn_part = attn_part + jnp.einsum(
        "rc,dc->rd", d_value, full_value, preferred_element_type=jnp.float32
    )
    d_normed = chain_sum(attn_part.astype(jnp.bfloat16), 3).astype(jnp.float32)
    d_in_norm, gain_first = norm_back(inputs, gain_float[0], d_normed)
    input_grad = d_middle + d_in_norm
    grad_gains = jnp.stack([gain_first, gain_second, gain_third, gain_fourth], axis=0)
    def scatter(grad, axis):
        return lax.psum_scatter(
            grad.astype(jnp.bfloat16), axes, scatter_dimension=axis, tiled=True
        ).astype(jnp.float32)

    side_grad = scatter(
        jnp.concatenate(
            [
                grad_query,
                grad_key,
                grad_value,
                jnp.pad(grad_gains.T, ((0, 0), (0, 128 - grad_gains.shape[0]))),
            ],
            axis=1,
        ),
        0,
    )
    shares = (
        side_grad[:, :query_width],
        side_grad[:, query_width : query_width + HEAD],
        side_grad[:, query_width + HEAD : query_width + 2 * HEAD],
        scatter(grad_out, 1),
        scatter(grad_gate, 0),
        scatter(grad_up, 0),
        scatter(grad_down, 1),
        side_grad[:, query_width + 2 * HEAD : query_width + 2 * HEAD + 4].T,
    )
    return (
        result.reshape(tokens.shape).astype(jnp.bfloat16),
        input_grad.reshape(tokens.shape),
        shares[0],
        shares[1],
        shares[2],
        shares[3],
        shares[4],
        shares[5],
        shares[6],
        shares[7],
    )


def solution(mesh):
    placed = (
        P("dp", "seq", None, None),
        P("dp", "seq", None, None),
        P("dp", "seq"),
        P(("dp", "seq"), "tensor"),
        P(("dp", "seq"), "tensor"),
        P(("dp", "seq"), "tensor"),
        P("tensor", ("dp", "seq")),
        P(("dp", "seq"), "tensor"),
        P(("dp", "seq"), "tensor"),
        P("tensor", ("dp", "seq")),
        P(None, ("dp", "seq")),
    )
    return jax.shard_map(
        per_device,
        mesh=mesh,
        in_specs=placed,
        out_specs=(
            P("dp", "seq", None, None),
            P("dp", "seq", None, None),
            P(("dp", "seq"), "tensor"),
            P(("dp", "seq"), "tensor"),
            P(("dp", "seq"), "tensor"),
            P("tensor", ("dp", "seq")),
            P(("dp", "seq"), "tensor"),
            P(("dp", "seq"), "tensor"),
            P("tensor", ("dp", "seq")),
            P(None, ("dp", "seq")),
        ),
        check_vma=False,
    )
```

```python
import functools

import jax
import jax.numpy as jnp
from jax import lax
from jax.experimental import pallas as pl
from jax.experimental.pallas import tpu as pltpu
from jax.sharding import PartitionSpec as P

MESH = pl.DeviceIdType.MESH

HEAD = 256
CONT = 32


EPS = 1e-06
SOFTCAP = 50.0
THETA = 10000.0


def chain_kernel(size, width, x_ref, o_ref, low_buf, high_buf, *sems):
    low_in, low_out, low_last_in, low_last_out, high_in, high_out, high_last_in, high_last_out = sems
    place = lax.axis_index("tensor")
    dp, seq = lax.axis_index("dp"), lax.axis_index("seq")
    down = (dp, seq, jnp.maximum(place - 1, 0))
    up = (dp, seq, jnp.minimum(place + 1, size - 1))
    first, last = place == 0, place == size - 1
    chunks = x_ref.shape[1] // width
    half = x_ref.shape[0] // 2
    rows = (pl.ds(0, half), pl.ds(half, half))
    barrier = pltpu.get_barrier_semaphore()

    @pl.when(jnp.logical_not(first))
    def _():
        pl.semaphore_signal(barrier, inc=1, device_id=down, device_id_type=MESH)

    @pl.when(jnp.logical_not(last))
    def _():
        pl.semaphore_signal(barrier, inc=1, device_id=up, device_id_type=MESH)
    pl.semaphore_wait(barrier, 2 - first.astype(jnp.int32) - last.astype(jnp.int32))

    def columns(c):
        return pl.ds(pl.multiple_of(c * width, 128), width)

    def side(which):
        buf = (low_buf, high_buf)[which]
        sin, sout, lin, lout = (sems[4 * which: 4 * which + 4])
        toward = (down, up)[which]
        back = (up, down)[which]
        start = (last, first)[which]
        end = (first, last)[which]
        rank = (size - 1 - place, place)[which]
        rs = rows[which]

        def passing(c, src):
            return pltpu.make_async_remote_copy(src, buf.at[c], sout.at[c], sin.at[c], device_id=toward, device_id_type=MESH)

        def sharing(c, ):
            view = o_ref.at[rs, columns(c)]
            return pltpu.make_async_remote_copy(view, view, lout.at[c], lin.at[c], device_id=back, device_id_type=MESH)

        def reduce_step(s):
            c = s - rank
            ok = (c >= 0) & (c < chunks)

            @pl.when(ok & start)
            def _():
                passing(c, x_ref.at[rs, columns(c)]).start()

            @pl.when(ok & jnp.logical_not(start))
            def _():
                passing(c, buf.at[c]).wait_recv()
                total = buf[c].astype(jnp.float32) + x_ref[rs, columns(c)].astype(jnp.float32)

                @pl.when(end)
                def _():
                    o_ref[rs, columns(c)] = total.astype(jnp.bfloat16)
                    sharing(c).start()

                @pl.when(jnp.logical_not(end))
                def _():
                    buf[c] = total.astype(jnp.bfloat16)
                    passing(c, buf.at[c]).start()

        def share_step(s):
            c = s - (size - 1) - (size - 1 - rank)
            ok = (c >= 0) & (c < chunks)

            @pl.when(ok & jnp.logical_not(end))
            def _():
                sharing(c).wait_recv()

                @pl.when(jnp.logical_not(start))
                def _():
                    sharing(c).start()

        def finish(c):
            @pl.when(jnp.logical_not(end))
            def _():
                passing(c, buf.at[c]).wait_send()

            @pl.when(jnp.logical_not(start))
            def _():
                sharing(c).wait_send()
        return reduce_step, share_step, finish

    sides = [side(0), side(1)]

    @pl.loop(0, chunks + 2 * (size - 1))
    def _(s):
        for one in sides:
            one[0](s)
        for one in sides:
            one[1](s)

    @pl.loop(0, chunks)
    def _(c):
        for one in sides:
            one[2](c)


def chain_sum(x, cid, width=256):
    size = lax.axis_size("tensor")
    rows, cols = x.shape
    chunks = cols // width
    return pl.pallas_call(
        functools.partial(chain_kernel, size, width),
        out_shape=jax.ShapeDtypeStruct(x.shape, jnp.bfloat16),
        in_specs=[pl.BlockSpec(memory_space=pltpu.VMEM)],
        out_specs=pl.BlockSpec(memory_space=pltpu.VMEM),
        scratch_shapes=[pltpu.VMEM((chunks, rows // 2, width), jnp.bfloat16)] * 2
        + [pltpu.SemaphoreType.DMA((chunks,))] * 8,
        compiler_params=pltpu.CompilerParams(collective_id=cid, has_side_effects=True, vmem_limit_bytes=48 * 2**20),
        cost_estimate=pl.CostEstimate(flops=rows*cols, bytes_accessed=200*2**20, transcendentals=0),
    )(x)


def normalize(values):
    return values * lax.rsqrt(jnp.mean(values * values, axis=-1, keepdims=True) + EPS)


def norm_back(values, gain, upstream):
    inverse = lax.rsqrt(jnp.mean(values * values, axis=-1, keepdims=True) + EPS)
    normed = values * inverse
    scaled = upstream * gain
    backed = inverse * (scaled - normed * jnp.mean(scaled * normed, axis=-1, keepdims=True))
    return (backed, jnp.sum(upstream * normed, axis=0))


def rotate(values, places):
    half_width = values.shape[-1] // 2
    spectrum = THETA ** (-2.0 * jnp.arange(half_width, dtype=jnp.float32) / values.shape[-1])
    angles = places.astype(jnp.float32)[..., None] * spectrum
    angles = jnp.concatenate([angles, angles], axis=-1)[..., None, :]
    turned = jnp.concatenate([-values[..., half_width:], values[..., :half_width]], axis=-1)
    return values * jnp.cos(angles) + turned * jnp.sin(angles)


def visibility(micro_count, row_count, prompt_dev, prompt_all, cont_rows, seq_pos, owners):
    local_rows = jnp.arange(row_count)
    prompt_rows = local_rows < prompt_dev
    places_local = jnp.where(
        prompt_rows, seq_pos * prompt_dev + local_rows, prompt_all + local_rows - prompt_dev
    )
    micro_ids = jnp.arange(micro_count)
    row_micro = jnp.repeat(micro_ids, row_count)
    row_prompt = jnp.tile(prompt_rows, micro_count)
    row_place = jnp.tile(places_local, micro_count)
    first_slot = jnp.where(row_prompt, row_micro, jnp.repeat(owners, row_count))
    second_slot = jnp.where(row_prompt, -1, micro_count + row_micro)
    key_slot = jnp.concatenate(
        [jnp.repeat(micro_ids, prompt_all), micro_count + jnp.repeat(micro_ids, cont_rows)]
    )
    key_place = jnp.concatenate(
        [
            jnp.tile(jnp.arange(prompt_all), micro_count),
            prompt_all + jnp.tile(jnp.arange(cont_rows), micro_count),
        ]
    )
    matched = (key_slot[None, :] == first_slot[:, None]) | (
        key_slot[None, :] == second_slot[:, None]
    )
    return (matched & (key_place[None, :] <= row_place[:, None]), row_place)


def scores_for(query, key_rows, visible, score_scale):
    raw_scores = jnp.einsum("rd,kd->rk", query, key_rows, preferred_element_type=jnp.float32)
    curved = jnp.tanh(raw_scores * score_scale / SOFTCAP)
    return (curved, jnp.where(visible, SOFTCAP * curved, -1e30))


def per_device(
    tokens,
    cotangent,
    prompt_of,
    query_weight,
    key_weight,
    value_weight,
    out_weight,
    gate_weight,
    up_weight,
    down_weight,
    norm_gains,
):
    micro_count = tokens.shape[0]
    row_count = tokens.shape[2]
    model_width = tokens.shape[3]
    seq_count = lax.axis_size("seq")
    seq_pos = lax.axis_index("seq")
    prompt_dev = row_count - CONT
    prompt_all = prompt_dev * seq_count
    total_rows = micro_count * row_count
    score_scale = HEAD ** (-0.5)
    visible, places = visibility(
        micro_count, row_count, prompt_dev, prompt_all, CONT, seq_pos, prompt_of[:, 0]
    )
    axes = ("dp", "seq")
    query_width = query_weight.shape[1]
    side_weights = jnp.concatenate(
        [
            query_weight,
            key_weight,
            value_weight,
            jnp.pad(norm_gains.T, ((0, 0), (0, 128 - norm_gains.shape[0]))),
        ],
        axis=1,
    )
    full_side = lax.all_gather(side_weights, axes, axis=0, tiled=True)
    full_query = full_side[:, :query_width]
    full_key = full_side[:, query_width : query_width + HEAD]
    full_value = full_side[:, query_width + HEAD : query_width + 2 * HEAD]
    gain_rows = full_side[:, query_width + 2 * HEAD : query_width + 2 * HEAD + 4].T
    full_out = lax.all_gather(out_weight, axes, axis=1, tiled=True)
    full_gate = lax.all_gather(gate_weight, axes, axis=0, tiled=True)
    full_up = lax.all_gather(up_weight, axes, axis=0, tiled=True)
    full_down = lax.all_gather(down_weight, axes, axis=1, tiled=True)
    gain_float = gain_rows.astype(jnp.float32)
    inputs = tokens.reshape(total_rows, model_width).astype(jnp.float32)
    normed_in = (normalize(inputs) * gain_float[0]).astype(jnp.bfloat16)
    query_heads = jnp.dot(normed_in, full_query, preferred_element_type=jnp.float32).reshape(
        total_rows, -1, HEAD
    )
    key_heads = jnp.dot(normed_in, full_key, preferred_element_type=jnp.float32).reshape(
        total_rows, 1, HEAD
    )
    value_raw = jnp.dot(normed_in, full_value, preferred_element_type=jnp.float32)
    query_rows = rotate(query_heads, places).astype(jnp.bfloat16)
    key_local = rotate(key_heads, places)[:, 0].astype(jnp.bfloat16)
    value_local = value_raw.astype(jnp.bfloat16)
    key_grid = key_local.reshape(micro_count, row_count, HEAD)
    value_grid = value_local.reshape(micro_count, row_count, HEAD)
    own_pair = jnp.concatenate([key_grid[:, :prompt_dev], value_grid[:, :prompt_dev]], axis=2)
    if seq_count == 2:
        other_pair = lax.ppermute(own_pair, "seq", [(0, 1), (1, 0)])
        early = seq_pos == 0
        prompt_pair = jnp.concatenate(
            [jnp.where(early, own_pair, other_pair), jnp.where(early, other_pair, own_pair)], axis=1
        )
    else:
        prompt_pair = lax.all_gather(own_pair, "seq", axis=1, tiled=True)
    prompt_keys, prompt_values = prompt_pair[..., :HEAD], prompt_pair[..., HEAD:]
    key_rows = jnp.concatenate(
        [
            prompt_keys.reshape(micro_count * prompt_all, HEAD),
            key_grid[:, prompt_dev:].reshape(micro_count * CONT, HEAD),
        ],
        axis=0,
    )
    value_rows = jnp.concatenate(
        [
            prompt_values.reshape(micro_count * prompt_all, HEAD),
            value_grid[:, prompt_dev:].reshape(micro_count * CONT, HEAD),
        ],
        axis=0,
    )
    head_count = query_rows.shape[1]
    contexts = []
    log_sums = []
    for head_pos in range(head_count):
        curved, masked = scores_for(query_rows[:, head_pos], key_rows, visible, score_scale)
        row_peak = jnp.max(masked, axis=-1, keepdims=True)
        weights = jnp.exp(masked - row_peak)
        summed = jnp.sum(weights, axis=-1, keepdims=True)
        probs = (weights / summed).astype(jnp.bfloat16)
        contexts.append(jnp.dot(probs, value_rows, preferred_element_type=jnp.float32))
        log_sums.append(row_peak + jnp.log(summed))
    context = jnp.stack(contexts, axis=1).reshape(total_rows, -1).astype(jnp.bfloat16)
    attn = chain_sum(
        jnp.dot(context, full_out, preferred_element_type=jnp.float32).astype(jnp.bfloat16),
        0,
    ).astype(jnp.float32)
    middle = inputs + normalize(attn) * gain_float[1]
    ffn_in = (normalize(middle) * gain_float[2]).astype(jnp.bfloat16)
    gate = jnp.dot(ffn_in, full_gate, preferred_element_type=jnp.float32)
    up_val = jnp.dot(ffn_in, full_up, preferred_element_type=jnp.float32)
    hidden_act, glu_pull = jax.vjp(
        lambda gate_in, up_in: jax.nn.gelu(gate_in, approximate=True) * up_in, gate, up_val
    )
    hidden = hidden_act.astype(jnp.bfloat16)
    ffn = chain_sum(
        jnp.dot(hidden, full_down, preferred_element_type=jnp.float32).astype(jnp.bfloat16),
        1,
    ).astype(jnp.float32)
    result = middle + normalize(ffn) * gain_float[3]
    upstream = cotangent.reshape(total_rows, model_width).astype(jnp.float32)
    d_ffn, gain_fourth = norm_back(ffn, gain_float[3], upstream)
    d_ffn = d_ffn.astype(jnp.bfloat16)
    grad_down = jnp.einsum("rf,rd->fd", hidden, d_ffn, preferred_element_type=jnp.float32)
    d_hidden = jnp.einsum("rd,fd->rf", d_ffn, full_down, preferred_element_type=jnp.float32)
    d_gate, d_up = glu_pull(d_hidden)
    d_gate = d_gate.astype(jnp.bfloat16)
    d_up = d_up.astype(jnp.bfloat16)
    grad_gate = jnp.einsum("rd,rf->df", ffn_in, d_gate, preferred_element_type=jnp.float32)
    grad_up = jnp.einsum("rd,rf->df", ffn_in, d_up, preferred_element_type=jnp.float32)
    ffn_part = jnp.einsum(
        "rf,df->rd", d_gate, full_gate, preferred_element_type=jnp.float32
    ) + jnp.einsum("rf,df->rd", d_up, full_up, preferred_element_type=jnp.float32)
    ffn_part, grad_down, grad_gate, grad_up = lax.optimization_barrier(
        (
            ffn_part.astype(jnp.bfloat16),
            grad_down.astype(jnp.bfloat16),
            grad_gate.astype(jnp.bfloat16),
            grad_up.astype(jnp.bfloat16),
        )
    )
    d_ffn_in = chain_sum(ffn_part, 2).astype(jnp.float32)
    d_mid_norm, gain_third = norm_back(middle, gain_float[2], d_ffn_in)
    d_middle = upstream + d_mid_norm
    d_attn, gain_second = norm_back(attn, gain_float[1], d_middle)
    d_attn = d_attn.astype(jnp.bfloat16)
    grad_out = jnp.einsum("rc,rd->cd", context, d_attn, preferred_element_type=jnp.float32)
    d_context = (
        jnp.einsum("rd,cd->rc", d_attn, full_out, preferred_element_type=jnp.float32)
        .astype(jnp.bfloat16)
        .reshape(total_rows, head_count, HEAD)
    )
    key_grad = jnp.zeros((key_rows.shape[0], HEAD), jnp.float32)
    value_grad = jnp.zeros((key_rows.shape[0], HEAD), jnp.float32)
    query_grads = []
    for head_pos in range(head_count):
        curved, masked = scores_for(query_rows[:, head_pos], key_rows, visible, score_scale)
        probs = jnp.where(visible, jnp.exp(masked - log_sums[head_pos]), 0.0)
        probs_low = probs.astype(jnp.bfloat16)
        d_probs = jnp.einsum(
            "rd,kd->rk", d_context[:, head_pos], value_rows, preferred_element_type=jnp.float32
        )
        inner_sum = jnp.sum(probs * d_probs, axis=-1, keepdims=True)
        d_scores = (probs * (d_probs - inner_sum) * score_scale * (1.0 - curved * curved)).astype(
            jnp.bfloat16
        )
        query_grads.append(jnp.dot(d_scores, key_rows, preferred_element_type=jnp.float32))
        key_grad = key_grad + jnp.einsum(
            "rk,rd->kd", d_scores, query_rows[:, head_pos], preferred_element_type=jnp.float32
        )
        value_grad = value_grad + jnp.einsum(
            "rk,rd->kd", probs_low, d_context[:, head_pos], preferred_element_type=jnp.float32
        )
    split_at = micro_count * prompt_all
    pair_grad = jnp.concatenate(
        [
            key_grad[:split_at].reshape(micro_count, prompt_all, HEAD),
            value_grad[:split_at].reshape(micro_count, prompt_all, HEAD),
        ],
        axis=2,
    )
    if seq_count == 2:
        low_part, high_part = pair_grad[:, :prompt_dev], pair_grad[:, prompt_dev:]
        early = seq_pos == 0
        sent = jnp.where(early, high_part, low_part).astype(jnp.bfloat16)
        kept = jnp.where(early, low_part, high_part)
        pair_grad = kept + lax.ppermute(sent, "seq", [(0, 1), (1, 0)]).astype(jnp.float32)
    else:
        pair_grad = lax.psum_scatter(
            pair_grad.astype(jnp.bfloat16), "seq", scatter_dimension=1, tiled=True
        ).astype(jnp.float32)
    prompt_key_grad, prompt_value_grad = pair_grad[..., :HEAD], pair_grad[..., HEAD:]
    own_keys = jnp.concatenate(
        [prompt_key_grad, key_grad[split_at:].reshape(micro_count, CONT, HEAD)], axis=1
    ).reshape(total_rows, HEAD)
    own_values = jnp.concatenate(
        [prompt_value_grad, value_grad[split_at:].reshape(micro_count, CONT, HEAD)], axis=1
    ).reshape(total_rows, HEAD)
    unused_query, unturn_query = jax.vjp(lambda turned_in: rotate(turned_in, places), query_heads)
    d_query = (
        unturn_query(jnp.stack(query_grads, axis=1))[0].reshape(total_rows, -1).astype(jnp.bfloat16)
    )
    unused_key, unturn_key = jax.vjp(lambda turned_in: rotate(turned_in, places), key_heads)
    d_key = unturn_key(own_keys[:, None, :])[0].reshape(total_rows, HEAD).astype(jnp.bfloat16)
    d_value = own_values.astype(jnp.bfloat16)
    grad_query = jnp.einsum("rd,rc->dc", normed_in, d_query, preferred_element_type=jnp.float32)
    grad_key = jnp.einsum("rd,rc->dc", normed_in, d_key, preferred_element_type=jnp.float32)
    grad_value = jnp.einsum("rd,rc->dc", normed_in, d_value, preferred_element_type=jnp.float32)
    attn_part = jnp.einsum("rc,dc->rd", d_query, full_query, preferred_element_type=jnp.float32)
    attn_part = attn_part + jnp.einsum(
        "rc,dc->rd", d_key, full_key, preferred_element_type=jnp.float32
    )
    attn_part = attn_part + jnp.einsum(
        "rc,dc->rd", d_value, full_value, preferred_element_type=jnp.float32
    )
    attn_part, grad_query, grad_key, grad_value = lax.optimization_barrier(
        (
            attn_part.astype(jnp.bfloat16),
            grad_query.astype(jnp.bfloat16),
            grad_key.astype(jnp.bfloat16),
            grad_value.astype(jnp.bfloat16),
        )
    )
    d_normed = chain_sum(attn_part, 3).astype(jnp.float32)
    d_in_norm, gain_first = norm_back(inputs, gain_float[0], d_normed)
    input_grad = d_middle + d_in_norm
    grad_gains = jnp.stack([gain_first, gain_second, gain_third, gain_fourth], axis=0)
    def scatter(grad, axis):
        return lax.psum_scatter(
            grad.astype(jnp.bfloat16), axes, scatter_dimension=axis, tiled=True
        ).astype(jnp.float32)

    side_grad = scatter(
        jnp.concatenate(
            [
                grad_query,
                grad_key,
                grad_value,
                jnp.pad(grad_gains.T, ((0, 0), (0, 128 - grad_gains.shape[0]))),
            ],
            axis=1,
        ),
        0,
    )
    shares = (
        side_grad[:, :query_width],
        side_grad[:, query_width : query_width + HEAD],
        side_grad[:, query_width + HEAD : query_width + 2 * HEAD],
        scatter(grad_out, 1),
        scatter(grad_gate, 0),
        scatter(grad_up, 0),
        scatter(grad_down, 1),
        side_grad[:, query_width + 2 * HEAD : query_width + 2 * HEAD + 4].T,
    )
    return (
        result.reshape(tokens.shape).astype(jnp.bfloat16),
        input_grad.reshape(tokens.shape),
        shares[0],
        shares[1],
        shares[2],
        shares[3],
        shares[4],
        shares[5],
        shares[6],
        shares[7],
    )


def solution(mesh):
    placed = (
        P("dp", "seq", None, None),
        P("dp", "seq", None, None),
        P("dp", "seq"),
        P(("dp", "seq"), "tensor"),
        P(("dp", "seq"), "tensor"),
        P(("dp", "seq"), "tensor"),
        P("tensor", ("dp", "seq")),
        P(("dp", "seq"), "tensor"),
        P(("dp", "seq"), "tensor"),
        P("tensor", ("dp", "seq")),
        P(None, ("dp", "seq")),
    )
    return jax.shard_map(
        per_device,
        mesh=mesh,
        in_specs=placed,
        out_specs=(
            P("dp", "seq", None, None),
            P("dp", "seq", None, None),
            P(("dp", "seq"), "tensor"),
            P(("dp", "seq"), "tensor"),
            P(("dp", "seq"), "tensor"),
            P("tensor", ("dp", "seq")),
            P(("dp", "seq"), "tensor"),
            P(("dp", "seq"), "tensor"),
            P("tensor", ("dp", "seq")),
            P(None, ("dp", "seq")),
        ),
        check_vma=False,
    )
```

```python
import functools

import jax
import jax.numpy as jnp
from jax import lax
from jax.experimental import pallas as pl
from jax.experimental.pallas import tpu as pltpu
from jax.sharding import PartitionSpec as P

MESH = pl.DeviceIdType.MESH

HEAD = 256
CONT = 32


EPS = 1e-06
SOFTCAP = 50.0
THETA = 10000.0


def chain_kernel(size, width, x_ref, o_ref, low_buf, high_buf, *sems):
    low_in, low_out, low_last_in, low_last_out, high_in, high_out, high_last_in, high_last_out = sems
    place = lax.axis_index("tensor")
    dp, seq = lax.axis_index("dp"), lax.axis_index("seq")
    down = (dp, seq, jnp.maximum(place - 1, 0))
    up = (dp, seq, jnp.minimum(place + 1, size - 1))
    first, last = place == 0, place == size - 1
    chunks = x_ref.shape[1] // width
    half = x_ref.shape[0] // 2
    rows = (pl.ds(0, half), pl.ds(half, half))
    barrier = pltpu.get_barrier_semaphore()

    @pl.when(jnp.logical_not(first))
    def _():
        pl.semaphore_signal(barrier, inc=1, device_id=down, device_id_type=MESH)

    @pl.when(jnp.logical_not(last))
    def _():
        pl.semaphore_signal(barrier, inc=1, device_id=up, device_id_type=MESH)
    pl.semaphore_wait(barrier, 2 - first.astype(jnp.int32) - last.astype(jnp.int32))

    def columns(c):
        return pl.ds(pl.multiple_of(c * width, 128), width)

    def side(which):
        buf = (low_buf, high_buf)[which]
        sin, sout, lin, lout = (sems[4 * which: 4 * which + 4])
        toward = (down, up)[which]
        back = (up, down)[which]
        start = (last, first)[which]
        end = (first, last)[which]
        rank = (size - 1 - place, place)[which]
        rs = rows[which]

        def passing(c, src):
            return pltpu.make_async_remote_copy(src, buf.at[c], sout.at[c], sin.at[c], device_id=toward, device_id_type=MESH)

        def sharing(c, ):
            view = o_ref.at[rs, columns(c)]
            return pltpu.make_async_remote_copy(view, view, lout.at[c], lin.at[c], device_id=back, device_id_type=MESH)

        def reduce_step(s):
            c = s - rank
            ok = (c >= 0) & (c < chunks)

            @pl.when(ok & start)
            def _():
                passing(c, x_ref.at[rs, columns(c)]).start()

            @pl.when(ok & jnp.logical_not(start))
            def _():
                passing(c, buf.at[c]).wait_recv()
                total = buf[c].astype(jnp.float32) + x_ref[rs, columns(c)].astype(jnp.float32)

                @pl.when(end)
                def _():
                    o_ref[rs, columns(c)] = total.astype(jnp.bfloat16)
                    sharing(c).start()

                @pl.when(jnp.logical_not(end))
                def _():
                    buf[c] = total.astype(jnp.bfloat16)
                    passing(c, buf.at[c]).start()

        def share_step(s):
            c = s - (size - 1) - (size - 1 - rank)
            ok = (c >= 0) & (c < chunks)

            @pl.when(ok & jnp.logical_not(end))
            def _():
                sharing(c).wait_recv()

                @pl.when(jnp.logical_not(start))
                def _():
                    sharing(c).start()

        def finish(c):
            @pl.when(jnp.logical_not(end))
            def _():
                passing(c, buf.at[c]).wait_send()

            @pl.when(jnp.logical_not(start))
            def _():
                sharing(c).wait_send()
        return reduce_step, share_step, finish

    sides = [side(0), side(1)]

    @pl.loop(0, chunks + 2 * (size - 1))
    def _(s):
        for one in sides:
            one[0](s)
        for one in sides:
            one[1](s)

    @pl.loop(0, chunks)
    def _(c):
        for one in sides:
            one[2](c)


def chain_sum(x, cid, width=256):
    size = lax.axis_size("tensor")
    rows, cols = x.shape
    chunks = cols // width
    return pl.pallas_call(
        functools.partial(chain_kernel, size, width),
        out_shape=jax.ShapeDtypeStruct(x.shape, jnp.bfloat16),
        in_specs=[pl.BlockSpec(memory_space=pltpu.VMEM)],
        out_specs=pl.BlockSpec(memory_space=pltpu.VMEM),
        scratch_shapes=[pltpu.VMEM((chunks, rows // 2, width), jnp.bfloat16)] * 2
        + [pltpu.SemaphoreType.DMA((chunks,))] * 8,
        compiler_params=pltpu.CompilerParams(collective_id=cid, has_side_effects=True, vmem_limit_bytes=48 * 2**20),
        cost_estimate=pl.CostEstimate(flops=rows*cols, bytes_accessed=200*2**20, transcendentals=0),
    )(x)


def normalize(values):
    return values * lax.rsqrt(jnp.mean(values * values, axis=-1, keepdims=True) + EPS)


def norm_back(values, gain, upstream):
    inverse = lax.rsqrt(jnp.mean(values * values, axis=-1, keepdims=True) + EPS)
    normed = values * inverse
    scaled = upstream * gain
    backed = inverse * (scaled - normed * jnp.mean(scaled * normed, axis=-1, keepdims=True))
    return (backed, jnp.sum(upstream * normed, axis=0))


def rotate(values, places):
    half_width = values.shape[-1] // 2
    spectrum = THETA ** (-2.0 * jnp.arange(half_width, dtype=jnp.float32) / values.shape[-1])
    angles = places.astype(jnp.float32)[..., None] * spectrum
    angles = jnp.concatenate([angles, angles], axis=-1)[..., None, :]
    turned = jnp.concatenate([-values[..., half_width:], values[..., :half_width]], axis=-1)
    return values * jnp.cos(angles) + turned * jnp.sin(angles)


def visibility(micro_count, row_count, prompt_dev, prompt_all, cont_rows, seq_pos, owners):
    local_rows = jnp.arange(row_count)
    prompt_rows = local_rows < prompt_dev
    places_local = jnp.where(
        prompt_rows, seq_pos * prompt_dev + local_rows, prompt_all + local_rows - prompt_dev
    )
    micro_ids = jnp.arange(micro_count)
    row_micro = jnp.repeat(micro_ids, row_count)
    row_prompt = jnp.tile(prompt_rows, micro_count)
    row_place = jnp.tile(places_local, micro_count)
    first_slot = jnp.where(row_prompt, row_micro, jnp.repeat(owners, row_count))
    second_slot = jnp.where(row_prompt, -1, micro_count + row_micro)
    key_slot = jnp.concatenate(
        [jnp.repeat(micro_ids, prompt_all), micro_count + jnp.repeat(micro_ids, cont_rows)]
    )
    key_place = jnp.concatenate(
        [
            jnp.tile(jnp.arange(prompt_all), micro_count),
            prompt_all + jnp.tile(jnp.arange(cont_rows), micro_count),
        ]
    )
    matched = (key_slot[None, :] == first_slot[:, None]) | (
        key_slot[None, :] == second_slot[:, None]
    )
    return (matched & (key_place[None, :] <= row_place[:, None]), row_place)


def scores_for(query, key_rows, visible, score_scale):
    raw_scores = jnp.einsum("rd,kd->rk", query, key_rows, preferred_element_type=jnp.float32)
    curved = jnp.tanh(raw_scores * score_scale / SOFTCAP)
    return (curved, jnp.where(visible, SOFTCAP * curved, -1e30))


def per_device(
    tokens,
    cotangent,
    prompt_of,
    query_weight,
    key_weight,
    value_weight,
    out_weight,
    gate_weight,
    up_weight,
    down_weight,
    norm_gains,
):
    micro_count = tokens.shape[0]
    row_count = tokens.shape[2]
    model_width = tokens.shape[3]
    seq_count = lax.axis_size("seq")
    seq_pos = lax.axis_index("seq")
    prompt_dev = row_count - CONT
    prompt_all = prompt_dev * seq_count
    total_rows = micro_count * row_count
    score_scale = HEAD ** (-0.5)
    visible, places = visibility(
        micro_count, row_count, prompt_dev, prompt_all, CONT, seq_pos, prompt_of[:, 0]
    )
    axes = ("dp", "seq")
    query_width = query_weight.shape[1]
    side_weights = jnp.concatenate(
        [
            query_weight,
            key_weight,
            value_weight,
            jnp.pad(norm_gains.T, ((0, 0), (0, 128 - norm_gains.shape[0]))),
        ],
        axis=1,
    )
    full_side = lax.all_gather(side_weights, axes, axis=0, tiled=True)
    full_query = full_side[:, :query_width]
    full_key = full_side[:, query_width : query_width + HEAD]
    full_value = full_side[:, query_width + HEAD : query_width + 2 * HEAD]
    gain_rows = full_side[:, query_width + 2 * HEAD : query_width + 2 * HEAD + 4].T
    full_out = lax.all_gather(out_weight, axes, axis=1, tiled=True)
    full_gate = lax.all_gather(gate_weight, axes, axis=0, tiled=True)
    full_up = lax.all_gather(up_weight, axes, axis=0, tiled=True)
    full_down = lax.all_gather(down_weight, axes, axis=1, tiled=True)
    gain_float = gain_rows.astype(jnp.float32)
    inputs = tokens.reshape(total_rows, model_width).astype(jnp.float32)
    normed_in = (normalize(inputs) * gain_float[0]).astype(jnp.bfloat16)
    query_heads = jnp.dot(normed_in, full_query, preferred_element_type=jnp.float32).reshape(
        total_rows, -1, HEAD
    )
    key_heads = jnp.dot(normed_in, full_key, preferred_element_type=jnp.float32).reshape(
        total_rows, 1, HEAD
    )
    value_raw = jnp.dot(normed_in, full_value, preferred_element_type=jnp.float32)
    query_rows = rotate(query_heads, places).astype(jnp.bfloat16)
    key_local = rotate(key_heads, places)[:, 0].astype(jnp.bfloat16)
    value_local = value_raw.astype(jnp.bfloat16)
    key_grid = key_local.reshape(micro_count, row_count, HEAD)
    value_grid = value_local.reshape(micro_count, row_count, HEAD)
    own_pair = jnp.concatenate([key_grid[:, :prompt_dev], value_grid[:, :prompt_dev]], axis=2)
    if seq_count == 2:
        other_pair = lax.ppermute(own_pair, "seq", [(0, 1), (1, 0)])
        early = seq_pos == 0
        prompt_pair = jnp.concatenate(
            [jnp.where(early, own_pair, other_pair), jnp.where(early, other_pair, own_pair)], axis=1
        )
    else:
        prompt_pair = lax.all_gather(own_pair, "seq", axis=1, tiled=True)
    prompt_keys, prompt_values = prompt_pair[..., :HEAD], prompt_pair[..., HEAD:]
    key_rows = jnp.concatenate(
        [
            prompt_keys.reshape(micro_count * prompt_all, HEAD),
            key_grid[:, prompt_dev:].reshape(micro_count * CONT, HEAD),
        ],
        axis=0,
    )
    value_rows = jnp.concatenate(
        [
            prompt_values.reshape(micro_count * prompt_all, HEAD),
            value_grid[:, prompt_dev:].reshape(micro_count * CONT, HEAD),
        ],
        axis=0,
    )
    head_count = query_rows.shape[1]
    contexts = []
    log_sums = []
    for head_pos in range(head_count):
        curved, masked = scores_for(query_rows[:, head_pos], key_rows, visible, score_scale)
        row_peak = jnp.max(masked, axis=-1, keepdims=True)
        weights = jnp.exp(masked - row_peak)
        summed = jnp.sum(weights, axis=-1, keepdims=True)
        probs = (weights / summed).astype(jnp.bfloat16)
        contexts.append(jnp.dot(probs, value_rows, preferred_element_type=jnp.float32))
        log_sums.append(row_peak + jnp.log(summed))
    context = jnp.stack(contexts, axis=1).reshape(total_rows, -1).astype(jnp.bfloat16)
    attn = chain_sum(
        jnp.dot(context, full_out, preferred_element_type=jnp.float32).astype(jnp.bfloat16),
        0,
    ).astype(jnp.float32)
    middle = inputs + normalize(attn) * gain_float[1]
    ffn_in = (normalize(middle) * gain_float[2]).astype(jnp.bfloat16)
    gate = jnp.dot(ffn_in, full_gate, preferred_element_type=jnp.float32)
    up_val = jnp.dot(ffn_in, full_up, preferred_element_type=jnp.float32)
    hidden_act, glu_pull = jax.vjp(
        lambda gate_in, up_in: jax.nn.gelu(gate_in, approximate=True) * up_in, gate, up_val
    )
    hidden = hidden_act.astype(jnp.bfloat16)
    ffn = chain_sum(
        jnp.dot(hidden, full_down, preferred_element_type=jnp.float32).astype(jnp.bfloat16),
        1,
    ).astype(jnp.float32)
    result = middle + normalize(ffn) * gain_float[3]
    upstream = cotangent.reshape(total_rows, model_width).astype(jnp.float32)
    d_ffn, gain_fourth = norm_back(ffn, gain_float[3], upstream)
    d_ffn = d_ffn.astype(jnp.bfloat16)
    grad_down = jnp.einsum("rf,rd->fd", hidden, d_ffn, preferred_element_type=jnp.float32)
    d_hidden = jnp.einsum("rd,fd->rf", d_ffn, full_down, preferred_element_type=jnp.float32)
    d_gate, d_up = glu_pull(d_hidden)
    d_gate = d_gate.astype(jnp.bfloat16)
    d_up = d_up.astype(jnp.bfloat16)
    grad_gate = jnp.einsum("rd,rf->df", ffn_in, d_gate, preferred_element_type=jnp.float32)
    grad_up = jnp.einsum("rd,rf->df", ffn_in, d_up, preferred_element_type=jnp.float32)
    ffn_part = jnp.einsum(
        "rf,df->rd", d_gate, full_gate, preferred_element_type=jnp.float32
    ) + jnp.einsum("rf,df->rd", d_up, full_up, preferred_element_type=jnp.float32)
    ffn_part, grad_down, grad_gate, grad_up = lax.optimization_barrier(
        (
            ffn_part.astype(jnp.bfloat16),
            grad_down.astype(jnp.bfloat16),
            grad_gate.astype(jnp.bfloat16),
            grad_up.astype(jnp.bfloat16),
        )
    )
    def scatter(grad, axis):
        return lax.psum_scatter(
            grad.astype(jnp.bfloat16), axes, scatter_dimension=axis, tiled=True
        ).astype(jnp.float32)

    d_ffn_in = chain_sum(ffn_part, 2)
    share_down = scatter(grad_down, 1)
    d_ffn_in, share_down = lax.optimization_barrier((d_ffn_in, share_down))
    d_ffn_in = d_ffn_in.astype(jnp.float32)
    share_gate = scatter(grad_gate, 0)
    d_mid_norm, gain_third = norm_back(middle, gain_float[2], d_ffn_in)
    d_middle = upstream + d_mid_norm
    d_attn, gain_second = norm_back(attn, gain_float[1], d_middle)
    d_attn = d_attn.astype(jnp.bfloat16)
    grad_out = jnp.einsum("rc,rd->cd", context, d_attn, preferred_element_type=jnp.float32)
    d_context = (
        jnp.einsum("rd,cd->rc", d_attn, full_out, preferred_element_type=jnp.float32)
        .astype(jnp.bfloat16)
        .reshape(total_rows, head_count, HEAD)
    )
    key_grad = jnp.zeros((key_rows.shape[0], HEAD), jnp.float32)
    value_grad = jnp.zeros((key_rows.shape[0], HEAD), jnp.float32)
    query_grads = []
    for head_pos in range(head_count):
        curved, masked = scores_for(query_rows[:, head_pos], key_rows, visible, score_scale)
        probs = jnp.where(visible, jnp.exp(masked - log_sums[head_pos]), 0.0)
        probs_low = probs.astype(jnp.bfloat16)
        d_probs = jnp.einsum(
            "rd,kd->rk", d_context[:, head_pos], value_rows, preferred_element_type=jnp.float32
        )
        inner_sum = jnp.sum(probs * d_probs, axis=-1, keepdims=True)
        d_scores = (probs * (d_probs - inner_sum) * score_scale * (1.0 - curved * curved)).astype(
            jnp.bfloat16
        )
        query_grads.append(jnp.dot(d_scores, key_rows, preferred_element_type=jnp.float32))
        key_grad = key_grad + jnp.einsum(
            "rk,rd->kd", d_scores, query_rows[:, head_pos], preferred_element_type=jnp.float32
        )
        value_grad = value_grad + jnp.einsum(
            "rk,rd->kd", probs_low, d_context[:, head_pos], preferred_element_type=jnp.float32
        )
    split_at = micro_count * prompt_all
    pair_grad = jnp.concatenate(
        [
            key_grad[:split_at].reshape(micro_count, prompt_all, HEAD),
            value_grad[:split_at].reshape(micro_count, prompt_all, HEAD),
        ],
        axis=2,
    )
    if seq_count == 2:
        low_part, high_part = pair_grad[:, :prompt_dev], pair_grad[:, prompt_dev:]
        early = seq_pos == 0
        sent = jnp.where(early, high_part, low_part).astype(jnp.bfloat16)
        kept = jnp.where(early, low_part, high_part)
        pair_grad = kept + lax.ppermute(sent, "seq", [(0, 1), (1, 0)]).astype(jnp.float32)
    else:
        pair_grad = lax.psum_scatter(
            pair_grad.astype(jnp.bfloat16), "seq", scatter_dimension=1, tiled=True
        ).astype(jnp.float32)
    prompt_key_grad, prompt_value_grad = pair_grad[..., :HEAD], pair_grad[..., HEAD:]
    own_keys = jnp.concatenate(
        [prompt_key_grad, key_grad[split_at:].reshape(micro_count, CONT, HEAD)], axis=1
    ).reshape(total_rows, HEAD)
    own_values = jnp.concatenate(
        [prompt_value_grad, value_grad[split_at:].reshape(micro_count, CONT, HEAD)], axis=1
    ).reshape(total_rows, HEAD)
    unused_query, unturn_query = jax.vjp(lambda turned_in: rotate(turned_in, places), query_heads)
    d_query = (
        unturn_query(jnp.stack(query_grads, axis=1))[0].reshape(total_rows, -1).astype(jnp.bfloat16)
    )
    unused_key, unturn_key = jax.vjp(lambda turned_in: rotate(turned_in, places), key_heads)
    d_key = unturn_key(own_keys[:, None, :])[0].reshape(total_rows, HEAD).astype(jnp.bfloat16)
    d_value = own_values.astype(jnp.bfloat16)
    grad_query = jnp.einsum("rd,rc->dc", normed_in, d_query, preferred_element_type=jnp.float32)
    grad_key = jnp.einsum("rd,rc->dc", normed_in, d_key, preferred_element_type=jnp.float32)
    grad_value = jnp.einsum("rd,rc->dc", normed_in, d_value, preferred_element_type=jnp.float32)
    attn_part = jnp.einsum("rc,dc->rd", d_query, full_query, preferred_element_type=jnp.float32)
    attn_part = attn_part + jnp.einsum(
        "rc,dc->rd", d_key, full_key, preferred_element_type=jnp.float32
    )
    attn_part = attn_part + jnp.einsum(
        "rc,dc->rd", d_value, full_value, preferred_element_type=jnp.float32
    )
    share_up = scatter(grad_up, 0)
    share_out = scatter(grad_out, 1)
    attn_part, share_gate, grad_query, grad_key, grad_value = lax.optimization_barrier(
        (
            attn_part.astype(jnp.bfloat16),
            share_gate,
            grad_query.astype(jnp.bfloat16),
            grad_key.astype(jnp.bfloat16),
            grad_value.astype(jnp.bfloat16),
        )
    )
    d_normed = chain_sum(attn_part, 3)
    d_normed, share_up = lax.optimization_barrier((d_normed, share_up))
    d_normed = d_normed.astype(jnp.float32)
    d_in_norm, gain_first = norm_back(inputs, gain_float[0], d_normed)
    input_grad = d_middle + d_in_norm
    grad_gains = jnp.stack([gain_first, gain_second, gain_third, gain_fourth], axis=0)
    side_grad = scatter(
        jnp.concatenate(
            [
                grad_query,
                grad_key,
                grad_value,
                jnp.pad(grad_gains.T, ((0, 0), (0, 128 - grad_gains.shape[0]))),
            ],
            axis=1,
        ),
        0,
    )
    shares = (
        side_grad[:, :query_width],
        side_grad[:, query_width : query_width + HEAD],
        side_grad[:, query_width + HEAD : query_width + 2 * HEAD],
        share_out,
        share_gate,
        share_up,
        share_down,
        side_grad[:, query_width + 2 * HEAD : query_width + 2 * HEAD + 4].T,
    )
    return (
        result.reshape(tokens.shape).astype(jnp.bfloat16),
        input_grad.reshape(tokens.shape),
        shares[0],
        shares[1],
        shares[2],
        shares[3],
        shares[4],
        shares[5],
        shares[6],
        shares[7],
    )


def solution(mesh):
    placed = (
        P("dp", "seq", None, None),
        P("dp", "seq", None, None),
        P("dp", "seq"),
        P(("dp", "seq"), "tensor"),
        P(("dp", "seq"), "tensor"),
        P(("dp", "seq"), "tensor"),
        P("tensor", ("dp", "seq")),
        P(("dp", "seq"), "tensor"),
        P(("dp", "seq"), "tensor"),
        P("tensor", ("dp", "seq")),
        P(None, ("dp", "seq")),
    )
    return jax.shard_map(
        per_device,
        mesh=mesh,
        in_specs=placed,
        out_specs=(
            P("dp", "seq", None, None),
            P("dp", "seq", None, None),
            P(("dp", "seq"), "tensor"),
            P(("dp", "seq"), "tensor"),
            P(("dp", "seq"), "tensor"),
            P("tensor", ("dp", "seq")),
            P(("dp", "seq"), "tensor"),
            P(("dp", "seq"), "tensor"),
            P("tensor", ("dp", "seq")),
            P(None, ("dp", "seq")),
        ),
        check_vma=False,
    )
```

```python
import functools

import jax
import jax.numpy as jnp
from jax import lax
from jax.experimental import pallas as pl
from jax.experimental.pallas import tpu as pltpu
from jax.sharding import PartitionSpec as P

MESH = pl.DeviceIdType.MESH

HEAD = 256
CONT = 32
BLOCK = 16


EPS = 1e-06
SOFTCAP = 50.0
THETA = 10000.0


def chain_kernel(size, width, x_ref, o_ref, low_buf, high_buf, *sems):
    low_in, low_out, low_last_in, low_last_out, high_in, high_out, high_last_in, high_last_out = sems
    place = lax.axis_index("tensor")
    dp, seq = lax.axis_index("dp"), lax.axis_index("seq")
    down = (dp, seq, jnp.maximum(place - 1, 0))
    up = (dp, seq, jnp.minimum(place + 1, size - 1))
    first, last = place == 0, place == size - 1
    chunks = x_ref.shape[1] // width
    half = x_ref.shape[0] // 2
    rows = (pl.ds(0, half), pl.ds(half, half))
    barrier = pltpu.get_barrier_semaphore()

    @pl.when(jnp.logical_not(first))
    def _():
        pl.semaphore_signal(barrier, inc=1, device_id=down, device_id_type=MESH)

    @pl.when(jnp.logical_not(last))
    def _():
        pl.semaphore_signal(barrier, inc=1, device_id=up, device_id_type=MESH)
    pl.semaphore_wait(barrier, 2 - first.astype(jnp.int32) - last.astype(jnp.int32))

    def columns(c):
        return pl.ds(pl.multiple_of(c * width, 128), width)

    def side(which):
        buf = (low_buf, high_buf)[which]
        sin, sout, lin, lout = (sems[4 * which: 4 * which + 4])
        toward = (down, up)[which]
        back = (up, down)[which]
        start = (last, first)[which]
        end = (first, last)[which]
        rank = (size - 1 - place, place)[which]
        rs = rows[which]

        def passing(c, src):
            return pltpu.make_async_remote_copy(src, buf.at[c], sout.at[c], sin.at[c], device_id=toward, device_id_type=MESH)

        def sharing(c, ):
            view = o_ref.at[rs, columns(c)]
            return pltpu.make_async_remote_copy(view, view, lout.at[c], lin.at[c], device_id=back, device_id_type=MESH)

        def reduce_step(s):
            c = s - rank
            ok = (c >= 0) & (c < chunks)

            @pl.when(ok & start)
            def _():
                passing(c, x_ref.at[rs, columns(c)]).start()

            @pl.when(ok & jnp.logical_not(start))
            def _():
                passing(c, buf.at[c]).wait_recv()
                total = buf[c].astype(jnp.float32) + x_ref[rs, columns(c)].astype(jnp.float32)

                @pl.when(end)
                def _():
                    o_ref[rs, columns(c)] = total.astype(jnp.bfloat16)
                    sharing(c).start()

                @pl.when(jnp.logical_not(end))
                def _():
                    buf[c] = total.astype(jnp.bfloat16)
                    passing(c, buf.at[c]).start()

        def share_step(s):
            c = s - (size - 1) - (size - 1 - rank)
            ok = (c >= 0) & (c < chunks)

            @pl.when(ok & jnp.logical_not(end))
            def _():
                sharing(c).wait_recv()

                @pl.when(jnp.logical_not(start))
                def _():
                    sharing(c).start()

        def finish(c):
            @pl.when(jnp.logical_not(end))
            def _():
                passing(c, buf.at[c]).wait_send()

            @pl.when(jnp.logical_not(start))
            def _():
                sharing(c).wait_send()
        return reduce_step, share_step, finish

    sides = [side(0), side(1)]

    @pl.loop(0, chunks + 2 * (size - 1))
    def _(s):
        for one in sides:
            one[0](s)
        for one in sides:
            one[1](s)

    @pl.loop(0, chunks)
    def _(c):
        for one in sides:
            one[2](c)


def chain_sum(x, cid, width=256):
    size = lax.axis_size("tensor")
    rows, cols = x.shape
    chunks = cols // width
    return pl.pallas_call(
        functools.partial(chain_kernel, size, width),
        out_shape=jax.ShapeDtypeStruct(x.shape, jnp.bfloat16),
        in_specs=[pl.BlockSpec(memory_space=pltpu.VMEM)],
        out_specs=pl.BlockSpec(memory_space=pltpu.VMEM),
        scratch_shapes=[pltpu.VMEM((chunks, rows // 2, width), jnp.bfloat16)] * 2
        + [pltpu.SemaphoreType.DMA((chunks,))] * 8,
        compiler_params=pltpu.CompilerParams(collective_id=cid, has_side_effects=True, vmem_limit_bytes=48 * 2**20),
        cost_estimate=pl.CostEstimate(flops=rows*cols, bytes_accessed=200*2**20, transcendentals=0),
    )(x)


TILE = 256
STAGES = 6
LAG = 2
PACE = 1


def chain_place(size):
    place = lax.axis_index("tensor")
    dp, seq = lax.axis_index("dp"), lax.axis_index("seq")
    down = (dp, seq, jnp.maximum(place - 1, 0))
    up = (dp, seq, jnp.minimum(place + 1, size - 1))
    return place, down, up, place == 0, place == size - 1


def greet_line(down, up, first, last):
    barrier = pltpu.get_barrier_semaphore()

    @pl.when(jnp.logical_not(first))
    def _():
        pl.semaphore_signal(barrier, inc=1, device_id=down, device_id_type=MESH)

    @pl.when(jnp.logical_not(last))
    def _():
        pl.semaphore_signal(barrier, inc=1, device_id=up, device_id_type=MESH)

    pl.semaphore_wait(barrier, 2 - first.astype(jnp.int32) - last.astype(jnp.int32))


def gelu_parts(gate):
    square = gate * gate
    slope = 0.7978845608028654
    curve = jnp.tanh(gate * (slope + (slope * 0.044715) * square))
    half = 0.5 + 0.5 * curve
    rise = (0.5 * gate) * (1.0 - curve * curve) * (slope + (3.0 * slope * 0.044715) * square)
    return gate * half, half + rise


def ffn_kernel(
    size, width, bases, schedule,
    part_ref, token_ref, cot_ref, gate_ref, up_ref, down_ref, gain_ref,
    sum_ref, out_ref, ffn_in_ref, hidden_ref, d_ffn_ref, d_gate_ref, d_up_ref, gain_grad_ref,
    parts, landing, act_a, act_b, stage_t, stage_a, stage_f, stage_c, cols, rows_w,
    pass_in, pass_out, share_in, share_out, local_done, col_sem, row_sem, io_sem,
):
    micro, rows, depth = parts.shape
    units = gate_ref.shape[1]
    half = rows // 2
    chunks = depth // width
    place, down, up, first, last = chain_place(size)
    greet_line(down, up, first, last)

    def side(which):
        toward, back = ((down, up), (up, down))[which]
        start, end = ((last, first), (first, last))[which]
        rank = (size - 1 - place, place)[which]
        span = pl.ds(which * half, half)

        def where_at(u):
            q = jnp.int32(0)
            base = jnp.int32(bases[0])
            for k in range(1, STAGES):
                past = (u >= bases[k]).astype(jnp.int32)
                q = q + past
                base = base + past * (bases[k] - bases[k - 1])
            c = u - base
            return q, c, (c >= 0) & (c < chunks)

        def columns(c):
            return pl.ds(pl.multiple_of(c * width, 128), width)

        def passing(q, c, source):
            return pltpu.make_async_remote_copy(
                source, landing.at[which, q, c], pass_out.at[which, q, c], pass_in.at[which, q, c],
                device_id=toward, device_id_type=MESH)

        def sharing(q, c, source):
            return pltpu.make_async_remote_copy(
                source, sum_ref.at[q, span, columns(c)], share_out.at[which, q, c], share_in.at[which, q, c],
                device_id=back, device_id_type=MESH)

        def local(q, c):
            return pltpu.make_async_copy(
                landing.at[which, q, c], sum_ref.at[q, span, columns(c)], local_done.at[which, q, c])

        def reduce_step(s):
            q, c, ok = where_at(s - LAG * rank)
            m = lax.rem(q, 2)

            @pl.when(ok & start)
            def _():
                passing(q, c, parts.at[m, span, columns(c)]).start()

            @pl.when(ok & jnp.logical_not(start))
            def _():
                passing(q, c, landing.at[which, q, c]).wait_recv()
                mine = parts[m, span, columns(c)].astype(jnp.float32)
                landing[which, q, c] = (landing[which, q, c].astype(jnp.float32) + mine).astype(jnp.bfloat16)

                @pl.when(end)
                def _():
                    sharing(q, c, landing.at[which, q, c]).start()
                    local(q, c).start()

                @pl.when(jnp.logical_not(end))
                def _():
                    passing(q, c, landing.at[which, q, c]).start()

        def share_step(s):
            q, c, ok = where_at(s - LAG * (2 * (size - 1) - rank))

            @pl.when(ok & jnp.logical_not(end))
            def _():
                view = sum_ref.at[q, span, columns(c)]
                sharing(q, c, view).wait_recv()

                @pl.when(jnp.logical_not(start))
                def _():
                    sharing(q, c, view).start()

        def settle(q):
            @pl.when(end)
            def _():
                @pl.loop(0, chunks)
                def _(c):
                    local(q, c).wait()

        def sent(q):
            @pl.when(jnp.logical_not(end))
            def _():
                @pl.loop(0, chunks)
                def _(c):
                    passing(q, c, landing.at[which, q, c]).wait_send()

        def shared(q):
            @pl.when(jnp.logical_not(start))
            def _():
                @pl.loop(0, chunks)
                def _(c):
                    sharing(q, c, landing.at[which, q, c]).wait_send()

        return reduce_step, share_step, settle, sent, shared

    sides = (side(0), side(1))

    def tick(s):
        for one in sides:
            one[0](s)
        for one in sides:
            one[1](s)

    def settle(q):
        for one in sides:
            one[2](q)

    def sent(q):
        for one in sides:
            one[3](q)

    def ticks(low, high):
        @pl.loop(low, high)
        def _(s):
            tick(s)

    def col_copy(kind, source, i, slot):
        return pltpu.make_async_copy(
            source.at[:, pl.ds(pl.multiple_of(i * TILE, TILE), TILE)], cols.at[kind, slot], col_sem.at[kind, slot])

    def row_copy(kind, source, i, slot):
        return pltpu.make_async_copy(
            source.at[pl.ds(pl.multiple_of(i * TILE, TILE), TILE)], rows_w.at[kind, slot], row_sem.at[kind, slot])

    def tiles(copy, sources, steps, body, clock):
        @pl.loop(0, steps)
        def _(i):
            slot = lax.rem(i, 2)

            @pl.when(i + 1 < steps)
            def _():
                for kind, source in enumerate(sources):
                    copy(kind, source, i + 1, 1 - slot).start()

            for kind, source in enumerate(sources):
                copy(kind, source, i, slot).wait()
            body(i, slot)

            @pl.when((lax.rem(i, PACE) == PACE - 1) | (i + 1 == steps))
            def _():
                tick(clock + i // PACE)

    def prime(copy, sources):
        for kind, source in enumerate(sources):
            copy(kind, source, 0, 0).start()

    def span_of(i):
        return pl.ds(pl.multiple_of(i * TILE, TILE), TILE)

    def io(index, source, target):
        return pltpu.make_async_copy(source, target, io_sem.at[index])

    def row_blocks(body, clock):
        count = rows // BLOCK
        for low, high, s in ((0, count // 2, clock), (count // 2, count, clock + 1)):
            @pl.loop(low, high)
            def _(b):
                body(pl.ds(pl.multiple_of(b * BLOCK, BLOCK), BLOCK))
            tick(s)

    def gain(k):
        return gain_ref[k : k + 1, :]

    def inverse(values):
        return lax.rsqrt(jnp.mean(values * values, axis=-1, keepdims=True) + EPS)

    def middle_of(span):
        attn = stage_a[span, :].astype(jnp.float32)
        return stage_t[span, :].astype(jnp.float32) + attn * inverse(attn) * gain(1)

    forward = ((gate_ref, up_ref), (down_ref,))

    def norm_before(m, clock):
        def body(span):
            middle = middle_of(span)
            stage_f[span, :] = (middle * inverse(middle) * gain(2)).astype(jnp.bfloat16)
        row_blocks(body, clock)

    def gate_and_up(m, clock):
        def body(i, slot):
            at = span_of(i)
            gate = jnp.dot(stage_f[...], cols[0, slot], preferred_element_type=jnp.float32)
            up_val = jnp.dot(stage_f[...], cols[1, slot], preferred_element_type=jnp.float32)
            active, slope = gelu_parts(gate)
            stage_c[:, at] = (active * up_val).astype(jnp.bfloat16)
            act_a[m, :, at] = active.astype(jnp.bfloat16)
            act_b[m, :, at] = (up_val * slope).astype(jnp.bfloat16)
        tiles(col_copy, (gate_ref, up_ref), units // TILE, body, clock)

    def down_proj(m, clock):
        def body(i, slot):
            parts[m, :, span_of(i)] = lax.dot_general(
                stage_c[...], rows_w[0, slot], (((1,), (1,)), ((), ())),
                preferred_element_type=jnp.float32).astype(jnp.bfloat16)
        tiles(row_copy, (down_ref,), depth // TILE, body, clock)

    def norm_after(m, clock):
        def body(span):
            middle = middle_of(span)
            ffn = stage_f[span, :].astype(jnp.float32)
            above = stage_c[span, :].astype(jnp.float32)
            inv = inverse(ffn)
            normed = ffn * inv
            stage_f[span, :] = (middle + normed * gain(3)).astype(jnp.bfloat16)
            scaled = above * gain(3)
            d_ffn = inv * (scaled - normed * jnp.mean(scaled * normed, axis=-1, keepdims=True))
            stage_c[span, :] = d_ffn.astype(jnp.bfloat16)
            term = above * normed
            gain_grad_ref[...] += term[:8] + term[8:]
        row_blocks(body, clock)

    def d_hidden(m, clock):
        def body(i, slot):
            at = span_of(i)
            d_hid = jnp.dot(stage_c[...], cols[0, slot], preferred_element_type=jnp.float32)
            act_a[m, :, at] = (d_hid * act_a[m, :, at].astype(jnp.float32)).astype(jnp.bfloat16)
            act_b[m, :, at] = (d_hid * act_b[m, :, at].astype(jnp.float32)).astype(jnp.bfloat16)
        tiles(col_copy, (down_ref,), units // TILE, body, clock)

    def d_input(m, clock):
        def body(i, slot):
            dims = (((1,), (1,)), ((), ()))
            parts[m, :, span_of(i)] = (
                lax.dot_general(act_b[m], rows_w[0, slot], dims, preferred_element_type=jnp.float32)
                + lax.dot_general(act_a[m], rows_w[1, slot], dims, preferred_element_type=jnp.float32)
            ).astype(jnp.bfloat16)
        tiles(row_copy, (gate_ref, up_ref), depth // TILE, body, clock)

    gain_grad_ref[...] = jnp.zeros_like(gain_grad_ref)
    for m in range(micro):
        io(m, part_ref.at[m], parts.at[m]).start()
    io(2, token_ref.at[0], stage_t).start()
    prime(col_copy, (gate_ref, up_ref))
    for m in range(micro):
        io(m, part_ref.at[m], parts.at[m]).wait()
    ticks(0, schedule["attn"][0])
    for m in range(micro):
        norm_s, gate_s, down_s, end_s = schedule["forward"][m]
        settle(m)
        io(3, sum_ref.at[m], stage_a).start()
        if m:
            io(2, token_ref.at[m], stage_t).start()
            io(6, stage_f, ffn_in_ref.at[m - 1]).wait()
            io(7, stage_c, hidden_ref.at[m - 1]).wait()
        io(2, token_ref.at[m], stage_t).wait()
        io(3, sum_ref.at[m], stage_a).wait()
        norm_before(m, norm_s)
        io(6, stage_f, ffn_in_ref.at[m]).start()
        prime(row_copy, (down_ref,))
        gate_and_up(m, gate_s)
        io(7, stage_c, hidden_ref.at[m]).start()
        sent(m)
        if m + 1 < micro:
            prime(col_copy, (gate_ref, up_ref))
        else:
            prime(col_copy, (down_ref,))
            io(2, token_ref.at[0], stage_t).start()
            io(3, sum_ref.at[0], stage_a).start()
        down_proj(m, down_s)
        ticks(down_s + -(-depth // (TILE * PACE)), end_s)
    io(6, stage_f, ffn_in_ref.at[micro - 1]).wait()
    io(7, stage_c, hidden_ref.at[micro - 1]).wait()
    for m in range(micro):
        norm_s, dh_s, di_s, end_s = schedule["backward"][m]
        settle(micro + m)
        io(4, sum_ref.at[micro + m], stage_f).start()
        io(5, cot_ref.at[m], stage_c).start()
        io(2, token_ref.at[m], stage_t).wait()
        io(3, sum_ref.at[m], stage_a).wait()
        io(4, sum_ref.at[micro + m], stage_f).wait()
        io(5, cot_ref.at[m], stage_c).wait()
        norm_after(m, norm_s)
        io(6, stage_f, out_ref.at[m]).start()
        io(7, stage_c, d_ffn_ref.at[m]).start()
        prime(row_copy, (gate_ref, up_ref))
        d_hidden(m, dh_s)
        io(8, act_b.at[m], d_gate_ref.at[m]).start()
        io(9, act_a.at[m], d_up_ref.at[m]).start()
        sent(micro + m)
        if m + 1 < micro:
            prime(col_copy, (down_ref,))
            io(2, token_ref.at[m + 1], stage_t).start()
            io(3, sum_ref.at[m + 1], stage_a).start()
        d_input(m, di_s)
        ticks(di_s + -(-depth // (TILE * PACE)), end_s)
        io(6, stage_f, out_ref.at[m]).wait()
        io(7, stage_c, d_ffn_ref.at[m]).wait()
        io(8, act_b.at[m], d_gate_ref.at[m]).wait()
        io(9, act_a.at[m], d_up_ref.at[m]).wait()
    for q in (STAGES - 2, STAGES - 1):
        settle(q)
        sent(q)

    @pl.loop(0, STAGES)
    def _(q):
        for one in sides:
            one[4](q)


def ffn_schedule(chunks, tiles, hops):
    whole = chunks + hops
    bases = [0, chunks]
    at = whole
    attn = (at,)
    forward = []
    for m in range(2):
        norm_s = at
        gate_s = norm_s + 2
        down_s = gate_s + tiles
        bases.append(max(down_s, bases[-1] + chunks))
        at = max(down_s + tiles, bases[m + 1] + whole)
        forward.append((norm_s, gate_s, down_s, at))
    backward = []
    for m in range(2):
        norm_s = at
        dh_s = norm_s + 2
        di_s = dh_s + tiles
        bases.append(max(di_s, bases[-1] + chunks))
        at = max(di_s + tiles, bases[m + 3] + whole)
        backward.append((norm_s, dh_s, di_s, at))
    last = backward[-1]
    backward[-1] = last[:3] + (max(last[3], bases[-1] + whole),)
    return tuple(bases), {"attn": attn, "forward": tuple(forward), "backward": tuple(backward)}


def ffn_block(parts, tokens, cotangent, gate, up, down, gains, cid, width=128):
    size = lax.axis_size("tensor")
    micro, rows, depth = tokens.shape
    units = gate.shape[1]
    chunks = depth // width
    bases, schedule = ffn_schedule(chunks, -(-units // (TILE * PACE)), 2 * LAG * (size - 1))
    bf16 = jnp.bfloat16
    any_spec = pl.BlockSpec(memory_space=pl.ANY)
    vmem_spec = pl.BlockSpec(memory_space=pltpu.VMEM)
    stack = jax.ShapeDtypeStruct((micro, rows, depth), bf16)
    wide = jax.ShapeDtypeStruct((micro, rows, units), bf16)
    dma = pltpu.SemaphoreType.DMA
    flops = 2 * micro * rows * depth * units * 6
    return pl.pallas_call(
        functools.partial(ffn_kernel, size, width, bases, schedule),
        out_shape=(
            jax.ShapeDtypeStruct((STAGES, rows, depth), bf16),
            stack, stack, wide, stack, wide, wide,
            jax.ShapeDtypeStruct((8, depth), jnp.float32),
        ),
        in_specs=[any_spec] * 6 + [vmem_spec],
        out_specs=(any_spec,) * 7 + (vmem_spec,),
        scratch_shapes=[
            pltpu.VMEM((micro, rows, depth), bf16),
            pltpu.VMEM((2, STAGES, chunks, rows // 2, width), bf16),
            pltpu.VMEM((micro, rows, units), bf16),
            pltpu.VMEM((micro, rows, units), bf16),
            pltpu.VMEM((rows, depth), bf16),
            pltpu.VMEM((rows, depth), bf16),
            pltpu.VMEM((rows, depth), bf16),
            pltpu.VMEM((rows, depth), bf16),
            pltpu.VMEM((2, 2, depth, TILE), bf16),
            pltpu.VMEM((2, 2, TILE, units), bf16),
        ]
        + [dma((2, STAGES, chunks))] * 5
        + [dma((2, 2)), dma((2, 2)), dma((10,))],
        compiler_params=pltpu.CompilerParams(
            collective_id=cid, has_side_effects=True, vmem_limit_bytes=60 * 2**20),
        cost_estimate=pl.CostEstimate(flops=flops, bytes_accessed=2**30, transcendentals=micro * rows * units),
    )(parts, tokens, cotangent, gate, up, down, gains)


def normalize(values):
    return values * lax.rsqrt(jnp.mean(values * values, axis=-1, keepdims=True) + EPS)


def norm_back(values, gain, upstream):
    inverse = lax.rsqrt(jnp.mean(values * values, axis=-1, keepdims=True) + EPS)
    normed = values * inverse
    scaled = upstream * gain
    backed = inverse * (scaled - normed * jnp.mean(scaled * normed, axis=-1, keepdims=True))
    return (backed, jnp.sum(upstream * normed, axis=0))


def rotate(values, places):
    half_width = values.shape[-1] // 2
    spectrum = THETA ** (-2.0 * jnp.arange(half_width, dtype=jnp.float32) / values.shape[-1])
    angles = places.astype(jnp.float32)[..., None] * spectrum
    angles = jnp.concatenate([angles, angles], axis=-1)[..., None, :]
    turned = jnp.concatenate([-values[..., half_width:], values[..., :half_width]], axis=-1)
    return values * jnp.cos(angles) + turned * jnp.sin(angles)


def visibility(micro_count, row_count, prompt_dev, prompt_all, cont_rows, seq_pos, owners):
    local_rows = jnp.arange(row_count)
    prompt_rows = local_rows < prompt_dev
    places_local = jnp.where(
        prompt_rows, seq_pos * prompt_dev + local_rows, prompt_all + local_rows - prompt_dev
    )
    micro_ids = jnp.arange(micro_count)
    row_micro = jnp.repeat(micro_ids, row_count)
    row_prompt = jnp.tile(prompt_rows, micro_count)
    row_place = jnp.tile(places_local, micro_count)
    first_slot = jnp.where(row_prompt, row_micro, jnp.repeat(owners, row_count))
    second_slot = jnp.where(row_prompt, -1, micro_count + row_micro)
    key_slot = jnp.concatenate(
        [jnp.repeat(micro_ids, prompt_all), micro_count + jnp.repeat(micro_ids, cont_rows)]
    )
    key_place = jnp.concatenate(
        [
            jnp.tile(jnp.arange(prompt_all), micro_count),
            prompt_all + jnp.tile(jnp.arange(cont_rows), micro_count),
        ]
    )
    matched = (key_slot[None, :] == first_slot[:, None]) | (
        key_slot[None, :] == second_slot[:, None]
    )
    return (matched & (key_place[None, :] <= row_place[:, None]), row_place)


def scores_for(query, key_rows, visible, score_scale):
    raw_scores = jnp.einsum("rd,kd->rk", query, key_rows, preferred_element_type=jnp.float32)
    curved = jnp.tanh(raw_scores * score_scale / SOFTCAP)
    return (curved, jnp.where(visible, SOFTCAP * curved, -1e30))


def per_device(
    tokens,
    cotangent,
    prompt_of,
    query_weight,
    key_weight,
    value_weight,
    out_weight,
    gate_weight,
    up_weight,
    down_weight,
    norm_gains,
):
    micro_count = tokens.shape[0]
    row_count = tokens.shape[2]
    model_width = tokens.shape[3]
    seq_count = lax.axis_size("seq")
    seq_pos = lax.axis_index("seq")
    prompt_dev = row_count - CONT
    prompt_all = prompt_dev * seq_count
    total_rows = micro_count * row_count
    score_scale = HEAD ** (-0.5)
    visible, places = visibility(
        micro_count, row_count, prompt_dev, prompt_all, CONT, seq_pos, prompt_of[:, 0]
    )
    axes = ("dp", "seq")
    query_width = query_weight.shape[1]
    side_weights = jnp.concatenate(
        [
            query_weight,
            key_weight,
            value_weight,
            jnp.pad(norm_gains.T, ((0, 0), (0, 128 - norm_gains.shape[0]))),
        ],
        axis=1,
    )
    full_side = lax.all_gather(side_weights, axes, axis=0, tiled=True)
    full_query = full_side[:, :query_width]
    full_key = full_side[:, query_width : query_width + HEAD]
    full_value = full_side[:, query_width + HEAD : query_width + 2 * HEAD]
    gain_rows = full_side[:, query_width + 2 * HEAD : query_width + 2 * HEAD + 4].T
    full_out = lax.all_gather(out_weight, axes, axis=1, tiled=True)
    full_gate = lax.all_gather(gate_weight, axes, axis=0, tiled=True)
    full_up = lax.all_gather(up_weight, axes, axis=0, tiled=True)
    full_down = lax.all_gather(down_weight.T, axes, axis=0, tiled=True)
    gain_float = gain_rows.astype(jnp.float32)
    inputs = tokens.reshape(total_rows, model_width).astype(jnp.float32)
    normed_in = (normalize(inputs) * gain_float[0]).astype(jnp.bfloat16)
    query_heads = jnp.dot(normed_in, full_query, preferred_element_type=jnp.float32).reshape(
        total_rows, -1, HEAD
    )
    key_heads = jnp.dot(normed_in, full_key, preferred_element_type=jnp.float32).reshape(
        total_rows, 1, HEAD
    )
    value_raw = jnp.dot(normed_in, full_value, preferred_element_type=jnp.float32)
    query_rows = rotate(query_heads, places).astype(jnp.bfloat16)
    key_local = rotate(key_heads, places)[:, 0].astype(jnp.bfloat16)
    value_local = value_raw.astype(jnp.bfloat16)
    key_grid = key_local.reshape(micro_count, row_count, HEAD)
    value_grid = value_local.reshape(micro_count, row_count, HEAD)
    own_pair = jnp.concatenate([key_grid[:, :prompt_dev], value_grid[:, :prompt_dev]], axis=2)
    if seq_count == 2:
        other_pair = lax.ppermute(own_pair, "seq", [(0, 1), (1, 0)])
        early = seq_pos == 0
        prompt_pair = jnp.concatenate(
            [jnp.where(early, own_pair, other_pair), jnp.where(early, other_pair, own_pair)], axis=1
        )
    else:
        prompt_pair = lax.all_gather(own_pair, "seq", axis=1, tiled=True)
    prompt_keys, prompt_values = prompt_pair[..., :HEAD], prompt_pair[..., HEAD:]
    key_rows = jnp.concatenate(
        [
            prompt_keys.reshape(micro_count * prompt_all, HEAD),
            key_grid[:, prompt_dev:].reshape(micro_count * CONT, HEAD),
        ],
        axis=0,
    )
    value_rows = jnp.concatenate(
        [
            prompt_values.reshape(micro_count * prompt_all, HEAD),
            value_grid[:, prompt_dev:].reshape(micro_count * CONT, HEAD),
        ],
        axis=0,
    )
    head_count = query_rows.shape[1]
    contexts = []
    log_sums = []
    for head_pos in range(head_count):
        curved, masked = scores_for(query_rows[:, head_pos], key_rows, visible, score_scale)
        row_peak = jnp.max(masked, axis=-1, keepdims=True)
        weights = jnp.exp(masked - row_peak)
        summed = jnp.sum(weights, axis=-1, keepdims=True)
        probs = (weights / summed).astype(jnp.bfloat16)
        contexts.append(jnp.dot(probs, value_rows, preferred_element_type=jnp.float32))
        log_sums.append(row_peak + jnp.log(summed))
    context = jnp.stack(contexts, axis=1).reshape(total_rows, -1).astype(jnp.bfloat16)
    attn_part = jnp.dot(context, full_out, preferred_element_type=jnp.float32).astype(jnp.bfloat16)
    gain_pad = jnp.pad(gain_float, ((0, 4), (0, 0)))
    sums, result, ffn_in, hidden, d_ffn, d_gate, d_up, gain_fourth = ffn_block(
        attn_part.reshape(tokens.shape[0], row_count, model_width),
        tokens[:, 0],
        cotangent[:, 0],
        full_gate,
        full_up,
        full_down,
        gain_pad,
        0,
    )
    gain_fourth = jnp.sum(gain_fourth, axis=0)
    attn = sums[:micro_count].reshape(total_rows, model_width).astype(jnp.float32)
    d_ffn_in = sums[2 * micro_count :].reshape(total_rows, model_width)
    middle = inputs + normalize(attn) * gain_float[1]
    upstream = cotangent.reshape(total_rows, model_width).astype(jnp.float32)
    ffn_in, hidden, d_ffn, d_gate, d_up = (
        kept.reshape(total_rows, -1) for kept in (ffn_in, hidden, d_ffn, d_gate, d_up)
    )

    def scatter(grad, axis):
        return lax.psum_scatter(
            grad.astype(jnp.bfloat16), axes, scatter_dimension=axis, tiled=True
        ).astype(jnp.float32)

    grad_down = jnp.einsum("rd,rf->df", d_ffn, hidden, preferred_element_type=jnp.float32)
    grad_gate = jnp.einsum("rd,rf->df", ffn_in, d_gate, preferred_element_type=jnp.float32)
    grad_up = jnp.einsum("rd,rf->df", ffn_in, d_up, preferred_element_type=jnp.float32)
    d_ffn_in, grad_down, grad_gate, grad_up = lax.optimization_barrier(
        (
            d_ffn_in,
            grad_down.astype(jnp.bfloat16),
            grad_gate.astype(jnp.bfloat16),
            grad_up.astype(jnp.bfloat16),
        )
    )
    d_ffn_in = d_ffn_in.astype(jnp.float32)
    share_down = scatter(grad_down, 0).T
    share_gate = scatter(grad_gate, 0)
    d_mid_norm, gain_third = norm_back(middle, gain_float[2], d_ffn_in)
    d_middle = upstream + d_mid_norm
    d_attn, gain_second = norm_back(attn, gain_float[1], d_middle)
    d_attn = d_attn.astype(jnp.bfloat16)
    grad_out = jnp.einsum("rc,rd->cd", context, d_attn, preferred_element_type=jnp.float32)
    d_attn, share_down = lax.optimization_barrier((d_attn, share_down))
    d_context = (
        jnp.einsum("rd,cd->rc", d_attn, full_out, preferred_element_type=jnp.float32)
        .astype(jnp.bfloat16)
        .reshape(total_rows, head_count, HEAD)
    )
    key_grad = jnp.zeros((key_rows.shape[0], HEAD), jnp.float32)
    value_grad = jnp.zeros((key_rows.shape[0], HEAD), jnp.float32)
    query_grads = []
    for head_pos in range(head_count):
        curved, masked = scores_for(query_rows[:, head_pos], key_rows, visible, score_scale)
        probs = jnp.where(visible, jnp.exp(masked - log_sums[head_pos]), 0.0)
        probs_low = probs.astype(jnp.bfloat16)
        d_probs = jnp.einsum(
            "rd,kd->rk", d_context[:, head_pos], value_rows, preferred_element_type=jnp.float32
        )
        inner_sum = jnp.sum(probs * d_probs, axis=-1, keepdims=True)
        d_scores = (probs * (d_probs - inner_sum) * score_scale * (1.0 - curved * curved)).astype(
            jnp.bfloat16
        )
        query_grads.append(jnp.dot(d_scores, key_rows, preferred_element_type=jnp.float32))
        key_grad = key_grad + jnp.einsum(
            "rk,rd->kd", d_scores, query_rows[:, head_pos], preferred_element_type=jnp.float32
        )
        value_grad = value_grad + jnp.einsum(
            "rk,rd->kd", probs_low, d_context[:, head_pos], preferred_element_type=jnp.float32
        )
    split_at = micro_count * prompt_all
    pair_grad = jnp.concatenate(
        [
            key_grad[:split_at].reshape(micro_count, prompt_all, HEAD),
            value_grad[:split_at].reshape(micro_count, prompt_all, HEAD),
        ],
        axis=2,
    )
    if seq_count == 2:
        low_part, high_part = pair_grad[:, :prompt_dev], pair_grad[:, prompt_dev:]
        early = seq_pos == 0
        sent = jnp.where(early, high_part, low_part).astype(jnp.bfloat16)
        kept = jnp.where(early, low_part, high_part)
        pair_grad = kept + lax.ppermute(sent, "seq", [(0, 1), (1, 0)]).astype(jnp.float32)
    else:
        pair_grad = lax.psum_scatter(
            pair_grad.astype(jnp.bfloat16), "seq", scatter_dimension=1, tiled=True
        ).astype(jnp.float32)
    prompt_key_grad, prompt_value_grad = pair_grad[..., :HEAD], pair_grad[..., HEAD:]
    own_keys = jnp.concatenate(
        [prompt_key_grad, key_grad[split_at:].reshape(micro_count, CONT, HEAD)], axis=1
    ).reshape(total_rows, HEAD)
    own_values = jnp.concatenate(
        [prompt_value_grad, value_grad[split_at:].reshape(micro_count, CONT, HEAD)], axis=1
    ).reshape(total_rows, HEAD)
    unused_query, unturn_query = jax.vjp(lambda turned_in: rotate(turned_in, places), query_heads)
    d_query = (
        unturn_query(jnp.stack(query_grads, axis=1))[0].reshape(total_rows, -1).astype(jnp.bfloat16)
    )
    unused_key, unturn_key = jax.vjp(lambda turned_in: rotate(turned_in, places), key_heads)
    d_key = unturn_key(own_keys[:, None, :])[0].reshape(total_rows, HEAD).astype(jnp.bfloat16)
    d_value = own_values.astype(jnp.bfloat16)
    grad_query = jnp.einsum("rd,rc->dc", normed_in, d_query, preferred_element_type=jnp.float32)
    grad_key = jnp.einsum("rd,rc->dc", normed_in, d_key, preferred_element_type=jnp.float32)
    grad_value = jnp.einsum("rd,rc->dc", normed_in, d_value, preferred_element_type=jnp.float32)
    attn_part = jnp.einsum("rc,dc->rd", d_query, full_query, preferred_element_type=jnp.float32)
    attn_part = attn_part + jnp.einsum(
        "rc,dc->rd", d_key, full_key, preferred_element_type=jnp.float32
    )
    attn_part = attn_part + jnp.einsum(
        "rc,dc->rd", d_value, full_value, preferred_element_type=jnp.float32
    )
    share_up = scatter(grad_up, 0)
    share_out = scatter(grad_out, 1)
    attn_part, share_gate, grad_query, grad_key, grad_value = lax.optimization_barrier(
        (
            attn_part.astype(jnp.bfloat16),
            share_gate,
            grad_query.astype(jnp.bfloat16),
            grad_key.astype(jnp.bfloat16),
            grad_value.astype(jnp.bfloat16),
        )
    )
    d_normed = chain_sum(attn_part, 3)
    d_normed, share_up = lax.optimization_barrier((d_normed, share_up))
    d_normed = d_normed.astype(jnp.float32)
    d_in_norm, gain_first = norm_back(inputs, gain_float[0], d_normed)
    input_grad = d_middle + d_in_norm
    grad_gains = jnp.stack([gain_first, gain_second, gain_third, gain_fourth], axis=0)
    side_grad = scatter(
        jnp.concatenate(
            [
                grad_query,
                grad_key,
                grad_value,
                jnp.pad(grad_gains.T, ((0, 0), (0, 128 - grad_gains.shape[0]))),
            ],
            axis=1,
        ),
        0,
    )
    shares = (
        side_grad[:, :query_width],
        side_grad[:, query_width : query_width + HEAD],
        side_grad[:, query_width + HEAD : query_width + 2 * HEAD],
        share_out,
        share_gate,
        share_up,
        share_down,
        side_grad[:, query_width + 2 * HEAD : query_width + 2 * HEAD + 4].T,
    )
    return (
        result.reshape(tokens.shape).astype(jnp.bfloat16),
        input_grad.reshape(tokens.shape),
        shares[0],
        shares[1],
        shares[2],
        shares[3],
        shares[4],
        shares[5],
        shares[6],
        shares[7],
    )


def solution(mesh):
    placed = (
        P("dp", "seq", None, None),
        P("dp", "seq", None, None),
        P("dp", "seq"),
        P(("dp", "seq"), "tensor"),
        P(("dp", "seq"), "tensor"),
        P(("dp", "seq"), "tensor"),
        P("tensor", ("dp", "seq")),
        P(("dp", "seq"), "tensor"),
        P(("dp", "seq"), "tensor"),
        P("tensor", ("dp", "seq")),
        P(None, ("dp", "seq")),
    )
    return jax.shard_map(
        per_device,
        mesh=mesh,
        in_specs=placed,
        out_specs=(
            P("dp", "seq", None, None),
            P("dp", "seq", None, None),
            P(("dp", "seq"), "tensor"),
            P(("dp", "seq"), "tensor"),
            P(("dp", "seq"), "tensor"),
            P("tensor", ("dp", "seq")),
            P(("dp", "seq"), "tensor"),
            P(("dp", "seq"), "tensor"),
            P("tensor", ("dp", "seq")),
            P(None, ("dp", "seq")),
        ),
        check_vma=False,
    )
```

```python
import functools

import jax
import jax.numpy as jnp
from jax import lax
from jax.experimental import pallas as pl
from jax.experimental.pallas import tpu as pltpu
from jax.sharding import PartitionSpec as P

MESH = pl.DeviceIdType.MESH

HEAD = 256
CONT = 32
BLOCK = 16


EPS = 1e-06
SOFTCAP = 50.0
THETA = 10000.0


def chain_kernel(size, width, x_ref, o_ref, low_buf, high_buf, *sems):
    low_in, low_out, low_last_in, low_last_out, high_in, high_out, high_last_in, high_last_out = sems
    place = lax.axis_index("tensor")
    dp, seq = lax.axis_index("dp"), lax.axis_index("seq")
    down = (dp, seq, jnp.maximum(place - 1, 0))
    up = (dp, seq, jnp.minimum(place + 1, size - 1))
    first, last = place == 0, place == size - 1
    chunks = x_ref.shape[1] // width
    half = x_ref.shape[0] // 2
    rows = (pl.ds(0, half), pl.ds(half, half))
    barrier = pltpu.get_barrier_semaphore()

    @pl.when(jnp.logical_not(first))
    def _():
        pl.semaphore_signal(barrier, inc=1, device_id=down, device_id_type=MESH)

    @pl.when(jnp.logical_not(last))
    def _():
        pl.semaphore_signal(barrier, inc=1, device_id=up, device_id_type=MESH)
    pl.semaphore_wait(barrier, 2 - first.astype(jnp.int32) - last.astype(jnp.int32))

    def columns(c):
        return pl.ds(pl.multiple_of(c * width, 128), width)

    def side(which):
        buf = (low_buf, high_buf)[which]
        sin, sout, lin, lout = (sems[4 * which: 4 * which + 4])
        toward = (down, up)[which]
        back = (up, down)[which]
        start = (last, first)[which]
        end = (first, last)[which]
        rank = (size - 1 - place, place)[which]
        rs = rows[which]

        def passing(c, src):
            return pltpu.make_async_remote_copy(src, buf.at[c], sout.at[c], sin.at[c], device_id=toward, device_id_type=MESH)

        def sharing(c, ):
            view = o_ref.at[rs, columns(c)]
            return pltpu.make_async_remote_copy(view, view, lout.at[c], lin.at[c], device_id=back, device_id_type=MESH)

        def reduce_step(s):
            c = s - rank
            ok = (c >= 0) & (c < chunks)

            @pl.when(ok & start)
            def _():
                passing(c, x_ref.at[rs, columns(c)]).start()

            @pl.when(ok & jnp.logical_not(start))
            def _():
                passing(c, buf.at[c]).wait_recv()
                total = buf[c].astype(jnp.float32) + x_ref[rs, columns(c)].astype(jnp.float32)

                @pl.when(end)
                def _():
                    o_ref[rs, columns(c)] = total.astype(jnp.bfloat16)
                    sharing(c).start()

                @pl.when(jnp.logical_not(end))
                def _():
                    buf[c] = total.astype(jnp.bfloat16)
                    passing(c, buf.at[c]).start()

        def share_step(s):
            c = s - (size - 1) - (size - 1 - rank)
            ok = (c >= 0) & (c < chunks)

            @pl.when(ok & jnp.logical_not(end))
            def _():
                sharing(c).wait_recv()

                @pl.when(jnp.logical_not(start))
                def _():
                    sharing(c).start()

        def finish(c):
            @pl.when(jnp.logical_not(end))
            def _():
                passing(c, buf.at[c]).wait_send()

            @pl.when(jnp.logical_not(start))
            def _():
                sharing(c).wait_send()
        return reduce_step, share_step, finish

    sides = [side(0), side(1)]

    @pl.loop(0, chunks + 2 * (size - 1))
    def _(s):
        for one in sides:
            one[0](s)
        for one in sides:
            one[1](s)

    @pl.loop(0, chunks)
    def _(c):
        for one in sides:
            one[2](c)


def chain_sum(x, cid, width=256):
    size = lax.axis_size("tensor")
    rows, cols = x.shape
    chunks = cols // width
    return pl.pallas_call(
        functools.partial(chain_kernel, size, width),
        out_shape=jax.ShapeDtypeStruct(x.shape, jnp.bfloat16),
        in_specs=[pl.BlockSpec(memory_space=pltpu.VMEM)],
        out_specs=pl.BlockSpec(memory_space=pltpu.VMEM),
        scratch_shapes=[pltpu.VMEM((chunks, rows // 2, width), jnp.bfloat16)] * 2
        + [pltpu.SemaphoreType.DMA((chunks,))] * 8,
        compiler_params=pltpu.CompilerParams(collective_id=cid, has_side_effects=True, vmem_limit_bytes=48 * 2**20),
        cost_estimate=pl.CostEstimate(flops=rows*cols, bytes_accessed=200*2**20, transcendentals=0),
    )(x)


TILE = 256
STAGES = 6
LAG = 2
PACE = 1


def chain_place(size):
    place = lax.axis_index("tensor")
    dp, seq = lax.axis_index("dp"), lax.axis_index("seq")
    down = (dp, seq, jnp.maximum(place - 1, 0))
    up = (dp, seq, jnp.minimum(place + 1, size - 1))
    return place, down, up, place == 0, place == size - 1


def plane_partners():
    dp, seq, place = (lax.axis_index(name) for name in ("dp", "seq", "tensor"))
    x, core = dp // 2, lax.rem(dp, 2)
    return ((1 - x) * 2 + core, seq, place), (dp, 1 - seq, place), (x * 2 + 1 - core, seq, place)


def greet_line(down, up, first, last, others=()):
    barrier = pltpu.get_barrier_semaphore()
    for partner in others:
        pl.semaphore_signal(barrier, inc=1, device_id=partner, device_id_type=MESH)

    @pl.when(jnp.logical_not(first))
    def _():
        pl.semaphore_signal(barrier, inc=1, device_id=down, device_id_type=MESH)

    @pl.when(jnp.logical_not(last))
    def _():
        pl.semaphore_signal(barrier, inc=1, device_id=up, device_id_type=MESH)

    pl.semaphore_wait(barrier, 2 + len(others) - first.astype(jnp.int32) - last.astype(jnp.int32))


def gelu_parts(gate):
    square = gate * gate
    slope = 0.7978845608028654
    curve = jnp.tanh(gate * (slope + (slope * 0.044715) * square))
    half = 0.5 + 0.5 * curve
    rise = (0.5 * gate) * (1.0 - curve * curve) * (slope + (3.0 * slope * 0.044715) * square)
    return gate * half, half + rise


def line_stream(size, width, bases, parts, landing, sum_ref, sems, spot):
    place, down, up, first, last = spot
    pass_in, pass_out, share_in, share_out, local_done = sems
    _, rows, depth = parts.shape
    half = rows // 2
    chunks = depth // width

    def side(which):
        toward, back = ((down, up), (up, down))[which]
        start, end = ((last, first), (first, last))[which]
        rank = (size - 1 - place, place)[which]
        span = pl.ds(which * half, half)

        def where_at(u):
            q = jnp.int32(0)
            base = jnp.int32(bases[0])
            for k in range(1, len(bases)):
                past = (u >= bases[k]).astype(jnp.int32)
                q = q + past
                base = base + past * (bases[k] - bases[k - 1])
            c = u - base
            return q, c, (c >= 0) & (c < chunks)

        def columns(c):
            return pl.ds(pl.multiple_of(c * width, 128), width)

        def passing(q, c, source):
            return pltpu.make_async_remote_copy(
                source, landing.at[which, q, c], pass_out.at[which, q, c], pass_in.at[which, q, c],
                device_id=toward, device_id_type=MESH)

        def sharing(q, c, source):
            return pltpu.make_async_remote_copy(
                source, sum_ref.at[q, span, columns(c)], share_out.at[which, q, c], share_in.at[which, q, c],
                device_id=back, device_id_type=MESH)

        def local(q, c):
            return pltpu.make_async_copy(
                landing.at[which, q, c], sum_ref.at[q, span, columns(c)], local_done.at[which, q, c])

        def reduce_step(s):
            q, c, ok = where_at(s - LAG * rank)
            m = lax.rem(q, 2)

            @pl.when(ok & start)
            def _():
                passing(q, c, parts.at[m, span, columns(c)]).start()

            @pl.when(ok & jnp.logical_not(start))
            def _():
                passing(q, c, landing.at[which, q, c]).wait_recv()
                mine = parts[m, span, columns(c)].astype(jnp.float32)
                landing[which, q, c] = (landing[which, q, c].astype(jnp.float32) + mine).astype(jnp.bfloat16)

                @pl.when(end)
                def _():
                    sharing(q, c, landing.at[which, q, c]).start()
                    local(q, c).start()

                @pl.when(jnp.logical_not(end))
                def _():
                    passing(q, c, landing.at[which, q, c]).start()

        def share_step(s):
            q, c, ok = where_at(s - LAG * (2 * (size - 1) - rank))

            @pl.when(ok & jnp.logical_not(end))
            def _():
                view = sum_ref.at[q, span, columns(c)]
                sharing(q, c, view).wait_recv()

                @pl.when(jnp.logical_not(start))
                def _():
                    sharing(q, c, view).start()

        def settle(q):
            @pl.when(end)
            def _():
                @pl.loop(0, chunks)
                def _(c):
                    local(q, c).wait()

        def sent(q):
            @pl.when(jnp.logical_not(end))
            def _():
                @pl.loop(0, chunks)
                def _(c):
                    passing(q, c, landing.at[which, q, c]).wait_send()

        def shared(q):
            @pl.when(jnp.logical_not(start))
            def _():
                @pl.loop(0, chunks)
                def _(c):
                    sharing(q, c, landing.at[which, q, c]).wait_send()

        return reduce_step, share_step, settle, sent, shared

    sides = (side(0), side(1))

    def tick(s):
        for one in sides:
            one[0](s)
        for one in sides:
            one[1](s)

    def settle(q):
        for one in sides:
            one[2](q)

    def sent(q):
        for one in sides:
            one[3](q)

    def shared():
        @pl.loop(0, len(bases))
        def _(q):
            for one in sides:
                one[4](q)

    def ticks(low, high):
        @pl.loop(low, high)
        def _(s):
            tick(s)

    return tick, ticks, settle, sent, shared


def ffn_kernel(
    size, width, bases, schedule, gather,
    part_ref, token_ref, cot_ref, gate_ref, up_own, down_own, gain_ref,
    sum_ref, out_ref, ffn_in_ref, hidden_ref, d_ffn_ref, d_attn_ref, d_middle_ref,
    grad_gate_ref, grad_up_ref, grad_down_ref, full_ref, gain_grad_ref,
    parts, landing, act_a, act_b, stage, cols, rows_w,
    pass_in, pass_out, share_in, share_out, local_done, col_sem, row_sem, io_sem, gather_in, gather_out, own_done,
):
    micro, rows, depth = parts.shape
    units = gate_ref.shape[1]
    stage_t, stage_a, stage_f, stage_c = (stage.at[pl.ds(k * rows, rows)] for k in range(4))
    up_ref, down_ref = (full_ref.at[0], full_ref.at[1]) if gather else (up_own, down_own)
    spot = place, down, up, first, last = chain_place(size)
    greet_line(down, up, first, last, plane_partners() if gather else ())

    tick, ticks, settle, sent, shared = line_stream(
        size, width, bases, parts, landing, sum_ref,
        (pass_in, pass_out, share_in, share_out, local_done), spot)

    def col_copy(kind, source, i, slot):
        return pltpu.make_async_copy(
            source.at[:, pl.ds(pl.multiple_of(i * TILE, TILE), TILE)], cols.at[kind, slot], col_sem.at[kind, slot])

    def row_copy(kind, source, i, slot):
        return pltpu.make_async_copy(
            source.at[pl.ds(pl.multiple_of(i * TILE, TILE), TILE)], rows_w.at[kind, slot], row_sem.at[kind, slot])

    def tiles(copy, sources, steps, body, clock):
        @pl.loop(0, steps)
        def _(i):
            slot = lax.rem(i, 2)

            @pl.when(i + 1 < steps)
            def _():
                for kind, source in enumerate(sources):
                    copy(kind, source, i + 1, 1 - slot).start()

            for kind, source in enumerate(sources):
                copy(kind, source, i, slot).wait()
            body(i, slot)

            @pl.when((lax.rem(i, PACE) == PACE - 1) | (i + 1 == steps))
            def _():
                tick(clock + i // PACE)

    def prime(copy, sources):
        for kind, source in enumerate(sources):
            copy(kind, source, 0, 0).start()

    def span_of(i):
        return pl.ds(pl.multiple_of(i * TILE, TILE), TILE)

    def io(index, source, target):
        return pltpu.make_async_copy(source, target, io_sem.at[index])

    def row_blocks(body, clock):
        count = rows // BLOCK
        for low, high, s in ((0, count // 2, clock), (count // 2, count, clock + 1)):
            @pl.loop(low, high)
            def _(b):
                body(pl.ds(pl.multiple_of(b * BLOCK, BLOCK), BLOCK))
            tick(s)

    def own_rows(m):
        return pl.ds(m * rows, rows)

    def gain(k):
        return gain_ref[k : k + 1, :]

    def inverse(values):
        return lax.rsqrt(jnp.mean(values * values, axis=-1, keepdims=True) + EPS)

    def middle_of(span):
        attn = stage_a[span, :].astype(jnp.float32)
        return stage_t[span, :].astype(jnp.float32) + attn * inverse(attn) * gain(1)

    def norm_before(m, clock):
        def body(span):
            middle = middle_of(span)
            stage_f[span, :] = (middle * inverse(middle) * gain(2)).astype(jnp.bfloat16)
        row_blocks(body, clock)

    def gate_and_up(m, clock):
        def body(i, slot):
            at = span_of(i)
            gate = jnp.dot(stage_f[...], cols[0, slot], preferred_element_type=jnp.float32)
            up_val = jnp.dot(stage_f[...], cols[1, slot], preferred_element_type=jnp.float32)
            active, slope = gelu_parts(gate)
            stage_c[:, at] = (active * up_val).astype(jnp.bfloat16)
            act_a[own_rows(m), at] = active.astype(jnp.bfloat16)
            act_b[own_rows(m), at] = (up_val * slope).astype(jnp.bfloat16)
        tiles(col_copy, (gate_ref, up_ref), units // TILE, body, clock)

    def down_proj(m, clock):
        def body(i, slot):
            parts[m, :, span_of(i)] = lax.dot_general(
                stage_c[...], rows_w[0, slot], (((1,), (1,)), ((), ())),
                preferred_element_type=jnp.float32).astype(jnp.bfloat16)
        tiles(row_copy, (down_ref,), depth // TILE, body, clock)

    def norm_after(m, clock):
        def body(span):
            middle = middle_of(span)
            ffn = stage_f[span, :].astype(jnp.float32)
            above = stage_c[span, :].astype(jnp.float32)
            inv = inverse(ffn)
            normed = ffn * inv
            stage_f[span, :] = (middle + normed * gain(3)).astype(jnp.bfloat16)
            scaled = above * gain(3)
            d_ffn = inv * (scaled - normed * jnp.mean(scaled * normed, axis=-1, keepdims=True))
            stage_c[span, :] = d_ffn.astype(jnp.bfloat16)
            term = above * normed
            gain_grad_ref[16:24, :] += term[:8] + term[8:]
        row_blocks(body, clock)

    def d_hidden(m, clock):
        def body(i, slot):
            at = span_of(i)
            d_hid = jnp.dot(stage_c[...], cols[0, slot], preferred_element_type=jnp.float32)
            mine = own_rows(m)
            act_a[mine, at] = (d_hid * act_a[mine, at].astype(jnp.float32)).astype(jnp.bfloat16)
            act_b[mine, at] = (d_hid * act_b[mine, at].astype(jnp.float32)).astype(jnp.bfloat16)
        tiles(col_copy, (down_ref,), units // TILE, body, clock)

    def d_input(m, clock):
        def body(i, slot):
            dims = (((1,), (1,)), ((), ()))
            parts[m, :, span_of(i)] = (
                lax.dot_general(act_b[own_rows(m), :], rows_w[0, slot], dims, preferred_element_type=jnp.float32)
                + lax.dot_general(act_a[own_rows(m), :], rows_w[1, slot], dims, preferred_element_type=jnp.float32)
            ).astype(jnp.bfloat16)
        tiles(row_copy, (gate_ref, up_ref), depth // TILE, body, clock)

    def norm_back_middle(m, clock):
        def body(span):
            attn = stage_a[span, :].astype(jnp.float32)
            attn_inv = inverse(attn)
            attn_normed = attn * attn_inv
            middle = stage_t[span, :].astype(jnp.float32) + attn_normed * gain(1)
            inv = inverse(middle)
            normed = middle * inv
            below = stage_f[span, :].astype(jnp.float32)
            scaled = below * gain(2)
            d_middle = stage_c[span, :].astype(jnp.float32) + inv * (
                scaled - normed * jnp.mean(scaled * normed, axis=-1, keepdims=True))
            term = below * normed
            gain_grad_ref[8:16, :] += term[:8] + term[8:]
            stage_c[span, :] = d_middle.astype(jnp.bfloat16)
            scaled = d_middle * gain(1)
            d_attn = attn_inv * (scaled - attn_normed * jnp.mean(scaled * attn_normed, axis=-1, keepdims=True))
            stage_f[span, :] = d_attn.astype(jnp.bfloat16)
            term = d_middle * attn_normed
            gain_grad_ref[0:8, :] += term[:8] + term[8:]
        row_blocks(body, clock)

    def tall_copy(source, i, slot, m):
        return pltpu.make_async_copy(
            source.at[m, :, span_of(i)], cols.at[0, slot, own_rows(m)], col_sem.at[m, slot])

    def weight_grads(source, pairs, steps, clock):
        def put(kind, target, i, slot):
            return pltpu.make_async_copy(rows_w.at[kind, slot], target.at[span_of(i)], row_sem.at[kind, slot])

        @pl.loop(0, steps)
        def _(i):
            slot = lax.rem(i, 2)

            @pl.when(i + 1 < steps)
            def _():
                for m in range(micro):
                    tall_copy(source, i + 1, 1 - slot, m).start()

            for m in range(micro):
                tall_copy(source, i, slot, m).wait()

            @pl.when(i >= 2)
            def _():
                for kind, (_, target) in enumerate(pairs):
                    put(kind, target, i - 2, slot).wait()

            left = cols[0, slot, : micro * rows, :]
            for kind, (right, target) in enumerate(pairs):
                for low in range(0, units, 3 * TILE):
                    high = min(units, low + 3 * TILE)
                    rows_w[kind, slot, :, low:high] = lax.dot_general(
                        left, right[: micro * rows, low:high], (((0,), (0,)), ((), ())),
                        preferred_element_type=jnp.float32).astype(jnp.bfloat16)
                put(kind, target, i, slot).start()
            tick(clock + i)

        for i in (steps - 2, steps - 1):
            for kind, (_, target) in enumerate(pairs):
                put(kind, target, i, i % 2).wait()

    if gather:
        share = up_own.shape[0]
        piece = share // 2
        dp, seq, _ = (lax.axis_index(name) for name in ("dp", "seq", "tensor"))
        x, core = dp // 2, lax.rem(dp, 2)
        over_x, over_y, over_core = plane_partners()

        def block(dx, dy, dc, u):
            nx, ny, nc = (jnp.abs(now - flip) for now, flip in ((x, dx), (seq, dy), (core, dc)))
            row = ((nx * 2 + nc) * 2 + ny) * share + (u % 2) * piece
            return pl.ds(pl.multiple_of(row, 16), piece)

        left_half, right_half = pl.ds(0, units // 2), pl.ds(units // 2, units // 2)
        everything = pl.ds(0, units)

        def view(u, dx, dy, dc, across=everything):
            return full_ref.at[u // 2, block(dx, dy, dc, u), across]

        def own(u):
            return (up_own, down_own)[u // 2].at[pl.ds((u % 2) * piece, piece)]

        def hop(u, kind, source, target, device):
            return pltpu.make_async_remote_copy(
                source, target, gather_out.at[u, kind], gather_in.at[u, kind],
                device_id=device, device_id_type=MESH)

        routes = (
            ((0, 0, 0), everything, over_x, (1, 0, 0)),
            ((0, 0, 0), everything, over_y, (0, 1, 0)),
            ((0, 0, 0), everything, over_core, (0, 0, 1)),
            ((1, 0, 0), left_half, over_y, (1, 1, 0)),
            ((0, 1, 0), right_half, over_x, (1, 1, 0)),
            ((1, 0, 0), everything, over_core, (1, 0, 1)),
            ((0, 1, 0), everything, over_core, (0, 1, 1)),
            ((1, 1, 0), left_half, over_core, (1, 1, 1)),
            ((1, 1, 0), right_half, over_core, (1, 1, 1)),
        )

        def send(u, kind):
            at, across, device, _ = routes[kind]
            source = own(u) if kind < 3 else view(u, *at, across)
            hop(u, kind, source, view(u, *at, across), device).start()

        def arrive(u, kind):
            _, across, device, at = routes[kind]
            target = view(u, *at, across)
            hop(u, kind, target, target, device).wait_recv()

        def own_copy(u):
            return pltpu.make_async_copy(own(u), view(u, 0, 0, 0), own_done.at[u])

        def gather_first(u):
            for kind in (0, 1, 2):
                send(u, kind)
            own_copy(u).start()

        def gather_second(u):
            arrive(u, 0)
            send(u, 3)
            send(u, 5)
            arrive(u, 1)
            send(u, 4)
            send(u, 6)

        def gather_third(u):
            arrive(u, 3)
            send(u, 7)
            arrive(u, 4)
            send(u, 8)

        def gather_last(u):
            own_copy(u).wait()
            for kind in (2, 5, 6, 7, 8):
                arrive(u, kind)

        def gather_sent():
            for u in range(4):
                for kind, (at, across, device, _) in enumerate(routes):
                    source = view(u, *at, across)
                    hop(u, kind, source, source, device).wait_send()

    gain_grad_ref[...] = jnp.zeros_like(gain_grad_ref)

    def load(index, source, target):
        return pltpu.make_async_copy(source, target, io_sem.at[index])

    def bring(m, third=None, fourth=None):
        found = [load(2, token_ref.at[m], stage_t), load(3, sum_ref.at[m], stage_a)]
        if third is not None:
            found += [load(4, third, stage_f), load(5, fourth, stage_c)]
        return found

    def start(copies):
        for copy in copies:
            copy.start()

    def wait(copies):
        for copy in copies:
            copy.wait()

    whole = schedule["attn"][0]
    entry = [load(m, part_ref.at[m], parts.at[m]) for m in range(micro)]
    start(entry)
    if gather:
        gather_first(0)
        gather_first(1)
    wait(entry)
    if gather:
        ticks(0, 7)
        gather_second(0)
        gather_first(2)
        ticks(7, 14)
        gather_second(1)
        gather_third(0)
        gather_first(3)
        ticks(14, 21)
        gather_second(2)
        gather_third(1)
        ticks(21, 28)
        gather_second(3)
        gather_third(2)
        ticks(28, whole)
    else:
        ticks(0, whole)
    kept = []
    for m in range(micro):
        norm_s, gate_s, down_s, end_s = schedule["forward"][m]
        settle(m)
        wait(kept)
        loads = bring(m)
        start(loads)
        wait(loads)
        norm_before(m, norm_s)
        kept = [load(6, stage_f, ffn_in_ref.at[m]), load(7, stage_c, hidden_ref.at[m])]
        kept[0].start()
        if gather and m == 0:
            gather_third(3)
            gather_last(0)
            gather_last(1)
        if m == 0:
            prime(col_copy, (gate_ref, up_ref))
        gate_and_up(m, gate_s)
        kept[1].start()
        sent(m)
        if gather and m == 0:
            gather_last(2)
            gather_last(3)
        prime(row_copy, (down_ref,))
        prime(col_copy, (gate_ref, up_ref) if m + 1 < micro else (down_ref,))
        down_proj(m, down_s)
        ticks(down_s + -(-depth // (TILE * PACE)), end_s)
    wait(kept)
    for m in range(micro):
        norm_s, dh_s, di_s, end_s = schedule["backward"][m]
        settle(micro + m)
        if m:
            wait(kept)
        loads = bring(m, sum_ref.at[micro + m], cot_ref.at[m])
        start(loads)
        wait(loads)
        norm_after(m, norm_s)
        kept = [load(6, stage_f, out_ref.at[m]), load(7, stage_c, d_ffn_ref.at[m])]
        start(kept)
        prime(row_copy, (gate_ref, up_ref))
        d_hidden(m, dh_s)
        sent(micro + m)
        if m + 1 < micro:
            prime(col_copy, (down_ref,))
        d_input(m, di_s)
        ticks(di_s + -(-depth // (TILE * PACE)), end_s)
    wait(kept)
    norm_s, grads_s, down_s, end_s = schedule["grads"]
    settle(2 * micro)
    loads = bring(0, sum_ref.at[2 * micro], cot_ref.at[0])
    start(loads)
    for m in range(micro):
        tall_copy(ffn_in_ref, 0, 0, m).start()
    wait(loads)
    norm_back_middle(0, norm_s)
    kept = [load(6, stage_f, d_attn_ref.at[0]), load(7, stage_c, d_middle_ref.at[0])]
    start(kept)
    hidden_loads = [load(2 + m, hidden_ref.at[m], stage.at[own_rows(m)]) for m in range(micro)]
    start(hidden_loads)
    steps = depth // TILE
    weight_grads(ffn_in_ref, ((act_b, grad_gate_ref), (act_a, grad_up_ref)), steps, grads_s)
    for m in range(micro):
        tall_copy(d_ffn_ref, 0, 0, m).start()
    wait(hidden_loads)
    weight_grads(d_ffn_ref, ((stage, grad_down_ref),), steps, down_s)
    wait(kept)
    tail = bring(1, None)
    tail.append(load(5, cot_ref.at[1], stage_c))
    start(tail)
    ticks(down_s + steps, end_s)
    settle(2 * micro + 1)
    tail.append(load(4, sum_ref.at[2 * micro + 1], stage_f))
    tail[-1].start()
    wait(tail)
    norm_back_middle(1, end_s)
    kept = [load(6, stage_f, d_attn_ref.at[1]), load(7, stage_c, d_middle_ref.at[1])]
    start(kept)
    sent(STAGES - 2)
    sent(STAGES - 1)
    if gather:
        gather_sent()
    wait(kept)

    shared()


def ffn_schedule(chunks, tiles, hops):
    whole = chunks + hops
    bases = [0, chunks]
    at = whole
    attn = (at,)
    forward = []
    for m in range(2):
        norm_s = at
        gate_s = norm_s + 2
        down_s = gate_s + tiles
        bases.append(max(down_s, bases[-1] + chunks))
        at = max(down_s + tiles, bases[m + 1] + whole)
        forward.append((norm_s, gate_s, down_s, at))
    backward = []
    for m in range(2):
        norm_s = at
        dh_s = norm_s + 2
        di_s = dh_s + tiles
        bases.append(max(di_s, bases[-1] + chunks))
        at = max(di_s + tiles, bases[m + 3] + whole)
        backward.append((norm_s, dh_s, di_s, at))
    grads_s = at + 2
    grads = (at, grads_s, grads_s + tiles, max(grads_s + 2 * tiles, bases[-1] + whole))
    return tuple(bases), {
        "attn": attn, "forward": tuple(forward), "backward": tuple(backward), "grads": grads
    }


def ffn_block(parts, tokens, cotangent, gate, up, down, gains, cid, width=128):
    size = lax.axis_size("tensor")
    micro, rows, depth = tokens.shape
    units = gate.shape[1]
    chunks = depth // width
    bases, schedule = ffn_schedule(chunks, -(-units // (TILE * PACE)), 2 * LAG * (size - 1))
    bf16 = jnp.bfloat16
    any_spec = pl.BlockSpec(memory_space=pl.ANY)
    vmem_spec = pl.BlockSpec(memory_space=pltpu.VMEM)
    gather = up.shape[0] != depth
    stack = jax.ShapeDtypeStruct((micro, rows, depth), bf16)
    wide = jax.ShapeDtypeStruct((micro, rows, units), bf16)
    grad = jax.ShapeDtypeStruct((depth, units), bf16)
    full = jax.ShapeDtypeStruct((2, depth, units) if gather else (2, 16, 128), bf16)
    dma = pltpu.SemaphoreType.DMA
    flops = 2 * micro * rows * depth * units * 9
    found = pl.pallas_call(
        functools.partial(ffn_kernel, size, width, bases, schedule, gather),
        out_shape=(
            jax.ShapeDtypeStruct((STAGES, rows, depth), bf16),
            stack, stack, wide, stack, stack, stack, grad, grad, grad, full,
            jax.ShapeDtypeStruct((24, depth), jnp.float32),
        ),
        in_specs=[any_spec] * 6 + [vmem_spec],
        out_specs=(any_spec,) * 11 + (vmem_spec,),
        scratch_shapes=[
            pltpu.VMEM((micro, rows, depth), bf16),
            pltpu.VMEM((2, STAGES, chunks, rows // 2, width), bf16),
            pltpu.VMEM((micro * rows, units), bf16),
            pltpu.VMEM((micro * rows, units), bf16),
            pltpu.VMEM((4 * rows, depth), bf16),
            pltpu.VMEM((2, 2, depth, TILE), bf16),
            pltpu.VMEM((2, 2, TILE, units), bf16),
        ]
        + [dma((2, STAGES, chunks))] * 5
        + [dma((2, 2)), dma((2, 2)), dma((8,)), dma((4, 9)), dma((4, 9)), dma((4,))],
        compiler_params=pltpu.CompilerParams(
            collective_id=cid, has_side_effects=True, vmem_limit_bytes=60 * 2**20),
        cost_estimate=pl.CostEstimate(
            flops=flops, bytes_accessed=2**30, transcendentals=micro * rows * units),
    )(parts, tokens, cotangent, gate, up, down, gains)
    return {
        "attn": found[0][:micro], "out": found[1], "d_attn": found[5], "d_middle": found[6],
        "grad_gate": found[7], "grad_up": found[8], "grad_down": found[9], "gain_grad": found[11],
        "sums": found[0], "ffn_in": found[2], "hidden": found[3], "d_ffn": found[4],
    }

SIDE_PAD = 128


def tail_kernel(
    size, width, bases,
    part_ref, up_grad_ref, normed_ref, d_attn_ref, d_qkv_ref, context_ref, gain_ref,
    sum_ref, up_share_ref, side_share_ref, gain_share_ref,
    parts, landing, up_acc, side_acc, up_first, side_first, up_second, side_second, up_third, side_third,
    cols, d_qkv, context, gain_in,
    pass_in, pass_out, share_in, share_out, local_done, col_sem, io_sem, hop_in, hop_out, gain_got, gain_sent,
):
    micro, rows, depth = parts.shape
    spot = place, down, up, first, last = chain_place(size)
    over_x, over_y, over_core = plane_partners()
    dp, seq = lax.axis_index("dp"), lax.axis_index("seq")
    x, core = dp // 2, lax.rem(dp, 2)
    others = [(dp, seq, lax.rem(place + k, size)) for k in range(1, size)]
    greet_plane(over_x, over_y, over_core, others)
    tick, ticks, settle, sent, shared = line_stream(
        size, width, bases, parts, landing, sum_ref,
        (pass_in, pass_out, share_in, share_out, local_done), spot)
    share = up_share_ref.shape[0]
    piece = share // 2
    widths = (up_share_ref.shape[1], side_share_ref.shape[1])
    qkv_width = d_qkv.shape[1]

    def load(index, source, target):
        return pltpu.make_async_copy(source, target, io_sem.at[index])

    def halves(p):
        all_columns = widths[p // 2]
        low = -(-all_columns // 256) * 128
        return (pl.ds(0, low), pl.ds(low, all_columns - low))

    def block_rows(bx, by, bc, p):
        return pl.ds(pl.multiple_of(((bx * 2 + bc) * 2 + by) * share + (p % 2) * piece, 16), piece)

    def acc(p, bx, by, across):
        if p < 2:
            return up_acc.at[bx * 2 + by, pl.ds((p % 2) * piece, piece), across]
        return side_acc.at[block_rows(bx, by, core, p), across]

    def whole(p):
        return pl.ds(0, widths[p // 2])

    first_buf, second_buf, third_buf = (up_first, side_first), (up_second, side_second), (up_third, side_third)

    def land(step, p, k, across):
        buf = (first_buf, second_buf, third_buf)[step][p // 2]
        return buf.at[p % 2, k, :, across]

    def hop(p, k, source, target, device):
        return pltpu.make_async_remote_copy(
            source, target, hop_out.at[p, k], hop_in.at[p, k], device_id=device, device_id_type=MESH)

    def hops(p):
        left, right = halves(p)
        found = []
        for k in range(4):
            bx, by = k // 2, k % 2
            if p < 2:
                source = up_grad_ref.at[block_rows(bx, by, 1 - core, p), :]
            else:
                source = side_acc.at[block_rows(bx, by, 1 - core, p), :]
            found.append((source, land(0, p, k, whole(p)), over_core))
        for k in range(2):
            found.append((acc(p, 1 - x, k, left), land(1, p, k, left), over_x))
        for k in range(2):
            found.append((acc(p, k, 1 - seq, right), land(1, p, k, right), over_y))
        found.append((acc(p, x, 1 - seq, left), land(2, p, 0, left), over_y))
        found.append((acc(p, 1 - x, seq, right), land(2, p, 0, right), over_x))
        return found

    def go(p, k):
        source, target, device = hops(p)[k]
        hop(p, k, source, target, device).start()

    def got(p, k):
        _, target, device = hops(p)[k]
        hop(p, k, target, target, device).wait_recv()
        return target

    def add(p, bx, by, across, arrived):
        mine = acc(p, bx, by, across)

        @pl.loop(0, piece // BLOCK)
        def _(b):
            span = pl.ds(pl.multiple_of(b * BLOCK, BLOCK), BLOCK)
            mine[span, :] = (
                mine[span, :].astype(jnp.float32) + arrived[span, :].astype(jnp.float32)
            ).astype(jnp.bfloat16)

    def scatter_first(p):
        for k in range(4):
            go(p, k)

    def scatter_second(p):
        for k in range(4):
            add(p, k // 2, k % 2, whole(p), got(p, k))
        for k in (4, 5, 6, 7):
            go(p, k)

    def scatter_third(p):
        left, right = halves(p)
        for k in range(2):
            add(p, x, k, left, got(p, 4 + k))
        go(p, 8)
        for k in range(2):
            add(p, k, seq, right, got(p, 6 + k))
        go(p, 9)

    def scatter_last(p):
        left, right = halves(p)
        add(p, x, seq, left, got(p, 8))
        add(p, x, seq, right, got(p, 9))
        put(p).start()

    def put(p):
        target = (up_share_ref, side_share_ref)[p // 2].at[pl.ds((p % 2) * piece, piece)]
        return load(12 + p, acc(p, x, seq, whole(p)), target)

    def scatter_sent(p):
        for k, (source, target, device) in enumerate(hops(p)):
            hop(p, k, source, target, device).wait_send()
        put(p).wait()

    def tile_copy(kind, i, slot):
        source = (normed_ref, d_attn_ref)[kind].at[:, pl.ds(pl.multiple_of(i * TILE, TILE), TILE)]
        return pltpu.make_async_copy(source, cols.at[kind, slot], col_sem.at[kind, slot])

    def side_grads(clock):
        steps = depth // TILE

        @pl.loop(0, steps)
        def _(i):
            slot = lax.rem(i, 2)

            @pl.when(i + 1 < steps)
            def _():
                tile_copy(0, i + 1, 1 - slot).start()
                tile_copy(1, i + 1, 1 - slot).start()

            tile_copy(0, i, slot).wait()
            tile_copy(1, i, slot).wait()
            span = pl.ds(pl.multiple_of(i * TILE, TILE), TILE)
            for kind, right, low in ((0, d_qkv, 0), (1, context, qkv_width)):
                side_acc[span, low : low + right.shape[1]] = lax.dot_general(
                    cols[kind, slot], right[...], (((0,), (0,)), ((), ())),
                    preferred_element_type=jnp.float32).astype(jnp.bfloat16)
            tick(clock + i)

    entry = [load(m, part_ref.at[m], parts.at[m]) for m in range(micro)]
    up_loads = [
        load(4 + k, up_grad_ref.at[pl.ds(pl.multiple_of(((k // 2 * 2 + core) * 2 + k % 2) * share, 16), share)], up_acc.at[k])
        for k in range(4)
    ]
    side_loads = [
        load(2, d_qkv_ref, d_qkv),
        load(3, context_ref, context),
        load(8, gain_ref, side_acc.at[:, pl.ds(widths[1] - SIDE_PAD, SIDE_PAD)]),
    ]
    for copy in entry:
        copy.start()
    scatter_first(0)
    scatter_first(1)
    for copy in side_loads + up_loads:
        copy.start()
    tile_copy(0, 0, 0).start()
    tile_copy(1, 0, 0).start()
    for copy in entry:
        copy.wait()
    ticks(0, 1)
    for copy in side_loads + up_loads:
        copy.wait()
    side_grads(1)
    clock = 1 + depth // TILE
    scatter_first(2)
    scatter_first(3)
    plan = (
        (0, (scatter_second, 0)), (1, (scatter_second, 1)), (3, (scatter_third, 0)), (3, (scatter_second, 2)),
        (4, (scatter_last, 0)), (2, (scatter_second, 3)), (3, (scatter_third, 1)), (4, (scatter_last, 1)),
        (3, (scatter_third, 2)), (4, (scatter_last, 2)), (3, (scatter_third, 3)), (4, (scatter_last, 3)),
    )
    for pause, (step, p) in plan:
        if pause:
            ticks(clock, clock + pause)
            clock += pause
        step(p)

    mine = side_acc.at[pl.ds(pl.multiple_of(((x * 2 + core) * 2 + seq) * share, 16), share), pl.ds(widths[1] - SIDE_PAD, SIDE_PAD)]

    def gain_hop(k):
        return pltpu.make_async_remote_copy(
            mine, gain_in.at[k], gain_sent.at[k], gain_got.at[k], device_id=others[k], device_id_type=MESH)

    for k in range(size - 1):
        gain_hop(k).start()
    ticks(clock, clock + 2)
    clock += 2
    for k in range(size - 1):
        gain_hop(k).wait_recv()
    total = mine[...].astype(jnp.float32)
    for k in range(size - 1):
        total = total + gain_in[k].astype(jnp.float32)
    gain_share_ref[...] = total
    ticks(clock, max(clock, bases[-1] + depth // width + 2 * LAG * (size - 1)))
    for q in range(micro):
        settle(q)
        sent(q)
    shared()
    for p in range(4):
        scatter_sent(p)
    for k in range(size - 1):
        gain_hop(k).wait_send()


def greet_plane(over_x, over_y, over_core, others):
    barrier = pltpu.get_barrier_semaphore()
    partners = (over_x, over_y, over_core, *others)
    for partner in partners:
        pl.semaphore_signal(barrier, inc=1, device_id=partner, device_id_type=MESH)
    pl.semaphore_wait(barrier, len(partners))


def tail_block(parts, up_grad, normed, d_attn, d_qkv, context, gain_cols, cid, width=128):
    size = lax.axis_size("tensor")
    micro, rows, depth = parts.shape
    units = up_grad.shape[1]
    chunks = depth // width
    total = micro * rows
    share = depth // (lax.axis_size("dp") * lax.axis_size("seq"))
    piece = share // 2
    side = d_qkv.shape[1] + context.shape[1] + SIDE_PAD
    bases = (0, chunks)
    bf16 = jnp.bfloat16
    any_spec = pl.BlockSpec(memory_space=pl.ANY)
    vmem_spec = pl.BlockSpec(memory_space=pltpu.VMEM)
    dma = pltpu.SemaphoreType.DMA
    return pl.pallas_call(
        functools.partial(tail_kernel, size, width, bases),
        out_shape=(
            jax.ShapeDtypeStruct((micro, rows, depth), bf16),
            jax.ShapeDtypeStruct((share, units), bf16),
            jax.ShapeDtypeStruct((share, side), bf16),
            jax.ShapeDtypeStruct((share, SIDE_PAD), jnp.float32),
        ),
        in_specs=[any_spec] * 7,
        out_specs=(any_spec,) * 3 + (vmem_spec,),
        scratch_shapes=[
            pltpu.VMEM((micro, rows, depth), bf16),
            pltpu.VMEM((2, 2, chunks, rows // 2, width), bf16),
            pltpu.VMEM((4, share, units), bf16),
            pltpu.VMEM((depth, side), bf16),
            pltpu.VMEM((2, 4, piece, units), bf16),
            pltpu.VMEM((2, 4, piece, side), bf16),
            pltpu.VMEM((2, 2, piece, units), bf16),
            pltpu.VMEM((2, 2, piece, side), bf16),
            pltpu.VMEM((2, 1, piece, units), bf16),
            pltpu.VMEM((2, 1, piece, side), bf16),
            pltpu.VMEM((2, 2, total, TILE), bf16),
            pltpu.VMEM(d_qkv.shape, bf16),
            pltpu.VMEM(context.shape, bf16),
            pltpu.VMEM((size - 1, share, SIDE_PAD), bf16),
        ]
        + [dma((2, 2, chunks))] * 5
        + [dma((2, 2)), dma((16,)), dma((4, 10)), dma((4, 10)), dma((size - 1,)), dma((size - 1,))],
        compiler_params=pltpu.CompilerParams(
            collective_id=cid, has_side_effects=True, vmem_limit_bytes=60 * 2**20),
        cost_estimate=pl.CostEstimate(
            flops=2 * total * depth * side, bytes_accessed=400 * 2**20, transcendentals=0),
    )(parts, up_grad, normed, d_attn, d_qkv, context, gain_cols)


def normalize(values):
    return values * lax.rsqrt(jnp.mean(values * values, axis=-1, keepdims=True) + EPS)


def norm_back(values, gain, upstream):
    inverse = lax.rsqrt(jnp.mean(values * values, axis=-1, keepdims=True) + EPS)
    normed = values * inverse
    scaled = upstream * gain
    return inverse * (scaled - normed * jnp.mean(scaled * normed, axis=-1, keepdims=True))


def turn_back(values, places):
    half_width = values.shape[-1] // 2
    spectrum = THETA ** (-2.0 * jnp.arange(half_width, dtype=jnp.float32) / values.shape[-1])
    angles = places.astype(jnp.float32)[..., None] * spectrum
    angles = jnp.concatenate([angles, angles], axis=-1)[..., None, :]
    turned = jnp.concatenate([values[..., half_width:], -values[..., :half_width]], axis=-1)
    return values * jnp.cos(angles) + turned * jnp.sin(angles)


def rotate(values, places):
    half_width = values.shape[-1] // 2
    spectrum = THETA ** (-2.0 * jnp.arange(half_width, dtype=jnp.float32) / values.shape[-1])
    angles = places.astype(jnp.float32)[..., None] * spectrum
    angles = jnp.concatenate([angles, angles], axis=-1)[..., None, :]
    turned = jnp.concatenate([-values[..., half_width:], values[..., :half_width]], axis=-1)
    return values * jnp.cos(angles) + turned * jnp.sin(angles)


def visibility(micro_count, row_count, prompt_dev, prompt_all, cont_rows, seq_pos, owners):
    local_rows = jnp.arange(row_count)
    prompt_rows = local_rows < prompt_dev
    places_local = jnp.where(
        prompt_rows, seq_pos * prompt_dev + local_rows, prompt_all + local_rows - prompt_dev
    )
    micro_ids = jnp.arange(micro_count)
    row_micro = jnp.repeat(micro_ids, row_count)
    row_prompt = jnp.tile(prompt_rows, micro_count)
    row_place = jnp.tile(places_local, micro_count)
    first_slot = jnp.where(row_prompt, row_micro, jnp.repeat(owners, row_count))
    second_slot = jnp.where(row_prompt, -1, micro_count + row_micro)
    key_slot = jnp.concatenate(
        [jnp.repeat(micro_ids, prompt_all), micro_count + jnp.repeat(micro_ids, cont_rows)]
    )
    key_place = jnp.concatenate(
        [
            jnp.tile(jnp.arange(prompt_all), micro_count),
            prompt_all + jnp.tile(jnp.arange(cont_rows), micro_count),
        ]
    )
    matched = (key_slot[None, :] == first_slot[:, None]) | (
        key_slot[None, :] == second_slot[:, None]
    )
    return (matched & (key_place[None, :] <= row_place[:, None]), row_place)


def scores_for(query, key_rows, visible, score_scale):
    raw_scores = jnp.einsum("rd,kd->rk", query, key_rows, preferred_element_type=jnp.float32)
    curved = jnp.tanh(raw_scores * score_scale / SOFTCAP)
    return (curved, jnp.where(visible, SOFTCAP * curved, -1e30))


def per_device(
    tokens,
    cotangent,
    prompt_of,
    query_weight,
    key_weight,
    value_weight,
    out_weight,
    gate_weight,
    up_weight,
    down_weight,
    norm_gains,
):
    micro_count = tokens.shape[0]
    row_count = tokens.shape[2]
    model_width = tokens.shape[3]
    seq_count = lax.axis_size("seq")
    seq_pos = lax.axis_index("seq")
    prompt_dev = row_count - CONT
    prompt_all = prompt_dev * seq_count
    total_rows = micro_count * row_count
    score_scale = HEAD ** (-0.5)
    axes = ("dp", "seq")
    planar = lax.axis_size("dp") == 4 and seq_count == 2
    query_width = query_weight.shape[1]
    qkv_width = query_width + 2 * HEAD
    f32, bf16 = jnp.float32, jnp.bfloat16
    visible, places = visibility(
        micro_count, row_count, prompt_dev, prompt_all, CONT, seq_pos, prompt_of[:, 0]
    )
    side_weights = jnp.concatenate(
        [
            query_weight,
            key_weight,
            value_weight,
            jnp.pad(norm_gains.T, ((0, 0), (0, SIDE_PAD - norm_gains.shape[0]))),
        ],
        axis=1,
    )
    full_side = lax.all_gather(side_weights, axes, axis=0, tiled=True)
    full_qkv = full_side[:, :qkv_width]
    gain_float = full_side[:, qkv_width : qkv_width + 4].T.astype(f32)
    full_out = lax.all_gather(out_weight, axes, axis=1, tiled=True)
    full_gate = lax.all_gather(gate_weight, axes, axis=0, tiled=True)
    down_turned = down_weight.T
    if planar:
        full_up, full_down = up_weight, down_turned
    else:
        full_up = lax.all_gather(up_weight, axes, axis=0, tiled=True)
        full_down = lax.all_gather(down_turned, axes, axis=0, tiled=True)
    inputs = tokens.reshape(total_rows, model_width).astype(f32)
    normed_in = (normalize(inputs) * gain_float[0]).astype(bf16)
    key_value = jnp.dot(normed_in, full_qkv[:, query_width:], preferred_element_type=f32)
    key_heads = key_value[:, :HEAD].reshape(total_rows, 1, HEAD)
    key_local = rotate(key_heads, places)[:, 0].astype(bf16)
    value_local = key_value[:, HEAD:].astype(bf16)
    key_grid = key_local.reshape(micro_count, row_count, HEAD)
    value_grid = value_local.reshape(micro_count, row_count, HEAD)
    own_pair = jnp.concatenate([key_grid[:, :prompt_dev], value_grid[:, :prompt_dev]], axis=2)
    if seq_count == 2:
        other_pair = lax.ppermute(own_pair, "seq", [(0, 1), (1, 0)])
        early = seq_pos == 0
        prompt_pair = jnp.concatenate(
            [jnp.where(early, own_pair, other_pair), jnp.where(early, other_pair, own_pair)], axis=1
        )
    else:
        prompt_pair = lax.all_gather(own_pair, "seq", axis=1, tiled=True)
    query_heads = jnp.dot(
        normed_in, full_qkv[:, :query_width], preferred_element_type=f32
    ).reshape(total_rows, -1, HEAD)
    query_rows = rotate(query_heads, places).astype(bf16)
    prompt_keys, prompt_values = prompt_pair[..., :HEAD], prompt_pair[..., HEAD:]
    key_rows = jnp.concatenate(
        [
            prompt_keys.reshape(micro_count * prompt_all, HEAD),
            key_grid[:, prompt_dev:].reshape(micro_count * CONT, HEAD),
        ],
        axis=0,
    )
    value_rows = jnp.concatenate(
        [
            prompt_values.reshape(micro_count * prompt_all, HEAD),
            value_grid[:, prompt_dev:].reshape(micro_count * CONT, HEAD),
        ],
        axis=0,
    )
    head_count = query_rows.shape[1]
    contexts = []
    log_sums = []
    for head_pos in range(head_count):
        curved, masked = scores_for(query_rows[:, head_pos], key_rows, visible, score_scale)
        row_peak = jnp.max(masked, axis=-1, keepdims=True)
        weights = jnp.exp(masked - row_peak)
        summed = jnp.sum(weights, axis=-1, keepdims=True)
        probs = (weights / summed).astype(bf16)
        contexts.append(jnp.dot(probs, value_rows, preferred_element_type=f32))
        log_sums.append(row_peak + jnp.log(summed))
    context = jnp.stack(contexts, axis=1).reshape(total_rows, -1).astype(bf16)
    attn_part = jnp.dot(context, full_out, preferred_element_type=f32).astype(bf16)
    block = ffn_block(
        attn_part.reshape(micro_count, row_count, model_width),
        tokens[:, 0],
        cotangent[:, 0],
        full_gate,
        full_up,
        full_down,
        jnp.pad(gain_float, ((0, 4), (0, 0))),
        0,
    )
    gain_sums = jnp.sum(block["gain_grad"].reshape(3, 8, model_width), axis=1)
    d_middle = block["d_middle"].reshape(total_rows, model_width).astype(f32)
    d_attn = block["d_attn"].reshape(total_rows, model_width)

    def scatter(grad, axis):
        return lax.psum_scatter(
            grad.astype(bf16), axes, scatter_dimension=axis, tiled=True
        ).astype(f32)

    share_down = scatter(block["grad_down"], 0).T
    share_gate = scatter(block["grad_gate"], 0)
    d_context = (
        jnp.einsum("rd,cd->rc", d_attn, full_out, preferred_element_type=f32)
        .astype(bf16)
        .reshape(total_rows, head_count, HEAD)
    )
    key_grad = jnp.zeros((key_rows.shape[0], HEAD), f32)
    value_grad = jnp.zeros((key_rows.shape[0], HEAD), f32)
    query_grads = []
    for head_pos in range(head_count):
        curved, masked = scores_for(query_rows[:, head_pos], key_rows, visible, score_scale)
        probs = jnp.where(visible, jnp.exp(masked - log_sums[head_pos]), 0.0)
        probs_low = probs.astype(bf16)
        d_probs = jnp.einsum(
            "rd,kd->rk", d_context[:, head_pos], value_rows, preferred_element_type=f32
        )
        inner_sum = jnp.sum(probs * d_probs, axis=-1, keepdims=True)
        d_scores = (probs * (d_probs - inner_sum) * score_scale * (1.0 - curved * curved)).astype(
            bf16
        )
        query_grads.append(jnp.dot(d_scores, key_rows, preferred_element_type=f32))
        key_grad = key_grad + jnp.einsum(
            "rk,rd->kd", d_scores, query_rows[:, head_pos], preferred_element_type=f32
        )
        value_grad = value_grad + jnp.einsum(
            "rk,rd->kd", probs_low, d_context[:, head_pos], preferred_element_type=f32
        )
    split_at = micro_count * prompt_all
    pair_grad = jnp.concatenate(
        [
            key_grad[:split_at].reshape(micro_count, prompt_all, HEAD),
            value_grad[:split_at].reshape(micro_count, prompt_all, HEAD),
        ],
        axis=2,
    )
    if seq_count == 2:
        low_part, high_part = pair_grad[:, :prompt_dev], pair_grad[:, prompt_dev:]
        early = seq_pos == 0
        sent = jnp.where(early, high_part, low_part).astype(bf16)
        kept = jnp.where(early, low_part, high_part)
        pair_grad = kept + lax.ppermute(sent, "seq", [(0, 1), (1, 0)]).astype(f32)
    else:
        pair_grad = lax.psum_scatter(
            pair_grad.astype(bf16), "seq", scatter_dimension=1, tiled=True
        ).astype(f32)
    prompt_key_grad, prompt_value_grad = pair_grad[..., :HEAD], pair_grad[..., HEAD:]
    own_keys = jnp.concatenate(
        [prompt_key_grad, key_grad[split_at:].reshape(micro_count, CONT, HEAD)], axis=1
    ).reshape(total_rows, HEAD)
    own_values = jnp.concatenate(
        [prompt_value_grad, value_grad[split_at:].reshape(micro_count, CONT, HEAD)], axis=1
    ).reshape(total_rows, HEAD)
    d_query = turn_back(jnp.stack(query_grads, axis=1), places).reshape(total_rows, -1)
    d_key = turn_back(own_keys[:, None, :], places).reshape(total_rows, HEAD)
    d_qkv = jnp.concatenate([d_query, d_key, own_values], axis=1).astype(bf16)
    attn_part = jnp.einsum("rc,dc->rd", d_qkv, full_qkv, preferred_element_type=f32)
    gain_first = jnp.sum(attn_part * normalize(inputs), axis=0)
    grad_gains = jnp.concatenate(
        [gain_first[None], jnp.where(lax.axis_index("tensor") == 0, gain_sums, 0.0)], axis=0
    )
    gain_cols = jnp.pad(grad_gains.T, ((0, 0), (0, SIDE_PAD - grad_gains.shape[0])))
    attn_part = attn_part.astype(bf16)
    if planar:
        d_normed, share_up, share_side, share_gains = tail_block(
            attn_part.reshape(micro_count, row_count, model_width),
            block["grad_up"],
            normed_in,
            d_attn,
            d_qkv,
            context,
            gain_cols.astype(bf16),
            1,
        )
        d_normed, share_gate, share_down = lax.optimization_barrier(
            (d_normed, share_gate, share_down)
        )
        d_normed = d_normed.reshape(total_rows, model_width)
        share_up, share_side = share_up.astype(f32), share_side.astype(f32)
        share_out = share_side[:, qkv_width : qkv_width + query_width].T
        share_gains = share_gains[:, :4].T
    else:
        share_up = scatter(block["grad_up"], 0)
        share_out = scatter(
            jnp.einsum("rc,rd->cd", context, d_attn, preferred_element_type=f32), 1
        )
        side_grad = jnp.einsum("rd,rc->dc", normed_in, d_qkv, preferred_element_type=f32)
        d_normed = chain_sum(attn_part, 1)
        share_side = scatter(jnp.concatenate([side_grad, gain_cols], axis=1), 0)
        share_gains = lax.psum(share_side[:, qkv_width : qkv_width + 4].T, "tensor")
    d_in_norm = norm_back(inputs, gain_float[0], d_normed.astype(f32))
    input_grad = d_middle + d_in_norm
    return (
        block["out"].reshape(tokens.shape),
        input_grad.reshape(tokens.shape),
        share_side[:, :query_width],
        share_side[:, query_width : query_width + HEAD],
        share_side[:, query_width + HEAD : qkv_width],
        share_out,
        share_gate,
        share_up,
        share_down,
        share_gains,
    )


def solution(mesh):
    placed = (
        P("dp", "seq", None, None),
        P("dp", "seq", None, None),
        P("dp", "seq"),
        P(("dp", "seq"), "tensor"),
        P(("dp", "seq"), "tensor"),
        P(("dp", "seq"), "tensor"),
        P("tensor", ("dp", "seq")),
        P(("dp", "seq"), "tensor"),
        P(("dp", "seq"), "tensor"),
        P("tensor", ("dp", "seq")),
        P(None, ("dp", "seq")),
    )
    return jax.shard_map(
        per_device,
        mesh=mesh,
        in_specs=placed,
        out_specs=(
            P("dp", "seq", None, None),
            P("dp", "seq", None, None),
            P(("dp", "seq"), "tensor"),
            P(("dp", "seq"), "tensor"),
            P(("dp", "seq"), "tensor"),
            P("tensor", ("dp", "seq")),
            P(("dp", "seq"), "tensor"),
            P(("dp", "seq"), "tensor"),
            P("tensor", ("dp", "seq")),
            P(None, ("dp", "seq")),
        ),
        check_vma=False,
    )
```

```python
import functools

import jax
import jax.numpy as jnp
from jax import lax
from jax.experimental import pallas as pl
from jax.experimental.pallas import tpu as pltpu
from jax.sharding import PartitionSpec as P

MESH = pl.DeviceIdType.MESH

HEAD = 256
CONT = 32
BLOCK = 16


EPS = 1e-06
SOFTCAP = 50.0
THETA = 10000.0


def chain_kernel(size, width, x_ref, o_ref, low_buf, high_buf, *sems):
    low_in, low_out, low_last_in, low_last_out, high_in, high_out, high_last_in, high_last_out = sems
    place = lax.axis_index("tensor")
    dp, seq = lax.axis_index("dp"), lax.axis_index("seq")
    down = (dp, seq, jnp.maximum(place - 1, 0))
    up = (dp, seq, jnp.minimum(place + 1, size - 1))
    first, last = place == 0, place == size - 1
    chunks = x_ref.shape[1] // width
    half = x_ref.shape[0] // 2
    rows = (pl.ds(0, half), pl.ds(half, half))
    barrier = pltpu.get_barrier_semaphore()

    @pl.when(jnp.logical_not(first))
    def _():
        pl.semaphore_signal(barrier, inc=1, device_id=down, device_id_type=MESH)

    @pl.when(jnp.logical_not(last))
    def _():
        pl.semaphore_signal(barrier, inc=1, device_id=up, device_id_type=MESH)
    pl.semaphore_wait(barrier, 2 - first.astype(jnp.int32) - last.astype(jnp.int32))

    def columns(c):
        return pl.ds(pl.multiple_of(c * width, 128), width)

    def side(which):
        buf = (low_buf, high_buf)[which]
        sin, sout, lin, lout = (sems[4 * which: 4 * which + 4])
        toward = (down, up)[which]
        back = (up, down)[which]
        start = (last, first)[which]
        end = (first, last)[which]
        rank = (size - 1 - place, place)[which]
        rs = rows[which]

        def passing(c, src):
            return pltpu.make_async_remote_copy(src, buf.at[c], sout.at[c], sin.at[c], device_id=toward, device_id_type=MESH)

        def sharing(c, ):
            view = o_ref.at[rs, columns(c)]
            return pltpu.make_async_remote_copy(view, view, lout.at[c], lin.at[c], device_id=back, device_id_type=MESH)

        def reduce_step(s):
            c = s - rank
            ok = (c >= 0) & (c < chunks)

            @pl.when(ok & start)
            def _():
                passing(c, x_ref.at[rs, columns(c)]).start()

            @pl.when(ok & jnp.logical_not(start))
            def _():
                passing(c, buf.at[c]).wait_recv()
                total = buf[c].astype(jnp.float32) + x_ref[rs, columns(c)].astype(jnp.float32)

                @pl.when(end)
                def _():
                    o_ref[rs, columns(c)] = total.astype(jnp.bfloat16)
                    sharing(c).start()

                @pl.when(jnp.logical_not(end))
                def _():
                    buf[c] = total.astype(jnp.bfloat16)
                    passing(c, buf.at[c]).start()

        def share_step(s):
            c = s - (size - 1) - (size - 1 - rank)
            ok = (c >= 0) & (c < chunks)

            @pl.when(ok & jnp.logical_not(end))
            def _():
                sharing(c).wait_recv()

                @pl.when(jnp.logical_not(start))
                def _():
                    sharing(c).start()

        def finish(c):
            @pl.when(jnp.logical_not(end))
            def _():
                passing(c, buf.at[c]).wait_send()

            @pl.when(jnp.logical_not(start))
            def _():
                sharing(c).wait_send()
        return reduce_step, share_step, finish

    sides = [side(0), side(1)]

    @pl.loop(0, chunks + 2 * (size - 1))
    def _(s):
        for one in sides:
            one[0](s)
        for one in sides:
            one[1](s)

    @pl.loop(0, chunks)
    def _(c):
        for one in sides:
            one[2](c)


def chain_sum(x, cid, width=256):
    size = lax.axis_size("tensor")
    rows, cols = x.shape
    chunks = cols // width
    return pl.pallas_call(
        functools.partial(chain_kernel, size, width),
        out_shape=jax.ShapeDtypeStruct(x.shape, jnp.bfloat16),
        in_specs=[pl.BlockSpec(memory_space=pltpu.VMEM)],
        out_specs=pl.BlockSpec(memory_space=pltpu.VMEM),
        scratch_shapes=[pltpu.VMEM((chunks, rows // 2, width), jnp.bfloat16)] * 2
        + [pltpu.SemaphoreType.DMA((chunks,))] * 8,
        compiler_params=pltpu.CompilerParams(collective_id=cid, has_side_effects=True, vmem_limit_bytes=48 * 2**20),
        cost_estimate=pl.CostEstimate(flops=rows*cols, bytes_accessed=200*2**20, transcendentals=0),
    )(x)


TILE = 256
STAGES = 6
LAG = 2
PACE = 1


def chain_place(size):
    place = lax.axis_index("tensor")
    dp, seq = lax.axis_index("dp"), lax.axis_index("seq")
    down = (dp, seq, jnp.maximum(place - 1, 0))
    up = (dp, seq, jnp.minimum(place + 1, size - 1))
    return place, down, up, place == 0, place == size - 1


def plane_partners():
    dp, seq, place = (lax.axis_index(name) for name in ("dp", "seq", "tensor"))
    x, core = dp // 2, lax.rem(dp, 2)
    return ((1 - x) * 2 + core, seq, place), (dp, 1 - seq, place), (x * 2 + 1 - core, seq, place)


def greet_line(down, up, first, last, others=()):
    barrier = pltpu.get_barrier_semaphore()
    for partner in others:
        pl.semaphore_signal(barrier, inc=1, device_id=partner, device_id_type=MESH)

    @pl.when(jnp.logical_not(first))
    def _():
        pl.semaphore_signal(barrier, inc=1, device_id=down, device_id_type=MESH)

    @pl.when(jnp.logical_not(last))
    def _():
        pl.semaphore_signal(barrier, inc=1, device_id=up, device_id_type=MESH)

    pl.semaphore_wait(barrier, 2 + len(others) - first.astype(jnp.int32) - last.astype(jnp.int32))


def gelu_parts(gate):
    square = gate * gate
    slope = 0.7978845608028654
    curve = jnp.tanh(gate * (slope + (slope * 0.044715) * square))
    half = 0.5 + 0.5 * curve
    rise = (0.5 * gate) * (1.0 - curve * curve) * (slope + (3.0 * slope * 0.044715) * square)
    return gate * half, half + rise


def plane_gather(full_ref, own_ref, pieces, sems_in, sems_out, own_done):
    share = own_ref.shape[0]
    dp, seq = lax.axis_index("dp"), lax.axis_index("seq")
    x, core = dp // 2, lax.rem(dp, 2)
    over_x, over_y, over_core = plane_partners()
    routes = (
        ((0, 0, 0), 0, over_x, (1, 0, 0)),
        ((0, 0, 0), 0, over_y, (0, 1, 0)),
        ((0, 0, 0), 0, over_core, (0, 0, 1)),
        ((1, 0, 0), 1, over_y, (1, 1, 0)),
        ((0, 1, 0), 2, over_x, (1, 1, 0)),
        ((1, 0, 0), 0, over_core, (1, 0, 1)),
        ((0, 1, 0), 0, over_core, (0, 1, 1)),
        ((1, 1, 0), 1, over_core, (1, 1, 1)),
        ((1, 1, 0), 2, over_core, (1, 1, 1)),
    )

    def across(u, part):
        _, _, low, count, left = pieces[u]
        return (pl.ds(low, count), pl.ds(low, left), pl.ds(low + left, count - left))[part]

    def live(u, kind):
        _, _, _, count, left = pieces[u]
        return routes[kind][1] != 2 or left < count

    def view(u, at, part):
        nx, ny, nc = (jnp.abs(now - flip) for now, flip in zip((x, seq, core), at))
        row = ((nx * 2 + nc) * 2 + ny) * share + pieces[u][0]
        return full_ref.at[pl.ds(pl.multiple_of(row, 16), pieces[u][1]), across(u, part)]

    def own(u):
        return own_ref.at[pl.ds(pieces[u][0], pieces[u][1]), across(u, 0)]

    def hop(u, kind, source, target):
        return pltpu.make_async_remote_copy(
            source, target, sems_out.at[u, kind], sems_in.at[u, kind],
            device_id=routes[kind][2], device_id_type=MESH)

    def send(u, kind):
        if live(u, kind):
            at, part, _, _ = routes[kind]
            target = view(u, at, part)
            hop(u, kind, own(u) if kind < 3 else target, target).start()

    def arrive(u, kind):
        if live(u, kind):
            _, part, _, at = routes[kind]
            target = view(u, at, part)
            hop(u, kind, target, target).wait_recv()

    def own_copy(u):
        return pltpu.make_async_copy(own(u), view(u, (0, 0, 0), 0), own_done.at[u])

    def first(u):
        for kind in (0, 1, 2):
            send(u, kind)
        own_copy(u).start()

    def second(u):
        arrive(u, 0)
        send(u, 3)
        send(u, 5)
        arrive(u, 1)
        send(u, 4)
        send(u, 6)

    def third(u):
        arrive(u, 3)
        send(u, 7)
        arrive(u, 4)
        send(u, 8)

    def finish(u):
        own_copy(u).wait()
        for kind in (2, 5, 6, 7, 8):
            arrive(u, kind)

    def all_sent():
        for u in range(len(pieces)):
            for kind, (at, part, _, _) in enumerate(routes):
                if live(u, kind):
                    target = view(u, at, part)
                    hop(u, kind, target, target).wait_send()

    return first, second, third, finish, all_sent


def line_stream(size, width, bases, parts, landing, sum_ref, sems, spot):
    place, down, up, first, last = spot
    pass_in, pass_out, share_in, share_out, local_done = sems
    _, rows, depth = parts.shape
    half = rows // 2
    chunks = depth // width

    def side(which):
        toward, back = ((down, up), (up, down))[which]
        start, end = ((last, first), (first, last))[which]
        rank = (size - 1 - place, place)[which]
        span = pl.ds(which * half, half)

        def where_at(u):
            q = jnp.int32(0)
            base = jnp.int32(bases[0])
            for k in range(1, len(bases)):
                past = (u >= bases[k]).astype(jnp.int32)
                q = q + past
                base = base + past * (bases[k] - bases[k - 1])
            c = u - base
            return q, c, (c >= 0) & (c < chunks)

        def columns(c):
            return pl.ds(pl.multiple_of(c * width, 128), width)

        def passing(q, c, source):
            return pltpu.make_async_remote_copy(
                source, landing.at[which, q, c], pass_out.at[which, q, c], pass_in.at[which, q, c],
                device_id=toward, device_id_type=MESH)

        def sharing(q, c, source):
            return pltpu.make_async_remote_copy(
                source, sum_ref.at[q, span, columns(c)], share_out.at[which, q, c], share_in.at[which, q, c],
                device_id=back, device_id_type=MESH)

        def local(q, c):
            return pltpu.make_async_copy(
                landing.at[which, q, c], sum_ref.at[q, span, columns(c)], local_done.at[which, q, c])

        def reduce_step(s):
            q, c, ok = where_at(s - LAG * rank)
            m = lax.rem(q, 2)

            @pl.when(ok & start)
            def _():
                passing(q, c, parts.at[m, span, columns(c)]).start()

            @pl.when(ok & jnp.logical_not(start))
            def _():
                passing(q, c, landing.at[which, q, c]).wait_recv()
                mine = parts[m, span, columns(c)].astype(jnp.float32)
                landing[which, q, c] = (landing[which, q, c].astype(jnp.float32) + mine).astype(jnp.bfloat16)

                @pl.when(end)
                def _():
                    sharing(q, c, landing.at[which, q, c]).start()
                    local(q, c).start()

                @pl.when(jnp.logical_not(end))
                def _():
                    passing(q, c, landing.at[which, q, c]).start()

        def share_step(s):
            q, c, ok = where_at(s - LAG * (2 * (size - 1) - rank))

            @pl.when(ok & jnp.logical_not(end))
            def _():
                view = sum_ref.at[q, span, columns(c)]
                sharing(q, c, view).wait_recv()

                @pl.when(jnp.logical_not(start))
                def _():
                    sharing(q, c, view).start()

        def settle(q):
            @pl.when(end)
            def _():
                @pl.loop(0, chunks)
                def _(c):
                    local(q, c).wait()

        def sent(q):
            @pl.when(jnp.logical_not(end))
            def _():
                @pl.loop(0, chunks)
                def _(c):
                    passing(q, c, landing.at[which, q, c]).wait_send()

        def shared(q):
            @pl.when(jnp.logical_not(start))
            def _():
                @pl.loop(0, chunks)
                def _(c):
                    sharing(q, c, landing.at[which, q, c]).wait_send()

        return reduce_step, share_step, settle, sent, shared

    sides = (side(0), side(1))

    def tick(s):
        for one in sides:
            one[0](s)
        for one in sides:
            one[1](s)

    def settle(q):
        for one in sides:
            one[2](q)

    def sent(q):
        for one in sides:
            one[3](q)

    def shared():
        @pl.loop(0, len(bases))
        def _(q):
            for one in sides:
                one[4](q)

    def ticks(low, high):
        @pl.loop(low, high)
        def _(s):
            tick(s)

    return tick, ticks, settle, sent, shared


def ffn_kernel(
    size, width, bases, schedule, gather,
    part_ref, token_ref, cot_ref, gate_own, up_own, down_own, gain_ref,
    sum_ref, out_ref, ffn_in_ref, hidden_ref, d_ffn_ref, d_attn_ref, d_middle_ref,
    grad_gate_ref, grad_up_ref, grad_down_ref, full_ref, gain_grad_ref,
    parts, landing, act_a, act_b, stage, cols, rows_w,
    pass_in, pass_out, share_in, share_out, local_done, col_sem, row_sem, io_sem, gather_in, gather_out, own_done,
):
    micro, rows, depth = parts.shape
    units = gate_own.shape[1]
    stage_t, stage_a, stage_f, stage_c = (stage.at[pl.ds(k * rows, rows)] for k in range(4))
    owned = (gate_own, up_own, down_own)
    gate_ref, up_ref, down_ref = (full_ref.at[k] for k in range(3)) if gather else owned
    spot = place, down, up, first, last = chain_place(size)
    greet_line(down, up, first, last, plane_partners() if gather else ())

    tick, ticks, settle, sent, shared = line_stream(
        size, width, bases, parts, landing, sum_ref,
        (pass_in, pass_out, share_in, share_out, local_done), spot)

    def col_copy(kind, source, i, slot):
        return pltpu.make_async_copy(
            source.at[:, pl.ds(pl.multiple_of(i * TILE, TILE), TILE)], cols.at[kind, slot], col_sem.at[kind, slot])

    def row_copy(kind, source, i, slot):
        return pltpu.make_async_copy(
            source.at[pl.ds(pl.multiple_of(i * TILE, TILE), TILE)], rows_w.at[kind, slot], row_sem.at[kind, slot])

    def tiles(copy, sources, steps, body, clock, beside=()):
        @pl.loop(0, steps)
        def _(i):
            slot = lax.rem(i, 2)

            @pl.when(i + 1 < steps)
            def _():
                for kind, source in enumerate(sources):
                    copy(kind, source, i + 1, 1 - slot).start()

            for kind, source in enumerate(sources):
                copy(kind, source, i, slot).wait()
            body(i, slot)
            for at, work in beside:
                pl.when(i == at)(work)

            @pl.when((lax.rem(i, PACE) == PACE - 1) | (i + 1 == steps))
            def _():
                tick(clock + i // PACE)

    def prime(copy, sources):
        for kind, source in enumerate(sources):
            copy(kind, source, 0, 0).start()

    def span_of(i):
        return pl.ds(pl.multiple_of(i * TILE, TILE), TILE)

    def io(index, source, target):
        return pltpu.make_async_copy(source, target, io_sem.at[index])

    def row_blocks(body, clock):
        count = rows // BLOCK
        for low, high, s in ((0, count // 2, clock), (count // 2, count, clock + 1)):
            @pl.loop(low, high)
            def _(b):
                body(pl.ds(pl.multiple_of(b * BLOCK, BLOCK), BLOCK))
            tick(s)

    def own_rows(m):
        return pl.ds(m * rows, rows)

    def gain(k):
        return gain_ref[k : k + 1, :]

    def inverse(values):
        return lax.rsqrt(jnp.mean(values * values, axis=-1, keepdims=True) + EPS)

    def middle_of(span):
        attn = stage_a[span, :].astype(jnp.float32)
        return stage_t[span, :].astype(jnp.float32) + attn * inverse(attn) * gain(1)

    def norm_before(m, clock):
        def body(span):
            middle = middle_of(span)
            stage_f[span, :] = (middle * inverse(middle) * gain(2)).astype(jnp.bfloat16)
        row_blocks(body, clock)

    def gate_and_up(m, clock):
        def body(i, slot):
            at = span_of(i)
            gate = jnp.dot(stage_f[...], cols[0, slot], preferred_element_type=jnp.float32)
            up_val = jnp.dot(stage_f[...], cols[1, slot], preferred_element_type=jnp.float32)
            active, slope = gelu_parts(gate)
            stage_c[:, at] = (active * up_val).astype(jnp.bfloat16)
            act_a[own_rows(m), at] = active.astype(jnp.bfloat16)
            act_b[own_rows(m), at] = (up_val * slope).astype(jnp.bfloat16)
        def down_one():
            moved(1, 4)

        def down_two():
            moved(2, 4)
            moved(1, 5)

        def down_three():
            moved(2, 5)

        beside = ((2, down_one), (5, down_two), (8, down_three)) if gather and m == 0 else ()
        tiles(col_copy, (gate_ref, up_ref), units // TILE, body, clock, beside)

    def down_proj(m, clock):
        def body(i, slot):
            parts[m, :, span_of(i)] = lax.dot_general(
                stage_c[...], rows_w[0, slot], (((1,), (1,)), ((), ())),
                preferred_element_type=jnp.float32).astype(jnp.bfloat16)
        tiles(row_copy, (down_ref,), depth // TILE, body, clock)

    def norm_after(m, clock):
        def body(span):
            middle = middle_of(span)
            ffn = stage_f[span, :].astype(jnp.float32)
            above = stage_c[span, :].astype(jnp.float32)
            inv = inverse(ffn)
            normed = ffn * inv
            stage_f[span, :] = (middle + normed * gain(3)).astype(jnp.bfloat16)
            scaled = above * gain(3)
            d_ffn = inv * (scaled - normed * jnp.mean(scaled * normed, axis=-1, keepdims=True))
            stage_c[span, :] = d_ffn.astype(jnp.bfloat16)
            term = above * normed
            gain_grad_ref[16:24, :] += term[:8] + term[8:]
        row_blocks(body, clock)

    def d_hidden(m, clock):
        def body(i, slot):
            at = span_of(i)
            d_hid = jnp.dot(stage_c[...], cols[0, slot], preferred_element_type=jnp.float32)
            mine = own_rows(m)
            act_a[mine, at] = (d_hid * act_a[mine, at].astype(jnp.float32)).astype(jnp.bfloat16)
            act_b[mine, at] = (d_hid * act_b[mine, at].astype(jnp.float32)).astype(jnp.bfloat16)
        tiles(col_copy, (down_ref,), units // TILE, body, clock)

    def d_input(m, clock):
        def body(i, slot):
            dims = (((1,), (1,)), ((), ()))
            parts[m, :, span_of(i)] = (
                lax.dot_general(act_b[own_rows(m), :], rows_w[0, slot], dims, preferred_element_type=jnp.float32)
                + lax.dot_general(act_a[own_rows(m), :], rows_w[1, slot], dims, preferred_element_type=jnp.float32)
            ).astype(jnp.bfloat16)
        tiles(row_copy, (gate_ref, up_ref), depth // TILE, body, clock)

    def norm_back_middle(m, clock):
        def body(span):
            attn = stage_a[span, :].astype(jnp.float32)
            attn_inv = inverse(attn)
            attn_normed = attn * attn_inv
            middle = stage_t[span, :].astype(jnp.float32) + attn_normed * gain(1)
            inv = inverse(middle)
            normed = middle * inv
            below = stage_f[span, :].astype(jnp.float32)
            scaled = below * gain(2)
            d_middle = stage_c[span, :].astype(jnp.float32) + inv * (
                scaled - normed * jnp.mean(scaled * normed, axis=-1, keepdims=True))
            term = below * normed
            gain_grad_ref[8:16, :] += term[:8] + term[8:]
            stage_c[span, :] = d_middle.astype(jnp.bfloat16)
            scaled = d_middle * gain(1)
            d_attn = attn_inv * (scaled - attn_normed * jnp.mean(scaled * attn_normed, axis=-1, keepdims=True))
            stage_f[span, :] = d_attn.astype(jnp.bfloat16)
            term = d_middle * attn_normed
            gain_grad_ref[0:8, :] += term[:8] + term[8:]
        row_blocks(body, clock)

    def tall_copy(source, i, slot, m):
        return pltpu.make_async_copy(
            source.at[m, :, span_of(i)], cols.at[0, slot, own_rows(m)], col_sem.at[m, slot])

    def weight_grads(source, pairs, steps, clock):
        def put(kind, target, i, slot):
            return pltpu.make_async_copy(rows_w.at[kind, slot], target.at[span_of(i)], row_sem.at[kind, slot])

        @pl.loop(0, steps)
        def _(i):
            slot = lax.rem(i, 2)

            @pl.when(i + 1 < steps)
            def _():
                for m in range(micro):
                    tall_copy(source, i + 1, 1 - slot, m).start()

            for m in range(micro):
                tall_copy(source, i, slot, m).wait()

            @pl.when(i >= 2)
            def _():
                for kind, (_, target) in enumerate(pairs):
                    put(kind, target, i - 2, slot).wait()

            left = cols[0, slot, : micro * rows, :]
            for kind, (right, target) in enumerate(pairs):
                for low in range(0, units, 3 * TILE):
                    high = min(units, low + 3 * TILE)
                    rows_w[kind, slot, :, low:high] = lax.dot_general(
                        left, right[: micro * rows, low:high], (((0,), (0,)), ((), ())),
                        preferred_element_type=jnp.float32).astype(jnp.bfloat16)
                put(kind, target, i, slot).start()
            tick(clock + i)

        for i in (steps - 2, steps - 1):
            for kind, (_, target) in enumerate(pairs):
                put(kind, target, i, i % 2).wait()

    if gather:
        piece = gate_own.shape[0] // 2
        pieces = tuple((h * piece, piece, 0, units, units // 2) for h in range(2))
        movers = [
            plane_gather(full_ref.at[k], owned[k], pieces, gather_in.at[k], gather_out.at[k], own_done.at[k])
            for k in range(3)
        ]

        def moved(phase, u):
            movers[u // 2][phase](u % 2)

    else:

        def moved(phase, u):
            pass

    gain_grad_ref[...] = jnp.zeros_like(gain_grad_ref)

    def load(index, source, target):
        return pltpu.make_async_copy(source, target, io_sem.at[index])

    def bring(m, third=None, fourth=None):
        found = [load(2, token_ref.at[m], stage_t), load(3, sum_ref.at[m], stage_a)]
        if third is not None:
            found += [load(4, third, stage_f), load(5, fourth, stage_c)]
        return found

    def start(copies):
        for copy in copies:
            copy.start()

    def wait(copies):
        for copy in copies:
            copy.wait()

    whole = schedule["attn"][0]
    entry = [load(m, part_ref.at[m], parts.at[m]) for m in range(micro)]
    start(entry)
    moved(0, 0)
    moved(0, 1)
    wait(entry)
    clock = 0
    for s, phases in (
        (7, ((1, 0), (0, 2))),
        (14, ((1, 1), (2, 0), (0, 3))),
        (21, ((1, 2), (2, 1), (0, 4))),
        (28, ((1, 3), (2, 2), (0, 5))),
    ):
        ticks(clock, s)
        clock = s
        for phase, u in phases:
            moved(phase, u)
    ticks(clock, whole)
    kept = []
    for m in range(micro):
        norm_s, gate_s, down_s, end_s = schedule["forward"][m]
        settle(m)
        wait(kept)
        loads = bring(m)
        start(loads)
        wait(loads)
        norm_before(m, norm_s)
        kept = [load(6, stage_f, ffn_in_ref.at[m]), load(7, stage_c, hidden_ref.at[m])]
        kept[0].start()
        if m == 0:
            moved(2, 3)
            for u in range(4):
                moved(3, u)
            prime(col_copy, (gate_ref, up_ref))
        gate_and_up(m, gate_s)
        kept[1].start()
        sent(m)
        if m == 0:
            moved(3, 4)
            moved(3, 5)
        prime(row_copy, (down_ref,))
        prime(col_copy, (gate_ref, up_ref) if m + 1 < micro else (down_ref,))
        down_proj(m, down_s)
        ticks(down_s + -(-depth // (TILE * PACE)), end_s)
    wait(kept)
    for m in range(micro):
        norm_s, dh_s, di_s, end_s = schedule["backward"][m]
        settle(micro + m)
        if m:
            wait(kept)
        loads = bring(m, sum_ref.at[micro + m], cot_ref.at[m])
        start(loads)
        wait(loads)
        norm_after(m, norm_s)
        kept = [load(6, stage_f, out_ref.at[m]), load(7, stage_c, d_ffn_ref.at[m])]
        start(kept)
        prime(row_copy, (gate_ref, up_ref))
        d_hidden(m, dh_s)
        sent(micro + m)
        if m + 1 < micro:
            prime(col_copy, (down_ref,))
        d_input(m, di_s)
        ticks(di_s + -(-depth // (TILE * PACE)), end_s)
    wait(kept)
    norm_s, grads_s, down_s, end_s = schedule["grads"]
    settle(2 * micro)
    loads = bring(0, sum_ref.at[2 * micro], cot_ref.at[0])
    start(loads)
    for m in range(micro):
        tall_copy(ffn_in_ref, 0, 0, m).start()
    wait(loads)
    norm_back_middle(0, norm_s)
    kept = [load(6, stage_f, d_attn_ref.at[0]), load(7, stage_c, d_middle_ref.at[0])]
    start(kept)
    hidden_loads = [load(2 + m, hidden_ref.at[m], stage.at[own_rows(m)]) for m in range(micro)]
    start(hidden_loads)
    steps = depth // TILE
    weight_grads(ffn_in_ref, ((act_b, grad_gate_ref), (act_a, grad_up_ref)), steps, grads_s)
    for m in range(micro):
        tall_copy(d_ffn_ref, 0, 0, m).start()
    wait(hidden_loads)
    weight_grads(d_ffn_ref, ((stage, grad_down_ref),), steps, down_s)
    wait(kept)
    tail = bring(1, None)
    tail.append(load(5, cot_ref.at[1], stage_c))
    start(tail)
    ticks(down_s + steps, end_s)
    settle(2 * micro + 1)
    tail.append(load(4, sum_ref.at[2 * micro + 1], stage_f))
    tail[-1].start()
    wait(tail)
    norm_back_middle(1, end_s)
    kept = [load(6, stage_f, d_attn_ref.at[1]), load(7, stage_c, d_middle_ref.at[1])]
    start(kept)
    sent(STAGES - 2)
    sent(STAGES - 1)
    if gather:
        for mover in movers:
            mover[4]()
    wait(kept)

    shared()


def ffn_schedule(chunks, tiles, hops):
    whole = chunks + hops
    bases = [0, chunks]
    at = whole
    attn = (at,)
    forward = []
    for m in range(2):
        norm_s = at
        gate_s = norm_s + 2
        down_s = gate_s + tiles
        bases.append(max(down_s, bases[-1] + chunks))
        at = max(down_s + tiles, bases[m + 1] + whole)
        forward.append((norm_s, gate_s, down_s, at))
    backward = []
    for m in range(2):
        norm_s = at
        dh_s = norm_s + 2
        di_s = dh_s + tiles
        bases.append(max(di_s, bases[-1] + chunks))
        at = max(di_s + tiles, bases[m + 3] + whole)
        backward.append((norm_s, dh_s, di_s, at))
    grads_s = at + 2
    grads = (at, grads_s, grads_s + tiles, max(grads_s + 2 * tiles, bases[-1] + whole))
    return tuple(bases), {
        "attn": attn, "forward": tuple(forward), "backward": tuple(backward), "grads": grads
    }


def ffn_block(parts, tokens, cotangent, gate, up, down, gains, cid, width=128):
    size = lax.axis_size("tensor")
    micro, rows, depth = tokens.shape
    units = gate.shape[1]
    chunks = depth // width
    bases, schedule = ffn_schedule(chunks, -(-units // (TILE * PACE)), 2 * LAG * (size - 1))
    bf16 = jnp.bfloat16
    any_spec = pl.BlockSpec(memory_space=pl.ANY)
    vmem_spec = pl.BlockSpec(memory_space=pltpu.VMEM)
    gather = up.shape[0] != depth
    stack = jax.ShapeDtypeStruct((micro, rows, depth), bf16)
    wide = jax.ShapeDtypeStruct((micro, rows, units), bf16)
    grad = jax.ShapeDtypeStruct((depth, units), bf16)
    full = jax.ShapeDtypeStruct((3, depth, units) if gather else (3, 16, 128), bf16)
    dma = pltpu.SemaphoreType.DMA
    flops = 2 * micro * rows * depth * units * 9
    found = pl.pallas_call(
        functools.partial(ffn_kernel, size, width, bases, schedule, gather),
        out_shape=(
            jax.ShapeDtypeStruct((STAGES, rows, depth), bf16),
            stack, stack, wide, stack, stack, stack, grad, grad, grad, full,
            jax.ShapeDtypeStruct((24, depth), jnp.float32),
        ),
        in_specs=[any_spec] * 6 + [vmem_spec],
        out_specs=(any_spec,) * 11 + (vmem_spec,),
        scratch_shapes=[
            pltpu.VMEM((micro, rows, depth), bf16),
            pltpu.VMEM((2, STAGES, chunks, rows // 2, width), bf16),
            pltpu.VMEM((micro * rows, units), bf16),
            pltpu.VMEM((micro * rows, units), bf16),
            pltpu.VMEM((4 * rows, depth), bf16),
            pltpu.VMEM((2, 2, depth, TILE), bf16),
            pltpu.VMEM((2, 2, TILE, units), bf16),
        ]
        + [dma((2, STAGES, chunks))] * 5
        + [dma((2, 2)), dma((2, 2)), dma((8,)), dma((3, 2, 9)), dma((3, 2, 9)), dma((3, 2))],
        compiler_params=pltpu.CompilerParams(
            collective_id=cid, has_side_effects=True, vmem_limit_bytes=60 * 2**20),
        cost_estimate=pl.CostEstimate(
            flops=flops, bytes_accessed=2**30, transcendentals=micro * rows * units),
    )(parts, tokens, cotangent, gate, up, down, gains)
    return {
        "attn": found[0][:micro], "out": found[1], "d_attn": found[5], "d_middle": found[6],
        "grad_gate": found[7], "grad_up": found[8], "grad_down": found[9], "gain_grad": found[11],
        "sums": found[0], "ffn_in": found[2], "hidden": found[3], "d_ffn": found[4],
    }

SIDE_PAD = 128


def tail_kernel(
    size, width, bases,
    part_ref, gate_grad_ref, up_grad_ref, normed_ref, d_attn_ref, d_qkv_ref, context_ref, gain_ref,
    sum_ref, gate_share_ref, up_share_ref, side_share_ref, gain_share_ref,
    parts, landing, mine_in, side_acc, ffn_first, side_first, ffn_second, side_second, ffn_third, side_third,
    cols, d_qkv, context, gain_in,
    pass_in, pass_out, share_in, share_out, local_done, col_sem, io_sem, mine_sem, hop_in, hop_out, gain_got, gain_sent,
):
    micro, rows, depth = parts.shape
    spot = place, down, up, first, last = chain_place(size)
    over_x, over_y, over_core = plane_partners()
    dp, seq = lax.axis_index("dp"), lax.axis_index("seq")
    x, core = dp // 2, lax.rem(dp, 2)
    others = [(dp, seq, lax.rem(place + k, size)) for k in range(1, size)]
    greet_plane(over_x, over_y, over_core, others)
    tick, ticks, settle, sent, shared = line_stream(
        size, width, bases, parts, landing, sum_ref,
        (pass_in, pass_out, share_in, share_out, local_done), spot)
    share = up_share_ref.shape[0]
    piece = share // 2
    widths = (up_share_ref.shape[1], side_share_ref.shape[1])
    grads = (gate_grad_ref, up_grad_ref)
    qkv_width = d_qkv.shape[1]

    def load(index, source, target):
        return pltpu.make_async_copy(source, target, io_sem.at[index])

    def halves(p):
        all_columns = widths[p // 4]
        low = -(-all_columns // 256) * 128
        return (pl.ds(0, low), pl.ds(low, all_columns - low))

    def block_rows(bx, by, bc, p):
        return pl.ds(pl.multiple_of(((bx * 2 + bc) * 2 + by) * share + (p % 2) * piece, 16), piece)

    def acc(p, bx, by, across):
        if p < 4:
            return ffn_first.at[p, bx * 2 + by, :, across]
        return side_acc.at[block_rows(bx, by, core, p), across]

    def whole(p):
        return pl.ds(0, widths[p // 4])

    first_buf, second_buf, third_buf = (ffn_first, side_first), (ffn_second, side_second), (ffn_third, side_third)

    def land(step, p, k, across):
        buf = (first_buf, second_buf, third_buf)[step][p // 4]
        return buf.at[p % 4, k, :, across]

    def hop(p, k, source, target, device):
        return pltpu.make_async_remote_copy(
            source, target, hop_out.at[p, k], hop_in.at[p, k], device_id=device, device_id_type=MESH)

    def hops(p):
        left, right = halves(p)
        found = []
        for k in range(4):
            bx, by = k // 2, k % 2
            if p < 4:
                source = grads[p // 2].at[block_rows(bx, by, 1 - core, p), :]
            else:
                source = side_acc.at[block_rows(bx, by, 1 - core, p), :]
            found.append((source, land(0, p, k, whole(p)), over_core))
        for k in range(2):
            found.append((acc(p, 1 - x, k, left), land(1, p, k, left), over_x))
        for k in range(2):
            found.append((acc(p, k, 1 - seq, right), land(1, p, k, right), over_y))
        found.append((acc(p, x, 1 - seq, left), land(2, p, 0, left), over_y))
        found.append((acc(p, 1 - x, seq, right), land(2, p, 0, right), over_x))
        return found

    def go(p, k):
        source, target, device = hops(p)[k]
        hop(p, k, source, target, device).start()

    def got(p, k):
        _, target, device = hops(p)[k]
        hop(p, k, target, target, device).wait_recv()
        return target

    def fetch(p, k):
        return pltpu.make_async_copy(
            grads[p // 2].at[block_rows(k // 2, k % 2, core, p), :], mine_in.at[k], mine_sem.at[k])

    def start_fetch(p):
        for k in range(4):
            fetch(p, k).start()

    def add(p, bx, by, across, arrived):
        mine = acc(p, bx, by, across)

        @pl.loop(0, piece // BLOCK)
        def _(b):
            span = pl.ds(pl.multiple_of(b * BLOCK, BLOCK), BLOCK)
            mine[span, :] = (
                mine[span, :].astype(jnp.float32) + arrived[span, :].astype(jnp.float32)
            ).astype(jnp.bfloat16)

    def scatter_first(p):
        for k in range(4):
            go(p, k)

    def scatter_second(p):
        for k in range(4):
            arrived = got(p, k)
            if p < 4:
                fetch(p, k).wait()
                arrived = mine_in.at[k]
            add(p, k // 2, k % 2, whole(p), arrived)
        for k in (4, 5, 6, 7):
            go(p, k)
        if p < 3:
            start_fetch(p + 1)

    def scatter_third(p):
        left, right = halves(p)
        for k in range(2):
            add(p, x, k, left, got(p, 4 + k))
        go(p, 8)
        for k in range(2):
            add(p, k, seq, right, got(p, 6 + k))
        go(p, 9)

    def scatter_last(p):
        left, right = halves(p)
        add(p, x, seq, left, got(p, 8))
        add(p, x, seq, right, got(p, 9))
        put(p).start()

    def put(p):
        target = (gate_share_ref, up_share_ref, side_share_ref)[p // 2].at[pl.ds((p % 2) * piece, piece)]
        return load(5 + p, acc(p, x, seq, whole(p)), target)

    def scatter_sent(p):
        for k, (source, target, device) in enumerate(hops(p)):
            hop(p, k, source, target, device).wait_send()
        put(p).wait()

    def tile_copy(kind, i, slot):
        source = (normed_ref, d_attn_ref)[kind].at[:, pl.ds(pl.multiple_of(i * TILE, TILE), TILE)]
        return pltpu.make_async_copy(source, cols.at[kind, slot], col_sem.at[kind, slot])

    def side_grads(clock):
        steps = depth // TILE

        @pl.loop(0, steps)
        def _(i):
            slot = lax.rem(i, 2)

            @pl.when(i + 1 < steps)
            def _():
                tile_copy(0, i + 1, 1 - slot).start()
                tile_copy(1, i + 1, 1 - slot).start()

            tile_copy(0, i, slot).wait()
            tile_copy(1, i, slot).wait()
            span = pl.ds(pl.multiple_of(i * TILE, TILE), TILE)
            for kind, right, low in ((0, d_qkv, 0), (1, context, qkv_width)):
                side_acc[span, low : low + right.shape[1]] = lax.dot_general(
                    cols[kind, slot], right[...], (((0,), (0,)), ((), ())),
                    preferred_element_type=jnp.float32).astype(jnp.bfloat16)
            tick(clock + i)

    entry = [load(m, part_ref.at[m], parts.at[m]) for m in range(micro)]
    side_loads = [
        load(2, d_qkv_ref, d_qkv),
        load(3, context_ref, context),
        load(4, gain_ref, side_acc.at[:, pl.ds(widths[1] - SIDE_PAD, SIDE_PAD)]),
    ]
    for copy in entry:
        copy.start()
    scatter_first(0)
    scatter_first(1)
    for copy in side_loads:
        copy.start()
    start_fetch(0)
    tile_copy(0, 0, 0).start()
    tile_copy(1, 0, 0).start()
    for copy in entry:
        copy.wait()
    ticks(0, 1)
    for copy in side_loads:
        copy.wait()
    ticks(1, 4)
    scatter_second(0)
    scatter_first(2)
    side_grads(4)
    clock = 4 + depth // TILE
    scatter_second(1)
    scatter_third(0)
    for p in (3, 4, 5):
        scatter_first(p)
    plan = (
        (2, (scatter_second, 2)), (2, (scatter_third, 1)), (2, (scatter_last, 0)), (2, (scatter_second, 3)),
        (2, (scatter_third, 2)), (2, (scatter_last, 1)), (2, (scatter_second, 4)), (2, (scatter_third, 3)),
        (2, (scatter_last, 2)), (1, (scatter_second, 5)), (2, (scatter_third, 4)), (2, (scatter_last, 3)),
        (2, (scatter_third, 5)), (2, (scatter_last, 4)), (2, (scatter_last, 5)),
    )
    for pause, (step, p) in plan:
        if pause:
            ticks(clock, clock + pause)
            clock += pause
        step(p)

    mine = side_acc.at[pl.ds(pl.multiple_of(((x * 2 + core) * 2 + seq) * share, 16), share), pl.ds(widths[1] - SIDE_PAD, SIDE_PAD)]

    def gain_hop(k):
        return pltpu.make_async_remote_copy(
            mine, gain_in.at[k], gain_sent.at[k], gain_got.at[k], device_id=others[k], device_id_type=MESH)

    for k in range(size - 1):
        gain_hop(k).start()
    ticks(clock, clock + 2)
    clock += 2
    for k in range(size - 1):
        gain_hop(k).wait_recv()
    total = mine[...].astype(jnp.float32)
    for k in range(size - 1):
        total = total + gain_in[k].astype(jnp.float32)
    gain_share_ref[...] = total
    ticks(clock, max(clock, bases[-1] + depth // width + 2 * LAG * (size - 1)))
    for q in range(micro):
        settle(q)
        sent(q)
    shared()
    for p in range(6):
        scatter_sent(p)
    for k in range(size - 1):
        gain_hop(k).wait_send()


def greet_plane(over_x, over_y, over_core, others):
    barrier = pltpu.get_barrier_semaphore()
    partners = (over_x, over_y, over_core, *others)
    for partner in partners:
        pl.semaphore_signal(barrier, inc=1, device_id=partner, device_id_type=MESH)
    pl.semaphore_wait(barrier, len(partners))


def tail_block(parts, gate_grad, up_grad, normed, d_attn, d_qkv, context, gain_cols, cid, width=128):
    size = lax.axis_size("tensor")
    micro, rows, depth = parts.shape
    units = up_grad.shape[1]
    chunks = depth // width
    total = micro * rows
    share = depth // (lax.axis_size("dp") * lax.axis_size("seq"))
    piece = share // 2
    side = d_qkv.shape[1] + context.shape[1] + SIDE_PAD
    bases = (0, chunks)
    bf16 = jnp.bfloat16
    any_spec = pl.BlockSpec(memory_space=pl.ANY)
    vmem_spec = pl.BlockSpec(memory_space=pltpu.VMEM)
    dma = pltpu.SemaphoreType.DMA
    return pl.pallas_call(
        functools.partial(tail_kernel, size, width, bases),
        out_shape=(
            jax.ShapeDtypeStruct((micro, rows, depth), bf16),
            jax.ShapeDtypeStruct((share, units), bf16),
            jax.ShapeDtypeStruct((share, units), bf16),
            jax.ShapeDtypeStruct((share, side), bf16),
            jax.ShapeDtypeStruct((share, SIDE_PAD), jnp.float32),
        ),
        in_specs=[any_spec] * 8,
        out_specs=(any_spec,) * 4 + (vmem_spec,),
        scratch_shapes=[
            pltpu.VMEM((micro, rows, depth), bf16),
            pltpu.VMEM((2, 2, chunks, rows // 2, width), bf16),
            pltpu.VMEM((4, piece, units), bf16),
            pltpu.VMEM((depth, side), bf16),
            pltpu.VMEM((4, 4, piece, units), bf16),
            pltpu.VMEM((2, 4, piece, side), bf16),
            pltpu.VMEM((4, 2, piece, units), bf16),
            pltpu.VMEM((2, 2, piece, side), bf16),
            pltpu.VMEM((4, 1, piece, units), bf16),
            pltpu.VMEM((2, 1, piece, side), bf16),
            pltpu.VMEM((2, 2, total, TILE), bf16),
            pltpu.VMEM(d_qkv.shape, bf16),
            pltpu.VMEM(context.shape, bf16),
            pltpu.VMEM((size - 1, share, SIDE_PAD), bf16),
        ]
        + [dma((2, 2, chunks))] * 5
        + [dma((2, 2)), dma((11,)), dma((4,)), dma((6, 10)), dma((6, 10)), dma((size - 1,)), dma((size - 1,))],
        compiler_params=pltpu.CompilerParams(
            collective_id=cid, has_side_effects=True, vmem_limit_bytes=60 * 2**20),
        cost_estimate=pl.CostEstimate(
            flops=2 * total * depth * side, bytes_accessed=400 * 2**20, transcendentals=0),
    )(parts, gate_grad, up_grad, normed, d_attn, d_qkv, context, gain_cols)

CAP_SCALE = HEAD ** -0.5 / SOFTCAP


def capped(query, keys):
    raw = lax.dot_general(query, keys, (((1,), (1,)), ((), ())), preferred_element_type=jnp.float32)
    curve = jnp.tanh(raw * CAP_SCALE)
    return curve, jnp.exp(SOFTCAP * curve)


def at_or_before(shape, row_at):
    return lax.broadcasted_iota(jnp.int32, shape, 1) <= lax.broadcasted_iota(jnp.int32, shape, 0) + row_at


def pick_rows(ref, rows, prompt, heads):
    found = []
    for m in range(2):
        for h in range(heads):
            found.append(ref[m * rows + prompt : (m + 1) * rows, h * HEAD : (h + 1) * HEAD])
    return jnp.concatenate(found, axis=0)


def cont_masks(prompt_of, group, cont, heads):
    count = 2 * heads * cont
    row = lax.broadcasted_iota(jnp.int32, (count, 1), 0)
    sees = jnp.where(row < heads * cont, prompt_of[0], prompt_of[1]) == group
    row = lax.broadcasted_iota(jnp.int32, (count, 2 * cont), 0)
    key = lax.broadcasted_iota(jnp.int32, (count, 2 * cont), 1)
    same = (row // (heads * cont)) == (key // cont)
    return sees, same & (lax.rem(key, cont) <= lax.rem(row, cont))


def turn(values, cosine, sine):
    half = HEAD // 2
    low, high = values[:, :half], values[:, half:]
    return jnp.concatenate([low * cosine - high * sine, high * cosine + low * sine], axis=1)


ROW_TILE = 256


def head_kernel(
    heads, cont,
    prompt_of, token_ref, own_ref, angle_ref,
    part_ref, context_ref, query_ref, kv_ref, other_ref, sum_ref, normed_ref, full_ref, gain_ref,
    tokens, normed, full, cosine_sine, queries, kv, other, total, sums, context,
    gather_in, gather_out, own_done, io_sem, swap_in, swap_out,
):
    rows_all, depth = tokens.shape
    rows = rows_all // 2
    prompt = rows - cont
    query_width = heads * HEAD
    qkv_width = query_width + 2 * HEAD
    over_x, over_y, over_core = plane_partners()
    seq = lax.axis_index("seq")
    greet_plane(over_x, over_y, over_core, ())
    share = own_ref.shape[0]
    piece = share // 2
    side = qkv_width + SIDE_PAD
    pieces = (
        (0, share, qkv_width, SIDE_PAD, SIDE_PAD),
        (0, piece, 0, qkv_width, qkv_width // 2),
        (piece, piece, 0, qkv_width, qkv_width // 2),
        (0, share, side, query_width, query_width // 2),
    )
    first, second, third, finish, all_sent = plane_gather(full, own_ref, pieces, gather_in, gather_out, own_done)

    def io(index, source, target):
        return pltpu.make_async_copy(source, target, io_sem.at[index])

    loads = [io(0, token_ref, tokens), io(1, angle_ref, cosine_sine)]
    for u in (0, 1, 2):
        first(u)
    for copy in loads:
        copy.start()
    second(0)
    third(0)
    first(3)
    for copy in loads:
        copy.wait()
    finish(0)
    gain_ref[...] = jnp.transpose(full[:, qkv_width:side].astype(jnp.float32))[:8, :]

    def normalize_rows(low, high):
        @pl.loop(low, high)
        def _(b):
            span = pl.ds(pl.multiple_of(b * BLOCK, BLOCK), BLOCK)
            values = tokens[span, :].astype(jnp.float32)
            inv = lax.rsqrt(jnp.mean(values * values, axis=-1, keepdims=True) + EPS)
            normed[span, :] = (values * inv * gain_ref[0:1, :]).astype(jnp.bfloat16)

    blocks = rows_all // BLOCK
    normalize_rows(0, blocks // 2)
    second(1)
    normalize_rows(blocks // 2, blocks)
    second(2)
    third(1)
    second(3)
    third(2)
    for u in (1, 2):
        finish(u)

    stores = [io(2, normed, normed_ref)]
    stores[0].start()
    half = HEAD // 2

    def project(m, low, count):
        return jnp.dot(normed[pl.ds(m * rows, rows), :], full[:, low : low + count], preferred_element_type=jnp.float32)

    def angles(m):
        span = pl.ds(m * rows, rows)
        return cosine_sine[span, :half], cosine_sine[span, half:]

    def swap(m):
        return pltpu.make_async_remote_copy(
            kv.at[m, pl.ds(0, prompt)], other.at[m], swap_out.at[m], swap_in.at[m],
            device_id=over_y, device_id_type=MESH)

    for m in range(2):
        kv[m, :, :HEAD] = turn(project(m, query_width, HEAD), *angles(m)).astype(jnp.bfloat16)
        kv[m, :, HEAD:] = project(m, query_width + HEAD, HEAD).astype(jnp.bfloat16)
        swap(m).start()
    for m in range(2):
        for h in range(heads):
            queries[pl.ds(m * rows, rows), h * HEAD : (h + 1) * HEAD] = turn(
                project(m, h * HEAD, HEAD), *angles(m)).astype(jnp.bfloat16)
    third(3)
    stores += [io(3, queries, query_ref), io(4, kv, kv_ref)]
    stores[1].start()
    stores[2].start()
    lanes = sums.shape[-1]

    def spots(i, low, count):
        m, h = i // heads, lax.rem(i, heads)
        return m, h, pl.ds(pl.multiple_of(m * rows + low, 16), count), pl.ds(pl.multiple_of(h * HEAD, HEAD), HEAD)

    def attend(weights, values):
        return jnp.dot(weights.astype(jnp.bfloat16), values, preferred_element_type=jnp.float32)

    tiles = [(low, min(ROW_TILE, prompt - low)) for low in range(0, prompt, ROW_TILE)]

    @pl.loop(0, 2 * heads)
    def _(i):
        for low, count in tiles:
            m, h, span, across = spots(i, low, count)
            reach = low + count
            keys = kv[m, :reach, :HEAD]
            values = kv[m, :reach, HEAD:]
            _, weights = capped(queries[span, across], keys)
            weights = jnp.where(at_or_before((count, reach), low), weights, 0.0)
            sums[h, span, :] = jnp.broadcast_to(jnp.sum(weights, axis=1, keepdims=True), (count, lanes))
            total[span, across] = attend(weights, values)

    for m in range(2):
        swap(m).wait_recv()

    @pl.when(seq == 1)
    def _():
        @pl.loop(0, 2 * heads)
        def _(i):
            for low, count in tiles:
                m, h, span, across = spots(i, low, count)
                _, weights = capped(queries[span, across], other[m, :, :HEAD])
                sums[h, span, :] += jnp.broadcast_to(jnp.sum(weights, axis=1, keepdims=True), (count, lanes))
                total[span, across] += attend(weights, other[m, :, HEAD:])

    picked = pick_rows(queries, rows, prompt, heads)
    weight_sum = jnp.zeros((picked.shape[0], 1), jnp.float32)
    weighted = jnp.zeros((picked.shape[0], HEAD), jnp.float32)
    for g in range(2):
        sees, near = cont_masks(prompt_of, g, cont, heads)
        for pair in (kv[g, :prompt, :], other[g]):
            _, weights = capped(picked, pair[:, :HEAD])
            weights = jnp.where(sees, weights, 0.0)
            weight_sum += jnp.sum(weights, axis=1, keepdims=True)
            weighted += attend(weights, pair[:, HEAD:])
    tail = jnp.concatenate([kv[m, prompt:, :] for m in range(2)], axis=0)
    _, weights = capped(picked, tail[:, :HEAD])
    weights = jnp.where(near, weights, 0.0)
    weight_sum += jnp.sum(weights, axis=1, keepdims=True)
    weighted += attend(weights, tail[:, HEAD:])
    for m in range(2):
        for h in range(heads):
            low = (m * heads + h) * cont
            span = pl.ds(m * rows + prompt, cont)
            sums[h, span, :] = jnp.broadcast_to(weight_sum[low : low + cont], (cont, lanes))
            total[span, h * HEAD : (h + 1) * HEAD] = weighted[low : low + cont]

    for h in range(heads):
        across = slice(h * HEAD, (h + 1) * HEAD)
        inverse = 1.0 / sums[h, :, :1]
        context[:, across] = (total[:, across] * inverse).astype(jnp.bfloat16)
        sums[h, :, :] = jnp.broadcast_to(inverse, (rows_all, lanes))
    finish(3)
    stores += [io(5, context, context_ref), io(6, sums, sum_ref), io(7, other, other_ref), io(8, full, full_ref)]
    for copy in stores[3:]:
        copy.start()

    @pl.loop(0, depth // TILE)
    def _(i):
        at = pl.ds(pl.multiple_of(i * TILE, TILE), TILE)
        tokens[:, at] = lax.dot_general(
            context[...], full[at, side : side + query_width], (((1,), (1,)), ((), ())),
            preferred_element_type=jnp.float32).astype(jnp.bfloat16)

    stores.append(io(9, tokens, part_ref))
    stores[-1].start()
    for m in range(2):
        swap(m).wait_send()
    all_sent()
    for copy in stores:
        copy.wait()


def head_block(tokens, own, angles, prompt_of, heads, cont, cid):
    rows, depth = tokens.shape
    half_rows = rows // 2
    prompt = half_rows - cont
    width = heads * HEAD
    group = lax.axis_size("dp") * lax.axis_size("seq")
    bf16, f32 = jnp.bfloat16, jnp.float32
    any_spec = pl.BlockSpec(memory_space=pl.ANY)
    vmem_spec = pl.BlockSpec(memory_space=pltpu.VMEM)
    dma = pltpu.SemaphoreType.DMA
    full = (own.shape[0] * group, own.shape[1])
    shape = jax.ShapeDtypeStruct
    return pl.pallas_call(
        functools.partial(head_kernel, heads, cont),
        out_shape=(
            shape((rows, depth), bf16),
            shape((rows, width), bf16),
            shape((rows, width), bf16),
            shape((2, half_rows, 2 * HEAD), bf16),
            shape((2, prompt, 2 * HEAD), bf16),
            shape((heads, rows, 128), f32),
            shape((rows, depth), bf16),
            shape(full, bf16),
            shape((8, depth), f32),
        ),
        in_specs=[pl.BlockSpec(memory_space=pltpu.SMEM)] + [any_spec] * 3,
        out_specs=(any_spec,) * 8 + (vmem_spec,),
        scratch_shapes=[
            pltpu.VMEM((rows, depth), bf16),
            pltpu.VMEM((rows, depth), bf16),
            pltpu.VMEM(full, bf16),
            pltpu.VMEM((rows, HEAD), f32),
            pltpu.VMEM((rows, width), bf16),
            pltpu.VMEM((2, half_rows, 2 * HEAD), bf16),
            pltpu.VMEM((2, prompt, 2 * HEAD), bf16),
            pltpu.VMEM((rows, width), f32),
            pltpu.VMEM((heads, rows, 128), f32),
            pltpu.VMEM((rows, width), bf16),
            dma((4, 9)), dma((4, 9)), dma((4,)), dma((10,)), dma((2,)), dma((2,)),
        ],
        compiler_params=pltpu.CompilerParams(
            collective_id=cid, has_side_effects=True, vmem_limit_bytes=56 * 2**20),
        cost_estimate=pl.CostEstimate(
            flops=2 * rows * depth * (full[1] + width), bytes_accessed=200 * 2**20, transcendentals=rows * 2048),
    )(prompt_of, tokens, own, angles)
def back_kernel(
    heads, cont,
    prompt_of, d_attn_ref, full_ref, query_ref, kv_ref, other_ref, context_ref, sum_ref, angle_ref, token_ref,
    d_qkv_ref, part_ref, gain_ref,
    d_attn, full, tokens, queries, kv, other, context, sums, cosine_sine,
    d_context, d_query, d_kv, d_other, sent_kv, got_kv, d_qkv, inverses, d_picked,
    io_sem, swap_in, swap_out,
):
    rows_all, depth = tokens.shape
    rows = rows_all // 2
    prompt = rows - cont
    query_width = heads * HEAD
    qkv_width = query_width + 2 * HEAD
    side = qkv_width + SIDE_PAD
    _, over_y, _ = plane_partners()
    seq = lax.axis_index("seq")
    barrier = pltpu.get_barrier_semaphore()
    pl.semaphore_signal(barrier, inc=1, device_id=over_y, device_id_type=MESH)
    pl.semaphore_wait(barrier, 1)

    def io(index, source, target):
        return pltpu.make_async_copy(source, target, io_sem.at[index])

    def swap(m):
        return pltpu.make_async_remote_copy(
            sent_kv.at[m], got_kv.at[m], swap_out.at[m], swap_in.at[m], device_id=over_y, device_id_type=MESH)

    pairs = (
        (d_attn_ref, d_attn), (full_ref, full), (query_ref, queries), (kv_ref, kv), (other_ref, other),
        (context_ref, context), (sum_ref, sums), (angle_ref, cosine_sine), (token_ref, tokens),
    )
    loads = [io(k, *pair) for k, pair in enumerate(pairs)]
    for copy in loads:
        copy.start()
    for copy in loads[:2]:
        copy.wait()
    for m in range(2):
        span = pl.ds(m * rows, rows)
        d_context[span, :] = jnp.dot(
            d_attn[span, :], full[:, side : side + query_width], preferred_element_type=jnp.float32
        ).astype(jnp.bfloat16)
    for copy in loads[2:]:
        copy.wait()

    def nt(left, right):
        return lax.dot_general(left, right, (((1,), (1,)), ((), ())), preferred_element_type=jnp.float32)

    def tn(left, right):
        return lax.dot_general(left, right, (((0,), (0,)), ((), ())), preferred_element_type=jnp.float32)

    def score_grads(query, above, found, inverse, pair, seen):
        keys, values = pair[:, :HEAD], pair[:, HEAD:]
        curve, weights = capped(query, keys)
        weights = weights * inverse
        if seen is not None:
            weights = jnp.where(seen, weights, 0.0)
        d_weights = nt(above, values)
        inner = jnp.sum(found.astype(jnp.float32) * above.astype(jnp.float32), axis=1, keepdims=True)
        d_scores = (weights * (d_weights - inner) * ((1.0 - curve * curve) * HEAD ** -0.5)).astype(jnp.bfloat16)
        d_pair = jnp.concatenate([tn(d_scores, query), tn(weights.astype(jnp.bfloat16), above)], axis=1)
        return jnp.dot(d_scores, keys, preferred_element_type=jnp.float32), d_pair

    picked = [pick_rows(ref, rows, prompt, heads) for ref in (queries, d_context, context)]
    picked_inverse = jnp.concatenate(
        [sums[h, m * rows + prompt : (m + 1) * rows, :1] for m in range(2) for h in range(heads)], axis=0)
    d_picked[...] = jnp.zeros_like(d_picked)
    for g in range(2):
        sees, near = cont_masks(prompt_of, g, cont, heads)
        d_rows, d_pair = score_grads(*picked, picked_inverse, other[g], sees)
        d_picked[...] += d_rows
        d_other[g] = d_pair
        d_rows, d_pair = score_grads(*picked, picked_inverse, kv[g, :prompt, :], sees)
        d_picked[...] += d_rows
        d_kv[g, :prompt, :] = d_pair
    tail = jnp.concatenate([kv[m, prompt:, :] for m in range(2)], axis=0)
    d_rows, d_pair = score_grads(*picked, picked_inverse, tail, near)
    d_picked[...] += d_rows
    for m in range(2):
        d_kv[m, prompt:, :] = d_pair[m * cont : (m + 1) * cont]

    def spots(i, low, count):
        m, h = i // heads, lax.rem(i, heads)
        return m, h, pl.ds(pl.multiple_of(m * rows + low, 16), count), pl.ds(pl.multiple_of(h * HEAD, HEAD), HEAD)

    tiles = [(low, min(ROW_TILE, prompt - low)) for low in range(0, prompt, ROW_TILE)]

    @pl.when(seq == 0)
    def _():
        d_query[...] = jnp.zeros_like(d_query)

    @pl.when(seq == 1)
    def _():
        @pl.loop(0, 2 * heads)
        def _(i):
            for low, count in tiles:
                m, h, span, across = spots(i, low, count)
                d_rows, d_pair = score_grads(
                    queries[span, across], d_context[span, across], context[span, across], sums[h, span, :1], other[m], None)
                d_query[span, across] = d_rows
                d_other[m] += d_pair

    for m in range(2):
        sent_kv[m] = d_other[m].astype(jnp.bfloat16)
        swap(m).start()
    for m in range(2):
        for h in range(heads):
            low = (m * heads + h) * cont
            d_query[m * rows + prompt : (m + 1) * rows, h * HEAD : (h + 1) * HEAD] = d_picked[low : low + cont]

    @pl.loop(0, 2 * heads)
    def _(i):
        for low, count in tiles:
            m, h, span, across = spots(i, low, count)
            reach = low + count
            d_rows, d_pair = score_grads(
                queries[span, across], d_context[span, across], context[span, across], sums[h, span, :1],
                kv[m, :reach, :], at_or_before((count, reach), low))
            d_query[span, across] += d_rows
            d_kv[m, :reach, :] += d_pair

    half = HEAD // 2

    def turn_back_rows(values, span):
        cosine, sine = cosine_sine[span, :half], cosine_sine[span, half:]
        return turn(values, cosine, -sine).astype(jnp.bfloat16)

    for m in range(2):
        span = pl.ds(m * rows, rows)
        for h in range(heads):
            across = slice(h * HEAD, (h + 1) * HEAD)
            d_qkv[span, across] = turn_back_rows(d_query[span, across], span)

    @pl.loop(0, rows_all // BLOCK)
    def _(b):
        span = pl.ds(pl.multiple_of(b * BLOCK, BLOCK), BLOCK)
        values = tokens[span, :].astype(jnp.float32)
        inverse = lax.rsqrt(jnp.mean(values * values, axis=-1, keepdims=True) + EPS)
        inverses[span, :] = jnp.broadcast_to(inverse, (BLOCK, inverses.shape[1]))

    for m in range(2):
        swap(m).wait_recv()
        span = pl.ds(m * rows, rows)
        d_kv[m, :prompt, :] += got_kv[m].astype(jnp.float32)
        d_qkv[span, query_width : query_width + HEAD] = turn_back_rows(d_kv[m, :, :HEAD], span)
        d_qkv[span, query_width + HEAD :] = d_kv[m, :, HEAD:].astype(jnp.bfloat16)
    stores = [io(9, d_qkv, d_qkv_ref)]
    stores[0].start()

    @pl.loop(0, depth // TILE)
    def _(i):
        at = pl.ds(pl.multiple_of(i * TILE, TILE), TILE)
        part = nt(d_qkv[...], full[at, :qkv_width])
        normed = tokens[:, at].astype(jnp.float32) * inverses[:, :1]
        gain_ref[0:1, at] = jnp.sum(part * normed, axis=0, keepdims=True)
        d_attn[:, at] = part.astype(jnp.bfloat16)

    stores.append(io(10, d_attn, part_ref))
    stores[1].start()
    for m in range(2):
        swap(m).wait_send()
    for copy in stores:
        copy.wait()


def back_block(prompt_of, d_attn, full, queries, kv, other, context, sums, angles, tokens, cont, cid):
    rows, depth = tokens.shape
    width = queries.shape[1]
    heads = width // HEAD
    qkv_width = width + 2 * HEAD
    bf16, f32 = jnp.bfloat16, jnp.float32
    any_spec = pl.BlockSpec(memory_space=pl.ANY)
    vmem_spec = pl.BlockSpec(memory_space=pltpu.VMEM)
    dma = pltpu.SemaphoreType.DMA
    shape = jax.ShapeDtypeStruct
    return pl.pallas_call(
        functools.partial(back_kernel, heads, cont),
        out_shape=(shape((rows, qkv_width), bf16), shape((rows, depth), bf16), shape((8, depth), f32)),
        in_specs=[pl.BlockSpec(memory_space=pltpu.SMEM)] + [any_spec] * 9,
        out_specs=(any_spec, any_spec, vmem_spec),
        scratch_shapes=[
            pltpu.VMEM(d_attn.shape, bf16),
            pltpu.VMEM(full.shape, bf16),
            pltpu.VMEM(tokens.shape, bf16),
            pltpu.VMEM(queries.shape, bf16),
            pltpu.VMEM(kv.shape, bf16),
            pltpu.VMEM(other.shape, bf16),
            pltpu.VMEM(context.shape, bf16),
            pltpu.VMEM(sums.shape, f32),
            pltpu.VMEM(angles.shape, f32),
            pltpu.VMEM(queries.shape, bf16),
            pltpu.VMEM(queries.shape, f32),
            pltpu.VMEM(kv.shape, f32),
            pltpu.VMEM(other.shape, f32),
            pltpu.VMEM(other.shape, bf16),
            pltpu.VMEM(other.shape, bf16),
            pltpu.VMEM((rows, qkv_width), bf16),
            pltpu.VMEM((rows, 128), f32),
            pltpu.VMEM((2 * heads * cont, HEAD), f32),
            dma((11,)), dma((2,)), dma((2,)),
        ],
        compiler_params=pltpu.CompilerParams(
            collective_id=cid, has_side_effects=True, vmem_limit_bytes=56 * 2**20),
        cost_estimate=pl.CostEstimate(
            flops=2 * rows * depth * (qkv_width + width), bytes_accessed=150 * 2**20, transcendentals=rows * 2048),
    )(prompt_of, d_attn, full, queries, kv, other, context, sums, angles, tokens)


def normalize(values):
    return values * lax.rsqrt(jnp.mean(values * values, axis=-1, keepdims=True) + EPS)


def norm_back(values, gain, upstream):
    inverse = lax.rsqrt(jnp.mean(values * values, axis=-1, keepdims=True) + EPS)
    normed = values * inverse
    scaled = upstream * gain
    return inverse * (scaled - normed * jnp.mean(scaled * normed, axis=-1, keepdims=True))


def turn_back(values, places):
    half_width = values.shape[-1] // 2
    spectrum = THETA ** (-2.0 * jnp.arange(half_width, dtype=jnp.float32) / values.shape[-1])
    angles = places.astype(jnp.float32)[..., None] * spectrum
    angles = jnp.concatenate([angles, angles], axis=-1)[..., None, :]
    turned = jnp.concatenate([values[..., half_width:], -values[..., :half_width]], axis=-1)
    return values * jnp.cos(angles) + turned * jnp.sin(angles)


def rotate(values, places):
    half_width = values.shape[-1] // 2
    spectrum = THETA ** (-2.0 * jnp.arange(half_width, dtype=jnp.float32) / values.shape[-1])
    angles = places.astype(jnp.float32)[..., None] * spectrum
    angles = jnp.concatenate([angles, angles], axis=-1)[..., None, :]
    turned = jnp.concatenate([-values[..., half_width:], values[..., :half_width]], axis=-1)
    return values * jnp.cos(angles) + turned * jnp.sin(angles)


def visibility(micro_count, row_count, prompt_dev, prompt_all, cont_rows, seq_pos, owners):
    local_rows = jnp.arange(row_count)
    prompt_rows = local_rows < prompt_dev
    places_local = jnp.where(
        prompt_rows, seq_pos * prompt_dev + local_rows, prompt_all + local_rows - prompt_dev
    )
    micro_ids = jnp.arange(micro_count)
    row_micro = jnp.repeat(micro_ids, row_count)
    row_prompt = jnp.tile(prompt_rows, micro_count)
    row_place = jnp.tile(places_local, micro_count)
    first_slot = jnp.where(row_prompt, row_micro, jnp.repeat(owners, row_count))
    second_slot = jnp.where(row_prompt, -1, micro_count + row_micro)
    key_slot = jnp.concatenate(
        [jnp.repeat(micro_ids, prompt_all), micro_count + jnp.repeat(micro_ids, cont_rows)]
    )
    key_place = jnp.concatenate(
        [
            jnp.tile(jnp.arange(prompt_all), micro_count),
            prompt_all + jnp.tile(jnp.arange(cont_rows), micro_count),
        ]
    )
    matched = (key_slot[None, :] == first_slot[:, None]) | (
        key_slot[None, :] == second_slot[:, None]
    )
    return (matched & (key_place[None, :] <= row_place[:, None]), row_place)


def scores_for(query, key_rows, visible, score_scale):
    raw_scores = jnp.einsum("rd,kd->rk", query, key_rows, preferred_element_type=jnp.float32)
    curved = jnp.tanh(raw_scores * score_scale / SOFTCAP)
    return (curved, jnp.where(visible, SOFTCAP * curved, -1e30))


def per_device_general(
    tokens,
    cotangent,
    prompt_of,
    query_weight,
    key_weight,
    value_weight,
    out_weight,
    gate_weight,
    up_weight,
    down_weight,
    norm_gains,
):
    micro_count = tokens.shape[0]
    row_count = tokens.shape[2]
    model_width = tokens.shape[3]
    seq_count = lax.axis_size("seq")
    seq_pos = lax.axis_index("seq")
    prompt_dev = row_count - CONT
    prompt_all = prompt_dev * seq_count
    total_rows = micro_count * row_count
    score_scale = HEAD ** (-0.5)
    axes = ("dp", "seq")
    query_width = query_weight.shape[1]
    qkv_width = query_width + 2 * HEAD
    f32, bf16 = jnp.float32, jnp.bfloat16
    visible, places = visibility(
        micro_count, row_count, prompt_dev, prompt_all, CONT, seq_pos, prompt_of[:, 0]
    )
    side_weights = jnp.concatenate(
        [
            query_weight,
            key_weight,
            value_weight,
            jnp.pad(norm_gains.T, ((0, 0), (0, SIDE_PAD - norm_gains.shape[0]))),
        ],
        axis=1,
    )
    full_side = lax.all_gather(side_weights, axes, axis=0, tiled=True)
    full_qkv = full_side[:, :qkv_width]
    gain_float = full_side[:, qkv_width : qkv_width + 4].T.astype(f32)
    full_out = lax.all_gather(out_weight, axes, axis=1, tiled=True)
    full_gate = lax.all_gather(gate_weight, axes, axis=0, tiled=True)
    down_turned = down_weight.T
    full_up = lax.all_gather(up_weight, axes, axis=0, tiled=True)
    full_down = lax.all_gather(down_turned, axes, axis=0, tiled=True)
    inputs = tokens.reshape(total_rows, model_width).astype(f32)
    normed_in = (normalize(inputs) * gain_float[0]).astype(bf16)
    key_value = jnp.dot(normed_in, full_qkv[:, query_width:], preferred_element_type=f32)
    key_heads = key_value[:, :HEAD].reshape(total_rows, 1, HEAD)
    key_local = rotate(key_heads, places)[:, 0].astype(bf16)
    value_local = key_value[:, HEAD:].astype(bf16)
    key_grid = key_local.reshape(micro_count, row_count, HEAD)
    value_grid = value_local.reshape(micro_count, row_count, HEAD)
    own_pair = jnp.concatenate([key_grid[:, :prompt_dev], value_grid[:, :prompt_dev]], axis=2)
    prompt_pair = lax.all_gather(own_pair, "seq", axis=1, tiled=True)
    query_heads = jnp.dot(
        normed_in, full_qkv[:, :query_width], preferred_element_type=f32
    ).reshape(total_rows, -1, HEAD)
    query_rows = rotate(query_heads, places).astype(bf16)
    prompt_keys, prompt_values = prompt_pair[..., :HEAD], prompt_pair[..., HEAD:]
    key_rows = jnp.concatenate(
        [
            prompt_keys.reshape(micro_count * prompt_all, HEAD),
            key_grid[:, prompt_dev:].reshape(micro_count * CONT, HEAD),
        ],
        axis=0,
    )
    value_rows = jnp.concatenate(
        [
            prompt_values.reshape(micro_count * prompt_all, HEAD),
            value_grid[:, prompt_dev:].reshape(micro_count * CONT, HEAD),
        ],
        axis=0,
    )
    head_count = query_rows.shape[1]
    contexts = []
    log_sums = []
    for head_pos in range(head_count):
        curved, masked = scores_for(query_rows[:, head_pos], key_rows, visible, score_scale)
        row_peak = jnp.max(masked, axis=-1, keepdims=True)
        weights = jnp.exp(masked - row_peak)
        summed = jnp.sum(weights, axis=-1, keepdims=True)
        probs = (weights / summed).astype(bf16)
        contexts.append(jnp.dot(probs, value_rows, preferred_element_type=f32))
        log_sums.append(row_peak + jnp.log(summed))
    context = jnp.stack(contexts, axis=1).reshape(total_rows, -1).astype(bf16)
    attn_part = jnp.dot(context, full_out, preferred_element_type=f32).astype(bf16)
    block = ffn_block(
        attn_part.reshape(micro_count, row_count, model_width),
        tokens[:, 0],
        cotangent[:, 0],
        full_gate,
        full_up,
        full_down,
        jnp.pad(gain_float, ((0, 4), (0, 0))),
        0,
    )
    gain_sums = jnp.sum(block["gain_grad"].reshape(3, 8, model_width), axis=1)
    d_middle = block["d_middle"].reshape(total_rows, model_width).astype(f32)
    d_attn = block["d_attn"].reshape(total_rows, model_width)

    def scatter(grad, axis):
        return lax.psum_scatter(
            grad.astype(bf16), axes, scatter_dimension=axis, tiled=True
        ).astype(f32)

    share_down = scatter(block["grad_down"], 0).T
    share_gate = scatter(block["grad_gate"], 0)
    d_context = (
        jnp.einsum("rd,cd->rc", d_attn, full_out, preferred_element_type=f32)
        .astype(bf16)
        .reshape(total_rows, head_count, HEAD)
    )
    key_grad = jnp.zeros((key_rows.shape[0], HEAD), f32)
    value_grad = jnp.zeros((key_rows.shape[0], HEAD), f32)
    query_grads = []
    for head_pos in range(head_count):
        curved, masked = scores_for(query_rows[:, head_pos], key_rows, visible, score_scale)
        probs = jnp.where(visible, jnp.exp(masked - log_sums[head_pos]), 0.0)
        probs_low = probs.astype(bf16)
        d_probs = jnp.einsum(
            "rd,kd->rk", d_context[:, head_pos], value_rows, preferred_element_type=f32
        )
        inner_sum = jnp.sum(probs * d_probs, axis=-1, keepdims=True)
        d_scores = (probs * (d_probs - inner_sum) * score_scale * (1.0 - curved * curved)).astype(
            bf16
        )
        query_grads.append(jnp.dot(d_scores, key_rows, preferred_element_type=f32))
        key_grad = key_grad + jnp.einsum(
            "rk,rd->kd", d_scores, query_rows[:, head_pos], preferred_element_type=f32
        )
        value_grad = value_grad + jnp.einsum(
            "rk,rd->kd", probs_low, d_context[:, head_pos], preferred_element_type=f32
        )
    split_at = micro_count * prompt_all
    pair_grad = jnp.concatenate(
        [
            key_grad[:split_at].reshape(micro_count, prompt_all, HEAD),
            value_grad[:split_at].reshape(micro_count, prompt_all, HEAD),
        ],
        axis=2,
    )
    pair_grad = lax.psum_scatter(
        pair_grad.astype(bf16), "seq", scatter_dimension=1, tiled=True
    ).astype(f32)
    prompt_key_grad, prompt_value_grad = pair_grad[..., :HEAD], pair_grad[..., HEAD:]
    own_keys = jnp.concatenate(
        [prompt_key_grad, key_grad[split_at:].reshape(micro_count, CONT, HEAD)], axis=1
    ).reshape(total_rows, HEAD)
    own_values = jnp.concatenate(
        [prompt_value_grad, value_grad[split_at:].reshape(micro_count, CONT, HEAD)], axis=1
    ).reshape(total_rows, HEAD)
    d_query = turn_back(jnp.stack(query_grads, axis=1), places).reshape(total_rows, -1)
    d_key = turn_back(own_keys[:, None, :], places).reshape(total_rows, HEAD)
    d_qkv = jnp.concatenate([d_query, d_key, own_values], axis=1).astype(bf16)
    attn_part = jnp.einsum("rc,dc->rd", d_qkv, full_qkv, preferred_element_type=f32)
    gain_first = jnp.sum(attn_part * normalize(inputs), axis=0)
    grad_gains = jnp.concatenate(
        [gain_first[None], jnp.where(lax.axis_index("tensor") == 0, gain_sums, 0.0)], axis=0
    )
    gain_cols = jnp.pad(grad_gains.T, ((0, 0), (0, SIDE_PAD - grad_gains.shape[0])))
    attn_part = attn_part.astype(bf16)
    share_up = scatter(block["grad_up"], 0)
    share_out = scatter(
        jnp.einsum("rc,rd->cd", context, d_attn, preferred_element_type=f32), 1
    )
    side_grad = jnp.einsum("rd,rc->dc", normed_in, d_qkv, preferred_element_type=f32)
    d_normed = chain_sum(attn_part, 1)
    share_side = scatter(jnp.concatenate([side_grad, gain_cols], axis=1), 0)
    share_gains = lax.psum(share_side[:, qkv_width : qkv_width + 4].T, "tensor")
    d_in_norm = norm_back(inputs, gain_float[0], d_normed.astype(f32))
    input_grad = d_middle + d_in_norm
    return (
        block["out"].reshape(tokens.shape),
        input_grad.reshape(tokens.shape),
        share_side[:, :query_width],
        share_side[:, query_width : query_width + HEAD],
        share_side[:, query_width + HEAD : qkv_width],
        share_out,
        share_gate,
        share_up,
        share_down,
        share_gains,
    )


def per_device_planar(
    tokens,
    cotangent,
    prompt_of,
    query_weight,
    key_weight,
    value_weight,
    out_weight,
    gate_weight,
    up_weight,
    down_weight,
    norm_gains,
):
    micro_count, _, row_count, model_width = tokens.shape
    seq_pos = lax.axis_index("seq")
    total_rows = micro_count * row_count
    axes = ("dp", "seq")
    query_width = query_weight.shape[1]
    qkv_width = query_width + 2 * HEAD
    heads = query_width // HEAD
    f32, bf16 = jnp.float32, jnp.bfloat16
    owners = prompt_of[:, 0]
    angles = turn_angles(row_count, seq_pos, micro_count)
    flat = tokens.reshape(total_rows, model_width)
    own_side = jnp.concatenate(
        [
            query_weight,
            key_weight,
            value_weight,
            jnp.pad(norm_gains.T, ((0, 0), (0, SIDE_PAD - norm_gains.shape[0]))),
            out_weight.T,
        ],
        axis=1,
    )
    attn_part, context, queries, own_kv, other_kv, sums, normed_in, full_side, gains = head_block(
        flat, own_side, angles, owners, heads, CONT, 0
    )
    stacked = (micro_count, row_count, model_width)
    block = ffn_block(
        attn_part.reshape(stacked),
        tokens[:, 0],
        cotangent[:, 0],
        gate_weight,
        up_weight,
        down_weight.T,
        gains,
        1,
    )
    gain_sums = jnp.sum(block["gain_grad"].reshape(3, 8, model_width), axis=1)
    d_attn = block["d_attn"].reshape(total_rows, model_width)

    def scatter(grad):
        return lax.psum_scatter(grad, axes, scatter_dimension=0, tiled=True).astype(f32)

    share_down = scatter(block["grad_down"]).T
    d_qkv, attn_part, gain_first = back_block(
        owners, d_attn, full_side, queries, own_kv, other_kv, context, sums, angles, flat, CONT, 2
    )
    grad_gains = jnp.concatenate(
        [gain_first[:1], jnp.where(lax.axis_index("tensor") == 0, gain_sums, 0.0)], axis=0
    )
    gain_cols = jnp.pad(grad_gains.T, ((0, 0), (0, SIDE_PAD - grad_gains.shape[0])))
    d_normed, share_gate, share_up, share_side, share_gains = tail_block(
        attn_part.reshape(stacked),
        block["grad_gate"],
        block["grad_up"],
        normed_in,
        d_attn,
        d_qkv,
        context,
        gain_cols.astype(bf16),
        3,
    )
    d_normed, share_down = lax.optimization_barrier((d_normed, share_down))
    share_side = share_side.astype(f32)
    d_in_norm = norm_back(
        flat.astype(f32), gains[0], d_normed.reshape(total_rows, model_width).astype(f32)
    )
    d_middle = block["d_middle"].reshape(total_rows, model_width).astype(f32)
    return (
        block["out"].reshape(tokens.shape),
        (d_middle + d_in_norm).reshape(tokens.shape),
        share_side[:, :query_width],
        share_side[:, query_width : query_width + HEAD],
        share_side[:, query_width + HEAD : qkv_width],
        share_side[:, qkv_width : qkv_width + query_width].T,
        share_gate.astype(f32),
        share_up.astype(f32),
        share_down,
        share_gains[:, :4].T,
    )


def turn_angles(row_count, seq_pos, micro_count):
    half_width = HEAD // 2
    rows = jnp.arange(row_count)
    prompt_dev = row_count - CONT
    prompt_all = prompt_dev * lax.axis_size("seq")
    places = jnp.where(
        rows < prompt_dev, seq_pos * prompt_dev + rows, prompt_all + rows - prompt_dev
    )
    spectrum = THETA ** (-2.0 * jnp.arange(half_width, dtype=jnp.float32) / HEAD)
    angles = places.astype(jnp.float32)[:, None] * spectrum
    both = jnp.concatenate([jnp.cos(angles), jnp.sin(angles)], axis=1)
    return jnp.tile(both, (micro_count, 1))


def per_device(*arrays):
    if lax.axis_size("dp") == 4 and lax.axis_size("seq") == 2:
        return per_device_planar(*arrays)
    return per_device_general(*arrays)


def solution(mesh):
    placed = (
        P("dp", "seq", None, None),
        P("dp", "seq", None, None),
        P("dp", "seq"),
        P(("dp", "seq"), "tensor"),
        P(("dp", "seq"), "tensor"),
        P(("dp", "seq"), "tensor"),
        P("tensor", ("dp", "seq")),
        P(("dp", "seq"), "tensor"),
        P(("dp", "seq"), "tensor"),
        P("tensor", ("dp", "seq")),
        P(None, ("dp", "seq")),
    )
    return jax.shard_map(
        per_device,
        mesh=mesh,
        in_specs=placed,
        out_specs=(
            P("dp", "seq", None, None),
            P("dp", "seq", None, None),
            P(("dp", "seq"), "tensor"),
            P(("dp", "seq"), "tensor"),
            P(("dp", "seq"), "tensor"),
            P("tensor", ("dp", "seq")),
            P(("dp", "seq"), "tensor"),
            P(("dp", "seq"), "tensor"),
            P("tensor", ("dp", "seq")),
            P(None, ("dp", "seq")),
        ),
        check_vma=False,
    )
```

```python
import functools

import jax
import jax.numpy as jnp
from jax import lax
from jax.experimental import pallas as pl
from jax.experimental.pallas import tpu as pltpu
from jax.sharding import PartitionSpec as P

MESH = pl.DeviceIdType.MESH

HEAD = 256
CONT = 32
BLOCK = 16


EPS = 1e-06
SOFTCAP = 50.0
THETA = 10000.0


def chain_kernel(size, width, x_ref, o_ref, low_buf, high_buf, *sems):
    low_in, low_out, low_last_in, low_last_out, high_in, high_out, high_last_in, high_last_out = sems
    place = lax.axis_index("tensor")
    dp, seq = lax.axis_index("dp"), lax.axis_index("seq")
    down = (dp, seq, jnp.maximum(place - 1, 0))
    up = (dp, seq, jnp.minimum(place + 1, size - 1))
    first, last = place == 0, place == size - 1
    chunks = x_ref.shape[1] // width
    half = x_ref.shape[0] // 2
    rows = (pl.ds(0, half), pl.ds(half, half))
    barrier = pltpu.get_barrier_semaphore()

    @pl.when(jnp.logical_not(first))
    def _():
        pl.semaphore_signal(barrier, inc=1, device_id=down, device_id_type=MESH)

    @pl.when(jnp.logical_not(last))
    def _():
        pl.semaphore_signal(barrier, inc=1, device_id=up, device_id_type=MESH)
    pl.semaphore_wait(barrier, 2 - first.astype(jnp.int32) - last.astype(jnp.int32))

    def columns(c):
        return pl.ds(pl.multiple_of(c * width, 128), width)

    def side(which):
        buf = (low_buf, high_buf)[which]
        sin, sout, lin, lout = (sems[4 * which: 4 * which + 4])
        toward = (down, up)[which]
        back = (up, down)[which]
        start = (last, first)[which]
        end = (first, last)[which]
        rank = (size - 1 - place, place)[which]
        rs = rows[which]

        def passing(c, src):
            return pltpu.make_async_remote_copy(src, buf.at[c], sout.at[c], sin.at[c], device_id=toward, device_id_type=MESH)

        def sharing(c, ):
            view = o_ref.at[rs, columns(c)]
            return pltpu.make_async_remote_copy(view, view, lout.at[c], lin.at[c], device_id=back, device_id_type=MESH)

        def reduce_step(s):
            c = s - rank
            ok = (c >= 0) & (c < chunks)

            @pl.when(ok & start)
            def _():
                passing(c, x_ref.at[rs, columns(c)]).start()

            @pl.when(ok & jnp.logical_not(start))
            def _():
                passing(c, buf.at[c]).wait_recv()
                total = buf[c].astype(jnp.float32) + x_ref[rs, columns(c)].astype(jnp.float32)

                @pl.when(end)
                def _():
                    o_ref[rs, columns(c)] = total.astype(jnp.bfloat16)
                    sharing(c).start()

                @pl.when(jnp.logical_not(end))
                def _():
                    buf[c] = total.astype(jnp.bfloat16)
                    passing(c, buf.at[c]).start()

        def share_step(s):
            c = s - (size - 1) - (size - 1 - rank)
            ok = (c >= 0) & (c < chunks)

            @pl.when(ok & jnp.logical_not(end))
            def _():
                sharing(c).wait_recv()

                @pl.when(jnp.logical_not(start))
                def _():
                    sharing(c).start()

        def finish(c):
            @pl.when(jnp.logical_not(end))
            def _():
                passing(c, buf.at[c]).wait_send()

            @pl.when(jnp.logical_not(start))
            def _():
                sharing(c).wait_send()
        return reduce_step, share_step, finish

    sides = [side(0), side(1)]

    @pl.loop(0, chunks + 2 * (size - 1))
    def _(s):
        for one in sides:
            one[0](s)
        for one in sides:
            one[1](s)

    @pl.loop(0, chunks)
    def _(c):
        for one in sides:
            one[2](c)


def chain_sum(x, cid, width=256):
    size = lax.axis_size("tensor")
    rows, cols = x.shape
    chunks = cols // width
    return pl.pallas_call(
        functools.partial(chain_kernel, size, width),
        out_shape=jax.ShapeDtypeStruct(x.shape, jnp.bfloat16),
        in_specs=[pl.BlockSpec(memory_space=pltpu.VMEM)],
        out_specs=pl.BlockSpec(memory_space=pltpu.VMEM),
        scratch_shapes=[pltpu.VMEM((chunks, rows // 2, width), jnp.bfloat16)] * 2
        + [pltpu.SemaphoreType.DMA((chunks,))] * 8,
        compiler_params=pltpu.CompilerParams(collective_id=cid, has_side_effects=True, vmem_limit_bytes=48 * 2**20),
        cost_estimate=pl.CostEstimate(flops=rows*cols, bytes_accessed=200*2**20, transcendentals=0),
    )(x)


TILE = 256
STAGES = 6
NORM_ROWS = 32
NORM_TICKS = 3
LAG = 2
PACE = 1


def chain_place(size):
    place = lax.axis_index("tensor")
    dp, seq = lax.axis_index("dp"), lax.axis_index("seq")
    down = (dp, seq, jnp.maximum(place - 1, 0))
    up = (dp, seq, jnp.minimum(place + 1, size - 1))
    return place, down, up, place == 0, place == size - 1


def plane_partners():
    dp, seq, place = (lax.axis_index(name) for name in ("dp", "seq", "tensor"))
    x, core = dp // 2, lax.rem(dp, 2)
    return ((1 - x) * 2 + core, seq, place), (dp, 1 - seq, place), (x * 2 + 1 - core, seq, place)


def greet_line(down, up, first, last, others=()):
    barrier = pltpu.get_barrier_semaphore()
    for partner in others:
        pl.semaphore_signal(barrier, inc=1, device_id=partner, device_id_type=MESH)

    @pl.when(jnp.logical_not(first))
    def _():
        pl.semaphore_signal(barrier, inc=1, device_id=down, device_id_type=MESH)

    @pl.when(jnp.logical_not(last))
    def _():
        pl.semaphore_signal(barrier, inc=1, device_id=up, device_id_type=MESH)

    pl.semaphore_wait(barrier, 2 + len(others) - first.astype(jnp.int32) - last.astype(jnp.int32))


def gelu_parts(gate):
    square = gate * gate
    slope = 0.7978845608028654
    curve = jnp.tanh(gate * (slope + (slope * 0.044715) * square))
    half = 0.5 + 0.5 * curve
    rise = (0.5 * gate) * (1.0 - curve * curve) * (slope + (3.0 * slope * 0.044715) * square)
    return gate * half, half + rise


def plane_gather(full_ref, own_ref, pieces, sems_in, sems_out, own_done):
    share = own_ref.shape[0]
    dp, seq = lax.axis_index("dp"), lax.axis_index("seq")
    x, core = dp // 2, lax.rem(dp, 2)
    over_x, over_y, over_core = plane_partners()
    routes = (
        ((0, 0, 0), 0, over_x, (1, 0, 0)),
        ((0, 0, 0), 0, over_y, (0, 1, 0)),
        ((0, 0, 0), 0, over_core, (0, 0, 1)),
        ((1, 0, 0), 1, over_y, (1, 1, 0)),
        ((0, 1, 0), 2, over_x, (1, 1, 0)),
        ((1, 0, 0), 0, over_core, (1, 0, 1)),
        ((0, 1, 0), 0, over_core, (0, 1, 1)),
        ((1, 1, 0), 1, over_core, (1, 1, 1)),
        ((1, 1, 0), 2, over_core, (1, 1, 1)),
    )

    def across(u, part):
        _, _, low, count, left = pieces[u]
        return (pl.ds(low, count), pl.ds(low, left), pl.ds(low + left, count - left))[part]

    def live(u, kind):
        _, _, _, count, left = pieces[u]
        return routes[kind][1] != 2 or left < count

    def view(u, at, part):
        nx, ny, nc = (jnp.abs(now - flip) for now, flip in zip((x, seq, core), at))
        row = ((nx * 2 + nc) * 2 + ny) * share + pieces[u][0]
        return full_ref.at[pl.ds(pl.multiple_of(row, 16), pieces[u][1]), across(u, part)]

    def own(u):
        return own_ref.at[pl.ds(pieces[u][0], pieces[u][1]), across(u, 0)]

    def hop(u, kind, source, target):
        return pltpu.make_async_remote_copy(
            source, target, sems_out.at[u, kind], sems_in.at[u, kind],
            device_id=routes[kind][2], device_id_type=MESH)

    def send(u, kind):
        if live(u, kind):
            at, part, _, _ = routes[kind]
            target = view(u, at, part)
            hop(u, kind, own(u) if kind < 3 else target, target).start()

    def arrive(u, kind):
        if live(u, kind):
            _, part, _, at = routes[kind]
            target = view(u, at, part)
            hop(u, kind, target, target).wait_recv()

    def own_copy(u):
        return pltpu.make_async_copy(own(u), view(u, (0, 0, 0), 0), own_done.at[u])

    def first(u):
        for kind in (0, 1, 2):
            send(u, kind)
        own_copy(u).start()

    def second(u):
        arrive(u, 0)
        send(u, 3)
        send(u, 5)
        arrive(u, 1)
        send(u, 4)
        send(u, 6)

    def third(u):
        arrive(u, 3)
        send(u, 7)
        arrive(u, 4)
        send(u, 8)

    def finish(u):
        own_copy(u).wait()
        for kind in (2, 5, 6, 7, 8):
            arrive(u, kind)

    def all_sent():
        for u in range(len(pieces)):
            for kind, (at, part, _, _) in enumerate(routes):
                if live(u, kind):
                    target = view(u, at, part)
                    hop(u, kind, target, target).wait_send()

    return first, second, third, finish, all_sent


def line_stream(size, width, bases, parts, landing, sum_ref, sems, spot):
    place, down, up, first, last = spot
    pass_in, pass_out, share_in, share_out, local_done = sems
    _, rows, depth = parts.shape
    half = rows // 2
    chunks = depth // width

    def side(which):
        toward, back = ((down, up), (up, down))[which]
        start, end = ((last, first), (first, last))[which]
        rank = (size - 1 - place, place)[which]
        span = pl.ds(which * half, half)

        def where_at(u):
            q = jnp.int32(0)
            base = jnp.int32(bases[0])
            for k in range(1, len(bases)):
                past = (u >= bases[k]).astype(jnp.int32)
                q = q + past
                base = base + past * (bases[k] - bases[k - 1])
            c = u - base
            return q, c, (c >= 0) & (c < chunks)

        def columns(c):
            return pl.ds(pl.multiple_of(c * width, 128), width)

        def passing(q, c, source):
            return pltpu.make_async_remote_copy(
                source, landing.at[which, q, c], pass_out.at[which, q, c], pass_in.at[which, q, c],
                device_id=toward, device_id_type=MESH)

        def sharing(q, c, source):
            return pltpu.make_async_remote_copy(
                source, sum_ref.at[q, span, columns(c)], share_out.at[which, q, c], share_in.at[which, q, c],
                device_id=back, device_id_type=MESH)

        def local(q, c):
            return pltpu.make_async_copy(
                landing.at[which, q, c], sum_ref.at[q, span, columns(c)], local_done.at[which, q, c])

        def reduce_step(s):
            q, c, ok = where_at(s - LAG * rank)
            m = lax.rem(q, 2)

            @pl.when(ok & start)
            def _():
                passing(q, c, parts.at[m, span, columns(c)]).start()

            @pl.when(ok & jnp.logical_not(start))
            def _():
                passing(q, c, landing.at[which, q, c]).wait_recv()
                mine = parts[m, span, columns(c)].astype(jnp.float32)
                landing[which, q, c] = (landing[which, q, c].astype(jnp.float32) + mine).astype(jnp.bfloat16)

                @pl.when(end)
                def _():
                    sharing(q, c, landing.at[which, q, c]).start()
                    local(q, c).start()

                @pl.when(jnp.logical_not(end))
                def _():
                    passing(q, c, landing.at[which, q, c]).start()

        def share_step(s):
            q, c, ok = where_at(s - LAG * (2 * (size - 1) - rank))

            @pl.when(ok & jnp.logical_not(end))
            def _():
                view = sum_ref.at[q, span, columns(c)]
                sharing(q, c, view).wait_recv()

                @pl.when(jnp.logical_not(start))
                def _():
                    sharing(q, c, view).start()

        def settle(q):
            @pl.when(end)
            def _():
                @pl.loop(0, chunks)
                def _(c):
                    local(q, c).wait()

        def sent(q):
            @pl.when(jnp.logical_not(end))
            def _():
                @pl.loop(0, chunks)
                def _(c):
                    passing(q, c, landing.at[which, q, c]).wait_send()

        def shared(q):
            @pl.when(jnp.logical_not(start))
            def _():
                @pl.loop(0, chunks)
                def _(c):
                    sharing(q, c, landing.at[which, q, c]).wait_send()

        return reduce_step, share_step, settle, sent, shared

    sides = (side(0), side(1))

    def tick(s):
        for one in sides:
            one[0](s)
        for one in sides:
            one[1](s)

    def settle(q):
        for one in sides:
            one[2](q)

    def sent(q):
        for one in sides:
            one[3](q)

    def shared():
        @pl.loop(0, len(bases))
        def _(q):
            for one in sides:
                one[4](q)

    def ticks(low, high):
        @pl.loop(low, high)
        def _(s):
            tick(s)

    return tick, ticks, settle, sent, shared


def ffn_kernel(
    size, width, bases, schedule, gather,
    part_ref, token_ref, cot_ref, gate_own, up_own, down_own, gain_ref,
    sum_ref, out_ref, ffn_in_ref, hidden_ref, d_ffn_ref, d_attn_ref, d_middle_ref,
    grad_gate_ref, grad_up_ref, grad_down_ref, full_ref, gain_grad_ref,
    parts, landing, act_a, act_b, stage, cols, rows_w,
    pass_in, pass_out, share_in, share_out, local_done, col_sem, row_sem, io_sem, gather_in, gather_out, own_done,
):
    micro, rows, depth = parts.shape
    units = gate_own.shape[1]
    stage_t, stage_a, stage_f, stage_c = (stage.at[pl.ds(k * rows, rows)] for k in range(4))
    owned = (gate_own, up_own, down_own)
    gate_ref, up_ref, down_ref = (full_ref.at[k] for k in range(3)) if gather else owned
    spot = place, down, up, first, last = chain_place(size)
    greet_line(down, up, first, last, plane_partners() if gather else ())

    tick, ticks, settle, sent, shared = line_stream(
        size, width, bases, parts, landing, sum_ref,
        (pass_in, pass_out, share_in, share_out, local_done), spot)

    def col_copy(kind, source, i, slot):
        return pltpu.make_async_copy(
            source.at[:, pl.ds(pl.multiple_of(i * TILE, TILE), TILE)], cols.at[kind, slot], col_sem.at[kind, slot])

    def row_copy(kind, source, i, slot):
        return pltpu.make_async_copy(
            source.at[pl.ds(pl.multiple_of(i * TILE, TILE), TILE)], rows_w.at[kind, slot], row_sem.at[kind, slot])

    def tiles(copy, sources, steps, body, clock, beside=()):
        @pl.loop(0, steps)
        def _(i):
            slot = lax.rem(i, 2)

            @pl.when(i + 1 < steps)
            def _():
                for kind, source in enumerate(sources):
                    copy(kind, source, i + 1, 1 - slot).start()

            for kind, source in enumerate(sources):
                copy(kind, source, i, slot).wait()
            body(i, slot)
            for at, work in beside:
                pl.when(i == at)(work)

            @pl.when((lax.rem(i, PACE) == PACE - 1) | (i + 1 == steps))
            def _():
                tick(clock + i // PACE)

    def prime(copy, sources):
        for kind, source in enumerate(sources):
            copy(kind, source, 0, 0).start()

    def span_of(i):
        return pl.ds(pl.multiple_of(i * TILE, TILE), TILE)

    def io(index, source, target):
        return pltpu.make_async_copy(source, target, io_sem.at[index])

    def row_blocks(body, clock):
        count = rows // NORM_ROWS
        marks = [count * k // NORM_TICKS for k in range(NORM_TICKS + 1)]
        for k, (low, high) in enumerate(zip(marks, marks[1:])):
            @pl.loop(low, high)
            def _(b):
                body(pl.ds(pl.multiple_of(b * NORM_ROWS, NORM_ROWS), NORM_ROWS))
            tick(clock + k)

    def own_rows(m):
        return pl.ds(m * rows, rows)

    def gain(k):
        return gain_ref[k : k + 1, :]

    def inverse(values):
        return lax.rsqrt(jnp.mean(values * values, axis=-1, keepdims=True) + EPS)

    def middle_of(span):
        attn = stage_a[span, :].astype(jnp.float32)
        return stage_t[span, :].astype(jnp.float32) + attn * inverse(attn) * gain(1)

    def norm_before(m, clock):
        def body(span):
            middle = middle_of(span)
            stage_f[span, :] = (middle * inverse(middle) * gain(2)).astype(jnp.bfloat16)
        row_blocks(body, clock)

    def gate_and_up(m, clock):
        def body(i, slot):
            at = span_of(i)
            gate = jnp.dot(stage_f[...], cols[0, slot], preferred_element_type=jnp.float32)
            up_val = jnp.dot(stage_f[...], cols[1, slot], preferred_element_type=jnp.float32)
            active, slope = gelu_parts(gate)
            stage_c[:, at] = (active * up_val).astype(jnp.bfloat16)
            act_a[own_rows(m), at] = active.astype(jnp.bfloat16)
            act_b[own_rows(m), at] = (up_val * slope).astype(jnp.bfloat16)
        def down_one():
            moved(1, 4)

        def down_two():
            moved(2, 4)
            moved(1, 5)

        def down_three():
            moved(2, 5)

        beside = ((2, down_one), (5, down_two), (8, down_three)) if gather and m == 0 else ()
        tiles(col_copy, (gate_ref, up_ref), units // TILE, body, clock, beside)

    def down_proj(m, clock):
        def body(i, slot):
            parts[m, :, span_of(i)] = lax.dot_general(
                stage_c[...], rows_w[0, slot], (((1,), (1,)), ((), ())),
                preferred_element_type=jnp.float32).astype(jnp.bfloat16)
        tiles(row_copy, (down_ref,), depth // TILE, body, clock)

    def norm_after(m, clock):
        def body(span):
            middle = middle_of(span)
            ffn = stage_f[span, :].astype(jnp.float32)
            above = stage_c[span, :].astype(jnp.float32)
            inv = inverse(ffn)
            normed = ffn * inv
            stage_f[span, :] = (middle + normed * gain(3)).astype(jnp.bfloat16)
            scaled = above * gain(3)
            d_ffn = inv * (scaled - normed * jnp.mean(scaled * normed, axis=-1, keepdims=True))
            stage_c[span, :] = d_ffn.astype(jnp.bfloat16)
            term = above * normed
            gain_grad_ref[16:24, :] += jnp.sum(term.reshape(NORM_ROWS // 8, 8, depth), axis=0)
        row_blocks(body, clock)

    def d_hidden(m, clock):
        def body(i, slot):
            at = span_of(i)
            d_hid = jnp.dot(stage_c[...], cols[0, slot], preferred_element_type=jnp.float32)
            mine = own_rows(m)
            act_a[mine, at] = (d_hid * act_a[mine, at].astype(jnp.float32)).astype(jnp.bfloat16)
            act_b[mine, at] = (d_hid * act_b[mine, at].astype(jnp.float32)).astype(jnp.bfloat16)
        tiles(col_copy, (down_ref,), units // TILE, body, clock)

    def d_input(m, clock):
        def body(i, slot):
            dims = (((1,), (1,)), ((), ()))
            parts[m, :, span_of(i)] = (
                lax.dot_general(act_b[own_rows(m), :], rows_w[0, slot], dims, preferred_element_type=jnp.float32)
                + lax.dot_general(act_a[own_rows(m), :], rows_w[1, slot], dims, preferred_element_type=jnp.float32)
            ).astype(jnp.bfloat16)
        tiles(row_copy, (gate_ref, up_ref), depth // TILE, body, clock)

    def norm_back_middle(m, clock):
        def body(span):
            attn = stage_a[span, :].astype(jnp.float32)
            attn_inv = inverse(attn)
            attn_normed = attn * attn_inv
            middle = stage_t[span, :].astype(jnp.float32) + attn_normed * gain(1)
            inv = inverse(middle)
            normed = middle * inv
            below = stage_f[span, :].astype(jnp.float32)
            scaled = below * gain(2)
            d_middle = stage_c[span, :].astype(jnp.float32) + inv * (
                scaled - normed * jnp.mean(scaled * normed, axis=-1, keepdims=True))
            term = below * normed
            gain_grad_ref[8:16, :] += jnp.sum(term.reshape(NORM_ROWS // 8, 8, depth), axis=0)
            stage_c[span, :] = d_middle.astype(jnp.bfloat16)
            scaled = d_middle * gain(1)
            d_attn = attn_inv * (scaled - attn_normed * jnp.mean(scaled * attn_normed, axis=-1, keepdims=True))
            stage_f[span, :] = d_attn.astype(jnp.bfloat16)
            term = d_middle * attn_normed
            gain_grad_ref[0:8, :] += jnp.sum(term.reshape(NORM_ROWS // 8, 8, depth), axis=0)
        row_blocks(body, clock)

    def tall_copy(source, i, slot, m):
        return pltpu.make_async_copy(
            source.at[m, :, span_of(i)], cols.at[0, slot, own_rows(m)], col_sem.at[m, slot])

    def weight_grads(source, pairs, steps, clock):
        def put(kind, target, i, slot):
            return pltpu.make_async_copy(rows_w.at[kind, slot], target.at[span_of(i)], row_sem.at[kind, slot])

        @pl.loop(0, steps)
        def _(i):
            slot = lax.rem(i, 2)

            @pl.when(i + 1 < steps)
            def _():
                for m in range(micro):
                    tall_copy(source, i + 1, 1 - slot, m).start()

            for m in range(micro):
                tall_copy(source, i, slot, m).wait()

            @pl.when(i >= 2)
            def _():
                for kind, (_, target) in enumerate(pairs):
                    put(kind, target, i - 2, slot).wait()

            left = cols[0, slot, : micro * rows, :]
            for kind, (right, target) in enumerate(pairs):
                for low in range(0, units, 3 * TILE):
                    high = min(units, low + 3 * TILE)
                    rows_w[kind, slot, :, low:high] = lax.dot_general(
                        left, right[: micro * rows, low:high], (((0,), (0,)), ((), ())),
                        preferred_element_type=jnp.float32).astype(jnp.bfloat16)
                put(kind, target, i, slot).start()
            tick(clock + i)

        for i in (steps - 2, steps - 1):
            for kind, (_, target) in enumerate(pairs):
                put(kind, target, i, i % 2).wait()

    if gather:
        piece = gate_own.shape[0] // 2
        pieces = tuple((h * piece, piece, 0, units, units // 2) for h in range(2))
        movers = [
            plane_gather(full_ref.at[k], owned[k], pieces, gather_in.at[k], gather_out.at[k], own_done.at[k])
            for k in range(3)
        ]

        def moved(phase, u):
            movers[u // 2][phase](u % 2)

    else:

        def moved(phase, u):
            pass

    gain_grad_ref[...] = jnp.zeros_like(gain_grad_ref)

    def load(index, source, target):
        return pltpu.make_async_copy(source, target, io_sem.at[index])

    def bring(m):
        return [load(2, token_ref.at[m], stage_t), load(3, sum_ref.at[m], stage_a)]

    def start(copies):
        for copy in copies:
            copy.start()

    def wait(copies):
        for copy in copies:
            copy.wait()

    whole = schedule["attn"][0]
    entry = [load(m, part_ref.at[m], parts.at[m]) for m in range(micro)]
    start(entry)
    moved(0, 0)
    moved(0, 1)
    wait(entry)
    clock = 0
    for s, phases in (
        (7, ((1, 0), (0, 2))),
        (14, ((1, 1), (2, 0), (0, 3))),
        (21, ((1, 2), (2, 1), (0, 4))),
        (28, ((1, 3), (2, 2), (0, 5))),
    ):
        ticks(clock, s)
        clock = s
        for phase, u in phases:
            moved(phase, u)
    ticks(clock, whole)
    kept = []
    loads = [load(2, token_ref.at[0], stage_t)]
    start(loads)
    for m in range(micro):
        norm_s, gate_s, down_s, end_s = schedule["forward"][m]
        settle(m)
        loads.append(load(3, sum_ref.at[m], stage_a))
        loads[-1].start()
        wait(kept)
        wait(loads)
        norm_before(m, norm_s)
        kept = [load(6, stage_f, ffn_in_ref.at[m]), load(7, stage_c, hidden_ref.at[m])]
        kept[0].start()
        if m + 1 < micro:
            loads = [load(2, token_ref.at[m + 1], stage_t)]
        else:
            loads = bring(0)
        start(loads)
        if m == 0:
            moved(2, 3)
            for u in range(4):
                moved(3, u)
            prime(col_copy, (gate_ref, up_ref))
        gate_and_up(m, gate_s)
        kept[1].start()
        sent(m)
        if m == 0:
            moved(3, 4)
            moved(3, 5)
        prime(row_copy, (down_ref,))
        prime(col_copy, (gate_ref, up_ref) if m + 1 < micro else (down_ref,))
        down_proj(m, down_s)
        if m + 1 == micro:
            wait(kept)
            loads.append(load(5, cot_ref.at[0], stage_c))
            loads[-1].start()
        ticks(down_s + -(-depth // (TILE * PACE)), end_s)
    kept = []
    for m in range(micro):
        norm_s, dh_s, di_s, end_s = schedule["backward"][m]
        settle(micro + m)
        wait(kept[:1])
        loads.append(load(4, sum_ref.at[micro + m], stage_f))
        loads[-1].start()
        wait(loads)
        norm_after(m, norm_s)
        kept = [load(6, stage_f, out_ref.at[m]), load(7, stage_c, d_ffn_ref.at[m])]
        start(kept)
        after = (m + 1) % micro
        loads = bring(after)
        start(loads)
        prime(row_copy, (gate_ref, up_ref))
        d_hidden(m, dh_s)
        sent(micro + m)
        if m + 1 < micro:
            prime(col_copy, (down_ref,))
        kept[1].wait()
        loads.append(load(5, cot_ref.at[after], stage_c))
        loads[-1].start()
        d_input(m, di_s)
        ticks(di_s + -(-depth // (TILE * PACE)), end_s)
    norm_s, grads_s, down_s, end_s = schedule["grads"]
    settle(2 * micro)
    wait(kept[:1])
    loads.append(load(4, sum_ref.at[2 * micro], stage_f))
    loads[-1].start()
    for m in range(micro):
        tall_copy(ffn_in_ref, 0, 0, m).start()
    wait(loads)
    norm_back_middle(0, norm_s)
    kept = [load(6, stage_f, d_attn_ref.at[0]), load(7, stage_c, d_middle_ref.at[0])]
    start(kept)
    hidden_loads = [load(2 + m, hidden_ref.at[m], stage.at[own_rows(m)]) for m in range(micro)]
    start(hidden_loads)
    steps = depth // TILE
    weight_grads(ffn_in_ref, ((act_b, grad_gate_ref), (act_a, grad_up_ref)), steps, grads_s)
    for m in range(micro):
        tall_copy(d_ffn_ref, 0, 0, m).start()
    wait(hidden_loads)
    weight_grads(d_ffn_ref, ((stage, grad_down_ref),), steps, down_s)
    wait(kept)
    tail = bring(1)
    tail.append(load(5, cot_ref.at[1], stage_c))
    start(tail)
    ticks(down_s + steps, end_s)
    settle(2 * micro + 1)
    tail.append(load(4, sum_ref.at[2 * micro + 1], stage_f))
    tail[-1].start()
    wait(tail)
    norm_back_middle(1, end_s)
    kept = [load(6, stage_f, d_attn_ref.at[1]), load(7, stage_c, d_middle_ref.at[1])]
    start(kept)
    sent(STAGES - 2)
    sent(STAGES - 1)
    if gather:
        for mover in movers:
            mover[4]()
    wait(kept)

    shared()


def ffn_schedule(chunks, tiles, hops):
    whole = chunks + hops
    bases = [0, chunks]
    at = whole
    attn = (at,)
    forward = []
    for m in range(2):
        norm_s = at
        gate_s = norm_s + NORM_TICKS
        down_s = gate_s + tiles
        bases.append(max(down_s, bases[-1] + chunks))
        at = max(down_s + tiles, bases[m + 1] + whole)
        forward.append((norm_s, gate_s, down_s, at))
    backward = []
    for m in range(2):
        norm_s = at
        dh_s = norm_s + NORM_TICKS
        di_s = dh_s + tiles
        bases.append(max(di_s, bases[-1] + chunks))
        at = max(di_s + tiles, bases[m + 3] + whole)
        backward.append((norm_s, dh_s, di_s, at))
    grads_s = at + NORM_TICKS
    grads = (at, grads_s, grads_s + tiles, max(grads_s + 2 * tiles, bases[-1] + whole))
    return tuple(bases), {
        "attn": attn, "forward": tuple(forward), "backward": tuple(backward), "grads": grads
    }


def ffn_block(parts, tokens, cotangent, gate, up, down, gains, cid, width=128):
    size = lax.axis_size("tensor")
    micro, rows, depth = tokens.shape
    units = gate.shape[1]
    chunks = depth // width
    bases, schedule = ffn_schedule(chunks, -(-units // (TILE * PACE)), 2 * LAG * (size - 1))
    bf16 = jnp.bfloat16
    any_spec = pl.BlockSpec(memory_space=pl.ANY)
    vmem_spec = pl.BlockSpec(memory_space=pltpu.VMEM)
    gather = up.shape[0] != depth
    stack = jax.ShapeDtypeStruct((micro, rows, depth), bf16)
    wide = jax.ShapeDtypeStruct((micro, rows, units), bf16)
    grad = jax.ShapeDtypeStruct((depth, units), bf16)
    full = jax.ShapeDtypeStruct((3, depth, units) if gather else (3, 16, 128), bf16)
    dma = pltpu.SemaphoreType.DMA
    flops = 2 * micro * rows * depth * units * 9
    found = pl.pallas_call(
        functools.partial(ffn_kernel, size, width, bases, schedule, gather),
        out_shape=(
            jax.ShapeDtypeStruct((STAGES, rows, depth), bf16),
            stack, stack, wide, stack, stack, stack, grad, grad, grad, full,
            jax.ShapeDtypeStruct((24, depth), jnp.float32),
        ),
        in_specs=[any_spec] * 6 + [vmem_spec],
        out_specs=(any_spec,) * 11 + (vmem_spec,),
        scratch_shapes=[
            pltpu.VMEM((micro, rows, depth), bf16),
            pltpu.VMEM((2, STAGES, chunks, rows // 2, width), bf16),
            pltpu.VMEM((micro * rows, units), bf16),
            pltpu.VMEM((micro * rows, units), bf16),
            pltpu.VMEM((4 * rows, depth), bf16),
            pltpu.VMEM((2, 2, depth, TILE), bf16),
            pltpu.VMEM((2, 2, TILE, units), bf16),
        ]
        + [dma((2, STAGES, chunks))] * 5
        + [dma((2, 2)), dma((2, 2)), dma((8,)), dma((3, 2, 9)), dma((3, 2, 9)), dma((3, 2))],
        compiler_params=pltpu.CompilerParams(
            collective_id=cid, has_side_effects=True, vmem_limit_bytes=60 * 2**20),
        cost_estimate=pl.CostEstimate(
            flops=flops, bytes_accessed=2**30, transcendentals=micro * rows * units),
    )(parts, tokens, cotangent, gate, up, down, gains)
    return {
        "attn": found[0][:micro], "out": found[1], "d_attn": found[5], "d_middle": found[6],
        "grad_gate": found[7], "grad_up": found[8], "grad_down": found[9], "gain_grad": found[11],
        "sums": found[0], "ffn_in": found[2], "hidden": found[3], "d_ffn": found[4],
    }

SIDE_PAD = 128


def tail_kernel(
    size, width, bases,
    part_ref, gate_grad_ref, up_grad_ref, normed_ref, d_attn_ref, d_qkv_ref, context_ref, gain_ref,
    sum_ref, gate_share_ref, up_share_ref, side_share_ref, gain_share_ref,
    parts, landing, mine_in, side_acc, ffn_first, side_first, ffn_second, side_second, ffn_third, side_third,
    cols, d_qkv, context, gain_in,
    pass_in, pass_out, share_in, share_out, local_done, col_sem, io_sem, mine_sem, hop_in, hop_out, gain_got, gain_sent,
):
    micro, rows, depth = parts.shape
    spot = place, down, up, first, last = chain_place(size)
    over_x, over_y, over_core = plane_partners()
    dp, seq = lax.axis_index("dp"), lax.axis_index("seq")
    x, core = dp // 2, lax.rem(dp, 2)
    others = [(dp, seq, lax.rem(place + k, size)) for k in range(1, size)]
    greet_plane(over_x, over_y, over_core, others)
    tick, ticks, settle, sent, shared = line_stream(
        size, width, bases, parts, landing, sum_ref,
        (pass_in, pass_out, share_in, share_out, local_done), spot)
    share = up_share_ref.shape[0]
    piece = share // 2
    widths = (up_share_ref.shape[1], side_share_ref.shape[1])
    grads = (gate_grad_ref, up_grad_ref)
    qkv_width = d_qkv.shape[1]

    def load(index, source, target):
        return pltpu.make_async_copy(source, target, io_sem.at[index])

    def halves(p):
        all_columns = widths[p // 4]
        low = -(-all_columns // 256) * 128
        return (pl.ds(0, low), pl.ds(low, all_columns - low))

    def block_rows(bx, by, bc, p):
        return pl.ds(pl.multiple_of(((bx * 2 + bc) * 2 + by) * share + (p % 2) * piece, 16), piece)

    def acc(p, bx, by, across):
        if p < 4:
            return ffn_first.at[p, bx * 2 + by, :, across]
        return side_acc.at[block_rows(bx, by, core, p), across]

    def whole(p):
        return pl.ds(0, widths[p // 4])

    first_buf, second_buf, third_buf = (ffn_first, side_first), (ffn_second, side_second), (ffn_third, side_third)

    def land(step, p, k, across):
        buf = (first_buf, second_buf, third_buf)[step][p // 4]
        return buf.at[p % 4, k, :, across]

    def hop(p, k, source, target, device):
        return pltpu.make_async_remote_copy(
            source, target, hop_out.at[p, k], hop_in.at[p, k], device_id=device, device_id_type=MESH)

    def hops(p):
        left, right = halves(p)
        found = []
        for k in range(4):
            bx, by = k // 2, k % 2
            if p < 4:
                source = grads[p // 2].at[block_rows(bx, by, 1 - core, p), :]
            else:
                source = side_acc.at[block_rows(bx, by, 1 - core, p), :]
            found.append((source, land(0, p, k, whole(p)), over_core))
        for k in range(2):
            found.append((acc(p, 1 - x, k, left), land(1, p, k, left), over_x))
        for k in range(2):
            found.append((acc(p, k, 1 - seq, right), land(1, p, k, right), over_y))
        found.append((acc(p, x, 1 - seq, left), land(2, p, 0, left), over_y))
        found.append((acc(p, 1 - x, seq, right), land(2, p, 0, right), over_x))
        return found

    def go(p, k):
        source, target, device = hops(p)[k]
        hop(p, k, source, target, device).start()

    def got(p, k):
        _, target, device = hops(p)[k]
        hop(p, k, target, target, device).wait_recv()
        return target

    def fetch(p, k):
        return pltpu.make_async_copy(
            grads[p // 2].at[block_rows(k // 2, k % 2, core, p), :], mine_in.at[k], mine_sem.at[k])

    def start_fetch(p):
        for k in range(4):
            fetch(p, k).start()

    def add(p, bx, by, across, arrived):
        mine = acc(p, bx, by, across)

        @pl.loop(0, piece // BLOCK)
        def _(b):
            span = pl.ds(pl.multiple_of(b * BLOCK, BLOCK), BLOCK)
            mine[span, :] = (
                mine[span, :].astype(jnp.float32) + arrived[span, :].astype(jnp.float32)
            ).astype(jnp.bfloat16)

    def scatter_first(p):
        for k in range(4):
            go(p, k)

    def scatter_second(p):
        for k in range(4):
            arrived = got(p, k)
            if p < 4:
                fetch(p, k).wait()
                arrived = mine_in.at[k]
            add(p, k // 2, k % 2, whole(p), arrived)
        for k in (4, 5, 6, 7):
            go(p, k)
        if p < 3:
            start_fetch(p + 1)

    def scatter_third(p):
        left, right = halves(p)
        for k in range(2):
            add(p, x, k, left, got(p, 4 + k))
        go(p, 8)
        for k in range(2):
            add(p, k, seq, right, got(p, 6 + k))
        go(p, 9)

    def scatter_last(p):
        left, right = halves(p)
        add(p, x, seq, left, got(p, 8))
        add(p, x, seq, right, got(p, 9))
        put(p).start()

    def put(p):
        target = (gate_share_ref, up_share_ref, side_share_ref)[p // 2].at[pl.ds((p % 2) * piece, piece)]
        return load(5 + p, acc(p, x, seq, whole(p)), target)

    def scatter_sent(p):
        for k, (source, target, device) in enumerate(hops(p)):
            hop(p, k, source, target, device).wait_send()
        put(p).wait()

    def tile_copy(kind, i, slot):
        source = (normed_ref, d_attn_ref)[kind].at[:, pl.ds(pl.multiple_of(i * TILE, TILE), TILE)]
        return pltpu.make_async_copy(source, cols.at[kind, slot], col_sem.at[kind, slot])

    def side_grads(clock):
        steps = depth // TILE

        @pl.loop(0, steps)
        def _(i):
            slot = lax.rem(i, 2)

            @pl.when(i + 1 < steps)
            def _():
                tile_copy(0, i + 1, 1 - slot).start()
                tile_copy(1, i + 1, 1 - slot).start()

            tile_copy(0, i, slot).wait()
            tile_copy(1, i, slot).wait()
            span = pl.ds(pl.multiple_of(i * TILE, TILE), TILE)
            for kind, right, low in ((0, d_qkv, 0), (1, context, qkv_width)):
                side_acc[span, low : low + right.shape[1]] = lax.dot_general(
                    cols[kind, slot], right[...], (((0,), (0,)), ((), ())),
                    preferred_element_type=jnp.float32).astype(jnp.bfloat16)
            tick(clock + i)

    entry = [load(m, part_ref.at[m], parts.at[m]) for m in range(micro)]
    side_loads = [
        load(2, d_qkv_ref, d_qkv),
        load(3, context_ref, context),
        load(4, gain_ref, side_acc.at[:, pl.ds(widths[1] - SIDE_PAD, SIDE_PAD)]),
    ]
    for copy in entry:
        copy.start()
    scatter_first(0)
    scatter_first(1)
    for copy in side_loads:
        copy.start()
    start_fetch(0)
    tile_copy(0, 0, 0).start()
    tile_copy(1, 0, 0).start()
    for copy in entry:
        copy.wait()
    ticks(0, 1)
    for copy in side_loads:
        copy.wait()
    ticks(1, 4)
    scatter_second(0)
    scatter_first(2)
    side_grads(4)
    clock = 4 + depth // TILE
    scatter_second(1)
    scatter_third(0)
    for p in (3, 4, 5):
        scatter_first(p)
    plan = (
        (2, (scatter_second, 2)), (2, (scatter_third, 1)), (2, (scatter_last, 0)), (2, (scatter_second, 3)),
        (2, (scatter_third, 2)), (2, (scatter_last, 1)), (2, (scatter_second, 4)), (2, (scatter_third, 3)),
        (2, (scatter_last, 2)), (1, (scatter_second, 5)), (2, (scatter_third, 4)), (2, (scatter_last, 3)),
        (2, (scatter_third, 5)), (2, (scatter_last, 4)), (2, (scatter_last, 5)),
    )
    for pause, (step, p) in plan:
        if pause:
            ticks(clock, clock + pause)
            clock += pause
        step(p)

    mine = side_acc.at[pl.ds(pl.multiple_of(((x * 2 + core) * 2 + seq) * share, 16), share), pl.ds(widths[1] - SIDE_PAD, SIDE_PAD)]

    def gain_hop(k):
        return pltpu.make_async_remote_copy(
            mine, gain_in.at[k], gain_sent.at[k], gain_got.at[k], device_id=others[k], device_id_type=MESH)

    for k in range(size - 1):
        gain_hop(k).start()
    ticks(clock, clock + 2)
    clock += 2
    for k in range(size - 1):
        gain_hop(k).wait_recv()
    total = mine[...].astype(jnp.float32)
    for k in range(size - 1):
        total = total + gain_in[k].astype(jnp.float32)
    gain_share_ref[...] = total
    ticks(clock, max(clock, bases[-1] + depth // width + 2 * LAG * (size - 1)))
    for q in range(micro):
        settle(q)
        sent(q)
    shared()
    for p in range(6):
        scatter_sent(p)
    for k in range(size - 1):
        gain_hop(k).wait_send()


def greet_plane(over_x, over_y, over_core, others):
    barrier = pltpu.get_barrier_semaphore()
    partners = (over_x, over_y, over_core, *others)
    for partner in partners:
        pl.semaphore_signal(barrier, inc=1, device_id=partner, device_id_type=MESH)
    pl.semaphore_wait(barrier, len(partners))


def tail_block(parts, gate_grad, up_grad, normed, d_attn, d_qkv, context, gain_cols, cid, width=128):
    size = lax.axis_size("tensor")
    micro, rows, depth = parts.shape
    units = up_grad.shape[1]
    chunks = depth // width
    total = micro * rows
    share = depth // (lax.axis_size("dp") * lax.axis_size("seq"))
    piece = share // 2
    side = d_qkv.shape[1] + context.shape[1] + SIDE_PAD
    bases = (0, chunks)
    bf16 = jnp.bfloat16
    any_spec = pl.BlockSpec(memory_space=pl.ANY)
    vmem_spec = pl.BlockSpec(memory_space=pltpu.VMEM)
    dma = pltpu.SemaphoreType.DMA
    return pl.pallas_call(
        functools.partial(tail_kernel, size, width, bases),
        out_shape=(
            jax.ShapeDtypeStruct((micro, rows, depth), bf16),
            jax.ShapeDtypeStruct((share, units), bf16),
            jax.ShapeDtypeStruct((share, units), bf16),
            jax.ShapeDtypeStruct((share, side), bf16),
            jax.ShapeDtypeStruct((share, SIDE_PAD), jnp.float32),
        ),
        in_specs=[any_spec] * 8,
        out_specs=(any_spec,) * 4 + (vmem_spec,),
        scratch_shapes=[
            pltpu.VMEM((micro, rows, depth), bf16),
            pltpu.VMEM((2, 2, chunks, rows // 2, width), bf16),
            pltpu.VMEM((4, piece, units), bf16),
            pltpu.VMEM((depth, side), bf16),
            pltpu.VMEM((4, 4, piece, units), bf16),
            pltpu.VMEM((2, 4, piece, side), bf16),
            pltpu.VMEM((4, 2, piece, units), bf16),
            pltpu.VMEM((2, 2, piece, side), bf16),
            pltpu.VMEM((4, 1, piece, units), bf16),
            pltpu.VMEM((2, 1, piece, side), bf16),
            pltpu.VMEM((2, 2, total, TILE), bf16),
            pltpu.VMEM(d_qkv.shape, bf16),
            pltpu.VMEM(context.shape, bf16),
            pltpu.VMEM((size - 1, share, SIDE_PAD), bf16),
        ]
        + [dma((2, 2, chunks))] * 5
        + [dma((2, 2)), dma((11,)), dma((4,)), dma((6, 10)), dma((6, 10)), dma((size - 1,)), dma((size - 1,))],
        compiler_params=pltpu.CompilerParams(
            collective_id=cid, has_side_effects=True, vmem_limit_bytes=60 * 2**20),
        cost_estimate=pl.CostEstimate(
            flops=2 * total * depth * side, bytes_accessed=400 * 2**20, transcendentals=0),
    )(parts, gate_grad, up_grad, normed, d_attn, d_qkv, context, gain_cols)

CAP_SCALE = HEAD ** -0.5 / SOFTCAP


def capped(query, keys):
    raw = lax.dot_general(query, keys, (((1,), (1,)), ((), ())), preferred_element_type=jnp.float32)
    curve = jnp.tanh(raw * CAP_SCALE)
    return curve, jnp.exp(SOFTCAP * curve)


def at_or_before(shape, row_at):
    return lax.broadcasted_iota(jnp.int32, shape, 1) <= lax.broadcasted_iota(jnp.int32, shape, 0) + row_at


def pick_rows(ref, rows, prompt, heads):
    found = []
    for m in range(2):
        for h in range(heads):
            found.append(ref[m * rows + prompt : (m + 1) * rows, h * HEAD : (h + 1) * HEAD])
    return jnp.concatenate(found, axis=0)


def cont_masks(prompt_of, group, cont, heads):
    count = 2 * heads * cont
    row = lax.broadcasted_iota(jnp.int32, (count, 1), 0)
    sees = jnp.where(row < heads * cont, prompt_of[0], prompt_of[1]) == group
    row = lax.broadcasted_iota(jnp.int32, (count, 2 * cont), 0)
    key = lax.broadcasted_iota(jnp.int32, (count, 2 * cont), 1)
    same = (row // (heads * cont)) == (key // cont)
    return sees, same & (lax.rem(key, cont) <= lax.rem(row, cont))


def turn(values, cosine, sine):
    half = HEAD // 2
    low, high = values[:, :half], values[:, half:]
    return jnp.concatenate([low * cosine - high * sine, high * cosine + low * sine], axis=1)


ROW_TILE = 256


def head_kernel(
    heads, cont,
    prompt_of, token_ref, own_ref, angle_ref,
    part_ref, context_ref, query_ref, kv_ref, other_ref, sum_ref, normed_ref, full_ref, gain_ref,
    tokens, normed, full, cosine_sine, queries, kv, other, total, sums, context,
    gather_in, gather_out, own_done, io_sem, swap_in, swap_out,
):
    rows_all, depth = tokens.shape
    rows = rows_all // 2
    prompt = rows - cont
    query_width = heads * HEAD
    qkv_width = query_width + 2 * HEAD
    over_x, over_y, over_core = plane_partners()
    seq = lax.axis_index("seq")
    greet_plane(over_x, over_y, over_core, ())
    share = own_ref.shape[0]
    piece = share // 2
    side = qkv_width + SIDE_PAD
    pieces = (
        (0, share, qkv_width, SIDE_PAD, SIDE_PAD),
        (0, piece, 0, qkv_width, qkv_width // 2),
        (piece, piece, 0, qkv_width, qkv_width // 2),
        (0, share, side, query_width, query_width // 2),
    )
    first, second, third, finish, all_sent = plane_gather(full, own_ref, pieces, gather_in, gather_out, own_done)

    def io(index, source, target):
        return pltpu.make_async_copy(source, target, io_sem.at[index])

    loads = [io(0, token_ref, tokens), io(1, angle_ref, cosine_sine)]
    for u in (0, 1, 2):
        first(u)
    for copy in loads:
        copy.start()
    second(0)
    third(0)
    first(3)
    for copy in loads:
        copy.wait()
    finish(0)
    gain_ref[...] = jnp.transpose(full[:, qkv_width:side].astype(jnp.float32))[:8, :]

    def normalize_rows(low, high):
        @pl.loop(low, high)
        def _(b):
            span = pl.ds(pl.multiple_of(b * BLOCK, BLOCK), BLOCK)
            values = tokens[span, :].astype(jnp.float32)
            inv = lax.rsqrt(jnp.mean(values * values, axis=-1, keepdims=True) + EPS)
            normed[span, :] = (values * inv * gain_ref[0:1, :]).astype(jnp.bfloat16)

    blocks = rows_all // BLOCK
    normalize_rows(0, blocks // 2)
    second(1)
    normalize_rows(blocks // 2, blocks)
    second(2)
    third(1)
    second(3)
    third(2)
    for u in (1, 2):
        finish(u)

    stores = [io(2, normed, normed_ref)]
    stores[0].start()
    half = HEAD // 2

    def project(m, low, count):
        return jnp.dot(normed[pl.ds(m * rows, rows), :], full[:, low : low + count], preferred_element_type=jnp.float32)

    def angles(m):
        span = pl.ds(m * rows, rows)
        return cosine_sine[span, :half], cosine_sine[span, half:]

    def swap(m):
        return pltpu.make_async_remote_copy(
            kv.at[m, pl.ds(0, prompt)], other.at[m], swap_out.at[m], swap_in.at[m],
            device_id=over_y, device_id_type=MESH)

    for m in range(2):
        kv[m, :, :HEAD] = turn(project(m, query_width, HEAD), *angles(m)).astype(jnp.bfloat16)
        kv[m, :, HEAD:] = project(m, query_width + HEAD, HEAD).astype(jnp.bfloat16)
        swap(m).start()
    for m in range(2):
        for h in range(heads):
            queries[pl.ds(m * rows, rows), h * HEAD : (h + 1) * HEAD] = turn(
                project(m, h * HEAD, HEAD), *angles(m)).astype(jnp.bfloat16)
    third(3)
    stores += [io(3, queries, query_ref), io(4, kv, kv_ref)]
    stores[1].start()
    stores[2].start()
    lanes = sums.shape[-1]

    def spots(i, low, count):
        m, h = i // heads, lax.rem(i, heads)
        return m, h, pl.ds(pl.multiple_of(m * rows + low, 16), count), pl.ds(pl.multiple_of(h * HEAD, HEAD), HEAD)

    def attend(weights, values):
        return jnp.dot(weights.astype(jnp.bfloat16), values, preferred_element_type=jnp.float32)

    tiles = [(low, min(ROW_TILE, prompt - low)) for low in range(0, prompt, ROW_TILE)]

    @pl.loop(0, 2 * heads)
    def _(i):
        for low, count in tiles:
            m, h, span, across = spots(i, low, count)
            reach = low + count
            keys = kv[m, :reach, :HEAD]
            values = kv[m, :reach, HEAD:]
            _, weights = capped(queries[span, across], keys)
            weights = jnp.where(at_or_before((count, reach), low), weights, 0.0)
            sums[h, span, :] = jnp.broadcast_to(jnp.sum(weights, axis=1, keepdims=True), (count, lanes))
            total[span, across] = attend(weights, values)

    for m in range(2):
        swap(m).wait_recv()

    @pl.when(seq == 1)
    def _():
        @pl.loop(0, 2 * heads)
        def _(i):
            for low, count in tiles:
                m, h, span, across = spots(i, low, count)
                _, weights = capped(queries[span, across], other[m, :, :HEAD])
                sums[h, span, :] += jnp.broadcast_to(jnp.sum(weights, axis=1, keepdims=True), (count, lanes))
                total[span, across] += attend(weights, other[m, :, HEAD:])

    picked = pick_rows(queries, rows, prompt, heads)
    weight_sum = jnp.zeros((picked.shape[0], 1), jnp.float32)
    weighted = jnp.zeros((picked.shape[0], HEAD), jnp.float32)
    for g in range(2):
        sees, near = cont_masks(prompt_of, g, cont, heads)
        for pair in (kv[g, :prompt, :], other[g]):
            _, weights = capped(picked, pair[:, :HEAD])
            weights = jnp.where(sees, weights, 0.0)
            weight_sum += jnp.sum(weights, axis=1, keepdims=True)
            weighted += attend(weights, pair[:, HEAD:])
    tail = jnp.concatenate([kv[m, prompt:, :] for m in range(2)], axis=0)
    _, weights = capped(picked, tail[:, :HEAD])
    weights = jnp.where(near, weights, 0.0)
    weight_sum += jnp.sum(weights, axis=1, keepdims=True)
    weighted += attend(weights, tail[:, HEAD:])
    for m in range(2):
        for h in range(heads):
            low = (m * heads + h) * cont
            span = pl.ds(m * rows + prompt, cont)
            sums[h, span, :] = jnp.broadcast_to(weight_sum[low : low + cont], (cont, lanes))
            total[span, h * HEAD : (h + 1) * HEAD] = weighted[low : low + cont]

    for h in range(heads):
        across = slice(h * HEAD, (h + 1) * HEAD)
        inverse = 1.0 / sums[h, :, :1]
        context[:, across] = (total[:, across] * inverse).astype(jnp.bfloat16)
        sums[h, :, :] = jnp.broadcast_to(inverse, (rows_all, lanes))
    finish(3)
    stores += [io(5, context, context_ref), io(6, sums, sum_ref), io(7, other, other_ref), io(8, full, full_ref)]
    for copy in stores[3:]:
        copy.start()

    @pl.loop(0, depth // TILE)
    def _(i):
        at = pl.ds(pl.multiple_of(i * TILE, TILE), TILE)
        tokens[:, at] = lax.dot_general(
            context[...], full[at, side : side + query_width], (((1,), (1,)), ((), ())),
            preferred_element_type=jnp.float32).astype(jnp.bfloat16)

    stores.append(io(9, tokens, part_ref))
    stores[-1].start()
    for m in range(2):
        swap(m).wait_send()
    all_sent()
    for copy in stores:
        copy.wait()


def head_block(tokens, own, angles, prompt_of, heads, cont, cid):
    rows, depth = tokens.shape
    half_rows = rows // 2
    prompt = half_rows - cont
    width = heads * HEAD
    group = lax.axis_size("dp") * lax.axis_size("seq")
    bf16, f32 = jnp.bfloat16, jnp.float32
    any_spec = pl.BlockSpec(memory_space=pl.ANY)
    vmem_spec = pl.BlockSpec(memory_space=pltpu.VMEM)
    dma = pltpu.SemaphoreType.DMA
    full = (own.shape[0] * group, own.shape[1])
    shape = jax.ShapeDtypeStruct
    return pl.pallas_call(
        functools.partial(head_kernel, heads, cont),
        out_shape=(
            shape((rows, depth), bf16),
            shape((rows, width), bf16),
            shape((rows, width), bf16),
            shape((2, half_rows, 2 * HEAD), bf16),
            shape((2, prompt, 2 * HEAD), bf16),
            shape((heads, rows, 128), f32),
            shape((rows, depth), bf16),
            shape(full, bf16),
            shape((8, depth), f32),
        ),
        in_specs=[pl.BlockSpec(memory_space=pltpu.SMEM)] + [any_spec] * 3,
        out_specs=(any_spec,) * 8 + (vmem_spec,),
        scratch_shapes=[
            pltpu.VMEM((rows, depth), bf16),
            pltpu.VMEM((rows, depth), bf16),
            pltpu.VMEM(full, bf16),
            pltpu.VMEM((rows, HEAD), f32),
            pltpu.VMEM((rows, width), bf16),
            pltpu.VMEM((2, half_rows, 2 * HEAD), bf16),
            pltpu.VMEM((2, prompt, 2 * HEAD), bf16),
            pltpu.VMEM((rows, width), f32),
            pltpu.VMEM((heads, rows, 128), f32),
            pltpu.VMEM((rows, width), bf16),
            dma((4, 9)), dma((4, 9)), dma((4,)), dma((10,)), dma((2,)), dma((2,)),
        ],
        compiler_params=pltpu.CompilerParams(
            collective_id=cid, has_side_effects=True, vmem_limit_bytes=56 * 2**20),
        cost_estimate=pl.CostEstimate(
            flops=2 * rows * depth * (full[1] + width), bytes_accessed=200 * 2**20, transcendentals=rows * 2048),
    )(prompt_of, tokens, own, angles)
def back_kernel(
    heads, cont,
    prompt_of, d_attn_ref, full_ref, query_ref, kv_ref, other_ref, context_ref, sum_ref, angle_ref, token_ref,
    d_qkv_ref, part_ref, gain_ref,
    d_attn, full, tokens, queries, kv, other, context, sums, cosine_sine,
    d_context, d_query, d_kv, d_other, sent_kv, got_kv, d_qkv, inverses, d_picked,
    io_sem, swap_in, swap_out,
):
    rows_all, depth = tokens.shape
    rows = rows_all // 2
    prompt = rows - cont
    query_width = heads * HEAD
    qkv_width = query_width + 2 * HEAD
    side = qkv_width + SIDE_PAD
    _, over_y, _ = plane_partners()
    seq = lax.axis_index("seq")
    barrier = pltpu.get_barrier_semaphore()
    pl.semaphore_signal(barrier, inc=1, device_id=over_y, device_id_type=MESH)
    pl.semaphore_wait(barrier, 1)

    def io(index, source, target):
        return pltpu.make_async_copy(source, target, io_sem.at[index])

    def swap(m):
        return pltpu.make_async_remote_copy(
            sent_kv.at[m], got_kv.at[m], swap_out.at[m], swap_in.at[m], device_id=over_y, device_id_type=MESH)

    pairs = (
        (d_attn_ref, d_attn), (full_ref, full), (query_ref, queries), (kv_ref, kv), (other_ref, other),
        (context_ref, context), (sum_ref, sums), (angle_ref, cosine_sine), (token_ref, tokens),
    )
    loads = [io(k, *pair) for k, pair in enumerate(pairs)]
    for copy in loads:
        copy.start()
    for copy in loads[:2]:
        copy.wait()
    for m in range(2):
        span = pl.ds(m * rows, rows)
        d_context[span, :] = jnp.dot(
            d_attn[span, :], full[:, side : side + query_width], preferred_element_type=jnp.float32
        ).astype(jnp.bfloat16)
    for copy in loads[2:]:
        copy.wait()

    def nt(left, right):
        return lax.dot_general(left, right, (((1,), (1,)), ((), ())), preferred_element_type=jnp.float32)

    def tn(left, right):
        return lax.dot_general(left, right, (((0,), (0,)), ((), ())), preferred_element_type=jnp.float32)

    def score_grads(query, above, found, inverse, pair, seen):
        keys, values = pair[:, :HEAD], pair[:, HEAD:]
        curve, weights = capped(query, keys)
        weights = weights * inverse
        if seen is not None:
            weights = jnp.where(seen, weights, 0.0)
        d_weights = nt(above, values)
        inner = jnp.sum(found.astype(jnp.float32) * above.astype(jnp.float32), axis=1, keepdims=True)
        d_scores = (weights * (d_weights - inner) * ((1.0 - curve * curve) * HEAD ** -0.5)).astype(jnp.bfloat16)
        d_pair = jnp.concatenate([tn(d_scores, query), tn(weights.astype(jnp.bfloat16), above)], axis=1)
        return jnp.dot(d_scores, keys, preferred_element_type=jnp.float32), d_pair

    picked = [pick_rows(ref, rows, prompt, heads) for ref in (queries, d_context, context)]
    picked_inverse = jnp.concatenate(
        [sums[h, m * rows + prompt : (m + 1) * rows, :1] for m in range(2) for h in range(heads)], axis=0)
    d_picked[...] = jnp.zeros_like(d_picked)
    for g in range(2):
        sees, near = cont_masks(prompt_of, g, cont, heads)
        d_rows, d_pair = score_grads(*picked, picked_inverse, other[g], sees)
        d_picked[...] += d_rows
        d_other[g] = d_pair
        d_rows, d_pair = score_grads(*picked, picked_inverse, kv[g, :prompt, :], sees)
        d_picked[...] += d_rows
        d_kv[g, :prompt, :] = d_pair
    tail = jnp.concatenate([kv[m, prompt:, :] for m in range(2)], axis=0)
    d_rows, d_pair = score_grads(*picked, picked_inverse, tail, near)
    d_picked[...] += d_rows
    for m in range(2):
        d_kv[m, prompt:, :] = d_pair[m * cont : (m + 1) * cont]

    def spots(i, low, count):
        m, h = i // heads, lax.rem(i, heads)
        return m, h, pl.ds(pl.multiple_of(m * rows + low, 16), count), pl.ds(pl.multiple_of(h * HEAD, HEAD), HEAD)

    tiles = [(low, min(ROW_TILE, prompt - low)) for low in range(0, prompt, ROW_TILE)]

    @pl.when(seq == 0)
    def _():
        d_query[...] = jnp.zeros_like(d_query)

    @pl.when(seq == 1)
    def _():
        @pl.loop(0, 2 * heads)
        def _(i):
            for low, count in tiles:
                m, h, span, across = spots(i, low, count)
                d_rows, d_pair = score_grads(
                    queries[span, across], d_context[span, across], context[span, across], sums[h, span, :1], other[m], None)
                d_query[span, across] = d_rows
                d_other[m] += d_pair

    for m in range(2):
        sent_kv[m] = d_other[m].astype(jnp.bfloat16)
        swap(m).start()
    for m in range(2):
        for h in range(heads):
            low = (m * heads + h) * cont
            d_query[m * rows + prompt : (m + 1) * rows, h * HEAD : (h + 1) * HEAD] = d_picked[low : low + cont]

    @pl.loop(0, 2 * heads)
    def _(i):
        for low, count in tiles:
            m, h, span, across = spots(i, low, count)
            reach = low + count
            d_rows, d_pair = score_grads(
                queries[span, across], d_context[span, across], context[span, across], sums[h, span, :1],
                kv[m, :reach, :], at_or_before((count, reach), low))
            d_query[span, across] += d_rows
            d_kv[m, :reach, :] += d_pair

    half = HEAD // 2

    def turn_back_rows(values, span):
        cosine, sine = cosine_sine[span, :half], cosine_sine[span, half:]
        return turn(values, cosine, -sine).astype(jnp.bfloat16)

    for m in range(2):
        span = pl.ds(m * rows, rows)
        for h in range(heads):
            across = slice(h * HEAD, (h + 1) * HEAD)
            d_qkv[span, across] = turn_back_rows(d_query[span, across], span)

    @pl.loop(0, rows_all // BLOCK)
    def _(b):
        span = pl.ds(pl.multiple_of(b * BLOCK, BLOCK), BLOCK)
        values = tokens[span, :].astype(jnp.float32)
        inverse = lax.rsqrt(jnp.mean(values * values, axis=-1, keepdims=True) + EPS)
        inverses[span, :] = jnp.broadcast_to(inverse, (BLOCK, inverses.shape[1]))

    for m in range(2):
        swap(m).wait_recv()
        span = pl.ds(m * rows, rows)
        d_kv[m, :prompt, :] += got_kv[m].astype(jnp.float32)
        d_qkv[span, query_width : query_width + HEAD] = turn_back_rows(d_kv[m, :, :HEAD], span)
        d_qkv[span, query_width + HEAD :] = d_kv[m, :, HEAD:].astype(jnp.bfloat16)
    stores = [io(9, d_qkv, d_qkv_ref)]
    stores[0].start()

    @pl.loop(0, depth // TILE)
    def _(i):
        at = pl.ds(pl.multiple_of(i * TILE, TILE), TILE)
        part = nt(d_qkv[...], full[at, :qkv_width])
        normed = tokens[:, at].astype(jnp.float32) * inverses[:, :1]
        gain_ref[0:1, at] = jnp.sum(part * normed, axis=0, keepdims=True)
        d_attn[:, at] = part.astype(jnp.bfloat16)

    stores.append(io(10, d_attn, part_ref))
    stores[1].start()
    for m in range(2):
        swap(m).wait_send()
    for copy in stores:
        copy.wait()


def back_block(prompt_of, d_attn, full, queries, kv, other, context, sums, angles, tokens, cont, cid):
    rows, depth = tokens.shape
    width = queries.shape[1]
    heads = width // HEAD
    qkv_width = width + 2 * HEAD
    bf16, f32 = jnp.bfloat16, jnp.float32
    any_spec = pl.BlockSpec(memory_space=pl.ANY)
    vmem_spec = pl.BlockSpec(memory_space=pltpu.VMEM)
    dma = pltpu.SemaphoreType.DMA
    shape = jax.ShapeDtypeStruct
    return pl.pallas_call(
        functools.partial(back_kernel, heads, cont),
        out_shape=(shape((rows, qkv_width), bf16), shape((rows, depth), bf16), shape((8, depth), f32)),
        in_specs=[pl.BlockSpec(memory_space=pltpu.SMEM)] + [any_spec] * 9,
        out_specs=(any_spec, any_spec, vmem_spec),
        scratch_shapes=[
            pltpu.VMEM(d_attn.shape, bf16),
            pltpu.VMEM(full.shape, bf16),
            pltpu.VMEM(tokens.shape, bf16),
            pltpu.VMEM(queries.shape, bf16),
            pltpu.VMEM(kv.shape, bf16),
            pltpu.VMEM(other.shape, bf16),
            pltpu.VMEM(context.shape, bf16),
            pltpu.VMEM(sums.shape, f32),
            pltpu.VMEM(angles.shape, f32),
            pltpu.VMEM(queries.shape, bf16),
            pltpu.VMEM(queries.shape, f32),
            pltpu.VMEM(kv.shape, f32),
            pltpu.VMEM(other.shape, f32),
            pltpu.VMEM(other.shape, bf16),
            pltpu.VMEM(other.shape, bf16),
            pltpu.VMEM((rows, qkv_width), bf16),
            pltpu.VMEM((rows, 128), f32),
            pltpu.VMEM((2 * heads * cont, HEAD), f32),
            dma((11,)), dma((2,)), dma((2,)),
        ],
        compiler_params=pltpu.CompilerParams(
            collective_id=cid, has_side_effects=True, vmem_limit_bytes=56 * 2**20),
        cost_estimate=pl.CostEstimate(
            flops=2 * rows * depth * (qkv_width + width), bytes_accessed=150 * 2**20, transcendentals=rows * 2048),
    )(prompt_of, d_attn, full, queries, kv, other, context, sums, angles, tokens)


FINAL_ROWS = 64


def final_kernel(
    sums_ref, token_ref, middle_ref, layer_ref, gain_ref, gate_ref, up_ref, down_ref, side_ref,
    layer_out, grad_ref, gate_out, up_out, down_out, query_out, key_out, value_out, out_out,
):
    values = token_ref[...].astype(jnp.float32)
    inverse = lax.rsqrt(jnp.mean(values * values, axis=-1, keepdims=True) + EPS)
    normed = values * inverse
    scaled = sums_ref[...].astype(jnp.float32) * gain_ref[0:1, :]
    backed = inverse * (scaled - normed * jnp.mean(scaled * normed, axis=-1, keepdims=True))
    grad_ref[...] = middle_ref[...].astype(jnp.float32) + backed
    layer_out[...] = layer_ref[...]
    for source, target in ((gate_ref, gate_out), (up_ref, up_out), (down_ref, down_out)):
        target[...] = source[...].astype(jnp.float32)
    low = 0
    for target in (query_out, key_out, value_out, out_out):
        target[...] = side_ref[:, low : low + target.shape[1]].astype(jnp.float32)
        low += target.shape[1]


def final_block(sums, tokens, middle, layer, gains, gate, up, down, side, query_width):
    rows, depth = tokens.shape
    share, units = gate.shape
    steps = share // BLOCK
    blocks = -(-rows // FINAL_ROWS)
    f32 = jnp.float32

    def wide(width):
        return pl.BlockSpec((FINAL_ROWS, width), lambda i: (jnp.minimum(i, blocks - 1), 0))

    def thin(width):
        return pl.BlockSpec((BLOCK, width), lambda i: (i, 0))

    widths = (units, units, units, query_width, HEAD, HEAD, query_width)
    return pl.pallas_call(
        final_kernel,
        grid=(steps,),
        out_shape=(jax.ShapeDtypeStruct((rows, depth), layer.dtype), jax.ShapeDtypeStruct((rows, depth), f32))
        + tuple(jax.ShapeDtypeStruct((share, width), f32) for width in widths),
        in_specs=[wide(depth)] * 4
        + [pl.BlockSpec(gains.shape, lambda i: (0, 0))]
        + [thin(units)] * 3
        + [thin(side.shape[1])],
        out_specs=(wide(depth),) * 2 + tuple(thin(width) for width in widths),
        compiler_params=pltpu.CompilerParams(vmem_limit_bytes=60 * 2**20),
    )(sums, tokens, middle, layer, gains, gate, up, down, side)


def normalize(values):
    return values * lax.rsqrt(jnp.mean(values * values, axis=-1, keepdims=True) + EPS)


def norm_back(values, gain, upstream):
    inverse = lax.rsqrt(jnp.mean(values * values, axis=-1, keepdims=True) + EPS)
    normed = values * inverse
    scaled = upstream * gain
    return inverse * (scaled - normed * jnp.mean(scaled * normed, axis=-1, keepdims=True))


def turn_back(values, places):
    half_width = values.shape[-1] // 2
    spectrum = THETA ** (-2.0 * jnp.arange(half_width, dtype=jnp.float32) / values.shape[-1])
    angles = places.astype(jnp.float32)[..., None] * spectrum
    angles = jnp.concatenate([angles, angles], axis=-1)[..., None, :]
    turned = jnp.concatenate([values[..., half_width:], -values[..., :half_width]], axis=-1)
    return values * jnp.cos(angles) + turned * jnp.sin(angles)


def rotate(values, places):
    half_width = values.shape[-1] // 2
    spectrum = THETA ** (-2.0 * jnp.arange(half_width, dtype=jnp.float32) / values.shape[-1])
    angles = places.astype(jnp.float32)[..., None] * spectrum
    angles = jnp.concatenate([angles, angles], axis=-1)[..., None, :]
    turned = jnp.concatenate([-values[..., half_width:], values[..., :half_width]], axis=-1)
    return values * jnp.cos(angles) + turned * jnp.sin(angles)


def visibility(micro_count, row_count, prompt_dev, prompt_all, cont_rows, seq_pos, owners):
    local_rows = jnp.arange(row_count)
    prompt_rows = local_rows < prompt_dev
    places_local = jnp.where(
        prompt_rows, seq_pos * prompt_dev + local_rows, prompt_all + local_rows - prompt_dev
    )
    micro_ids = jnp.arange(micro_count)
    row_micro = jnp.repeat(micro_ids, row_count)
    row_prompt = jnp.tile(prompt_rows, micro_count)
    row_place = jnp.tile(places_local, micro_count)
    first_slot = jnp.where(row_prompt, row_micro, jnp.repeat(owners, row_count))
    second_slot = jnp.where(row_prompt, -1, micro_count + row_micro)
    key_slot = jnp.concatenate(
        [jnp.repeat(micro_ids, prompt_all), micro_count + jnp.repeat(micro_ids, cont_rows)]
    )
    key_place = jnp.concatenate(
        [
            jnp.tile(jnp.arange(prompt_all), micro_count),
            prompt_all + jnp.tile(jnp.arange(cont_rows), micro_count),
        ]
    )
    matched = (key_slot[None, :] == first_slot[:, None]) | (
        key_slot[None, :] == second_slot[:, None]
    )
    return (matched & (key_place[None, :] <= row_place[:, None]), row_place)


def scores_for(query, key_rows, visible, score_scale):
    raw_scores = jnp.einsum("rd,kd->rk", query, key_rows, preferred_element_type=jnp.float32)
    curved = jnp.tanh(raw_scores * score_scale / SOFTCAP)
    return (curved, jnp.where(visible, SOFTCAP * curved, -1e30))


def per_device_general(
    tokens,
    cotangent,
    prompt_of,
    query_weight,
    key_weight,
    value_weight,
    out_weight,
    gate_weight,
    up_weight,
    down_weight,
    norm_gains,
):
    micro_count = tokens.shape[0]
    row_count = tokens.shape[2]
    model_width = tokens.shape[3]
    seq_count = lax.axis_size("seq")
    seq_pos = lax.axis_index("seq")
    prompt_dev = row_count - CONT
    prompt_all = prompt_dev * seq_count
    total_rows = micro_count * row_count
    score_scale = HEAD ** (-0.5)
    axes = ("dp", "seq")
    query_width = query_weight.shape[1]
    qkv_width = query_width + 2 * HEAD
    f32, bf16 = jnp.float32, jnp.bfloat16
    visible, places = visibility(
        micro_count, row_count, prompt_dev, prompt_all, CONT, seq_pos, prompt_of[:, 0]
    )
    side_weights = jnp.concatenate(
        [
            query_weight,
            key_weight,
            value_weight,
            jnp.pad(norm_gains.T, ((0, 0), (0, SIDE_PAD - norm_gains.shape[0]))),
        ],
        axis=1,
    )
    full_side = lax.all_gather(side_weights, axes, axis=0, tiled=True)
    full_qkv = full_side[:, :qkv_width]
    gain_float = full_side[:, qkv_width : qkv_width + 4].T.astype(f32)
    full_out = lax.all_gather(out_weight, axes, axis=1, tiled=True)
    full_gate = lax.all_gather(gate_weight, axes, axis=0, tiled=True)
    down_turned = down_weight.T
    full_up = lax.all_gather(up_weight, axes, axis=0, tiled=True)
    full_down = lax.all_gather(down_turned, axes, axis=0, tiled=True)
    inputs = tokens.reshape(total_rows, model_width).astype(f32)
    normed_in = (normalize(inputs) * gain_float[0]).astype(bf16)
    key_value = jnp.dot(normed_in, full_qkv[:, query_width:], preferred_element_type=f32)
    key_heads = key_value[:, :HEAD].reshape(total_rows, 1, HEAD)
    key_local = rotate(key_heads, places)[:, 0].astype(bf16)
    value_local = key_value[:, HEAD:].astype(bf16)
    key_grid = key_local.reshape(micro_count, row_count, HEAD)
    value_grid = value_local.reshape(micro_count, row_count, HEAD)
    own_pair = jnp.concatenate([key_grid[:, :prompt_dev], value_grid[:, :prompt_dev]], axis=2)
    prompt_pair = lax.all_gather(own_pair, "seq", axis=1, tiled=True)
    query_heads = jnp.dot(
        normed_in, full_qkv[:, :query_width], preferred_element_type=f32
    ).reshape(total_rows, -1, HEAD)
    query_rows = rotate(query_heads, places).astype(bf16)
    prompt_keys, prompt_values = prompt_pair[..., :HEAD], prompt_pair[..., HEAD:]
    key_rows = jnp.concatenate(
        [
            prompt_keys.reshape(micro_count * prompt_all, HEAD),
            key_grid[:, prompt_dev:].reshape(micro_count * CONT, HEAD),
        ],
        axis=0,
    )
    value_rows = jnp.concatenate(
        [
            prompt_values.reshape(micro_count * prompt_all, HEAD),
            value_grid[:, prompt_dev:].reshape(micro_count * CONT, HEAD),
        ],
        axis=0,
    )
    head_count = query_rows.shape[1]
    contexts = []
    log_sums = []
    for head_pos in range(head_count):
        curved, masked = scores_for(query_rows[:, head_pos], key_rows, visible, score_scale)
        row_peak = jnp.max(masked, axis=-1, keepdims=True)
        weights = jnp.exp(masked - row_peak)
        summed = jnp.sum(weights, axis=-1, keepdims=True)
        probs = (weights / summed).astype(bf16)
        contexts.append(jnp.dot(probs, value_rows, preferred_element_type=f32))
        log_sums.append(row_peak + jnp.log(summed))
    context = jnp.stack(contexts, axis=1).reshape(total_rows, -1).astype(bf16)
    attn_part = jnp.dot(context, full_out, preferred_element_type=f32).astype(bf16)
    block = ffn_block(
        attn_part.reshape(micro_count, row_count, model_width),
        tokens[:, 0],
        cotangent[:, 0],
        full_gate,
        full_up,
        full_down,
        jnp.pad(gain_float, ((0, 4), (0, 0))),
        0,
    )
    gain_sums = jnp.sum(block["gain_grad"].reshape(3, 8, model_width), axis=1)
    d_middle = block["d_middle"].reshape(total_rows, model_width).astype(f32)
    d_attn = block["d_attn"].reshape(total_rows, model_width)

    def scatter(grad, axis):
        return lax.psum_scatter(
            grad.astype(bf16), axes, scatter_dimension=axis, tiled=True
        ).astype(f32)

    share_down = scatter(block["grad_down"], 0).T
    share_gate = scatter(block["grad_gate"], 0)
    d_context = (
        jnp.einsum("rd,cd->rc", d_attn, full_out, preferred_element_type=f32)
        .astype(bf16)
        .reshape(total_rows, head_count, HEAD)
    )
    key_grad = jnp.zeros((key_rows.shape[0], HEAD), f32)
    value_grad = jnp.zeros((key_rows.shape[0], HEAD), f32)
    query_grads = []
    for head_pos in range(head_count):
        curved, masked = scores_for(query_rows[:, head_pos], key_rows, visible, score_scale)
        probs = jnp.where(visible, jnp.exp(masked - log_sums[head_pos]), 0.0)
        probs_low = probs.astype(bf16)
        d_probs = jnp.einsum(
            "rd,kd->rk", d_context[:, head_pos], value_rows, preferred_element_type=f32
        )
        inner_sum = jnp.sum(probs * d_probs, axis=-1, keepdims=True)
        d_scores = (probs * (d_probs - inner_sum) * score_scale * (1.0 - curved * curved)).astype(
            bf16
        )
        query_grads.append(jnp.dot(d_scores, key_rows, preferred_element_type=f32))
        key_grad = key_grad + jnp.einsum(
            "rk,rd->kd", d_scores, query_rows[:, head_pos], preferred_element_type=f32
        )
        value_grad = value_grad + jnp.einsum(
            "rk,rd->kd", probs_low, d_context[:, head_pos], preferred_element_type=f32
        )
    split_at = micro_count * prompt_all
    pair_grad = jnp.concatenate(
        [
            key_grad[:split_at].reshape(micro_count, prompt_all, HEAD),
            value_grad[:split_at].reshape(micro_count, prompt_all, HEAD),
        ],
        axis=2,
    )
    pair_grad = lax.psum_scatter(
        pair_grad.astype(bf16), "seq", scatter_dimension=1, tiled=True
    ).astype(f32)
    prompt_key_grad, prompt_value_grad = pair_grad[..., :HEAD], pair_grad[..., HEAD:]
    own_keys = jnp.concatenate(
        [prompt_key_grad, key_grad[split_at:].reshape(micro_count, CONT, HEAD)], axis=1
    ).reshape(total_rows, HEAD)
    own_values = jnp.concatenate(
        [prompt_value_grad, value_grad[split_at:].reshape(micro_count, CONT, HEAD)], axis=1
    ).reshape(total_rows, HEAD)
    d_query = turn_back(jnp.stack(query_grads, axis=1), places).reshape(total_rows, -1)
    d_key = turn_back(own_keys[:, None, :], places).reshape(total_rows, HEAD)
    d_qkv = jnp.concatenate([d_query, d_key, own_values], axis=1).astype(bf16)
    attn_part = jnp.einsum("rc,dc->rd", d_qkv, full_qkv, preferred_element_type=f32)
    gain_first = jnp.sum(attn_part * normalize(inputs), axis=0)
    grad_gains = jnp.concatenate(
        [gain_first[None], jnp.where(lax.axis_index("tensor") == 0, gain_sums, 0.0)], axis=0
    )
    gain_cols = jnp.pad(grad_gains.T, ((0, 0), (0, SIDE_PAD - grad_gains.shape[0])))
    attn_part = attn_part.astype(bf16)
    share_up = scatter(block["grad_up"], 0)
    share_out = scatter(
        jnp.einsum("rc,rd->cd", context, d_attn, preferred_element_type=f32), 1
    )
    side_grad = jnp.einsum("rd,rc->dc", normed_in, d_qkv, preferred_element_type=f32)
    d_normed = chain_sum(attn_part, 1)
    share_side = scatter(jnp.concatenate([side_grad, gain_cols], axis=1), 0)
    share_gains = lax.psum(share_side[:, qkv_width : qkv_width + 4].T, "tensor")
    d_in_norm = norm_back(inputs, gain_float[0], d_normed.astype(f32))
    input_grad = d_middle + d_in_norm
    return (
        block["out"].reshape(tokens.shape),
        input_grad.reshape(tokens.shape),
        share_side[:, :query_width],
        share_side[:, query_width : query_width + HEAD],
        share_side[:, query_width + HEAD : qkv_width],
        share_out,
        share_gate,
        share_up,
        share_down,
        share_gains,
    )


def per_device_planar(
    tokens,
    cotangent,
    prompt_of,
    query_weight,
    key_weight,
    value_weight,
    out_weight,
    gate_weight,
    up_weight,
    down_weight,
    norm_gains,
):
    micro_count, _, row_count, model_width = tokens.shape
    seq_pos = lax.axis_index("seq")
    total_rows = micro_count * row_count
    axes = ("dp", "seq")
    query_width = query_weight.shape[1]
    qkv_width = query_width + 2 * HEAD
    heads = query_width // HEAD
    bf16 = jnp.bfloat16
    owners = prompt_of[:, 0]
    angles = turn_angles(row_count, seq_pos, micro_count)
    flat = tokens.reshape(total_rows, model_width)
    own_side = jnp.concatenate(
        [
            query_weight,
            key_weight,
            value_weight,
            jnp.pad(norm_gains.T, ((0, 0), (0, SIDE_PAD - norm_gains.shape[0]))),
            out_weight.T,
        ],
        axis=1,
    )
    attn_part, context, queries, own_kv, other_kv, sums, normed_in, full_side, gains = head_block(
        flat, own_side, angles, owners, heads, CONT, 0
    )
    stacked = (micro_count, row_count, model_width)
    block = ffn_block(
        attn_part.reshape(stacked),
        tokens[:, 0],
        cotangent[:, 0],
        gate_weight,
        up_weight,
        down_weight.T,
        gains,
        1,
    )
    gain_sums = jnp.sum(block["gain_grad"].reshape(3, 8, model_width), axis=1)
    d_attn = block["d_attn"].reshape(total_rows, model_width)

    def scatter(grad):
        return lax.psum_scatter(grad, axes, scatter_dimension=0, tiled=True)

    share_down = scatter(block["grad_down"])
    d_qkv, attn_part, gain_first = back_block(
        owners, d_attn, full_side, queries, own_kv, other_kv, context, sums, angles, flat, CONT, 2
    )
    grad_gains = jnp.concatenate(
        [gain_first[:1], jnp.where(lax.axis_index("tensor") == 0, gain_sums, 0.0)], axis=0
    )
    gain_cols = jnp.pad(grad_gains.T, ((0, 0), (0, SIDE_PAD - grad_gains.shape[0])))
    d_normed, share_gate, share_up, share_side, share_gains = tail_block(
        attn_part.reshape(stacked),
        block["grad_gate"],
        block["grad_up"],
        normed_in,
        d_attn,
        d_qkv,
        context,
        gain_cols.astype(bf16),
        3,
    )
    d_normed, share_down = lax.optimization_barrier((d_normed, share_down))
    layer, input_grad, *grads = final_block(
        d_normed.reshape(total_rows, model_width),
        flat,
        block["d_middle"].reshape(total_rows, model_width),
        block["out"].reshape(total_rows, model_width),
        gains,
        share_gate,
        share_up,
        share_down,
        share_side,
        query_width,
    )
    grad_gate, grad_up, grad_down, grad_query, grad_key, grad_value, grad_out = grads
    return (
        layer.reshape(tokens.shape),
        input_grad.reshape(tokens.shape),
        grad_query,
        grad_key,
        grad_value,
        grad_out.T,
        grad_gate,
        grad_up,
        grad_down.T,
        share_gains[:, :4].T,
    )


def turn_angles(row_count, seq_pos, micro_count):
    half_width = HEAD // 2
    rows = jnp.arange(row_count)
    prompt_dev = row_count - CONT
    prompt_all = prompt_dev * lax.axis_size("seq")
    places = jnp.where(
        rows < prompt_dev, seq_pos * prompt_dev + rows, prompt_all + rows - prompt_dev
    )
    spectrum = THETA ** (-2.0 * jnp.arange(half_width, dtype=jnp.float32) / HEAD)
    angles = places.astype(jnp.float32)[:, None] * spectrum
    both = jnp.concatenate([jnp.cos(angles), jnp.sin(angles)], axis=1)
    return jnp.tile(both, (micro_count, 1))


def per_device(*arrays):
    if lax.axis_size("dp") == 4 and lax.axis_size("seq") == 2:
        return per_device_planar(*arrays)
    return per_device_general(*arrays)


def solution(mesh):
    placed = (
        P("dp", "seq", None, None),
        P("dp", "seq", None, None),
        P("dp", "seq"),
        P(("dp", "seq"), "tensor"),
        P(("dp", "seq"), "tensor"),
        P(("dp", "seq"), "tensor"),
        P("tensor", ("dp", "seq")),
        P(("dp", "seq"), "tensor"),
        P(("dp", "seq"), "tensor"),
        P("tensor", ("dp", "seq")),
        P(None, ("dp", "seq")),
    )
    return jax.shard_map(
        per_device,
        mesh=mesh,
        in_specs=placed,
        out_specs=(
            P("dp", "seq", None, None),
            P("dp", "seq", None, None),
            P(("dp", "seq"), "tensor"),
            P(("dp", "seq"), "tensor"),
            P(("dp", "seq"), "tensor"),
            P("tensor", ("dp", "seq")),
            P(("dp", "seq"), "tensor"),
            P(("dp", "seq"), "tensor"),
            P("tensor", ("dp", "seq")),
            P(None, ("dp", "seq")),
        ),
        check_vma=False,
    )
```

```python
import functools

import jax
import jax.numpy as jnp
from jax import lax
from jax.experimental import pallas as pl
from jax.experimental.pallas import tpu as pltpu
from jax.sharding import PartitionSpec as P

MESH = pl.DeviceIdType.MESH

HEAD = 256
CONT = 32
BLOCK = 16


EPS = 1e-06
SOFTCAP = 50.0
THETA = 10000.0


def chain_kernel(size, width, x_ref, o_ref, low_buf, high_buf, *sems):
    low_in, low_out, low_last_in, low_last_out, high_in, high_out, high_last_in, high_last_out = sems
    place = lax.axis_index("tensor")
    dp, seq = lax.axis_index("dp"), lax.axis_index("seq")
    down = (dp, seq, jnp.maximum(place - 1, 0))
    up = (dp, seq, jnp.minimum(place + 1, size - 1))
    first, last = place == 0, place == size - 1
    chunks = x_ref.shape[1] // width
    half = x_ref.shape[0] // 2
    rows = (pl.ds(0, half), pl.ds(half, half))
    barrier = pltpu.get_barrier_semaphore()

    @pl.when(jnp.logical_not(first))
    def _():
        pl.semaphore_signal(barrier, inc=1, device_id=down, device_id_type=MESH)

    @pl.when(jnp.logical_not(last))
    def _():
        pl.semaphore_signal(barrier, inc=1, device_id=up, device_id_type=MESH)
    pl.semaphore_wait(barrier, 2 - first.astype(jnp.int32) - last.astype(jnp.int32))

    def columns(c):
        return pl.ds(pl.multiple_of(c * width, 128), width)

    def side(which):
        buf = (low_buf, high_buf)[which]
        sin, sout, lin, lout = (sems[4 * which: 4 * which + 4])
        toward = (down, up)[which]
        back = (up, down)[which]
        start = (last, first)[which]
        end = (first, last)[which]
        rank = (size - 1 - place, place)[which]
        rs = rows[which]

        def passing(c, src):
            return pltpu.make_async_remote_copy(src, buf.at[c], sout.at[c], sin.at[c], device_id=toward, device_id_type=MESH)

        def sharing(c, ):
            view = o_ref.at[rs, columns(c)]
            return pltpu.make_async_remote_copy(view, view, lout.at[c], lin.at[c], device_id=back, device_id_type=MESH)

        def reduce_step(s):
            c = s - rank
            ok = (c >= 0) & (c < chunks)

            @pl.when(ok & start)
            def _():
                passing(c, x_ref.at[rs, columns(c)]).start()

            @pl.when(ok & jnp.logical_not(start))
            def _():
                passing(c, buf.at[c]).wait_recv()
                total = buf[c].astype(jnp.float32) + x_ref[rs, columns(c)].astype(jnp.float32)

                @pl.when(end)
                def _():
                    o_ref[rs, columns(c)] = total.astype(jnp.bfloat16)
                    sharing(c).start()

                @pl.when(jnp.logical_not(end))
                def _():
                    buf[c] = total.astype(jnp.bfloat16)
                    passing(c, buf.at[c]).start()

        def share_step(s):
            c = s - (size - 1) - (size - 1 - rank)
            ok = (c >= 0) & (c < chunks)

            @pl.when(ok & jnp.logical_not(end))
            def _():
                sharing(c).wait_recv()

                @pl.when(jnp.logical_not(start))
                def _():
                    sharing(c).start()

        def finish(c):
            @pl.when(jnp.logical_not(end))
            def _():
                passing(c, buf.at[c]).wait_send()

            @pl.when(jnp.logical_not(start))
            def _():
                sharing(c).wait_send()
        return reduce_step, share_step, finish

    sides = [side(0), side(1)]

    @pl.loop(0, chunks + 2 * (size - 1))
    def _(s):
        for one in sides:
            one[0](s)
        for one in sides:
            one[1](s)

    @pl.loop(0, chunks)
    def _(c):
        for one in sides:
            one[2](c)


def chain_sum(x, cid, width=256):
    size = lax.axis_size("tensor")
    rows, cols = x.shape
    chunks = cols // width
    return pl.pallas_call(
        functools.partial(chain_kernel, size, width),
        out_shape=jax.ShapeDtypeStruct(x.shape, jnp.bfloat16),
        in_specs=[pl.BlockSpec(memory_space=pltpu.VMEM)],
        out_specs=pl.BlockSpec(memory_space=pltpu.VMEM),
        scratch_shapes=[pltpu.VMEM((chunks, rows // 2, width), jnp.bfloat16)] * 2
        + [pltpu.SemaphoreType.DMA((chunks,))] * 8,
        compiler_params=pltpu.CompilerParams(collective_id=cid, has_side_effects=True, vmem_limit_bytes=48 * 2**20),
        cost_estimate=pl.CostEstimate(flops=rows*cols, bytes_accessed=200*2**20, transcendentals=0),
    )(x)


TILE = 256
STAGES = 6
NORM_ROWS = 32
NORM_TICKS = 3
LAG = 2
PACE = 1


def chain_place(size):
    place = lax.axis_index("tensor")
    dp, seq = lax.axis_index("dp"), lax.axis_index("seq")
    down = (dp, seq, jnp.maximum(place - 1, 0))
    up = (dp, seq, jnp.minimum(place + 1, size - 1))
    return place, down, up, place == 0, place == size - 1


def plane_partners():
    dp, seq, place = (lax.axis_index(name) for name in ("dp", "seq", "tensor"))
    x, core = dp // 2, lax.rem(dp, 2)
    return ((1 - x) * 2 + core, seq, place), (dp, 1 - seq, place), (x * 2 + 1 - core, seq, place)


def greet_line(down, up, first, last, others=()):
    barrier = pltpu.get_barrier_semaphore()
    for partner in others:
        pl.semaphore_signal(barrier, inc=1, device_id=partner, device_id_type=MESH)

    @pl.when(jnp.logical_not(first))
    def _():
        pl.semaphore_signal(barrier, inc=1, device_id=down, device_id_type=MESH)

    @pl.when(jnp.logical_not(last))
    def _():
        pl.semaphore_signal(barrier, inc=1, device_id=up, device_id_type=MESH)

    pl.semaphore_wait(barrier, 2 + len(others) - first.astype(jnp.int32) - last.astype(jnp.int32))


def gelu_parts(gate):
    square = gate * gate
    slope = 0.7978845608028654
    curve = jnp.tanh(gate * (slope + (slope * 0.044715) * square))
    half = 0.5 + 0.5 * curve
    rise = (0.5 * gate) * (1.0 - curve * curve) * (slope + (3.0 * slope * 0.044715) * square)
    return gate * half, half + rise


def plane_gather(full_ref, own_ref, pieces, sems_in, sems_out, own_done):
    share = own_ref.shape[0]
    dp, seq = lax.axis_index("dp"), lax.axis_index("seq")
    x, core = dp // 2, lax.rem(dp, 2)
    over_x, over_y, over_core = plane_partners()
    routes = (
        ((0, 0, 0), 0, over_x, (1, 0, 0)),
        ((0, 0, 0), 0, over_y, (0, 1, 0)),
        ((0, 0, 0), 0, over_core, (0, 0, 1)),
        ((1, 0, 0), 1, over_y, (1, 1, 0)),
        ((0, 1, 0), 2, over_x, (1, 1, 0)),
        ((1, 0, 0), 0, over_core, (1, 0, 1)),
        ((0, 1, 0), 0, over_core, (0, 1, 1)),
        ((1, 1, 0), 1, over_core, (1, 1, 1)),
        ((1, 1, 0), 2, over_core, (1, 1, 1)),
    )

    def across(u, part):
        _, _, low, count, left = pieces[u]
        return (pl.ds(low, count), pl.ds(low, left), pl.ds(low + left, count - left))[part]

    def live(u, kind):
        _, _, _, count, left = pieces[u]
        return routes[kind][1] != 2 or left < count

    def view(u, at, part):
        nx, ny, nc = (jnp.abs(now - flip) for now, flip in zip((x, seq, core), at))
        row = ((nx * 2 + nc) * 2 + ny) * share + pieces[u][0]
        return full_ref.at[pl.ds(pl.multiple_of(row, 16), pieces[u][1]), across(u, part)]

    def own(u):
        return own_ref.at[pl.ds(pieces[u][0], pieces[u][1]), across(u, 0)]

    def hop(u, kind, source, target):
        return pltpu.make_async_remote_copy(
            source, target, sems_out.at[u, kind], sems_in.at[u, kind],
            device_id=routes[kind][2], device_id_type=MESH)

    def send(u, kind):
        if live(u, kind):
            at, part, _, _ = routes[kind]
            target = view(u, at, part)
            hop(u, kind, own(u) if kind < 3 else target, target).start()

    def arrive(u, kind):
        if live(u, kind):
            _, part, _, at = routes[kind]
            target = view(u, at, part)
            hop(u, kind, target, target).wait_recv()

    def own_copy(u):
        return pltpu.make_async_copy(own(u), view(u, (0, 0, 0), 0), own_done.at[u])

    def first(u):
        for kind in (0, 1, 2):
            send(u, kind)
        own_copy(u).start()

    def second(u):
        arrive(u, 0)
        send(u, 3)
        send(u, 5)
        arrive(u, 1)
        send(u, 4)
        send(u, 6)

    def third(u):
        arrive(u, 3)
        send(u, 7)
        arrive(u, 4)
        send(u, 8)

    def finish(u):
        own_copy(u).wait()
        for kind in (2, 5, 6, 7, 8):
            arrive(u, kind)

    def all_sent():
        for u in range(len(pieces)):
            for kind, (at, part, _, _) in enumerate(routes):
                if live(u, kind):
                    target = view(u, at, part)
                    hop(u, kind, target, target).wait_send()

    return first, second, third, finish, all_sent


def line_stream(size, width, bases, parts, landing, sum_ref, sems, spot):
    place, down, up, first, last = spot
    pass_in, pass_out, share_in, share_out, local_done = sems
    _, rows, depth = parts.shape
    half = rows // 2
    chunks = depth // width

    def side(which):
        toward, back = ((down, up), (up, down))[which]
        start, end = ((last, first), (first, last))[which]
        rank = (size - 1 - place, place)[which]
        span = pl.ds(which * half, half)

        def where_at(u):
            q = jnp.int32(0)
            base = jnp.int32(bases[0])
            for k in range(1, len(bases)):
                past = (u >= bases[k]).astype(jnp.int32)
                q = q + past
                base = base + past * (bases[k] - bases[k - 1])
            c = u - base
            return q, c, (c >= 0) & (c < chunks)

        def columns(c):
            return pl.ds(pl.multiple_of(c * width, 128), width)

        def passing(q, c, source):
            return pltpu.make_async_remote_copy(
                source, landing.at[which, q, c], pass_out.at[which, q, c], pass_in.at[which, q, c],
                device_id=toward, device_id_type=MESH)

        def sharing(q, c, source):
            return pltpu.make_async_remote_copy(
                source, sum_ref.at[q, span, columns(c)], share_out.at[which, q, c], share_in.at[which, q, c],
                device_id=back, device_id_type=MESH)

        def local(q, c):
            return pltpu.make_async_copy(
                landing.at[which, q, c], sum_ref.at[q, span, columns(c)], local_done.at[which, q, c])

        def reduce_step(s):
            q, c, ok = where_at(s - LAG * rank)
            m = lax.rem(q, 2)

            @pl.when(ok & start)
            def _():
                passing(q, c, parts.at[m, span, columns(c)]).start()

            @pl.when(ok & jnp.logical_not(start))
            def _():
                passing(q, c, landing.at[which, q, c]).wait_recv()
                mine = parts[m, span, columns(c)].astype(jnp.float32)
                landing[which, q, c] = (landing[which, q, c].astype(jnp.float32) + mine).astype(jnp.bfloat16)

                @pl.when(end)
                def _():
                    sharing(q, c, landing.at[which, q, c]).start()
                    local(q, c).start()

                @pl.when(jnp.logical_not(end))
                def _():
                    passing(q, c, landing.at[which, q, c]).start()

        def share_step(s):
            q, c, ok = where_at(s - LAG * (2 * (size - 1) - rank))

            @pl.when(ok & jnp.logical_not(end))
            def _():
                view = sum_ref.at[q, span, columns(c)]
                sharing(q, c, view).wait_recv()

                @pl.when(jnp.logical_not(start))
                def _():
                    sharing(q, c, view).start()

        def settle(q):
            @pl.when(end)
            def _():
                @pl.loop(0, chunks)
                def _(c):
                    local(q, c).wait()

        def sent(q):
            @pl.when(jnp.logical_not(end))
            def _():
                @pl.loop(0, chunks)
                def _(c):
                    passing(q, c, landing.at[which, q, c]).wait_send()

        def shared(q):
            @pl.when(jnp.logical_not(start))
            def _():
                @pl.loop(0, chunks)
                def _(c):
                    sharing(q, c, landing.at[which, q, c]).wait_send()

        return reduce_step, share_step, settle, sent, shared

    sides = (side(0), side(1))

    def tick(s):
        for one in sides:
            one[0](s)
        for one in sides:
            one[1](s)

    def settle(q):
        for one in sides:
            one[2](q)

    def sent(q):
        for one in sides:
            one[3](q)

    def shared():
        @pl.loop(0, len(bases))
        def _(q):
            for one in sides:
                one[4](q)

    def ticks(low, high):
        @pl.loop(low, high)
        def _(s):
            tick(s)

    return tick, ticks, settle, sent, shared


def ffn_kernel(
    size, width, bases, schedule, gather,
    part_ref, token_ref, cot_ref, gate_own, up_own, down_own, gain_ref,
    sum_ref, out_ref, ffn_in_ref, hidden_ref, d_ffn_ref, d_attn_ref, d_middle_ref,
    grad_gate_ref, grad_up_ref, grad_down_ref, full_ref, gain_grad_ref,
    parts, landing, act_a, act_b, stage, cols, rows_w,
    pass_in, pass_out, share_in, share_out, local_done, col_sem, row_sem, io_sem, gather_in, gather_out, own_done,
):
    micro, rows, depth = parts.shape
    units = gate_own.shape[1]
    stage_t, stage_a, stage_f, stage_c = (stage.at[pl.ds(k * rows, rows)] for k in range(4))
    owned = (gate_own, up_own, down_own)
    gate_ref, up_ref, down_ref = (full_ref.at[k] for k in range(3)) if gather else owned
    spot = place, down, up, first, last = chain_place(size)
    greet_line(down, up, first, last, plane_partners() if gather else ())

    tick, ticks, settle, sent, shared = line_stream(
        size, width, bases, parts, landing, sum_ref,
        (pass_in, pass_out, share_in, share_out, local_done), spot)

    def col_copy(kind, source, i, slot):
        return pltpu.make_async_copy(
            source.at[:, pl.ds(pl.multiple_of(i * TILE, TILE), TILE)], cols.at[kind, slot], col_sem.at[kind, slot])

    def row_copy(kind, source, i, slot):
        return pltpu.make_async_copy(
            source.at[pl.ds(pl.multiple_of(i * TILE, TILE), TILE)], rows_w.at[kind, slot], row_sem.at[kind, slot])

    def tiles(copy, sources, steps, body, clock, beside=()):
        @pl.loop(0, steps)
        def _(i):
            slot = lax.rem(i, 2)

            @pl.when(i + 1 < steps)
            def _():
                for kind, source in enumerate(sources):
                    copy(kind, source, i + 1, 1 - slot).start()

            for kind, source in enumerate(sources):
                copy(kind, source, i, slot).wait()
            body(i, slot)
            for at, work in beside:
                pl.when(i == at)(work)

            @pl.when((lax.rem(i, PACE) == PACE - 1) | (i + 1 == steps))
            def _():
                tick(clock + i // PACE)

    def prime(copy, sources):
        for kind, source in enumerate(sources):
            copy(kind, source, 0, 0).start()

    def span_of(i):
        return pl.ds(pl.multiple_of(i * TILE, TILE), TILE)

    def io(index, source, target):
        return pltpu.make_async_copy(source, target, io_sem.at[index])

    def row_blocks(body, clock):
        count = rows // NORM_ROWS
        marks = [count * k // NORM_TICKS for k in range(NORM_TICKS + 1)]
        for k, (low, high) in enumerate(zip(marks, marks[1:])):
            @pl.loop(low, high)
            def _(b):
                body(pl.ds(pl.multiple_of(b * NORM_ROWS, NORM_ROWS), NORM_ROWS))
            tick(clock + k)

    def own_rows(m):
        return pl.ds(m * rows, rows)

    def gain(k):
        return gain_ref[k : k + 1, :]

    def inverse(values):
        return lax.rsqrt(jnp.mean(values * values, axis=-1, keepdims=True) + EPS)

    def middle_of(span):
        attn = stage_a[span, :].astype(jnp.float32)
        return stage_t[span, :].astype(jnp.float32) + attn * inverse(attn) * gain(1)

    def norm_before(m, clock):
        def body(span):
            middle = middle_of(span)
            stage_f[span, :] = (middle * inverse(middle) * gain(2)).astype(jnp.bfloat16)
        row_blocks(body, clock)

    def gate_and_up(m, clock):
        def body(i, slot):
            at = span_of(i)
            gate = jnp.dot(stage_f[...], cols[0, slot], preferred_element_type=jnp.float32)
            up_val = jnp.dot(stage_f[...], cols[1, slot], preferred_element_type=jnp.float32)
            active, slope = gelu_parts(gate)
            stage_c[:, at] = (active * up_val).astype(jnp.bfloat16)
            act_a[own_rows(m), at] = active.astype(jnp.bfloat16)
            act_b[own_rows(m), at] = (up_val * slope).astype(jnp.bfloat16)
        def down_one():
            moved(1, 4)

        def down_two():
            moved(2, 4)
            moved(1, 5)

        def down_three():
            moved(2, 5)

        beside = ((2, down_one), (5, down_two), (8, down_three)) if gather and m == 0 else ()
        tiles(col_copy, (gate_ref, up_ref), units // TILE, body, clock, beside)

    def down_proj(m, clock):
        def body(i, slot):
            parts[m, :, span_of(i)] = lax.dot_general(
                stage_c[...], rows_w[0, slot], (((1,), (1,)), ((), ())),
                preferred_element_type=jnp.float32).astype(jnp.bfloat16)
        tiles(row_copy, (down_ref,), depth // TILE, body, clock)

    def norm_after(m, clock):
        def body(span):
            middle = middle_of(span)
            ffn = stage_f[span, :].astype(jnp.float32)
            above = stage_c[span, :].astype(jnp.float32)
            inv = inverse(ffn)
            normed = ffn * inv
            stage_f[span, :] = (middle + normed * gain(3)).astype(jnp.bfloat16)
            scaled = above * gain(3)
            d_ffn = inv * (scaled - normed * jnp.mean(scaled * normed, axis=-1, keepdims=True))
            stage_c[span, :] = d_ffn.astype(jnp.bfloat16)
            term = above * normed
            gain_grad_ref[16:24, :] += jnp.sum(term.reshape(NORM_ROWS // 8, 8, depth), axis=0)
        row_blocks(body, clock)

    def d_hidden(m, clock):
        def body(i, slot):
            at = span_of(i)
            d_hid = jnp.dot(stage_c[...], cols[0, slot], preferred_element_type=jnp.float32)
            mine = own_rows(m)
            act_a[mine, at] = (d_hid * act_a[mine, at].astype(jnp.float32)).astype(jnp.bfloat16)
            act_b[mine, at] = (d_hid * act_b[mine, at].astype(jnp.float32)).astype(jnp.bfloat16)
        tiles(col_copy, (down_ref,), units // TILE, body, clock)

    def d_input(m, clock):
        def body(i, slot):
            dims = (((1,), (1,)), ((), ()))
            parts[m, :, span_of(i)] = (
                lax.dot_general(act_b[own_rows(m), :], rows_w[0, slot], dims, preferred_element_type=jnp.float32)
                + lax.dot_general(act_a[own_rows(m), :], rows_w[1, slot], dims, preferred_element_type=jnp.float32)
            ).astype(jnp.bfloat16)
        tiles(row_copy, (gate_ref, up_ref), depth // TILE, body, clock)

    def norm_back_middle(m, clock):
        def body(span):
            attn = stage_a[span, :].astype(jnp.float32)
            attn_inv = inverse(attn)
            attn_normed = attn * attn_inv
            middle = stage_t[span, :].astype(jnp.float32) + attn_normed * gain(1)
            inv = inverse(middle)
            normed = middle * inv
            below = stage_f[span, :].astype(jnp.float32)
            scaled = below * gain(2)
            d_middle = stage_c[span, :].astype(jnp.float32) + inv * (
                scaled - normed * jnp.mean(scaled * normed, axis=-1, keepdims=True))
            term = below * normed
            gain_grad_ref[8:16, :] += jnp.sum(term.reshape(NORM_ROWS // 8, 8, depth), axis=0)
            stage_c[span, :] = d_middle.astype(jnp.bfloat16)
            scaled = d_middle * gain(1)
            d_attn = attn_inv * (scaled - attn_normed * jnp.mean(scaled * attn_normed, axis=-1, keepdims=True))
            stage_f[span, :] = d_attn.astype(jnp.bfloat16)
            term = d_middle * attn_normed
            gain_grad_ref[0:8, :] += jnp.sum(term.reshape(NORM_ROWS // 8, 8, depth), axis=0)
        row_blocks(body, clock)

    def tall_copy(source, i, slot, m):
        return pltpu.make_async_copy(
            source.at[m, :, span_of(i)], cols.at[0, slot, own_rows(m)], col_sem.at[m, slot])

    def weight_grads(source, pairs, steps, clock):
        def put(kind, target, i, slot):
            return pltpu.make_async_copy(rows_w.at[kind, slot], target.at[span_of(i)], row_sem.at[kind, slot])

        @pl.loop(0, steps)
        def _(i):
            slot = lax.rem(i, 2)

            @pl.when(i + 1 < steps)
            def _():
                for m in range(micro):
                    tall_copy(source, i + 1, 1 - slot, m).start()

            for m in range(micro):
                tall_copy(source, i, slot, m).wait()

            @pl.when(i >= 2)
            def _():
                for kind, (_, target) in enumerate(pairs):
                    put(kind, target, i - 2, slot).wait()

            left = cols[0, slot, : micro * rows, :]
            for kind, (right, target) in enumerate(pairs):
                for low in range(0, units, 3 * TILE):
                    high = min(units, low + 3 * TILE)
                    rows_w[kind, slot, :, low:high] = lax.dot_general(
                        left, right[: micro * rows, low:high], (((0,), (0,)), ((), ())),
                        preferred_element_type=jnp.float32).astype(jnp.bfloat16)
                put(kind, target, i, slot).start()
            tick(clock + i)

        for i in (steps - 2, steps - 1):
            for kind, (_, target) in enumerate(pairs):
                put(kind, target, i, i % 2).wait()

    if gather:
        piece = gate_own.shape[0] // 2
        pieces = tuple((h * piece, piece, 0, units, units // 2) for h in range(2))
        movers = [
            plane_gather(full_ref.at[k], owned[k], pieces, gather_in.at[k], gather_out.at[k], own_done.at[k])
            for k in range(3)
        ]

        def moved(phase, u):
            movers[u // 2][phase](u % 2)

    else:

        def moved(phase, u):
            pass

    gain_grad_ref[...] = jnp.zeros_like(gain_grad_ref)

    def load(index, source, target):
        return pltpu.make_async_copy(source, target, io_sem.at[index])

    def bring(m):
        return [load(2, token_ref.at[m], stage_t), load(3, sum_ref.at[m], stage_a)]

    def start(copies):
        for copy in copies:
            copy.start()

    def wait(copies):
        for copy in copies:
            copy.wait()

    whole = schedule["attn"][0]
    entry = [load(m, part_ref.at[m], parts.at[m]) for m in range(micro)]
    start(entry)
    moved(0, 0)
    moved(0, 1)
    wait(entry)
    clock = 0
    for s, phases in (
        (7, ((1, 0), (0, 2))),
        (14, ((1, 1), (2, 0), (0, 3))),
        (21, ((1, 2), (2, 1), (0, 4))),
        (28, ((1, 3), (2, 2), (0, 5))),
    ):
        ticks(clock, s)
        clock = s
        for phase, u in phases:
            moved(phase, u)
    ticks(clock, whole)
    kept = []
    loads = [load(2, token_ref.at[0], stage_t)]
    start(loads)
    for m in range(micro):
        norm_s, gate_s, down_s, end_s = schedule["forward"][m]
        settle(m)
        loads.append(load(3, sum_ref.at[m], stage_a))
        loads[-1].start()
        wait(kept)
        wait(loads)
        norm_before(m, norm_s)
        kept = [load(6, stage_f, ffn_in_ref.at[m]), load(7, stage_c, hidden_ref.at[m])]
        kept[0].start()
        if m + 1 < micro:
            loads = [load(2, token_ref.at[m + 1], stage_t)]
        else:
            loads = bring(0)
        start(loads)
        if m == 0:
            moved(2, 3)
            for u in range(4):
                moved(3, u)
            prime(col_copy, (gate_ref, up_ref))
        gate_and_up(m, gate_s)
        kept[1].start()
        sent(m)
        if m == 0:
            moved(3, 4)
            moved(3, 5)
        prime(row_copy, (down_ref,))
        prime(col_copy, (gate_ref, up_ref) if m + 1 < micro else (down_ref,))
        down_proj(m, down_s)
        if m + 1 == micro:
            wait(kept)
            loads.append(load(5, cot_ref.at[0], stage_c))
            loads[-1].start()
        ticks(down_s + -(-depth // (TILE * PACE)), end_s)
    kept = []
    for m in range(micro):
        norm_s, dh_s, di_s, end_s = schedule["backward"][m]
        settle(micro + m)
        wait(kept[:1])
        loads.append(load(4, sum_ref.at[micro + m], stage_f))
        loads[-1].start()
        wait(loads)
        norm_after(m, norm_s)
        kept = [load(6, stage_f, out_ref.at[m]), load(7, stage_c, d_ffn_ref.at[m])]
        start(kept)
        after = (m + 1) % micro
        loads = bring(after)
        start(loads)
        prime(row_copy, (gate_ref, up_ref))
        d_hidden(m, dh_s)
        sent(micro + m)
        if m + 1 < micro:
            prime(col_copy, (down_ref,))
        kept[1].wait()
        loads.append(load(5, cot_ref.at[after], stage_c))
        loads[-1].start()
        d_input(m, di_s)
        ticks(di_s + -(-depth // (TILE * PACE)), end_s)
    norm_s, grads_s, down_s, end_s = schedule["grads"]
    settle(2 * micro)
    wait(kept[:1])
    loads.append(load(4, sum_ref.at[2 * micro], stage_f))
    loads[-1].start()
    for m in range(micro):
        tall_copy(ffn_in_ref, 0, 0, m).start()
    wait(loads)
    norm_back_middle(0, norm_s)
    kept = [load(6, stage_f, d_attn_ref.at[0]), load(7, stage_c, d_middle_ref.at[0])]
    start(kept)
    hidden_loads = [load(2 + m, hidden_ref.at[m], stage.at[own_rows(m)]) for m in range(micro)]
    start(hidden_loads)
    steps = depth // TILE
    weight_grads(ffn_in_ref, ((act_b, grad_gate_ref), (act_a, grad_up_ref)), steps, grads_s)
    for m in range(micro):
        tall_copy(d_ffn_ref, 0, 0, m).start()
    wait(hidden_loads)
    weight_grads(d_ffn_ref, ((stage, grad_down_ref),), steps, down_s)
    wait(kept)
    tail = bring(1)
    tail.append(load(5, cot_ref.at[1], stage_c))
    start(tail)
    ticks(down_s + steps, end_s)
    settle(2 * micro + 1)
    tail.append(load(4, sum_ref.at[2 * micro + 1], stage_f))
    tail[-1].start()
    wait(tail)
    norm_back_middle(1, end_s)
    kept = [load(6, stage_f, d_attn_ref.at[1]), load(7, stage_c, d_middle_ref.at[1])]
    start(kept)
    sent(STAGES - 2)
    sent(STAGES - 1)
    if gather:
        for mover in movers:
            mover[4]()
    wait(kept)

    shared()


def ffn_schedule(chunks, tiles, hops):
    whole = chunks + hops
    bases = [0, chunks]
    at = whole
    attn = (at,)
    forward = []
    for m in range(2):
        norm_s = at
        gate_s = norm_s + NORM_TICKS
        down_s = gate_s + tiles
        bases.append(max(down_s, bases[-1] + chunks))
        at = max(down_s + tiles, bases[m + 1] + whole)
        forward.append((norm_s, gate_s, down_s, at))
    backward = []
    for m in range(2):
        norm_s = at
        dh_s = norm_s + NORM_TICKS
        di_s = dh_s + tiles
        bases.append(max(di_s, bases[-1] + chunks))
        at = max(di_s + tiles, bases[m + 3] + whole)
        backward.append((norm_s, dh_s, di_s, at))
    grads_s = at + NORM_TICKS
    grads = (at, grads_s, grads_s + tiles, max(grads_s + 2 * tiles, bases[-1] + whole))
    return tuple(bases), {
        "attn": attn, "forward": tuple(forward), "backward": tuple(backward), "grads": grads
    }


def ffn_block(parts, tokens, cotangent, gate, up, down, gains, cid, width=128):
    size = lax.axis_size("tensor")
    micro, rows, depth = tokens.shape
    units = gate.shape[1]
    chunks = depth // width
    bases, schedule = ffn_schedule(chunks, -(-units // (TILE * PACE)), 2 * LAG * (size - 1))
    bf16 = jnp.bfloat16
    any_spec = pl.BlockSpec(memory_space=pl.ANY)
    vmem_spec = pl.BlockSpec(memory_space=pltpu.VMEM)
    gather = up.shape[0] != depth
    stack = jax.ShapeDtypeStruct((micro, rows, depth), bf16)
    wide = jax.ShapeDtypeStruct((micro, rows, units), bf16)
    grad = jax.ShapeDtypeStruct((depth, units), bf16)
    full = jax.ShapeDtypeStruct((3, depth, units) if gather else (3, 16, 128), bf16)
    dma = pltpu.SemaphoreType.DMA
    flops = 2 * micro * rows * depth * units * 9
    found = pl.pallas_call(
        functools.partial(ffn_kernel, size, width, bases, schedule, gather),
        out_shape=(
            jax.ShapeDtypeStruct((STAGES, rows, depth), bf16),
            stack, stack, wide, stack, stack, stack, grad, grad, grad, full,
            jax.ShapeDtypeStruct((24, depth), jnp.float32),
        ),
        in_specs=[any_spec] * 6 + [vmem_spec],
        out_specs=(any_spec,) * 11 + (vmem_spec,),
        scratch_shapes=[
            pltpu.VMEM((micro, rows, depth), bf16),
            pltpu.VMEM((2, STAGES, chunks, rows // 2, width), bf16),
            pltpu.VMEM((micro * rows, units), bf16),
            pltpu.VMEM((micro * rows, units), bf16),
            pltpu.VMEM((4 * rows, depth), bf16),
            pltpu.VMEM((2, 2, depth, TILE), bf16),
            pltpu.VMEM((2, 2, TILE, units), bf16),
        ]
        + [dma((2, STAGES, chunks))] * 5
        + [dma((2, 2)), dma((2, 2)), dma((8,)), dma((3, 2, 9)), dma((3, 2, 9)), dma((3, 2))],
        compiler_params=pltpu.CompilerParams(
            collective_id=cid, has_side_effects=True, vmem_limit_bytes=60 * 2**20),
        cost_estimate=pl.CostEstimate(
            flops=flops, bytes_accessed=2**30, transcendentals=micro * rows * units),
    )(parts, tokens, cotangent, gate, up, down, gains)
    return {
        "attn": found[0][:micro], "out": found[1], "d_attn": found[5], "d_middle": found[6],
        "grad_gate": found[7], "grad_up": found[8], "grad_down": found[9], "gain_grad": found[11],
        "sums": found[0], "ffn_in": found[2], "hidden": found[3], "d_ffn": found[4],
    }

SIDE_PAD = 128


def tail_kernel(
    size, width, bases,
    part_ref, gate_grad_ref, up_grad_ref, normed_ref, d_attn_ref, d_qkv_ref, context_ref, gain_ref,
    sum_ref, gate_share_ref, up_share_ref, side_share_ref, gain_share_ref,
    parts, landing, mine_in, side_acc, ffn_first, side_first, ffn_second, side_second, ffn_third, side_third,
    cols, d_qkv, context, gain_in,
    pass_in, pass_out, share_in, share_out, local_done, col_sem, io_sem, mine_sem, hop_in, hop_out, gain_got, gain_sent,
):
    micro, rows, depth = parts.shape
    spot = place, down, up, first, last = chain_place(size)
    over_x, over_y, over_core = plane_partners()
    dp, seq = lax.axis_index("dp"), lax.axis_index("seq")
    x, core = dp // 2, lax.rem(dp, 2)
    others = [(dp, seq, lax.rem(place + k, size)) for k in range(1, size)]
    greet_plane(over_x, over_y, over_core, others)
    tick, ticks, settle, sent, shared = line_stream(
        size, width, bases, parts, landing, sum_ref,
        (pass_in, pass_out, share_in, share_out, local_done), spot)
    share = up_share_ref.shape[0]
    piece = share // 2
    widths = (up_share_ref.shape[1], side_share_ref.shape[1])
    grads = (gate_grad_ref, up_grad_ref)
    qkv_width = d_qkv.shape[1]

    def load(index, source, target):
        return pltpu.make_async_copy(source, target, io_sem.at[index])

    def halves(p):
        all_columns = widths[p // 4]
        low = -(-all_columns // 256) * 128
        return (pl.ds(0, low), pl.ds(low, all_columns - low))

    def block_rows(bx, by, bc, p):
        return pl.ds(pl.multiple_of(((bx * 2 + bc) * 2 + by) * share + (p % 2) * piece, 16), piece)

    def acc(p, bx, by, across):
        if p < 4:
            return ffn_first.at[p, bx * 2 + by, :, across]
        return side_acc.at[block_rows(bx, by, core, p), across]

    def whole(p):
        return pl.ds(0, widths[p // 4])

    first_buf, second_buf, third_buf = (ffn_first, side_first), (ffn_second, side_second), (ffn_third, side_third)

    def land(step, p, k, across):
        buf = (first_buf, second_buf, third_buf)[step][p // 4]
        return buf.at[p % 4, k, :, across]

    def hop(p, k, source, target, device):
        return pltpu.make_async_remote_copy(
            source, target, hop_out.at[p, k], hop_in.at[p, k], device_id=device, device_id_type=MESH)

    def hops(p):
        left, right = halves(p)
        found = []
        for k in range(4):
            bx, by = k // 2, k % 2
            if p < 4:
                source = grads[p // 2].at[block_rows(bx, by, 1 - core, p), :]
            else:
                source = side_acc.at[block_rows(bx, by, 1 - core, p), :]
            found.append((source, land(0, p, k, whole(p)), over_core))
        for k in range(2):
            found.append((acc(p, 1 - x, k, left), land(1, p, k, left), over_x))
        for k in range(2):
            found.append((acc(p, k, 1 - seq, right), land(1, p, k, right), over_y))
        found.append((acc(p, x, 1 - seq, left), land(2, p, 0, left), over_y))
        found.append((acc(p, 1 - x, seq, right), land(2, p, 0, right), over_x))
        return found

    def go(p, k):
        source, target, device = hops(p)[k]
        hop(p, k, source, target, device).start()

    def got(p, k):
        _, target, device = hops(p)[k]
        hop(p, k, target, target, device).wait_recv()
        return target

    def fetch(p, k):
        return pltpu.make_async_copy(
            grads[p // 2].at[block_rows(k // 2, k % 2, core, p), :], mine_in.at[k], mine_sem.at[k])

    def start_fetch(p):
        for k in range(4):
            fetch(p, k).start()

    def add(p, bx, by, across, arrived):
        mine = acc(p, bx, by, across)

        @pl.loop(0, piece // BLOCK)
        def _(b):
            span = pl.ds(pl.multiple_of(b * BLOCK, BLOCK), BLOCK)
            mine[span, :] = (
                mine[span, :].astype(jnp.float32) + arrived[span, :].astype(jnp.float32)
            ).astype(jnp.bfloat16)

    def scatter_first(p):
        for k in range(4):
            go(p, k)

    def scatter_second(p):
        for k in range(4):
            arrived = got(p, k)
            if p < 4:
                fetch(p, k).wait()
                arrived = mine_in.at[k]
            add(p, k // 2, k % 2, whole(p), arrived)
        for k in (4, 5, 6, 7):
            go(p, k)
        if p < 3:
            start_fetch(p + 1)

    def scatter_third(p):
        left, right = halves(p)
        for k in range(2):
            add(p, x, k, left, got(p, 4 + k))
        go(p, 8)
        for k in range(2):
            add(p, k, seq, right, got(p, 6 + k))
        go(p, 9)

    def scatter_last(p):
        left, right = halves(p)
        add(p, x, seq, left, got(p, 8))
        add(p, x, seq, right, got(p, 9))
        put(p).start()

    def put(p):
        target = (gate_share_ref, up_share_ref, side_share_ref)[p // 2].at[pl.ds((p % 2) * piece, piece)]
        return load(5 + p, acc(p, x, seq, whole(p)), target)

    def scatter_sent(p):
        for k, (source, target, device) in enumerate(hops(p)):
            hop(p, k, source, target, device).wait_send()
        put(p).wait()

    def tile_copy(kind, i, slot):
        source = (normed_ref, d_attn_ref)[kind].at[:, pl.ds(pl.multiple_of(i * TILE, TILE), TILE)]
        return pltpu.make_async_copy(source, cols.at[kind, slot], col_sem.at[kind, slot])

    def side_grads(clock):
        steps = depth // TILE

        @pl.loop(0, steps)
        def _(i):
            slot = lax.rem(i, 2)

            @pl.when(i + 1 < steps)
            def _():
                tile_copy(0, i + 1, 1 - slot).start()
                tile_copy(1, i + 1, 1 - slot).start()

            tile_copy(0, i, slot).wait()
            tile_copy(1, i, slot).wait()
            span = pl.ds(pl.multiple_of(i * TILE, TILE), TILE)
            for kind, right, low in ((0, d_qkv, 0), (1, context, qkv_width)):
                side_acc[span, low : low + right.shape[1]] = lax.dot_general(
                    cols[kind, slot], right[...], (((0,), (0,)), ((), ())),
                    preferred_element_type=jnp.float32).astype(jnp.bfloat16)
            tick(clock + i)

    entry = [load(m, part_ref.at[m], parts.at[m]) for m in range(micro)]
    side_loads = [
        load(2, d_qkv_ref, d_qkv),
        load(3, context_ref, context),
        load(4, gain_ref, side_acc.at[:, pl.ds(widths[1] - SIDE_PAD, SIDE_PAD)]),
    ]
    for copy in entry:
        copy.start()
    scatter_first(0)
    scatter_first(1)
    for copy in side_loads:
        copy.start()
    start_fetch(0)
    tile_copy(0, 0, 0).start()
    tile_copy(1, 0, 0).start()
    for copy in entry:
        copy.wait()
    ticks(0, 1)
    for copy in side_loads:
        copy.wait()
    ticks(1, 4)
    scatter_second(0)
    scatter_first(2)
    side_grads(4)
    clock = 4 + depth // TILE
    scatter_second(1)
    scatter_third(0)
    for p in (3, 4, 5):
        scatter_first(p)
    plan = (
        (2, (scatter_second, 2)), (2, (scatter_third, 1)), (2, (scatter_last, 0)), (2, (scatter_second, 3)),
        (2, (scatter_third, 2)), (2, (scatter_last, 1)), (2, (scatter_second, 4)), (2, (scatter_third, 3)),
        (2, (scatter_last, 2)), (1, (scatter_second, 5)), (2, (scatter_third, 4)), (2, (scatter_last, 3)),
        (2, (scatter_third, 5)), (2, (scatter_last, 4)), (2, (scatter_last, 5)),
    )
    for pause, (step, p) in plan:
        if pause:
            ticks(clock, clock + pause)
            clock += pause
        step(p)

    mine = side_acc.at[pl.ds(pl.multiple_of(((x * 2 + core) * 2 + seq) * share, 16), share), pl.ds(widths[1] - SIDE_PAD, SIDE_PAD)]

    def gain_hop(k):
        return pltpu.make_async_remote_copy(
            mine, gain_in.at[k], gain_sent.at[k], gain_got.at[k], device_id=others[k], device_id_type=MESH)

    for k in range(size - 1):
        gain_hop(k).start()
    ticks(clock, clock + 2)
    clock += 2
    for k in range(size - 1):
        gain_hop(k).wait_recv()
    total = mine[...].astype(jnp.float32)
    for k in range(size - 1):
        total = total + gain_in[k].astype(jnp.float32)
    gain_share_ref[...] = total
    ticks(clock, max(clock, bases[-1] + depth // width + 2 * LAG * (size - 1)))
    for q in range(micro):
        settle(q)
        sent(q)
    shared()
    for p in range(6):
        scatter_sent(p)
    for k in range(size - 1):
        gain_hop(k).wait_send()


def greet_plane(over_x, over_y, over_core, others):
    barrier = pltpu.get_barrier_semaphore()
    partners = (over_x, over_y, over_core, *others)
    for partner in partners:
        pl.semaphore_signal(barrier, inc=1, device_id=partner, device_id_type=MESH)
    pl.semaphore_wait(barrier, len(partners))


def tail_block(parts, gate_grad, up_grad, normed, d_attn, d_qkv, context, gain_cols, cid, width=128):
    size = lax.axis_size("tensor")
    micro, rows, depth = parts.shape
    units = up_grad.shape[1]
    chunks = depth // width
    total = micro * rows
    share = depth // (lax.axis_size("dp") * lax.axis_size("seq"))
    piece = share // 2
    side = d_qkv.shape[1] + context.shape[1] + SIDE_PAD
    bases = (0, chunks)
    bf16 = jnp.bfloat16
    any_spec = pl.BlockSpec(memory_space=pl.ANY)
    vmem_spec = pl.BlockSpec(memory_space=pltpu.VMEM)
    dma = pltpu.SemaphoreType.DMA
    return pl.pallas_call(
        functools.partial(tail_kernel, size, width, bases),
        out_shape=(
            jax.ShapeDtypeStruct((micro, rows, depth), bf16),
            jax.ShapeDtypeStruct((share, units), bf16),
            jax.ShapeDtypeStruct((share, units), bf16),
            jax.ShapeDtypeStruct((share, side), bf16),
            jax.ShapeDtypeStruct((share, SIDE_PAD), jnp.float32),
        ),
        in_specs=[any_spec] * 8,
        out_specs=(any_spec,) * 4 + (vmem_spec,),
        scratch_shapes=[
            pltpu.VMEM((micro, rows, depth), bf16),
            pltpu.VMEM((2, 2, chunks, rows // 2, width), bf16),
            pltpu.VMEM((4, piece, units), bf16),
            pltpu.VMEM((depth, side), bf16),
            pltpu.VMEM((4, 4, piece, units), bf16),
            pltpu.VMEM((2, 4, piece, side), bf16),
            pltpu.VMEM((4, 2, piece, units), bf16),
            pltpu.VMEM((2, 2, piece, side), bf16),
            pltpu.VMEM((4, 1, piece, units), bf16),
            pltpu.VMEM((2, 1, piece, side), bf16),
            pltpu.VMEM((2, 2, total, TILE), bf16),
            pltpu.VMEM(d_qkv.shape, bf16),
            pltpu.VMEM(context.shape, bf16),
            pltpu.VMEM((size - 1, share, SIDE_PAD), bf16),
        ]
        + [dma((2, 2, chunks))] * 5
        + [dma((2, 2)), dma((11,)), dma((4,)), dma((6, 10)), dma((6, 10)), dma((size - 1,)), dma((size - 1,))],
        compiler_params=pltpu.CompilerParams(
            collective_id=cid, has_side_effects=True, vmem_limit_bytes=60 * 2**20),
        cost_estimate=pl.CostEstimate(
            flops=2 * total * depth * side, bytes_accessed=400 * 2**20, transcendentals=0),
    )(parts, gate_grad, up_grad, normed, d_attn, d_qkv, context, gain_cols)

CAP_SCALE = HEAD ** -0.5 / SOFTCAP


def capped(query, keys):
    raw = lax.dot_general(query, keys, (((1,), (1,)), ((), ())), preferred_element_type=jnp.float32)
    curve = jnp.tanh(raw * CAP_SCALE)
    return curve, jnp.exp(SOFTCAP * curve)


def at_or_before(shape, row_at):
    return lax.broadcasted_iota(jnp.int32, shape, 1) <= lax.broadcasted_iota(jnp.int32, shape, 0) + row_at


def pick_rows(ref, rows, prompt, heads):
    found = []
    for m in range(2):
        for h in range(heads):
            found.append(ref[m * rows + prompt : (m + 1) * rows, h * HEAD : (h + 1) * HEAD])
    return jnp.concatenate(found, axis=0)


def cont_masks(prompt_of, group, cont, heads):
    count = 2 * heads * cont
    row = lax.broadcasted_iota(jnp.int32, (count, 1), 0)
    sees = jnp.where(row < heads * cont, prompt_of[0], prompt_of[1]) == group
    row = lax.broadcasted_iota(jnp.int32, (count, 2 * cont), 0)
    key = lax.broadcasted_iota(jnp.int32, (count, 2 * cont), 1)
    same = (row // (heads * cont)) == (key // cont)
    return sees, same & (lax.rem(key, cont) <= lax.rem(row, cont))


def turn(values, cosine, sine):
    half = HEAD // 2
    low, high = values[:, :half], values[:, half:]
    return jnp.concatenate([low * cosine - high * sine, high * cosine + low * sine], axis=1)


ROW_TILE = 256


def head_kernel(
    heads, cont,
    prompt_of, token_ref, own_ref, angle_ref,
    part_ref, context_ref, query_ref, kv_ref, other_ref, sum_ref, normed_ref, full_ref, gain_ref,
    tokens, normed, full, cosine_sine, queries, kv, other, total, sums, context,
    gather_in, gather_out, own_done, io_sem, part_sem, swap_in, swap_out,
):
    rows_all, depth = tokens.shape
    rows = rows_all // 2
    prompt = rows - cont
    query_width = heads * HEAD
    qkv_width = query_width + 2 * HEAD
    over_x, over_y, over_core = plane_partners()
    seq = lax.axis_index("seq")
    greet_plane(over_x, over_y, over_core, ())
    share = own_ref.shape[0]
    piece = share // 2
    side = qkv_width + SIDE_PAD
    pieces = (
        (0, share, qkv_width, SIDE_PAD, SIDE_PAD),
        (0, piece, 0, qkv_width, qkv_width // 2),
        (piece, piece, 0, qkv_width, qkv_width // 2),
        (0, share, side, query_width, query_width // 2),
    )
    first, second, third, finish, all_sent = plane_gather(full, own_ref, pieces, gather_in, gather_out, own_done)

    def io(index, source, target):
        return pltpu.make_async_copy(source, target, io_sem.at[index])

    loads = [io(0, token_ref, tokens), io(1, angle_ref, cosine_sine)]
    for u in (0, 1, 2):
        first(u)
    for copy in loads:
        copy.start()
    second(0)
    third(0)
    first(3)
    for copy in loads:
        copy.wait()
    finish(0)
    gain_ref[...] = jnp.transpose(full[:, qkv_width:side].astype(jnp.float32))[:8, :]

    def normalize_rows(low, high):
        @pl.loop(low, high)
        def _(b):
            span = pl.ds(pl.multiple_of(b * BLOCK, BLOCK), BLOCK)
            values = tokens[span, :].astype(jnp.float32)
            inv = lax.rsqrt(jnp.mean(values * values, axis=-1, keepdims=True) + EPS)
            normed[span, :] = (values * inv * gain_ref[0:1, :]).astype(jnp.bfloat16)

    blocks = rows_all // BLOCK
    normalize_rows(0, blocks // 2)
    second(1)
    normalize_rows(blocks // 2, blocks)
    second(2)
    third(1)
    second(3)
    third(2)
    for u in (1, 2):
        finish(u)

    stores = [io(2, normed, normed_ref)]
    stores[0].start()
    half = HEAD // 2

    def project(m, low, count):
        return jnp.dot(normed[pl.ds(m * rows, rows), :], full[:, low : low + count], preferred_element_type=jnp.float32)

    def angles():
        return cosine_sine[:, :half], cosine_sine[:, half:]

    def swap(m):
        return pltpu.make_async_remote_copy(
            kv.at[m, pl.ds(0, prompt)], other.at[m], swap_out.at[m], swap_in.at[m],
            device_id=over_y, device_id_type=MESH)

    for m in range(2):
        kv[m, :, :HEAD] = turn(project(m, query_width, HEAD), *angles()).astype(jnp.bfloat16)
        kv[m, :, HEAD:] = project(m, query_width + HEAD, HEAD).astype(jnp.bfloat16)
        swap(m).start()
    for m in range(2):
        for h in range(heads):
            queries[pl.ds(m * rows, rows), h * HEAD : (h + 1) * HEAD] = turn(
                project(m, h * HEAD, HEAD), *angles()).astype(jnp.bfloat16)
    third(3)
    stores += [io(3, queries, query_ref), io(4, kv, kv_ref)]
    stores[1].start()
    stores[2].start()
    lanes = sums.shape[-1]

    def spots(i, low, count):
        m, h = i // heads, lax.rem(i, heads)
        return m, h, pl.ds(pl.multiple_of(m * rows + low, 16), count), pl.ds(pl.multiple_of(h * HEAD, HEAD), HEAD)

    def attend(weights, values):
        return jnp.dot(weights.astype(jnp.bfloat16), values, preferred_element_type=jnp.float32)

    tiles = [(low, min(ROW_TILE, prompt - low)) for low in range(0, prompt, ROW_TILE)]

    @pl.loop(0, 2 * heads)
    def _(i):
        for low, count in tiles:
            m, h, span, across = spots(i, low, count)
            reach = low + count
            keys = kv[m, :reach, :HEAD]
            values = kv[m, :reach, HEAD:]
            _, weights = capped(queries[span, across], keys)
            weights = jnp.where(at_or_before((count, reach), low), weights, 0.0)
            sums[h, span, :] = jnp.broadcast_to(jnp.sum(weights, axis=1, keepdims=True), (count, lanes))
            total[span, across] = attend(weights, values)

    for m in range(2):
        swap(m).wait_recv()

    @pl.when(seq == 1)
    def _():
        @pl.loop(0, 2 * heads)
        def _(i):
            for low, count in tiles:
                m, h, span, across = spots(i, low, count)
                _, weights = capped(queries[span, across], other[m, :, :HEAD])
                sums[h, span, :] += jnp.broadcast_to(jnp.sum(weights, axis=1, keepdims=True), (count, lanes))
                total[span, across] += attend(weights, other[m, :, HEAD:])

    picked = pick_rows(queries, rows, prompt, heads)
    weight_sum = jnp.zeros((picked.shape[0], 1), jnp.float32)
    weighted = jnp.zeros((picked.shape[0], HEAD), jnp.float32)
    for g in range(2):
        sees, near = cont_masks(prompt_of, g, cont, heads)
        for pair in (kv[g, :prompt, :], other[g]):
            _, weights = capped(picked, pair[:, :HEAD])
            weights = jnp.where(sees, weights, 0.0)
            weight_sum += jnp.sum(weights, axis=1, keepdims=True)
            weighted += attend(weights, pair[:, HEAD:])
    tail = jnp.concatenate([kv[m, prompt:, :] for m in range(2)], axis=0)
    _, weights = capped(picked, tail[:, :HEAD])
    weights = jnp.where(near, weights, 0.0)
    weight_sum += jnp.sum(weights, axis=1, keepdims=True)
    weighted += attend(weights, tail[:, HEAD:])
    for m in range(2):
        for h in range(heads):
            low = (m * heads + h) * cont
            span = pl.ds(m * rows + prompt, cont)
            sums[h, span, :] = jnp.broadcast_to(weight_sum[low : low + cont], (cont, lanes))
            total[span, h * HEAD : (h + 1) * HEAD] = weighted[low : low + cont]

    for h in range(heads):
        across = slice(h * HEAD, (h + 1) * HEAD)
        inverse = 1.0 / sums[h, :, :1]
        context[:, across] = (total[:, across] * inverse).astype(jnp.bfloat16)
        sums[h, :, :] = jnp.broadcast_to(inverse, (rows_all, lanes))
    finish(3)
    stores += [io(5, context, context_ref), io(6, sums, sum_ref), io(7, other, other_ref), io(8, full, full_ref)]
    for copy in stores[3:]:
        copy.start()

    def part_copy(i):
        at = pl.ds(pl.multiple_of(i * TILE, TILE), TILE)
        return pltpu.make_async_copy(tokens.at[:, at], part_ref.at[:, at], part_sem.at[i])

    @pl.loop(0, depth // TILE)
    def _(i):
        at = pl.ds(pl.multiple_of(i * TILE, TILE), TILE)
        tokens[:, at] = lax.dot_general(
            context[...], full[at, side : side + query_width], (((1,), (1,)), ((), ())),
            preferred_element_type=jnp.float32).astype(jnp.bfloat16)
        part_copy(i).start()

    for m in range(2):
        swap(m).wait_send()
    all_sent()
    for copy in stores:
        copy.wait()

    @pl.loop(0, depth // TILE)
    def _(i):
        part_copy(i).wait()


def head_block(tokens, own, angles, prompt_of, heads, cont, cid):
    rows, depth = tokens.shape
    half_rows = rows // 2
    prompt = half_rows - cont
    width = heads * HEAD
    group = lax.axis_size("dp") * lax.axis_size("seq")
    bf16, f32 = jnp.bfloat16, jnp.float32
    any_spec = pl.BlockSpec(memory_space=pl.ANY)
    vmem_spec = pl.BlockSpec(memory_space=pltpu.VMEM)
    dma = pltpu.SemaphoreType.DMA
    full = (own.shape[0] * group, own.shape[1])
    shape = jax.ShapeDtypeStruct
    return pl.pallas_call(
        functools.partial(head_kernel, heads, cont),
        out_shape=(
            shape((rows, depth), bf16),
            shape((rows, width), bf16),
            shape((rows, width), bf16),
            shape((2, half_rows, 2 * HEAD), bf16),
            shape((2, prompt, 2 * HEAD), bf16),
            shape((heads, rows, 128), f32),
            shape((rows, depth), bf16),
            shape(full, bf16),
            shape((8, depth), f32),
        ),
        in_specs=[pl.BlockSpec(memory_space=pltpu.SMEM)] + [any_spec] * 3,
        out_specs=(any_spec,) * 8 + (vmem_spec,),
        scratch_shapes=[
            pltpu.VMEM((rows, depth), bf16),
            pltpu.VMEM((rows, depth), bf16),
            pltpu.VMEM(full, bf16),
            pltpu.VMEM((half_rows, HEAD), f32),
            pltpu.VMEM((rows, width), bf16),
            pltpu.VMEM((2, half_rows, 2 * HEAD), bf16),
            pltpu.VMEM((2, prompt, 2 * HEAD), bf16),
            pltpu.VMEM((rows, width), f32),
            pltpu.VMEM((heads, rows, 128), f32),
            pltpu.VMEM((rows, width), bf16),
            dma((4, 9)), dma((4, 9)), dma((4,)), dma((9,)), dma((depth // TILE,)), dma((2,)), dma((2,)),
        ],
        compiler_params=pltpu.CompilerParams(
            collective_id=cid, has_side_effects=True, vmem_limit_bytes=56 * 2**20),
        cost_estimate=pl.CostEstimate(
            flops=2 * rows * depth * (full[1] + width), bytes_accessed=200 * 2**20, transcendentals=rows * 2048),
    )(prompt_of, tokens, own, angles)
def back_kernel(
    heads, cont,
    prompt_of, d_attn_ref, full_ref, query_ref, kv_ref, other_ref, context_ref, sum_ref, angle_ref, token_ref,
    d_qkv_ref, part_ref, gain_ref,
    d_attn, full, tokens, queries, kv, other, context, sums, cosine_sine,
    d_context, d_query, d_kv, d_other, sent_kv, got_kv, d_qkv, inverses, d_picked,
    io_sem, part_sem, swap_in, swap_out,
):
    rows_all, depth = tokens.shape
    rows = rows_all // 2
    prompt = rows - cont
    query_width = heads * HEAD
    qkv_width = query_width + 2 * HEAD
    side = qkv_width + SIDE_PAD
    _, over_y, _ = plane_partners()
    seq = lax.axis_index("seq")
    barrier = pltpu.get_barrier_semaphore()
    pl.semaphore_signal(barrier, inc=1, device_id=over_y, device_id_type=MESH)
    pl.semaphore_wait(barrier, 1)

    def io(index, source, target):
        return pltpu.make_async_copy(source, target, io_sem.at[index])

    def swap(m):
        return pltpu.make_async_remote_copy(
            sent_kv.at[m], got_kv.at[m], swap_out.at[m], swap_in.at[m], device_id=over_y, device_id_type=MESH)

    pairs = (
        (d_attn_ref, d_attn), (full_ref.at[:, pl.ds(side, query_width)], full.at[:, pl.ds(side, query_width)]),
        (query_ref, queries), (kv_ref, kv), (other_ref, other),
        (context_ref, context), (sum_ref, sums), (angle_ref, cosine_sine), (token_ref, tokens),
        (full_ref.at[:, pl.ds(0, side)], full.at[:, pl.ds(0, side)]),
    )
    loads = [io(k, *pair) for k, pair in enumerate(pairs)]
    for copy in loads:
        copy.start()
    for copy in loads[:2]:
        copy.wait()
    for m in range(2):
        span = pl.ds(m * rows, rows)
        d_context[span, :] = jnp.dot(
            d_attn[span, :], full[:, side : side + query_width], preferred_element_type=jnp.float32
        ).astype(jnp.bfloat16)
    for copy in loads[2:]:
        copy.wait()

    def nt(left, right):
        return lax.dot_general(left, right, (((1,), (1,)), ((), ())), preferred_element_type=jnp.float32)

    def tn(left, right):
        return lax.dot_general(left, right, (((0,), (0,)), ((), ())), preferred_element_type=jnp.float32)

    def score_grads(query, above, found, inverse, pair, seen):
        keys, values = pair[:, :HEAD], pair[:, HEAD:]
        curve, weights = capped(query, keys)
        weights = weights * inverse
        if seen is not None:
            weights = jnp.where(seen, weights, 0.0)
        d_weights = nt(above, values)
        inner = jnp.sum(found.astype(jnp.float32) * above.astype(jnp.float32), axis=1, keepdims=True)
        d_scores = (weights * (d_weights - inner) * ((1.0 - curve * curve) * HEAD ** -0.5)).astype(jnp.bfloat16)
        d_pair = jnp.concatenate([tn(d_scores, query), tn(weights.astype(jnp.bfloat16), above)], axis=1)
        return jnp.dot(d_scores, keys, preferred_element_type=jnp.float32), d_pair

    picked = [pick_rows(ref, rows, prompt, heads) for ref in (queries, d_context, context)]
    picked_inverse = jnp.concatenate(
        [sums[h, m * rows + prompt : (m + 1) * rows, :1] for m in range(2) for h in range(heads)], axis=0)
    d_picked[...] = jnp.zeros_like(d_picked)
    for g in range(2):
        sees, near = cont_masks(prompt_of, g, cont, heads)
        d_rows, d_pair = score_grads(*picked, picked_inverse, other[g], sees)
        d_picked[...] += d_rows
        d_other[g] = d_pair
        d_rows, d_pair = score_grads(*picked, picked_inverse, kv[g, :prompt, :], sees)
        d_picked[...] += d_rows
        d_kv[g, :prompt, :] = d_pair
    tail = jnp.concatenate([kv[m, prompt:, :] for m in range(2)], axis=0)
    d_rows, d_pair = score_grads(*picked, picked_inverse, tail, near)
    d_picked[...] += d_rows
    for m in range(2):
        d_kv[m, prompt:, :] = d_pair[m * cont : (m + 1) * cont]

    def spots(i, low, count):
        m, h = i // heads, lax.rem(i, heads)
        return m, h, pl.ds(pl.multiple_of(m * rows + low, 16), count), pl.ds(pl.multiple_of(h * HEAD, HEAD), HEAD)

    tiles = [(low, min(ROW_TILE, prompt - low)) for low in range(0, prompt, ROW_TILE)]

    @pl.when(seq == 0)
    def _():
        d_query[...] = jnp.zeros_like(d_query)

    @pl.when(seq == 1)
    def _():
        @pl.loop(0, 2 * heads)
        def _(i):
            for low, count in tiles:
                m, h, span, across = spots(i, low, count)
                d_rows, d_pair = score_grads(
                    queries[span, across], d_context[span, across], context[span, across], sums[h, span, :1], other[m], None)
                d_query[span, across] = d_rows
                d_other[m] += d_pair

    for m in range(2):
        sent_kv[m] = d_other[m].astype(jnp.bfloat16)
        swap(m).start()
    for m in range(2):
        for h in range(heads):
            low = (m * heads + h) * cont
            d_query[m * rows + prompt : (m + 1) * rows, h * HEAD : (h + 1) * HEAD] = d_picked[low : low + cont]

    @pl.loop(0, 2 * heads)
    def _(i):
        for low, count in tiles:
            m, h, span, across = spots(i, low, count)
            reach = low + count
            d_rows, d_pair = score_grads(
                queries[span, across], d_context[span, across], context[span, across], sums[h, span, :1],
                kv[m, :reach, :], at_or_before((count, reach), low))
            d_query[span, across] += d_rows
            d_kv[m, :reach, :] += d_pair

    half = HEAD // 2

    def turn_back_rows(values):
        return turn(values, cosine_sine[:, :half], -cosine_sine[:, half:]).astype(jnp.bfloat16)

    for m in range(2):
        span = pl.ds(m * rows, rows)
        for h in range(heads):
            across = slice(h * HEAD, (h + 1) * HEAD)
            d_qkv[span, across] = turn_back_rows(d_query[span, across])

    @pl.loop(0, rows_all // BLOCK)
    def _(b):
        span = pl.ds(pl.multiple_of(b * BLOCK, BLOCK), BLOCK)
        values = tokens[span, :].astype(jnp.float32)
        inverse = lax.rsqrt(jnp.mean(values * values, axis=-1, keepdims=True) + EPS)
        inverses[span, :] = jnp.broadcast_to(inverse, (BLOCK, inverses.shape[1]))

    for m in range(2):
        swap(m).wait_recv()
        span = pl.ds(m * rows, rows)
        d_kv[m, :prompt, :] += got_kv[m].astype(jnp.float32)
        d_qkv[span, query_width : query_width + HEAD] = turn_back_rows(d_kv[m, :, :HEAD])
        d_qkv[span, query_width + HEAD :] = d_kv[m, :, HEAD:].astype(jnp.bfloat16)
    stores = [io(10, d_qkv, d_qkv_ref)]
    stores[0].start()

    def part_copy(i):
        at = pl.ds(pl.multiple_of(i * TILE, TILE), TILE)
        return pltpu.make_async_copy(d_attn.at[:, at], part_ref.at[:, at], part_sem.at[i])

    @pl.loop(0, depth // TILE)
    def _(i):
        at = pl.ds(pl.multiple_of(i * TILE, TILE), TILE)
        part = nt(d_qkv[...], full[at, :qkv_width])
        normed = tokens[:, at].astype(jnp.float32) * inverses[:, :1]
        gain_ref[0:1, at] = jnp.sum(part * normed, axis=0, keepdims=True)
        d_attn[:, at] = part.astype(jnp.bfloat16)
        part_copy(i).start()

    for m in range(2):
        swap(m).wait_send()
    for copy in stores:
        copy.wait()

    @pl.loop(0, depth // TILE)
    def _(i):
        part_copy(i).wait()


def back_block(prompt_of, d_attn, full, queries, kv, other, context, sums, angles, tokens, cont, cid):
    rows, depth = tokens.shape
    width = queries.shape[1]
    heads = width // HEAD
    qkv_width = width + 2 * HEAD
    bf16, f32 = jnp.bfloat16, jnp.float32
    any_spec = pl.BlockSpec(memory_space=pl.ANY)
    vmem_spec = pl.BlockSpec(memory_space=pltpu.VMEM)
    dma = pltpu.SemaphoreType.DMA
    shape = jax.ShapeDtypeStruct
    return pl.pallas_call(
        functools.partial(back_kernel, heads, cont),
        out_shape=(shape((rows, qkv_width), bf16), shape((rows, depth), bf16), shape((8, depth), f32)),
        in_specs=[pl.BlockSpec(memory_space=pltpu.SMEM)] + [any_spec] * 9,
        out_specs=(any_spec, any_spec, vmem_spec),
        scratch_shapes=[
            pltpu.VMEM(d_attn.shape, bf16),
            pltpu.VMEM(full.shape, bf16),
            pltpu.VMEM(tokens.shape, bf16),
            pltpu.VMEM(queries.shape, bf16),
            pltpu.VMEM(kv.shape, bf16),
            pltpu.VMEM(other.shape, bf16),
            pltpu.VMEM(context.shape, bf16),
            pltpu.VMEM(sums.shape, f32),
            pltpu.VMEM(angles.shape, f32),
            pltpu.VMEM(queries.shape, bf16),
            pltpu.VMEM(queries.shape, f32),
            pltpu.VMEM(kv.shape, f32),
            pltpu.VMEM(other.shape, f32),
            pltpu.VMEM(other.shape, bf16),
            pltpu.VMEM(other.shape, bf16),
            pltpu.VMEM((rows, qkv_width), bf16),
            pltpu.VMEM((rows, 128), f32),
            pltpu.VMEM((2 * heads * cont, HEAD), f32),
            dma((11,)), dma((depth // TILE,)), dma((2,)), dma((2,)),
        ],
        compiler_params=pltpu.CompilerParams(
            collective_id=cid, has_side_effects=True, vmem_limit_bytes=56 * 2**20),
        cost_estimate=pl.CostEstimate(
            flops=2 * rows * depth * (qkv_width + width), bytes_accessed=150 * 2**20, transcendentals=rows * 2048),
    )(prompt_of, d_attn, full, queries, kv, other, context, sums, angles, tokens)


FINAL_ROWS = 128
SHARE_ROWS = 32


def final_kernel(
    sums_ref, token_ref, middle_ref, layer_ref, gain_ref, gate_ref, up_ref, down_ref, side_ref,
    layer_out, grad_ref, gate_out, up_out, down_out, query_out, key_out, value_out, out_out,
):
    values = token_ref[...].astype(jnp.float32)
    inverse = lax.rsqrt(jnp.mean(values * values, axis=-1, keepdims=True) + EPS)
    normed = values * inverse
    scaled = sums_ref[...].astype(jnp.float32) * gain_ref[0:1, :]
    backed = inverse * (scaled - normed * jnp.mean(scaled * normed, axis=-1, keepdims=True))
    grad_ref[...] = middle_ref[...].astype(jnp.float32) + backed
    layer_out[...] = layer_ref[...]
    for source, target in ((gate_ref, gate_out), (up_ref, up_out), (down_ref, down_out)):
        target[...] = source[...].astype(jnp.float32)
    low = 0
    for target in (query_out, key_out, value_out, out_out):
        target[...] = side_ref[:, low : low + target.shape[1]].astype(jnp.float32)
        low += target.shape[1]


def final_block(sums, tokens, middle, layer, gains, gate, up, down, side, query_width):
    rows, depth = tokens.shape
    share, units = gate.shape
    steps = share // SHARE_ROWS
    blocks = -(-rows // FINAL_ROWS)
    assert blocks <= steps
    f32 = jnp.float32

    def wide(width):
        return pl.BlockSpec((FINAL_ROWS, width), lambda i: (jnp.minimum(i, blocks - 1), 0))

    def thin(width):
        return pl.BlockSpec((SHARE_ROWS, width), lambda i: (i, 0))

    widths = (units, units, units, query_width, HEAD, HEAD, query_width)
    return pl.pallas_call(
        final_kernel,
        grid=(steps,),
        out_shape=(jax.ShapeDtypeStruct((rows, depth), layer.dtype), jax.ShapeDtypeStruct((rows, depth), f32))
        + tuple(jax.ShapeDtypeStruct((share, width), f32) for width in widths),
        in_specs=[wide(depth)] * 4
        + [pl.BlockSpec(gains.shape, lambda i: (0, 0))]
        + [thin(units)] * 3
        + [thin(side.shape[1])],
        out_specs=(wide(depth),) * 2 + tuple(thin(width) for width in widths),
        compiler_params=pltpu.CompilerParams(vmem_limit_bytes=60 * 2**20),
    )(sums, tokens, middle, layer, gains, gate, up, down, side)


def normalize(values):
    return values * lax.rsqrt(jnp.mean(values * values, axis=-1, keepdims=True) + EPS)


def norm_back(values, gain, upstream):
    inverse = lax.rsqrt(jnp.mean(values * values, axis=-1, keepdims=True) + EPS)
    normed = values * inverse
    scaled = upstream * gain
    return inverse * (scaled - normed * jnp.mean(scaled * normed, axis=-1, keepdims=True))


def turn_back(values, places):
    half_width = values.shape[-1] // 2
    spectrum = THETA ** (-2.0 * jnp.arange(half_width, dtype=jnp.float32) / values.shape[-1])
    angles = places.astype(jnp.float32)[..., None] * spectrum
    angles = jnp.concatenate([angles, angles], axis=-1)[..., None, :]
    turned = jnp.concatenate([values[..., half_width:], -values[..., :half_width]], axis=-1)
    return values * jnp.cos(angles) + turned * jnp.sin(angles)


def rotate(values, places):
    half_width = values.shape[-1] // 2
    spectrum = THETA ** (-2.0 * jnp.arange(half_width, dtype=jnp.float32) / values.shape[-1])
    angles = places.astype(jnp.float32)[..., None] * spectrum
    angles = jnp.concatenate([angles, angles], axis=-1)[..., None, :]
    turned = jnp.concatenate([-values[..., half_width:], values[..., :half_width]], axis=-1)
    return values * jnp.cos(angles) + turned * jnp.sin(angles)


def visibility(micro_count, row_count, prompt_dev, prompt_all, cont_rows, seq_pos, owners):
    local_rows = jnp.arange(row_count)
    prompt_rows = local_rows < prompt_dev
    places_local = jnp.where(
        prompt_rows, seq_pos * prompt_dev + local_rows, prompt_all + local_rows - prompt_dev
    )
    micro_ids = jnp.arange(micro_count)
    row_micro = jnp.repeat(micro_ids, row_count)
    row_prompt = jnp.tile(prompt_rows, micro_count)
    row_place = jnp.tile(places_local, micro_count)
    first_slot = jnp.where(row_prompt, row_micro, jnp.repeat(owners, row_count))
    second_slot = jnp.where(row_prompt, -1, micro_count + row_micro)
    key_slot = jnp.concatenate(
        [jnp.repeat(micro_ids, prompt_all), micro_count + jnp.repeat(micro_ids, cont_rows)]
    )
    key_place = jnp.concatenate(
        [
            jnp.tile(jnp.arange(prompt_all), micro_count),
            prompt_all + jnp.tile(jnp.arange(cont_rows), micro_count),
        ]
    )
    matched = (key_slot[None, :] == first_slot[:, None]) | (
        key_slot[None, :] == second_slot[:, None]
    )
    return (matched & (key_place[None, :] <= row_place[:, None]), row_place)


def scores_for(query, key_rows, visible, score_scale):
    raw_scores = jnp.einsum("rd,kd->rk", query, key_rows, preferred_element_type=jnp.float32)
    curved = jnp.tanh(raw_scores * score_scale / SOFTCAP)
    return (curved, jnp.where(visible, SOFTCAP * curved, -1e30))


def per_device_general(
    tokens,
    cotangent,
    prompt_of,
    query_weight,
    key_weight,
    value_weight,
    out_weight,
    gate_weight,
    up_weight,
    down_weight,
    norm_gains,
):
    micro_count = tokens.shape[0]
    row_count = tokens.shape[2]
    model_width = tokens.shape[3]
    seq_count = lax.axis_size("seq")
    seq_pos = lax.axis_index("seq")
    prompt_dev = row_count - CONT
    prompt_all = prompt_dev * seq_count
    total_rows = micro_count * row_count
    score_scale = HEAD ** (-0.5)
    axes = ("dp", "seq")
    query_width = query_weight.shape[1]
    qkv_width = query_width + 2 * HEAD
    f32, bf16 = jnp.float32, jnp.bfloat16
    visible, places = visibility(
        micro_count, row_count, prompt_dev, prompt_all, CONT, seq_pos, prompt_of[:, 0]
    )
    side_weights = jnp.concatenate(
        [
            query_weight,
            key_weight,
            value_weight,
            jnp.pad(norm_gains.T, ((0, 0), (0, SIDE_PAD - norm_gains.shape[0]))),
        ],
        axis=1,
    )
    full_side = lax.all_gather(side_weights, axes, axis=0, tiled=True)
    full_qkv = full_side[:, :qkv_width]
    gain_float = full_side[:, qkv_width : qkv_width + 4].T.astype(f32)
    full_out = lax.all_gather(out_weight, axes, axis=1, tiled=True)
    full_gate = lax.all_gather(gate_weight, axes, axis=0, tiled=True)
    down_turned = down_weight.T
    full_up = lax.all_gather(up_weight, axes, axis=0, tiled=True)
    full_down = lax.all_gather(down_turned, axes, axis=0, tiled=True)
    inputs = tokens.reshape(total_rows, model_width).astype(f32)
    normed_in = (normalize(inputs) * gain_float[0]).astype(bf16)
    key_value = jnp.dot(normed_in, full_qkv[:, query_width:], preferred_element_type=f32)
    key_heads = key_value[:, :HEAD].reshape(total_rows, 1, HEAD)
    key_local = rotate(key_heads, places)[:, 0].astype(bf16)
    value_local = key_value[:, HEAD:].astype(bf16)
    key_grid = key_local.reshape(micro_count, row_count, HEAD)
    value_grid = value_local.reshape(micro_count, row_count, HEAD)
    own_pair = jnp.concatenate([key_grid[:, :prompt_dev], value_grid[:, :prompt_dev]], axis=2)
    prompt_pair = lax.all_gather(own_pair, "seq", axis=1, tiled=True)
    query_heads = jnp.dot(
        normed_in, full_qkv[:, :query_width], preferred_element_type=f32
    ).reshape(total_rows, -1, HEAD)
    query_rows = rotate(query_heads, places).astype(bf16)
    prompt_keys, prompt_values = prompt_pair[..., :HEAD], prompt_pair[..., HEAD:]
    key_rows = jnp.concatenate(
        [
            prompt_keys.reshape(micro_count * prompt_all, HEAD),
            key_grid[:, prompt_dev:].reshape(micro_count * CONT, HEAD),
        ],
        axis=0,
    )
    value_rows = jnp.concatenate(
        [
            prompt_values.reshape(micro_count * prompt_all, HEAD),
            value_grid[:, prompt_dev:].reshape(micro_count * CONT, HEAD),
        ],
        axis=0,
    )
    head_count = query_rows.shape[1]
    contexts = []
    log_sums = []
    for head_pos in range(head_count):
        curved, masked = scores_for(query_rows[:, head_pos], key_rows, visible, score_scale)
        row_peak = jnp.max(masked, axis=-1, keepdims=True)
        weights = jnp.exp(masked - row_peak)
        summed = jnp.sum(weights, axis=-1, keepdims=True)
        probs = (weights / summed).astype(bf16)
        contexts.append(jnp.dot(probs, value_rows, preferred_element_type=f32))
        log_sums.append(row_peak + jnp.log(summed))
    context = jnp.stack(contexts, axis=1).reshape(total_rows, -1).astype(bf16)
    attn_part = jnp.dot(context, full_out, preferred_element_type=f32).astype(bf16)
    block = ffn_block(
        attn_part.reshape(micro_count, row_count, model_width),
        tokens[:, 0],
        cotangent[:, 0],
        full_gate,
        full_up,
        full_down,
        jnp.pad(gain_float, ((0, 4), (0, 0))),
        0,
    )
    gain_sums = jnp.sum(block["gain_grad"].reshape(3, 8, model_width), axis=1)
    d_middle = block["d_middle"].reshape(total_rows, model_width).astype(f32)
    d_attn = block["d_attn"].reshape(total_rows, model_width)

    def scatter(grad, axis):
        return lax.psum_scatter(
            grad.astype(bf16), axes, scatter_dimension=axis, tiled=True
        ).astype(f32)

    share_down = scatter(block["grad_down"], 0).T
    share_gate = scatter(block["grad_gate"], 0)
    d_context = (
        jnp.einsum("rd,cd->rc", d_attn, full_out, preferred_element_type=f32)
        .astype(bf16)
        .reshape(total_rows, head_count, HEAD)
    )
    key_grad = jnp.zeros((key_rows.shape[0], HEAD), f32)
    value_grad = jnp.zeros((key_rows.shape[0], HEAD), f32)
    query_grads = []
    for head_pos in range(head_count):
        curved, masked = scores_for(query_rows[:, head_pos], key_rows, visible, score_scale)
        probs = jnp.where(visible, jnp.exp(masked - log_sums[head_pos]), 0.0)
        probs_low = probs.astype(bf16)
        d_probs = jnp.einsum(
            "rd,kd->rk", d_context[:, head_pos], value_rows, preferred_element_type=f32
        )
        inner_sum = jnp.sum(probs * d_probs, axis=-1, keepdims=True)
        d_scores = (probs * (d_probs - inner_sum) * score_scale * (1.0 - curved * curved)).astype(
            bf16
        )
        query_grads.append(jnp.dot(d_scores, key_rows, preferred_element_type=f32))
        key_grad = key_grad + jnp.einsum(
            "rk,rd->kd", d_scores, query_rows[:, head_pos], preferred_element_type=f32
        )
        value_grad = value_grad + jnp.einsum(
            "rk,rd->kd", probs_low, d_context[:, head_pos], preferred_element_type=f32
        )
    split_at = micro_count * prompt_all
    pair_grad = jnp.concatenate(
        [
            key_grad[:split_at].reshape(micro_count, prompt_all, HEAD),
            value_grad[:split_at].reshape(micro_count, prompt_all, HEAD),
        ],
        axis=2,
    )
    pair_grad = lax.psum_scatter(
        pair_grad.astype(bf16), "seq", scatter_dimension=1, tiled=True
    ).astype(f32)
    prompt_key_grad, prompt_value_grad = pair_grad[..., :HEAD], pair_grad[..., HEAD:]
    own_keys = jnp.concatenate(
        [prompt_key_grad, key_grad[split_at:].reshape(micro_count, CONT, HEAD)], axis=1
    ).reshape(total_rows, HEAD)
    own_values = jnp.concatenate(
        [prompt_value_grad, value_grad[split_at:].reshape(micro_count, CONT, HEAD)], axis=1
    ).reshape(total_rows, HEAD)
    d_query = turn_back(jnp.stack(query_grads, axis=1), places).reshape(total_rows, -1)
    d_key = turn_back(own_keys[:, None, :], places).reshape(total_rows, HEAD)
    d_qkv = jnp.concatenate([d_query, d_key, own_values], axis=1).astype(bf16)
    attn_part = jnp.einsum("rc,dc->rd", d_qkv, full_qkv, preferred_element_type=f32)
    gain_first = jnp.sum(attn_part * normalize(inputs), axis=0)
    grad_gains = jnp.concatenate(
        [gain_first[None], jnp.where(lax.axis_index("tensor") == 0, gain_sums, 0.0)], axis=0
    )
    gain_cols = jnp.pad(grad_gains.T, ((0, 0), (0, SIDE_PAD - grad_gains.shape[0])))
    attn_part = attn_part.astype(bf16)
    share_up = scatter(block["grad_up"], 0)
    share_out = scatter(
        jnp.einsum("rc,rd->cd", context, d_attn, preferred_element_type=f32), 1
    )
    side_grad = jnp.einsum("rd,rc->dc", normed_in, d_qkv, preferred_element_type=f32)
    d_normed = chain_sum(attn_part, 1)
    share_side = scatter(jnp.concatenate([side_grad, gain_cols], axis=1), 0)
    share_gains = lax.psum(share_side[:, qkv_width : qkv_width + 4].T, "tensor")
    d_in_norm = norm_back(inputs, gain_float[0], d_normed.astype(f32))
    input_grad = d_middle + d_in_norm
    return (
        block["out"].reshape(tokens.shape),
        input_grad.reshape(tokens.shape),
        share_side[:, :query_width],
        share_side[:, query_width : query_width + HEAD],
        share_side[:, query_width + HEAD : qkv_width],
        share_out,
        share_gate,
        share_up,
        share_down,
        share_gains,
    )


def per_device_planar(
    tokens,
    cotangent,
    prompt_of,
    query_weight,
    key_weight,
    value_weight,
    out_weight,
    gate_weight,
    up_weight,
    down_weight,
    norm_gains,
):
    micro_count, _, row_count, model_width = tokens.shape
    seq_pos = lax.axis_index("seq")
    total_rows = micro_count * row_count
    axes = ("dp", "seq")
    query_width = query_weight.shape[1]
    qkv_width = query_width + 2 * HEAD
    heads = query_width // HEAD
    bf16 = jnp.bfloat16
    owners = prompt_of[:, 0]
    angles = turn_angles(row_count, seq_pos)
    flat = tokens.reshape(total_rows, model_width)
    own_side = jnp.concatenate(
        [
            query_weight,
            key_weight,
            value_weight,
            jnp.pad(norm_gains.T, ((0, 0), (0, SIDE_PAD - norm_gains.shape[0]))),
            out_weight.T,
        ],
        axis=1,
    )
    attn_part, context, queries, own_kv, other_kv, sums, normed_in, full_side, gains = head_block(
        flat, own_side, angles, owners, heads, CONT, 0
    )
    stacked = (micro_count, row_count, model_width)
    block = ffn_block(
        attn_part.reshape(stacked),
        tokens[:, 0],
        cotangent[:, 0],
        gate_weight,
        up_weight,
        down_weight.T,
        gains,
        1,
    )
    gain_sums = jnp.sum(block["gain_grad"].reshape(3, 8, model_width), axis=1)
    d_attn = block["d_attn"].reshape(total_rows, model_width)

    def scatter(grad):
        return lax.psum_scatter(grad, axes, scatter_dimension=0, tiled=True)

    share_down = scatter(block["grad_down"])
    d_qkv, attn_part, gain_first = back_block(
        owners, d_attn, full_side, queries, own_kv, other_kv, context, sums, angles, flat, CONT, 2
    )
    grad_gains = jnp.concatenate(
        [gain_first[:1], jnp.where(lax.axis_index("tensor") == 0, gain_sums, 0.0)], axis=0
    )
    gain_cols = jnp.pad(grad_gains.T, ((0, 0), (0, SIDE_PAD - grad_gains.shape[0])))
    d_normed, share_gate, share_up, share_side, share_gains = tail_block(
        attn_part.reshape(stacked),
        block["grad_gate"],
        block["grad_up"],
        normed_in,
        d_attn,
        d_qkv,
        context,
        gain_cols.astype(bf16),
        3,
    )
    d_normed, share_down = lax.optimization_barrier((d_normed, share_down))
    layer, input_grad, *grads = final_block(
        d_normed.reshape(total_rows, model_width),
        flat,
        block["d_middle"].reshape(total_rows, model_width),
        block["out"].reshape(total_rows, model_width),
        gains,
        share_gate,
        share_up,
        share_down,
        share_side,
        query_width,
    )
    grad_gate, grad_up, grad_down, grad_query, grad_key, grad_value, grad_out = grads
    return (
        layer.reshape(tokens.shape),
        input_grad.reshape(tokens.shape),
        grad_query,
        grad_key,
        grad_value,
        grad_out.T,
        grad_gate,
        grad_up,
        grad_down.T,
        share_gains[:, :4].T,
    )


def turn_angles(row_count, seq_pos):
    half_width = HEAD // 2
    rows = jnp.arange(row_count)
    prompt_dev = row_count - CONT
    prompt_all = prompt_dev * lax.axis_size("seq")
    places = jnp.where(
        rows < prompt_dev, seq_pos * prompt_dev + rows, prompt_all + rows - prompt_dev
    )
    spectrum = THETA ** (-2.0 * jnp.arange(half_width, dtype=jnp.float32) / HEAD)
    angles = places.astype(jnp.float32)[:, None] * spectrum
    return jnp.concatenate([jnp.cos(angles), jnp.sin(angles)], axis=1)


def per_device(*arrays):
    if lax.axis_size("dp") == 4 and lax.axis_size("seq") == 2:
        return per_device_planar(*arrays)
    return per_device_general(*arrays)


def solution(mesh):
    placed = (
        P("dp", "seq", None, None),
        P("dp", "seq", None, None),
        P("dp", "seq"),
        P(("dp", "seq"), "tensor"),
        P(("dp", "seq"), "tensor"),
        P(("dp", "seq"), "tensor"),
        P("tensor", ("dp", "seq")),
        P(("dp", "seq"), "tensor"),
        P(("dp", "seq"), "tensor"),
        P("tensor", ("dp", "seq")),
        P(None, ("dp", "seq")),
    )
    return jax.shard_map(
        per_device,
        mesh=mesh,
        in_specs=placed,
        out_specs=(
            P("dp", "seq", None, None),
            P("dp", "seq", None, None),
            P(("dp", "seq"), "tensor"),
            P(("dp", "seq"), "tensor"),
            P(("dp", "seq"), "tensor"),
            P("tensor", ("dp", "seq")),
            P(("dp", "seq"), "tensor"),
            P(("dp", "seq"), "tensor"),
            P("tensor", ("dp", "seq")),
            P(None, ("dp", "seq")),
        ),
        check_vma=False,
    )
```
